32 devices in a mesh: gz: 8 (over z, core), xy: 4 (over y, x).
Axes of the slice: x: 2, y: 2, z: 4, core: 2. Of those that a mesh axis runs over, the one named last changes fastest.
Arguments:
- density: float32 [512, 32, 512], P('xy', 'gz'), may hold values from 0.5 to 2
- momentum: float32 [3, 512, 32, 512], P(None, 'xy', 'gz'), may hold values from -3 to 3
- magnetic: float32 [3, 512, 32, 512], P(None, 'xy', 'gz'), may hold values from -3 to 3
- arm_potential: float32 [512, 512], P('xy'), may hold values from -10 to 10
- sn_cells: int32 [32, 3], P(('gz', 'xy')), may hold values from 0 to 511, as said below
- sn_counts: int32 [32], P(('gz', 'xy')), may hold values from 0 to 3
Outputs:
- new_density: float32 [512, 32, 512], P('xy', 'gz')
- new_momentum: float32 [3, 512, 32, 512], P(None, 'xy', 'gz')
- new_magnetic: float32 [3, 512, 32, 512], P(None, 'xy', 'gz')
- density_modes: float32 [2, 32, 512, 512], P(None, 'gz', 'xy')
The draws below stay inside these ranges and needn't reach their ends.
Inputs may be any that keep to these rules, and one draw needn't show every extreme that they name: `sn_cells`: row e is the centre of an event held by device e // 1 of the joined axes gz+xy (gz slowest); its x lies among that device's 128 x rows and its z among its 4 z planes. `sn_counts`: 0 marks an empty slot.
All inputs are finite; a program needn't handle non-finite values.
Results may differ from the reference program's by a relative error of at most 0.00023.
Values sent between devices are 32-bit elements; how exact they have to be, the bound alone decides.
No kernel may reach another device: no remote copies, remote signals or barrier semaphores. Data moves between devices by JAX's collectives and lax.ppermute only.
A program may use at most 384 MiB of HBM per device.

```python
import math
import jax
import jax.numpy as jnp
from jax import lax

NX = 512
NY = 512
ZPL = 4
EV_DEV = 1
SUPERNOVA_RADIUS = 16
NZ = 32
XROWS = 128
EVENTS = 32


def draw_sn_cells(key, part):
    slot_ids = jnp.arange(EVENTS, dtype=jnp.int32)
    owner = slot_ids // EV_DEV
    across = NX // XROWS
    tile_row = owner % across
    tile_plane = owner // across
    keys = jax.random.split(key, 3)
    cell_row = tile_row * XROWS + jax.random.randint(keys[0], (EVENTS,), 0, XROWS, dtype=jnp.int32)
    cell_col = jax.random.randint(keys[1], (EVENTS,), 0, NY, dtype=jnp.int32)
    cell_col = jnp.where(slot_ids == 0, 0, cell_col).astype(jnp.int32)
    cell_col = jnp.where(slot_ids == EVENTS - 1, NY - 1, cell_col).astype(jnp.int32)
    cell_plane = tile_plane * ZPL + jax.random.randint(keys[2], (EVENTS,), 0, ZPL, dtype=jnp.int32)
    return jnp.stack([cell_row, cell_col, cell_plane], axis=1)


def set_ends(array, key, least, largest):
    longest = array.shape.index(max(array.shape))
    spots = []
    for shift in (0, 1):
        where = [jax.random.randint(jax.random.fold_in(key, axis), (), 0, length) for axis, length in enumerate(array.shape)]
        where[longest] = (where[longest] + shift) % array.shape[longest]
        spots.append(tuple(where))
    return array.at[spots[0]].set(least).at[spots[1]].set(largest)


def block_levels(key, shape, pieces, least, top_value):
    def one(dim, shards_of):
        heights = jax.random.uniform(jax.random.fold_in(jax.random.fold_in(key, 6), dim), (shards_of,), jnp.float32, least / len(pieces), top_value / len(pieces))
        return jnp.repeat(jnp.exp(heights), shape[dim] // shards_of).reshape((-1,) + (1,) * (len(shape) - dim - 1))

    gain = one(*pieces[0])
    for cut in pieces[1:]:
        gain = gain * one(*cut)
    return gain


def normal_values(own_key, dims, scale, bound, shards=(), kind=jnp.bfloat16):
    factor_of = block_levels(own_key, dims, shards, -0.22, 0.18) if shards else 1.0
    drawn = jax.random.normal(own_key, dims, jnp.float32) * scale * factor_of
    return jnp.minimum(jnp.maximum(drawn, -bound), bound).astype(kind)


def setup_inputs(seed: int = 0) -> dict:
    key_list = jax.random.split(jax.random.key(seed), 7)
    density = jnp.clip(jnp.exp(math.log(2.0) - 1.3862944 * jax.random.uniform(key_list[0], (NX, NZ, NY), jnp.float32) ** block_levels(key_list[0], (NX, NZ, NY), ((0, 4), (1, 8)), -0.2, 0.2)), 0.5, 2.0)
    momentum = normal_values(key_list[1], (3, NX, NZ, NY), 0.5, 3.0, ((1, 4), (2, 8)), jnp.float32)
    magnetic = normal_values(key_list[2], (3, NX, NZ, NY), 0.5, 3.0, ((1, 4), (2, 8)), jnp.float32)
    arm_potential = normal_values(key_list[3], (NX, NY), 2.0, 10.0, ((0, 4),), jnp.float32)
    sn_cells = draw_sn_cells(jax.random.fold_in(key_list[6], 71), 0)
    sn_counts = set_ends(jax.random.randint(key_list[5], (EVENTS,), 0, 4), jax.random.fold_in(key_list[5], 1), 0, 3).astype(jnp.int32)
    return {"density": density, "momentum": momentum, "magnetic": magnetic, "arm_potential": arm_potential, "sn_cells": sn_cells, "sn_counts": sn_counts}


sound_square = 1.0
time_step = 0.1
diffusion = 0.05
mass_yield = 1.0
push_yield = 2.0

def fluxes(mass_density, momenta, induction, direction):
    velocity = [momenta[component] / mass_density for component in range(3)]
    pressure = sound_square * mass_density + 0.5 * (induction[0] * induction[0] + induction[1] * induction[1] + induction[2] * induction[2])
    result = [momenta[direction]]
    for component in range(3):
        term = momenta[component] * velocity[direction] - induction[component] * induction[direction]
        if component == direction:
            term = term + pressure
        result.append(term)
    for component in range(3):
        result.append(velocity[direction] * induction[component] - induction[direction] * velocity[component])
    return result

def central_wrap(field, axis):
    return (jnp.roll(field, 2, axis) - 8.0 * jnp.roll(field, 1, axis) + 8.0 * jnp.roll(field, -1, axis) - jnp.roll(field, -2, axis)) / 12.0

def second_wrap(field, axis):
    return jnp.roll(field, 1, axis) + jnp.roll(field, -1, axis) - 2.0 * field

def reference(density, momentum, magnetic, arm_potential, sn_cells, sn_counts):
    window = jnp.arange(-SUPERNOVA_RADIUS, SUPERNOVA_RADIUS, dtype=jnp.int32)
    radial_distance = window.astype(jnp.float32)
    radius_squared = radial_distance[:, None, None] * radial_distance[:, None, None] + radial_distance[None, :, None] * radial_distance[None, :, None] + radial_distance[None, None, :] * radial_distance[None, None, :]
    blast_profile = jnp.maximum(1.0 - radius_squared / (SUPERNOVA_RADIUS * SUPERNOVA_RADIUS), 0.0)
    impulse = push_yield / SUPERNOVA_RADIUS * blast_profile
    blocks = jnp.stack([mass_yield * blast_profile, impulse * radial_distance[:, None, None], impulse * radial_distance[None, None, :], impulse * radial_distance[None, :, None]])

    def add_event(number, total):
        centre = sn_cells[number]
        row_ids = ((centre[0] + window) % NX).astype(jnp.int32)
        col_ids = ((centre[1] + window) % NY).astype(jnp.int32)
        plane_ids = ((centre[2] + window) % NZ).astype(jnp.int32)
        weighting = sn_counts[number].astype(jnp.float32)
        return total.at[:, row_ids[:, None, None], plane_ids[None, :, None], col_ids[None, None, :]].add(weighting * blocks)
    source = lax.fori_loop(0, sn_counts.shape[0], add_event, jnp.zeros((4, NX, NZ, NY), jnp.float32))
    mass_density = density + source[0]
    momenta = [momentum[component] + source[1 + component] for component in range(3)]
    induction = [magnetic[component] for component in range(3)]
    fields_all = [mass_density] + momenta + induction
    axes = (0, 2, 1)
    updated = list(fields_all)
    for direction in range(3):
        flux_list = fluxes(mass_density, momenta, induction, direction)
        for component in range(7):
            updated[component] = updated[component] - time_step * central_wrap(flux_list[component], axes[direction]) + diffusion * second_wrap(fields_all[component], axes[direction])
    potential = arm_potential[:, None, :]
    updated[1] = updated[1] - time_step * mass_density * central_wrap(potential, 0)
    updated[2] = updated[2] - time_step * mass_density * central_wrap(potential, 2)
    spectrum = jnp.fft.fft2(updated[0], axes=(0, 2)) / math.sqrt(NX * NY)
    stacked = jnp.stack([jnp.real(spectrum), jnp.imag(spectrum)]).astype(jnp.float32)
    stacked = jnp.transpose(stacked, (0, 2, 3, 1))
    stacked = stacked.at[:, :, 0, 0].set(0.0)
    return (updated[0], jnp.stack(updated[1:4]), jnp.stack(updated[4:7]), stacked)
```

```python
import math

import jax
import jax.numpy as jnp
from jax import lax
from jax.sharding import PartitionSpec as P

NX = 512
NY = 512
SUPERNOVA_RADIUS = 16


sound_square = 1.0
time_step = 0.1
diffusion = 0.05
mass_yield = 1.0
push_yield = 2.0


def neighbours(array, axis, dim, width):
    peers, length = (lax.axis_size(axis), array.shape[dim])
    up = [(i, (i + 1) % peers) for i in range(peers)]
    down = [(j, i) for i, j in up]
    last = lax.slice_in_dim(array, length - width, length, axis=dim)
    leading = lax.slice_in_dim(array, 0, width, axis=dim)
    return lax.ppermute(last, axis, up), lax.ppermute(leading, axis, down)


def fluxes(mass_density, momenta, induction, direction):
    velocity = [momenta[component] / mass_density for component in range(3)]
    pressure = sound_square * mass_density + 0.5 * (
        induction[0] * induction[0] + induction[1] * induction[1] + induction[2] * induction[2]
    )
    result = [momenta[direction]]
    for component in range(3):
        term = (
            momenta[component] * velocity[direction] - induction[component] * induction[direction]
        )
        if component == direction:
            term = term + pressure
        result.append(term)
    for component in range(3):
        result.append(
            velocity[direction] * induction[component] - induction[direction] * velocity[component]
        )
    return jnp.stack(result)


def pick_rows(field, start, count, axis):
    return lax.slice_in_dim(field, start, start + count, axis=axis)


def central_pad(field, axis):
    count = field.shape[axis] - 4
    return (
        pick_rows(field, 0, count, axis)
        - 8.0 * pick_rows(field, 1, count, axis)
        + 8.0 * pick_rows(field, 3, count, axis)
        - pick_rows(field, 4, count, axis)
    ) / 12.0


def second_pad(field, axis):
    count = field.shape[axis] - 4
    return (
        pick_rows(field, 1, count, axis)
        + pick_rows(field, 3, count, axis)
        - 2.0 * pick_rows(field, 2, count, axis)
    )


def central_wrap(field, axis):
    return (
        jnp.roll(field, 2, axis)
        - 8.0 * jnp.roll(field, 1, axis)
        + 8.0 * jnp.roll(field, -1, axis)
        - jnp.roll(field, -2, axis)
    ) / 12.0


def second_wrap(field, axis):
    return jnp.roll(field, 1, axis) + jnp.roll(field, -1, axis) - 2.0 * field


def deposit(event_cells, counts, row_start, row_count, plane_start, planes, depth_all):
    centre_row = event_cells[:, 0][:, None]
    centre_col = event_cells[:, 1][:, None]
    centre_plane = event_cells[:, 2][:, None]
    along_row = row_start + jnp.arange(row_count, dtype=jnp.int32)
    along_plane = plane_start + jnp.arange(planes, dtype=jnp.int32)
    along_col = jnp.arange(NY, dtype=jnp.int32)
    row_offset = ((along_row[None, :] - centre_row + NX // 2) % NX - NX // 2).astype(jnp.float32)[
        :, :, None, None
    ]
    plane_offset = (
        (along_plane[None, :] - centre_plane + depth_all // 2) % depth_all - depth_all // 2
    ).astype(jnp.float32)[:, None, :, None]
    column_offset = ((along_col[None, :] - centre_col + NY // 2) % NY - NY // 2).astype(
        jnp.float32
    )[:, None, None, :]
    radius_squared = (
        row_offset * row_offset + plane_offset * plane_offset + column_offset * column_offset
    )
    weights = (
        jnp.maximum(1.0 - radius_squared / (SUPERNOVA_RADIUS * SUPERNOVA_RADIUS), 0.0)
        * counts.astype(jnp.float32)[:, None, None, None]
    )
    impulse = push_yield / SUPERNOVA_RADIUS
    return jnp.stack(
        [
            mass_yield * jnp.sum(weights, axis=0),
            impulse * jnp.sum(weights * row_offset, axis=0),
            impulse * jnp.sum(weights * column_offset, axis=0),
            impulse * jnp.sum(weights * plane_offset, axis=0),
        ]
    )


def on_device(density, momentum, magnetic, arm_potential, sn_cells, sn_counts):
    row_count, planes, columns = density.shape
    layers = lax.axis_size("gz")
    tile_row = lax.axis_index("xy")
    tile_plane = lax.axis_index("gz")
    depth_all = planes * layers
    events = jnp.concatenate([sn_cells, sn_counts[:, None]], axis=1)
    events = lax.all_gather(events, ("gz", "xy"), axis=0, tiled=True)
    below_a, above_a = neighbours(jnp.stack([density, momentum[2]]), "gz", 2, 2)
    below_b, above_b = neighbours(jnp.concatenate([momentum[:2], magnetic]), "gz", 2, 2)
    raw = jnp.concatenate([density[None], momentum, magnetic], axis=0)
    before, after = neighbours(raw, "xy", 1, 2)
    p_before, p_after = neighbours(arm_potential, "xy", 0, 2)
    row_start = tile_row * row_count
    plane_start = tile_plane * planes
    source_x = deposit(events[:, :3], events[:, 3], row_start - 2, row_count + 4, plane_start, planes, depth_all)

    def near(a, b, start):
        field = jnp.concatenate([a[:1], b[:2], a[1:], b[2:]], axis=0)
        extra = deposit(events[:, :3], events[:, 3], row_start, row_count, start, 2, depth_all)
        return field.at[:4].add(extra)

    along_x = jnp.concatenate([before, raw, after], axis=1)
    along_x = along_x.at[:4].add(source_x)
    interior = along_x[:, 2:-2]
    along_z = jnp.concatenate(
        [near(below_a, below_b, plane_start - 2), interior, near(above_a, above_b, plane_start + planes)], axis=2
    )
    mass_density = interior[0]
    potential = jnp.concatenate([p_before, arm_potential, p_after], axis=0)
    divergence = central_pad(fluxes(along_x[0], along_x[1:4], along_x[4:7], 0), 1)
    divergence = divergence + central_wrap(fluxes(interior[0], interior[1:4], interior[4:7], 1), 3)
    divergence = divergence + central_pad(fluxes(along_z[0], along_z[1:4], along_z[4:7], 2), 2)
    smooth = second_pad(along_x, 1) + second_wrap(interior, 3) + second_pad(along_z, 2)
    updated = interior - time_step * divergence + diffusion * smooth
    slope_x = central_pad(potential, 0)[:, None, :]
    slope_y = central_wrap(arm_potential, 1)[:, None, :]
    new_density = updated[0]
    new_momentum = jnp.stack(
        [
            updated[1] - time_step * mass_density * slope_x,
            updated[2] - time_step * mass_density * slope_y,
            updated[3],
        ]
    )
    new_magnetic = updated[4:7]
    wave_y = jnp.arange(NY, dtype=jnp.int32)
    angle_y = (wave_y[:, None] * wave_y[None, :] % NY).astype(jnp.float32) * (2.0 * math.pi / NY)
    cosine_y = jnp.cos(angle_y)
    sine_y = jnp.sin(angle_y)
    wave_x = jnp.arange(NX, dtype=jnp.int32)
    angle_x = (wave_x[:, None] * wave_x[None, :] % NX).astype(jnp.float32) * (2.0 * math.pi / NX)
    cosine_x = jnp.cos(angle_x)
    sine_x = jnp.sin(angle_x)
    real_y = jnp.einsum("xzy,yk->zkx", new_density, cosine_y, precision=lax.Precision.HIGH)
    imag_y = -jnp.einsum("xzy,yk->zkx", new_density, sine_y, precision=lax.Precision.HIGH)
    stacked = jnp.stack([real_y, imag_y])
    portion = lax.all_to_all(stacked, "xy", split_axis=2, concat_axis=3, tiled=True)
    real_part = portion[0]
    imag_part = portion[1]
    out_real = jnp.einsum(
        "zkx,xj->zkj", real_part, cosine_x, precision=lax.Precision.HIGH
    ) + jnp.einsum("zkx,xj->zkj", imag_part, sine_x, precision=lax.Precision.HIGH)
    out_imag = jnp.einsum(
        "zkx,xj->zkj", imag_part, cosine_x, precision=lax.Precision.HIGH
    ) - jnp.einsum("zkx,xj->zkj", real_part, sine_x, precision=lax.Precision.HIGH)
    spectrum = jnp.stack([out_real, out_imag])
    band = spectrum.shape[2]
    wave_ky = tile_row * band + jnp.arange(band, dtype=jnp.int32)
    keep = jnp.where((wave_ky[:, None] == 0) & (wave_x[None, :] == 0), 0.0, 1.0)
    spectrum = spectrum * (keep / math.sqrt(NX * NY))
    return (new_density, new_momentum, new_magnetic, spectrum)


def solution(mesh):
    in_specs = (
        P("xy", "gz", None),
        P(None, "xy", "gz", None),
        P(None, "xy", "gz", None),
        P("xy", None),
        P(("gz", "xy"), None),
        P(("gz", "xy")),
    )
    out_specs = (
        P("xy", "gz", None),
        P(None, "xy", "gz", None),
        P(None, "xy", "gz", None),
        P(None, "gz", "xy", None),
    )
    return jax.shard_map(
        on_device, mesh=mesh, in_specs=in_specs, out_specs=out_specs, check_vma=False
    )
```

```python
import functools
import math

import jax
import jax.numpy as jnp
import ml_dtypes
import numpy as np
from jax import lax
from jax.experimental import pallas as pl
from jax.experimental.pallas import tpu as pltpu
from jax.sharding import PartitionSpec as P

NX = 512
RADIUS = 16
IMPULSE = 2.0 / 16
TIME_STEP = 0.1
DIFFUSION = 0.05
NEAR = 8.0 * TIME_STEP / 12.0
FAR = TIME_STEP / 12.0
VMEM = 56 * 1024 * 1024


def pair(ref, *index):
    return jnp.concatenate([ref[(*index[:-1], 0, index[-1])], ref[(*index[:-1], 1, index[-1])]], axis=0)


def unpair(ref, value, *index):
    ref[(*index[:-1], 0, index[-1])] = value[:4]
    ref[(*index[:-1], 1, index[-1])] = value[4:]


def slots(shape):
    sub = lax.broadcasted_iota(jnp.int32, shape, len(shape) - 2)
    return jnp.where(sub >= 4, sub - 4, sub)


def turn(value, shift, axis):
    return pltpu.roll(value, shift % value.shape[axis], axis)


def gather_planes(values, plane):
    slot = slots(values[0].shape)
    out = turn(values[-1], len(values) - 1 - plane, 0)
    for c in reversed(range(len(values) - 1)):
        out = jnp.where(slot == c, turn(values[c], c - plane, 0), out)
    return out


def fluxes(rho, m, b, k):
    inv = 1.0 / rho
    v = [m[i] * inv for i in range(3)]
    total = rho + 0.5 * (b[0] * b[0] + b[1] * b[1] + b[2] * b[2])
    push = [m[i] * v[k] - b[i] * b[k] + (total if i == k else 0.0) for i in range(3)]
    turned = [None if i == k else v[k] * b[i] - b[k] * v[i] for i in range(3)]
    return push + turned


def pack_kernel(rho_ref, mz_ref, bx_ref, up_ref, down_ref):
    half = rho_ref.shape[1]

    def body(p, _):
        rho, mz, bx = pair(rho_ref, p), pair(mz_ref, 0, p), pair(bx_ref, 0, p)
        slot = slots(rho.shape)
        up = jnp.where(slot == 2, mz, gather_planes([rho, mz, mz, bx], 3))
        down = jnp.where(slot == 2, turn(mz, 1, 0), gather_planes([rho, mz, mz, bx], 0))
        unpair(up_ref, up, p)
        unpair(down_ref, down, p)
        return 0

    lax.fori_loop(0, half, body, 0)


def state_kernel(
    ev_ref, at_ref, rho_ref, mom_ref, mag_ref, before_ref, after_ref,
    u_ref, sb_ref, sa_ref, up_near, down_near, up_far, down_far, up_last, down_last, *, depth,
):
    half, ny = rho_ref.shape[1], rho_ref.shape[3]
    rows, events = 2 * half, ev_ref.shape[0] // 4
    row_start, plane_start = at_ref[0], at_ref[1]

    def raw(f, h, p):
        if f == 0:
            return rho_ref[h, p]
        return mom_ref[f - 1, h, p] if f < 4 else mag_ref[f - 4, h, p]

    def fill(p, _):
        for f in range(7):
            u_ref[f, p + 2] = jnp.concatenate([raw(f, 0, p), raw(f, 1, p)], axis=0)
        return 0

    lax.fori_loop(0, half, fill, 0)
    for f in range(7):
        for j in range(2):
            u_ref[f, j] = jnp.concatenate([before_ref[f, j], raw(f, 0, half - 2 + j)], axis=0)
            u_ref[f, half + 2 + j] = jnp.concatenate([raw(f, 1, j), after_ref[f, j]], axis=0)
    sb_ref[...] = jnp.zeros_like(sb_ref)
    sa_ref[...] = jnp.zeros_like(sa_ref)

    shape = (4, 8, 128)
    slot = slots(shape)
    sub = lax.broadcasted_iota(jnp.int32, shape, 1)
    step = lax.broadcasted_iota(jnp.int32, shape, 0)
    lane = lax.broadcasted_iota(jnp.int32, shape, 2)

    def wrapped(distance, size):
        distance = jnp.where(distance >= size // 2, distance - size, distance)
        return jnp.where(distance < -(size // 2), distance + size, distance)

    def event(e, _):
        row, col, plane, count = (ev_ref[4 * e + i] for i in range(4))
        rel = wrapped(row - row_start - half, NX)
        rel = rel + half

        @pl.when((count > 0) & (rel > -2 - RADIUS) & (rel < rows + 2 + RADIUS))
        def _():
            base = plane_start - plane
            dz = wrapped(slot + base, depth).astype(jnp.float32)
            dzb = wrapped(jnp.where(slot == 2, -2, -1) + base, depth).astype(jnp.float32)
            dza = wrapped(jnp.where(slot == 2, 5, 4) + base, depth).astype(jnp.float32)
            share = lambda d: jnp.where(slot == 0, 1.0, jnp.where(slot == 3, 0.0, IMPULSE * d))
            first = jnp.bitwise_and(col - RADIUS, ny - 1) // 128
            second = jnp.bitwise_and(col + RADIUS - 1, ny - 1) // 128

            def tile(t, _):
                index = jnp.where(t == 0, first, second)
                lanes = pl.ds(pl.multiple_of(index * 128, 128), 128)
                dy = wrapped(lane + index * 128 - col, ny).astype(jnp.float32)
                dy2 = dy * dy
                for h in range(2):
                    weight = jnp.where((sub >= 4) == (h == 1), count, 0).astype(jnp.float32)
                    low = jnp.clip(rel - RADIUS + 1 - h * half + 2, 0, half + 4) // 4
                    high = (jnp.clip(rel + RADIUS - 1 - h * half + 2, -1, half + 3) + 4) // 4

                    def chunk(n, _):
                        q = pl.ds(n * 4, 4)
                        dx = (step + (n * 4 - 2 + h * half - rel)).astype(jnp.float32)
                        flat = dx * dx + dy2
                        size = lambda d: jnp.maximum(1.0 - (flat + d * d) * (1.0 / (RADIUS * RADIUS)), 0.0) * weight
                        w = size(dz)
                        u_ref[0, q, :, lanes] += w
                        w = w * IMPULSE
                        u_ref[1, q, :, lanes] += w * dx
                        u_ref[2, q, :, lanes] += w * dy
                        u_ref[3, q, :, lanes] += w * dz
                        sb_ref[q, :, lanes] += size(dzb) * share(dzb)
                        sa_ref[q, :, lanes] += size(dza) * share(dza)
                        return 0

                    lax.fori_loop(low, high, chunk, 0)
                return 0

            lax.fori_loop(0, jnp.where(first == second, 1, 2), tile, 0)

        return 0

    lax.fori_loop(0, events, event, 0)

    def messages(p, _):
        u = [u_ref[f, p + 2] for f in range(7)]
        near = [u[1], u[2], u[5], u[6]]
        unpair(up_near, gather_planes(near, 3), p)
        unpair(down_near, gather_planes(near, 0), p)
        f = fluxes(u[0], u[1:4], u[4:7], 2)
        unpair(up_far, gather_planes(f[:4], 2), p)
        unpair(down_far, gather_planes(f[:4], 1), p)
        for ref, plane in ((up_last, 2), (down_last, 1)):
            low, high = turn(f[4], -plane, 0), turn(f[4], -plane - 3, 0)
            ref[p] = jnp.where(slots(low.shape) == 0, low, high)[:2]
        return 0

    lax.fori_loop(0, half, messages, 0)


def ends(below, above, c, fill):
    slot = slots(below.shape)
    rest = jnp.where(slot == 3, turn(above, 3 - c, 0), fill)
    return jnp.where(slot == 0, turn(below, -c, 0), rest)


def signs(shape):
    slot = slots(shape)
    return jnp.where(slot == 0, 1.0, jnp.where(slot == 3, -1.0, 0.0))


def along_y(f, u):
    low, high = NEAR * f + DIFFUSION * u, DIFFUSION * u - NEAR * f
    far = FAR * f
    return turn(low, 1, 1) + turn(high, -1, 1) + turn(far, -2, 1) - turn(far, 2, 1)


def along_z(f, u):
    slot = slots(u.shape)
    part = lambda keep, v: jnp.where(keep, v, 0.0)
    if f is None:
        return part(slot >= 1, turn(DIFFUSION * u, 1, 0)) + part(slot <= 2, turn(DIFFUSION * u, -1, 0))
    low, high = NEAR * f + DIFFUSION * u, DIFFUSION * u - NEAR * f
    far = FAR * f
    return (
        part(slot >= 1, turn(low, 1, 0)) + part(slot <= 2, turn(high, -1, 0))
        + part(slot <= 1, turn(far, -2, 0)) - part(slot >= 2, turn(far, 2, 0))
    )


def near_planes(f, u, sign):
    outer = DIFFUSION * u
    if f is None:
        return outer
    slot = slots(u.shape)
    t = (FAR * sign) * f
    inner = jnp.where(slot == 1, turn(t, 1, 0), jnp.where(slot == 2, turn(t, -1, 0), 0.0))
    return outer + 8.0 * t - inner


def density_kernel(u_ref, below_ref, above_ref, sb_ref, sa_ref, order_ref, high_ref, low_ref, out_ref, wave_ref, d_ref):
    half = below_ref.shape[1]
    rows = 2 * half

    def body(p, _):
        rho, my, mz = u_ref[0, p + 2], u_ref[2, p + 2], u_ref[3, p + 2]
        below, above = pair(below_ref, p) + sb_ref[p + 2], pair(above_ref, p) + sa_ref[p + 2]
        slot, sign = slots(rho.shape), signs(rho.shape)
        new = rho * (1.0 - 6.0 * DIFFUSION)
        new += DIFFUSION * (u_ref[0, p + 1] + u_ref[0, p + 3])
        new += NEAR * (u_ref[1, p + 1] - u_ref[1, p + 3]) + FAR * (u_ref[1, p + 4] - u_ref[1, p])
        new += along_y(my, rho) + along_z(mz, rho)
        new += near_planes(ends(below, above, 1, 0.0), ends(below, above, 0, 0.0), sign)
        new -= (FAR * sign) * ends(below, above, 2, 0.0)
        unpair(out_ref, new, p)
        d_ref[pl.ds(pl.multiple_of(p * 8, 8), 8), :] = new
        return 0

    lax.fori_loop(0, half, body, 0)
    d = d_ref[...]
    order = order_ref[...]
    dot = functools.partial(jnp.dot, preferred_element_type=jnp.float32)
    high = d.astype(jnp.bfloat16)
    low = (d - high.astype(jnp.float32)).astype(jnp.bfloat16)
    high = dot(order, high).astype(jnp.bfloat16)
    low = dot(order, low).astype(jnp.bfloat16)
    across = lambda a, b: lax.dot_general(a, b, (((1,), (1,)), ((), ())), preferred_element_type=jnp.float32)
    for part in range(2):
        c_high, c_low = high_ref[part], low_ref[part]
        for z in range(4):
            r_high, r_low = high[z * rows : (z + 1) * rows], low[z * rows : (z + 1) * rows]
            wave_ref[part, z] = across(c_high, r_high) + across(c_low, r_high) + across(c_high, r_low)


def main_kernel(u_ref, ba_ref, aa_ref, sb_ref, sa_ref, bn_ref, an_ref, g_ref, mom_ref, mag_ref, f_ref):
    chunk = ba_ref.shape[1]
    start = pl.program_id(0) * chunk
    total = u_ref.shape[1]
    kept = (0, 1, 2, 4, 5)

    @pl.when(pl.program_id(0) == 0)
    def _():
        def fx(q, _):
            u = [u_ref[f, q] for f in range(7)]
            f = fluxes(u[0], u[1:4], u[4:7], 0)
            for i, c in enumerate(kept):
                f_ref[i, q] = f[c]
            return 0

        lax.fori_loop(0, total, fx, 0)

    def body(r, _):
        q = start + r + 2
        u = [u_ref[f, q] for f in range(7)]
        fy = fluxes(u[0], u[1:4], u[4:7], 1)
        fz = fluxes(u[0], u[1:4], u[4:7], 2)
        sign = signs(u[0].shape)
        ba, aa = pair(ba_ref, r) + sb_ref[q], pair(aa_ref, r) + sa_ref[q]
        bn, an = pair(bn_ref, r), pair(an_ref, r)
        hm = [ends(bn, an, 0, 0.0), ends(bn, an, 1, 0.0), ends(ba, aa, 1, 0.0)]
        hb = [ends(ba, aa, 3, 0.0), ends(bn, an, 2, 0.0), ends(bn, an, 3, 0.0)]
        fh = fluxes(ends(ba, aa, 0, 1.0), hm, hb, 2)
        halo = hm + hb
        for c in range(6):
            field = u[c + 1]
            new = field * (1.0 - 6.0 * DIFFUSION)
            new += DIFFUSION * (u_ref[c + 1, q - 1] + u_ref[c + 1, q + 1])
            if c in kept:
                i = kept.index(c)
                new += NEAR * (f_ref[i, q - 1] - f_ref[i, q + 1]) + FAR * (f_ref[i, q + 2] - f_ref[i, q - 2])
            if fy[c] is None:
                new += DIFFUSION * (turn(field, 1, 1) + turn(field, -1, 1))
            else:
                new += along_y(fy[c], field)
            new += along_z(fz[c], field)
            new += near_planes(fh[c], halo[c], sign)
            if c < 2:
                g = [jnp.broadcast_to(g_ref[c, h, r], (4, field.shape[1])) for h in range(2)]
                new += u[0] * jnp.concatenate(g, axis=0)
            if c < 3:
                unpair(mom_ref, new, c, r)
            else:
                unpair(mag_ref, new, c - 3, r)
        return 0

    lax.fori_loop(0, chunk, body, 0)


def far_kernel(bf_ref, af_ref, bl_ref, al_ref, mom_in, mag_in, mom_ref, mag_ref):
    chunk = bf_ref.shape[1]

    def body(r, _):
        below, above = pair(bf_ref, r), pair(af_ref, r)
        sign = FAR * signs(below.shape)
        sub = lax.broadcasted_iota(jnp.int32, below.shape, 0)
        bl, al = bl_ref[r], al_ref[r]
        last = jnp.zeros_like(below)
        for h in range(2):
            last = jnp.where(sub == 4 * h, bl[h : h + 1], jnp.where(sub == 4 * h + 3, al[h : h + 1], last))
        for c in range(4):
            term = sign * ends(below, above, c, 0.0)
            if c < 3:
                unpair(mom_ref, pair(mom_in, c, r) - term, c, r)
            else:
                unpair(mag_ref, pair(mag_in, 0, r) - term, 0, r)
        unpair(mag_ref, pair(mag_in, 1, r) - sign * last, 1, r)
        return 0

    lax.fori_loop(0, chunk, body, 0)


def modes_kernel(at_ref, w_ref, ch_ref, cl_ref, sh_ref, sl_ref, out_ref):
    dot = functools.partial(jnp.dot, preferred_element_type=jnp.float32)

    def split(x):
        high = x.astype(jnp.bfloat16)
        return high, (x - high.astype(jnp.float32)).astype(jnp.bfloat16)

    re, im = split(w_ref[0, 0]), split(w_ref[1, 0])
    times = lambda x, h, l: dot(x[0], h[...]) + dot(x[0], l[...]) + dot(x[1], h[...])
    scale = 1.0 / math.sqrt(NX * w_ref.shape[3])
    shape = out_ref.shape[2:]
    ky = lax.broadcasted_iota(jnp.int32, shape, 0) + at_ref[2]
    kx = lax.broadcasted_iota(jnp.int32, shape, 1)
    keep = jnp.where((ky == 0) & (kx == 0), 0.0, scale)
    out_ref[0, 0] = (times(re, ch_ref, cl_ref) + times(im, sh_ref, sl_ref)) * keep
    out_ref[1, 0] = (times(im, ch_ref, cl_ref) - times(re, sh_ref, sl_ref)) * keep


def cost(flops, bytes_accessed):
    return pl.CostEstimate(flops=int(flops), bytes_accessed=int(bytes_accessed), transcendentals=0)


def tables(size):
    angle = (np.outer(np.arange(size), np.arange(size)) % size) * (2.0 * np.pi / size)
    result = []
    for table in (np.cos(angle), np.sin(angle)):
        high = table.astype(np.float32).astype(ml_dtypes.bfloat16)
        low = (table - high.astype(np.float64)).astype(np.float32).astype(ml_dtypes.bfloat16)
        result += [high, low]
    return result


def row_order(half):
    matrix = np.zeros((8 * half, 8 * half), np.float32)
    for z in range(4):
        for h in range(2):
            for p in range(half):
                matrix[(z * 2 + h) * half + p, p * 8 + h * 4 + z] = 1.0
    return matrix.astype(ml_dtypes.bfloat16)


def shift(block, axis, step):
    n = lax.axis_size(axis)
    return lax.ppermute(block, axis, [(i, (i + step) % n) for i in range(n)])


def on_device(density, momentum, magnetic, arm_potential, sn_cells, sn_counts):
    rows, planes, ny = density.shape
    half = rows // 2
    layers, across = lax.axis_size("gz"), lax.axis_size("xy")
    devices = layers * across
    tile_row, tile_plane = lax.axis_index("xy"), lax.axis_index("gz")
    field = rows * planes * ny
    f32 = jnp.float32
    shape = jax.ShapeDtypeStruct
    whole = pl.BlockSpec(memory_space=pltpu.VMEM)
    smem = pl.BlockSpec(memory_space=pltpu.SMEM)
    params = pltpu.CompilerParams(vmem_limit_bytes=VMEM)
    message = shape((2, half, planes, ny), f32)

    slots_here = sn_cells.shape[0]
    mine = jnp.concatenate([sn_cells, sn_counts[:, None]], axis=1).reshape(1, 1, 4 * slots_here)
    mine = jnp.pad(mine, ((0, 0), (0, 0), (0, -(4 * slots_here) % 128)))
    events = lax.all_to_all(
        jnp.broadcast_to(mine, (devices, 1, mine.shape[2])), ("gz", "xy"), split_axis=0, concat_axis=0, tiled=True
    )
    events = events[:, 0, : 4 * slots_here].reshape(-1)
    at = jnp.stack([tile_row * rows, tile_plane * planes, tile_row * (ny // across)]).astype(jnp.int32)

    rho = density.reshape(2, half, planes, ny)
    mom = momentum.reshape(3, 2, half, planes, ny)
    mag = magnetic.reshape(3, 2, half, planes, ny)

    edge = lambda s: jnp.concatenate([density[None, s], momentum[:, s], magnetic[:, s]], axis=0)
    before = shift(edge(slice(rows - 2, rows)), "xy", 1)
    after = shift(edge(slice(0, 2)), "xy", -1)
    p_before = shift(arm_potential[rows - 2 :], "xy", 1)
    p_after = shift(arm_potential[:2], "xy", -1)

    one = lambda f: pl.BlockSpec((1, 2, half, planes, ny), lambda i, f=f: (f, 0, 0, 0, 0))
    full = lambda s: pl.BlockSpec(s, lambda i: (0,) * len(s))
    up, down = pl.pallas_call(
        pack_kernel,
        grid=(1,),
        in_specs=[full(message.shape), one(2), one(0)],
        out_specs=[full(message.shape)] * 2,
        out_shape=[message] * 2,
        compiler_params=params,
        cost_estimate=cost(20 * field, 5 * 4 * field),
        name="pack",
    )(rho, mom, mag)
    below_a, above_a = shift(up, "gz", 1), shift(down, "gz", -1)

    side = shape((half + 4, 8, ny), f32)
    last = shape((half, 2, ny), f32)
    state, sb, sa, up_n, down_n, up_f, down_f, up_l, down_l = pl.pallas_call(
        functools.partial(state_kernel, depth=planes * layers),
        in_specs=[smem, smem] + [whole] * 5,
        out_specs=[whole] * 9,
        out_shape=[shape((7, half + 4, 8, ny), f32), side, side] + [message] * 4 + [last] * 2,
        compiler_params=params,
        cost_estimate=cost(100 * field, 21 * 4 * field),
        name="state",
    )(events, at, rho, mom, mag, before, after)
    below_n, above_n = shift(up_n, "gz", 1), shift(down_n, "gz", -1)
    below_f, above_f = shift(up_f, "gz", 1), shift(down_f, "gz", -1)
    below_l, above_l = shift(up_l, "gz", 1), shift(down_l, "gz", -1)

    cos_high, cos_low, sin_high, sin_low = tables(ny)
    new_density, wave = pl.pallas_call(
        density_kernel,
        grid=(1,),
        in_specs=[
            full((4, half + 4, 8, ny)), full(message.shape), full(message.shape), full(side.shape), full(side.shape),
            full((8 * half, 8 * half)), full((2, ny, ny)), full((2, ny, ny)),
        ],
        out_specs=[full(message.shape), full((2, planes, ny, rows))],
        out_shape=[message, shape((2, planes, ny, rows), f32)],
        scratch_shapes=[pltpu.VMEM((8 * half, ny), f32)],
        compiler_params=params,
        cost_estimate=cost(60 * field, 13 * 4 * field),
        name="density",
    )(
        state, below_a, above_a, sb, sa, row_order(half), np.stack([cos_high, -sin_high]), np.stack([cos_low, -sin_low]),
    )
    portion = lax.all_to_all(wave, "xy", split_axis=2, concat_axis=3, tiled=True)

    p_all = jnp.concatenate([p_before, arm_potential, p_after], axis=0)
    grad_x = NEAR * (p_all[1:-3] - p_all[3:-1]) + FAR * (p_all[4:] - p_all[:-4])
    grad_y = NEAR * (jnp.roll(arm_potential, 1, 1) - jnp.roll(arm_potential, -1, 1)) + FAR * (
        jnp.roll(arm_potential, -2, 1) - jnp.roll(arm_potential, 2, 1)
    )
    gradient = jnp.stack([grad_x, grad_y]).reshape(2, 2, half, 1, ny)

    chunk = math.gcd(half, 8)
    steps = half // chunk
    halo = pl.BlockSpec((2, chunk, planes, ny), lambda i: (0, i, 0, 0))
    three = pl.BlockSpec((3, 2, chunk, planes, ny), lambda i: (0, 0, i, 0, 0))
    new_mom, new_mag = pl.pallas_call(
        main_kernel,
        grid=(steps,),
        in_specs=[
            full((7, half + 4, 8, ny)), halo, halo, full(side.shape), full(side.shape), halo, halo,
            pl.BlockSpec((2, 2, chunk, 1, ny), lambda i: (0, 0, i, 0, 0)),
        ],
        out_specs=[three, three],
        out_shape=[shape((3, 2, half, planes, ny), f32)] * 2,
        scratch_shapes=[pltpu.VMEM((5, half + 4, 8, ny), f32)],
        compiler_params=params,
        cost_estimate=cost(300 * field, 20 * 4 * field),
        name="main",
    )(state, below_a, above_a, sb, sa, below_n, above_n, gradient)

    row_spec = pl.BlockSpec((chunk, 2, ny), lambda i: (i, 0, 0))
    two = pl.BlockSpec((2, 2, chunk, planes, ny), lambda i: (0, 0, i, 0, 0))
    new_mom, new_mag = pl.pallas_call(
        far_kernel,
        grid=(steps,),
        in_specs=[halo, halo, row_spec, row_spec, three, two],
        out_specs=[three, two],
        out_shape=[shape((3, 2, half, planes, ny), f32)] * 2,
        input_output_aliases={4: 0, 5: 1},
        compiler_params=params,
        cost_estimate=cost(30 * field, 13 * 4 * field),
        name="far",
    )(below_f, above_f, below_l, above_l, new_mom, new_mag)

    band = ny // across
    block = pl.BlockSpec((2, 1, band, NX), lambda z: (0, z, 0, 0))
    modes = pl.pallas_call(
        modes_kernel,
        grid=(planes,),
        in_specs=[smem, block] + [full((NX, NX))] * 4,
        out_specs=block,
        out_shape=shape((2, planes, band, NX), f32),
        compiler_params=params,
        cost_estimate=cost(20 * field, 5 * 4 * field),
        name="modes",
    )(at, portion, *tables(NX))
    return (
        new_density.reshape(rows, planes, ny),
        new_mom.reshape(3, rows, planes, ny),
        new_mag.reshape(3, rows, planes, ny),
        modes,
    )


def solution(mesh):
    in_specs = (
        P("xy", "gz", None),
        P(None, "xy", "gz", None),
        P(None, "xy", "gz", None),
        P("xy", None),
        P(("gz", "xy"), None),
        P(("gz", "xy")),
    )
    out_specs = (
        P("xy", "gz", None),
        P(None, "xy", "gz", None),
        P(None, "xy", "gz", None),
        P(None, "gz", "xy", None),
    )
    return jax.shard_map(
        on_device, mesh=mesh, in_specs=in_specs, out_specs=out_specs, check_vma=False
    )
```

```python
import functools
import math

import jax
import jax.numpy as jnp
import ml_dtypes
import numpy as np
from jax import lax
from jax.experimental import pallas as pl
from jax.experimental.pallas import tpu as pltpu
from jax.sharding import PartitionSpec as P

NX = 512
RADIUS = 16
IMPULSE = 2.0 / 16
TIME_STEP = 0.1
DIFFUSION = 0.05
NEAR = 8.0 * TIME_STEP / 12.0
FAR = TIME_STEP / 12.0
VMEM = 56 * 1024 * 1024
PACK_COST = STATE_COST = DENSITY_COST = MAIN_COST = MODES_COST = (1e6, 1e5)


def pair(ref, *index):
    return jnp.concatenate([ref[(*index[:-1], 0, index[-1])], ref[(*index[:-1], 1, index[-1])]], axis=0)


def unpair(ref, value, *index):
    ref[(*index[:-1], 0, index[-1])] = value[:4]
    ref[(*index[:-1], 1, index[-1])] = value[4:]


def slots(shape):
    sub = lax.broadcasted_iota(jnp.int32, shape, len(shape) - 2)
    return jnp.where(sub >= 4, sub - 4, sub)


def turn(value, shift, axis):
    return pltpu.roll(value, shift % value.shape[axis], axis)


def gather_planes(values, plane):
    slot = slots(values[0].shape)
    out = turn(values[-1], len(values) - 1 - plane, 0)
    for c in reversed(range(len(values) - 1)):
        out = jnp.where(slot == c, turn(values[c], c - plane, 0), out)
    return out


def fluxes(rho, m, b, k):
    inv = 1.0 / rho
    v = [m[i] * inv for i in range(3)]
    total = rho + 0.5 * (b[0] * b[0] + b[1] * b[1] + b[2] * b[2])
    push = [m[i] * v[k] - b[i] * b[k] + (total if i == k else 0.0) for i in range(3)]
    turned = [None if i == k else v[k] * b[i] - b[k] * v[i] for i in range(3)]
    return push + turned


def pack_kernel(rho_ref, mz_ref, bx_ref, up_ref, down_ref):
    half = rho_ref.shape[1]

    def body(p, _):
        rho, mz, bx = pair(rho_ref, p), pair(mz_ref, 0, p), pair(bx_ref, 0, p)
        slot = slots(rho.shape)
        up = jnp.where(slot == 2, mz, gather_planes([rho, mz, mz, bx], 3))
        down = jnp.where(slot == 2, turn(mz, 1, 0), gather_planes([rho, mz, mz, bx], 0))
        up_ref[p] = up
        down_ref[p] = down
        return 0

    lax.fori_loop(0, half, body, 0)


def state_kernel(
    ev_ref, at_ref, rho_ref, mom_ref, mag_ref, pot_ref, before_ref, after_ref,
    u_ref, sb_out, sa_out, up_0, down_0, up_1, down_1, sb_ref, sa_ref, *, depth,
):
    half, ny = rho_ref.shape[1], rho_ref.shape[3]
    rows, events = 2 * half, ev_ref.shape[0] // 4
    row_start, plane_start = at_ref[0], at_ref[1]

    def raw(f, h, p):
        if f == 0:
            return rho_ref[h, p]
        if f == 7:
            return jnp.broadcast_to(pot_ref[pl.ds(h * half + p, 1), :], (4, ny))
        return mom_ref[f - 1, h, p] if f < 4 else mag_ref[f - 4, h, p]

    def fill(p, _):
        for f in range(8):
            u_ref[f, p + 2] = jnp.concatenate([raw(f, 0, p), raw(f, 1, p)], axis=0)
        return 0

    lax.fori_loop(0, half, fill, 0)
    for f in range(8):
        for j in range(2):
            u_ref[f, j] = jnp.concatenate([before_ref[f, j], raw(f, 0, half - 2 + j)], axis=0)
            u_ref[f, half + 2 + j] = jnp.concatenate([raw(f, 1, j), after_ref[f, j]], axis=0)
    sb_ref[...] = jnp.zeros_like(sb_ref)
    sa_ref[...] = jnp.zeros_like(sa_ref)

    shape = (4, 8, 128)
    slot = slots(shape)
    sub = lax.broadcasted_iota(jnp.int32, shape, 1)
    step = lax.broadcasted_iota(jnp.int32, shape, 0)
    lane = lax.broadcasted_iota(jnp.int32, shape, 2)

    def wrapped(distance, size):
        distance = jnp.where(distance >= size // 2, distance - size, distance)
        return jnp.where(distance < -(size // 2), distance + size, distance)

    def event(e, _):
        row, col, plane, count = (ev_ref[4 * e + i] for i in range(4))
        rel = wrapped(row - row_start - half, NX)
        rel = rel + half

        @pl.when((count > 0) & (rel > -2 - RADIUS) & (rel < rows + 2 + RADIUS))
        def _():
            base = plane_start - plane
            dz = wrapped(slot + base, depth).astype(jnp.float32)
            dzb = wrapped(jnp.where(slot == 2, -2, -1) + base, depth).astype(jnp.float32)
            dza = wrapped(jnp.where(slot == 2, 5, 4) + base, depth).astype(jnp.float32)
            share = lambda d: jnp.where(slot == 0, 1.0, jnp.where(slot == 3, 0.0, IMPULSE * d))
            first = jnp.bitwise_and(col - RADIUS, ny - 1) // 128
            second = jnp.bitwise_and(col + RADIUS - 1, ny - 1) // 128

            def tile(t, _):
                index = jnp.where(t == 0, first, second)
                lanes = pl.ds(pl.multiple_of(index * 128, 128), 128)
                dy = wrapped(lane + index * 128 - col, ny).astype(jnp.float32)
                dy2 = dy * dy
                for h in range(2):
                    weight = jnp.where((sub >= 4) == (h == 1), count, 0).astype(jnp.float32)
                    low = jnp.clip(rel - RADIUS + 1 - h * half + 2, 0, half + 4) // 4
                    high = (jnp.clip(rel + RADIUS - 1 - h * half + 2, -1, half + 3) + 4) // 4

                    def chunk(n, _):
                        q = pl.ds(n * 4, 4)
                        dx = (step + (n * 4 - 2 + h * half - rel)).astype(jnp.float32)
                        flat = dx * dx + dy2
                        size = lambda d: jnp.maximum(1.0 - (flat + d * d) * (1.0 / (RADIUS * RADIUS)), 0.0) * weight
                        w = size(dz)
                        u_ref[0, q, :, lanes] += w
                        w = w * IMPULSE
                        u_ref[1, q, :, lanes] += w * dx
                        u_ref[2, q, :, lanes] += w * dy
                        u_ref[3, q, :, lanes] += w * dz
                        sb_ref[q, :, lanes] += size(dzb) * share(dzb)
                        sa_ref[q, :, lanes] += size(dza) * share(dza)
                        return 0

                    lax.fori_loop(low, high, chunk, 0)
                return 0

            lax.fori_loop(0, jnp.where(first == second, 1, 2), tile, 0)

        return 0

    lax.fori_loop(0, events, event, 0)

    def group(up_ref, down_ref, first, count):
        def messages(g, _):
            sub = lax.broadcasted_iota(jnp.int32, (8, ny), 0)
            lasts = [jnp.zeros((8, ny), jnp.float32) for _ in range(2)]
            for j in range(4):
                r = 4 * g + j
                p = r + first
                sb_out[p] = sb_ref[p + 2]
                sa_out[p] = sa_ref[p + 2]
                u = [u_ref[f, p + 2] for f in range(7)]
                near = [u[1], u[2], u[5], u[6]]
                up_ref[r] = gather_planes(near, 3)
                down_ref[r] = gather_planes(near, 0)
                f = fluxes(u[0], u[1:4], u[4:7], 2)
                up_ref[count + r] = gather_planes(f[:4], 2)
                down_ref[count + r] = gather_planes(f[:4], 1)
                for i, plane in enumerate((2, 1)):
                    for h in range(2):
                        moved = turn(f[4], 2 * j + h - 4 * h - plane, 0)
                        lasts[i] = jnp.where(sub == 2 * j + h, moved, lasts[i])
            up_ref[2 * count + g] = lasts[0]
            down_ref[2 * count + g] = lasts[1]
            return 0

        lax.fori_loop(0, count // 4, messages, 0)

    split = up_0.shape[0] * 4 // 9
    group(up_0, down_0, 0, split)
    group(up_1, down_1, split, half - split)


def ends(below, above, c, fill):
    slot = slots(below.shape)
    rest = jnp.where(slot == 3, turn(above, 3 - c, 0), fill)
    return jnp.where(slot == 0, turn(below, -c, 0), rest)


def signs(shape):
    slot = slots(shape)
    return jnp.where(slot == 0, 1.0, jnp.where(slot == 3, -1.0, 0.0))


def along_y(f, u):
    low, high = NEAR * f + DIFFUSION * u, DIFFUSION * u - NEAR * f
    far = FAR * f
    return turn(low, 1, 1) + turn(high, -1, 1) + turn(far, -2, 1) - turn(far, 2, 1)


def along_z(f, u):
    slot = slots(u.shape)
    part = lambda keep, v: jnp.where(keep, v, 0.0)
    if f is None:
        return part(slot >= 1, turn(DIFFUSION * u, 1, 0)) + part(slot <= 2, turn(DIFFUSION * u, -1, 0))
    low, high = NEAR * f + DIFFUSION * u, DIFFUSION * u - NEAR * f
    far = FAR * f
    return (
        part(slot >= 1, turn(low, 1, 0)) + part(slot <= 2, turn(high, -1, 0))
        + part(slot <= 1, turn(far, -2, 0)) - part(slot >= 2, turn(far, 2, 0))
    )


def near_planes(f, u, sign):
    outer = DIFFUSION * u
    if f is None:
        return outer
    slot = slots(u.shape)
    t = (FAR * sign) * f
    inner = jnp.where(slot == 1, turn(t, 1, 0), jnp.where(slot == 2, turn(t, -1, 0), 0.0))
    return outer + 8.0 * t - inner


def density_kernel(u_ref, below_ref, above_ref, sb_ref, sa_ref, order_ref, high_ref, low_ref, out_ref, wave_ref, d_ref):
    half = below_ref.shape[0]
    rows = 2 * half

    def body(p, _):
        rho, my, mz = u_ref[0, p + 2], u_ref[2, p + 2], u_ref[3, p + 2]
        below, above = below_ref[p] + sb_ref[p], above_ref[p] + sa_ref[p]
        slot, sign = slots(rho.shape), signs(rho.shape)
        new = rho * (1.0 - 6.0 * DIFFUSION)
        new += DIFFUSION * (u_ref[0, p + 1] + u_ref[0, p + 3])
        new += NEAR * (u_ref[1, p + 1] - u_ref[1, p + 3]) + FAR * (u_ref[1, p + 4] - u_ref[1, p])
        new += along_y(my, rho) + along_z(mz, rho)
        new += near_planes(ends(below, above, 1, 0.0), ends(below, above, 0, 0.0), sign)
        new -= (FAR * sign) * ends(below, above, 2, 0.0)
        unpair(out_ref, new, p)
        d_ref[pl.ds(pl.multiple_of(p * 8, 8), 8), :] = new
        return 0

    lax.fori_loop(0, half, body, 0)
    d = d_ref[...]
    order = order_ref[...]
    dot = functools.partial(jnp.dot, preferred_element_type=jnp.float32)
    high = d.astype(jnp.bfloat16)
    low = (d - high.astype(jnp.float32)).astype(jnp.bfloat16)
    high = dot(order, high).astype(jnp.bfloat16)
    low = dot(order, low).astype(jnp.bfloat16)
    for part in range(2):
        c_high, c_low = high_ref[part], low_ref[part]
        wave = dot(high, c_high) + dot(high, c_low) + dot(low, c_high)
        peers, band = wave_ref.shape[0], wave_ref.shape[4]
        for j in range(peers):
            for z in range(4):
                wave_ref[j, part, z] = wave[z * rows : (z + 1) * rows, j * band : (j + 1) * band]


def last_plane(below, above, j):
    sub = lax.broadcasted_iota(jnp.int32, below.shape, 0)
    out = jnp.zeros_like(below)
    for h in range(2):
        out = jnp.where(sub == 4 * h, turn(below, 4 * h - (2 * j + h), 0), out)
        out = jnp.where(sub == 4 * h + 3, turn(above, 4 * h + 3 - (2 * j + h), 0), out)
    return out


def main_kernel(
    u_hbm, ba_ref, aa_ref, sb_ref, sa_ref, bn_ref, an_ref, bf_ref, af_ref, bl_ref, al_ref, *rest, first,
):
    mom_ref, mag_ref, u_ref, f_ref, sem = rest[-5:]
    chunk, total = ba_ref.shape[0], u_ref.shape[1]
    start = pl.program_id(0) * chunk
    kept = (0, 1, 2, 4, 5)

    @pl.when(pl.program_id(0) == 0)
    def _():
        copy = pltpu.make_async_copy(u_hbm.at[:, pl.ds(first, total)], u_ref, sem)
        copy.start()
        copy.wait()

        def fx(q, _):
            u = [u_ref[f, q] for f in range(7)]
            f = fluxes(u[0], u[1:4], u[4:7], 0)
            for i, c in enumerate(kept):
                f_ref[i, q] = f[c]
            return 0

        lax.fori_loop(0, total, fx, 0)

    def row(r, g, j):
        q = start + r + 2
        u = [u_ref[f, q] for f in range(7)]
        fy = fluxes(u[0], u[1:4], u[4:7], 1)
        fz = fluxes(u[0], u[1:4], u[4:7], 2)
        sign = signs(u[0].shape)
        ba, aa = ba_ref[r] + sb_ref[r], aa_ref[r] + sa_ref[r]
        bn, an, bf, af = bn_ref[r], an_ref[r], bf_ref[r], af_ref[r]
        hm = [ends(bn, an, 0, 0.0), ends(bn, an, 1, 0.0), ends(ba, aa, 1, 0.0)]
        hb = [ends(ba, aa, 3, 0.0), ends(bn, an, 2, 0.0), ends(bn, an, 3, 0.0)]
        fh = fluxes(ends(ba, aa, 0, 1.0), hm, hb, 2)
        halo = hm + hb
        far = [ends(bf, af, c, 0.0) for c in range(4)] + [last_plane(bl_ref[g], al_ref[g], j), None]
        for c in range(6):
            field = u[c + 1]
            new = field * (1.0 - 6.0 * DIFFUSION)
            new += DIFFUSION * (u_ref[c + 1, q - 1] + u_ref[c + 1, q + 1])
            if c in kept:
                i = kept.index(c)
                new += NEAR * (f_ref[i, q - 1] - f_ref[i, q + 1]) + FAR * (f_ref[i, q + 2] - f_ref[i, q - 2])
            if fy[c] is None:
                new += DIFFUSION * (turn(field, 1, 1) + turn(field, -1, 1))
            else:
                new += along_y(fy[c], field)
            new += along_z(fz[c], field)
            new += near_planes(fh[c], halo[c], sign)
            if far[c] is not None:
                new -= (FAR * sign) * far[c]
            if c == 0:
                slope = NEAR * (u_ref[7, q - 1] - u_ref[7, q + 1]) + FAR * (u_ref[7, q + 2] - u_ref[7, q - 2])
                new += u[0] * slope
            if c == 1:
                potential = u_ref[7, q]
                slope = NEAR * (turn(potential, 1, 1) - turn(potential, -1, 1))
                new += u[0] * (slope + FAR * (turn(potential, -2, 1) - turn(potential, 2, 1)))
            if c < 3:
                unpair(mom_ref, new, c, r)
            else:
                unpair(mag_ref, new, c - 3, r)

    def body(g, _):
        for j in range(4):
            row(4 * g + j, g, j)
        return 0

    lax.fori_loop(0, chunk // 4, body, 0)


def modes_kernel(at_ref, w_ref, ch_ref, cl_ref, sh_ref, sl_ref, out_ref, *, turned):
    dot = functools.partial(jnp.dot, preferred_element_type=jnp.float32)
    planes, band, nx = out_ref.shape[1:]

    def split(part):
        if turned:
            x = jnp.concatenate([w_ref[part, z] for z in range(planes)], axis=0)
        else:
            column = lambda z: jnp.concatenate([w_ref[j, part, z] for j in range(w_ref.shape[0])], axis=0)
            x = jnp.concatenate([column(z).T for z in range(planes)], axis=0)
        high = x.astype(jnp.bfloat16)
        return high, (x - high.astype(jnp.float32)).astype(jnp.bfloat16)

    re, im = split(0), split(1)
    times = lambda x, h, l: dot(x[0], h[...]) + dot(x[0], l[...]) + dot(x[1], h[...])
    scale = 1.0 / math.sqrt(NX * nx)
    shape = (band, nx)
    ky = lax.broadcasted_iota(jnp.int32, shape, 0) + at_ref[2]
    kx = lax.broadcasted_iota(jnp.int32, shape, 1)
    keep = jnp.where((ky == 0) & (kx == 0), 0.0, scale)
    out_re = times(re, ch_ref, cl_ref) + times(im, sh_ref, sl_ref)
    out_im = times(im, ch_ref, cl_ref) - times(re, sh_ref, sl_ref)
    for z in range(planes):
        out_ref[0, z] = out_re[z * band : (z + 1) * band] * keep
        out_ref[1, z] = out_im[z * band : (z + 1) * band] * keep


def cost(flops, bytes_accessed):
    return pl.CostEstimate(flops=int(flops), bytes_accessed=int(bytes_accessed), transcendentals=0)


def tables(size):
    angle = (np.outer(np.arange(size), np.arange(size)) % size) * (2.0 * np.pi / size)
    result = []
    for table in (np.cos(angle), np.sin(angle)):
        high = table.astype(np.float32).astype(ml_dtypes.bfloat16)
        low = (table - high.astype(np.float64)).astype(np.float32).astype(ml_dtypes.bfloat16)
        result += [high, low]
    return result


def row_order(half):
    matrix = np.zeros((8 * half, 8 * half), np.float32)
    for z in range(4):
        for h in range(2):
            for p in range(half):
                matrix[(z * 2 + h) * half + p, p * 8 + h * 4 + z] = 1.0
    return matrix.astype(ml_dtypes.bfloat16)


def shift(block, axis, step):
    n = lax.axis_size(axis)
    return lax.ppermute(block, axis, [(i, (i + step) % n) for i in range(n)])


def on_device(density, momentum, magnetic, arm_potential, sn_cells, sn_counts):
    rows, planes, ny = density.shape
    half = rows // 2
    layers, across = lax.axis_size("gz"), lax.axis_size("xy")
    devices = layers * across
    tile_row, tile_plane = lax.axis_index("xy"), lax.axis_index("gz")
    field = rows * planes * ny
    f32 = jnp.float32
    shape = jax.ShapeDtypeStruct
    whole = pl.BlockSpec(memory_space=pltpu.VMEM)
    smem = pl.BlockSpec(memory_space=pltpu.SMEM)
    params = pltpu.CompilerParams(vmem_limit_bytes=VMEM)
    message = shape((2, half, planes, ny), f32)
    tile = shape((half, 8, ny), f32)
    n0 = max(4, half * 5 // 32 * 4)
    counts = (n0, half - n0)

    slots_here = sn_cells.shape[0]
    mine = jnp.concatenate([sn_cells, sn_counts[:, None]], axis=1).reshape(1, 1, 4 * slots_here)
    mine = jnp.pad(mine, ((0, 0), (0, 0), (0, -(4 * slots_here) % 128)))
    events = lax.all_to_all(
        jnp.broadcast_to(mine, (devices, 1, mine.shape[2])), ("gz", "xy"), split_axis=0, concat_axis=0, tiled=True
    )
    events = events[:, 0, : 4 * slots_here].reshape(-1)
    at = jnp.stack([tile_row * rows, tile_plane * planes, tile_row * (ny // across)]).astype(jnp.int32)

    rho = density.reshape(2, half, planes, ny)
    mom = momentum.reshape(3, 2, half, planes, ny)
    mag = magnetic.reshape(3, 2, half, planes, ny)

    def edge(s):
        potential = jnp.broadcast_to(arm_potential[s][None, :, None, :], (1, 2, planes, ny))
        return jnp.concatenate([density[None, s], momentum[:, s], magnetic[:, s], potential], axis=0)

    before = shift(edge(slice(rows - 2, rows)), "xy", 1)
    after = shift(edge(slice(0, 2)), "xy", -1)

    one = lambda f: pl.BlockSpec((1, 2, half, planes, ny), lambda i, f=f: (f, 0, 0, 0, 0))
    full = lambda s: pl.BlockSpec(s, lambda i: (0,) * len(s))
    up, down = pl.pallas_call(
        pack_kernel,
        grid=(1,),
        in_specs=[full(message.shape), one(2), one(0)],
        out_specs=[full(tile.shape)] * 2,
        out_shape=[tile] * 2,
        compiler_params=params,
        cost_estimate=cost(*PACK_COST),
        name="pack",
    )(rho, mom, mag)
    below_a, above_a = shift(up, "gz", 1), shift(down, "gz", -1)

    parcels = [shape((9 * n // 4, 8, ny), f32) for n in counts]
    side = pltpu.VMEM((half + 4, 8, ny), f32)
    state, sb, sa, up_0, down_0, up_1, down_1 = pl.pallas_call(
        functools.partial(state_kernel, depth=planes * layers),
        in_specs=[smem, smem] + [whole] * 6,
        out_specs=[whole] * 7,
        out_shape=[shape((8, half + 4, 8, ny), f32), tile, tile, parcels[0], parcels[0], parcels[1], parcels[1]],
        scratch_shapes=[side, side],
        compiler_params=params,
        cost_estimate=cost(*STATE_COST),
        name="state",
    )(events, at, rho, mom, mag, arm_potential, before, after)
    parcels_below = [shift(up_0, "gz", 1)]
    parcels_above = [shift(down_0, "gz", -1)]
    parcels_below.append(shift(up_1, "gz", 1))
    parcels_above.append(shift(down_1, "gz", -1))

    cos_high, cos_low, sin_high, sin_low = tables(ny)
    band = ny // across
    new_density, wave = pl.pallas_call(
        density_kernel,
        grid=(1,),
        in_specs=[
            full((4, half + 4, 8, ny)), full(tile.shape), full(tile.shape), full(tile.shape), full(tile.shape),
            full((8 * half, 8 * half)), full((2, ny, ny)), full((2, ny, ny)),
        ],
        out_specs=[full(message.shape), full((across, 2, planes, rows, band))],
        out_shape=[message, shape((across, 2, planes, rows, band), f32)],
        scratch_shapes=[pltpu.VMEM((8 * half, ny), f32)],
        compiler_params=params,
        cost_estimate=cost(*DENSITY_COST),
        name="density",
    )(
        state, below_a, above_a, sb, sa, row_order(half), np.stack([cos_high, -sin_high]), np.stack([cos_low, -sin_low]),
    )
    portion = lax.all_to_all(wave, "xy", split_axis=0, concat_axis=0, tiled=True)

    results = [shape((3, 2, half, planes, ny), f32)] * 2
    new = []
    for i, n in enumerate(counts):
        first = i * n0
        chunk = math.gcd(math.gcd(n0, half - n0), 8)
        here = pl.BlockSpec((chunk, 8, ny), lambda k, o=first // chunk: (o + k, 0, 0))
        near = pl.BlockSpec((chunk, 8, ny), lambda k: (k, 0, 0))
        far = pl.BlockSpec((chunk, 8, ny), lambda k, o=n // chunk: (o + k, 0, 0))
        last = pl.BlockSpec((chunk // 4, 8, ny), lambda k, o=8 * n // chunk: (o + k, 0, 0))
        three = pl.BlockSpec((3, 2, chunk, planes, ny), lambda k, o=first // chunk: (0, 0, o + k, 0, 0))
        below, above = parcels_below[i], parcels_above[i]
        new = pl.pallas_call(
            functools.partial(main_kernel, first=first),
            grid=(n // chunk,),
            in_specs=[pl.BlockSpec(memory_space=pl.ANY)] + [here] * 4 + [near] * 2 + [far] * 2 + [last] * 2
            + [pl.BlockSpec(memory_space=pl.ANY)] * len(new),
            out_specs=[three, three],
            out_shape=results,
            scratch_shapes=[
                pltpu.VMEM((8, n + 4, 8, ny), f32), pltpu.VMEM((5, n + 4, 8, ny), f32), pltpu.SemaphoreType.DMA,
            ],
            input_output_aliases={11: 0, 12: 1} if new else {},
            compiler_params=params,
            cost_estimate=cost(*MAIN_COST),
            name=f"main{i}",
        )(state, below_a, above_a, sb, sa, below, above, below, above, below, above, *new)
    new_mom, new_mag = new

    turned = band % 128 != 0
    if turned:
        portion = portion.transpose(1, 2, 4, 0, 3).reshape(2, planes, band, NX)
    modes = pl.pallas_call(
        functools.partial(modes_kernel, turned=turned),
        in_specs=[smem] + [whole] * 5,
        out_specs=whole,
        out_shape=shape((2, planes, band, NX), f32),
        compiler_params=params,
        cost_estimate=cost(*MODES_COST),
        name="modes",
    )(at, portion, *tables(NX))
    return (
        new_density.reshape(rows, planes, ny),
        new_mom.reshape(3, rows, planes, ny),
        new_mag.reshape(3, rows, planes, ny),
        modes,
    )


def solution(mesh):
    in_specs = (
        P("xy", "gz", None),
        P(None, "xy", "gz", None),
        P(None, "xy", "gz", None),
        P("xy", None),
        P(("gz", "xy"), None),
        P(("gz", "xy")),
    )
    out_specs = (
        P("xy", "gz", None),
        P(None, "xy", "gz", None),
        P(None, "xy", "gz", None),
        P(None, "gz", "xy", None),
    )
    return jax.shard_map(
        on_device, mesh=mesh, in_specs=in_specs, out_specs=out_specs, check_vma=False
    )
```

```python
import functools
import math

import jax
import jax.numpy as jnp
import ml_dtypes
import numpy as np
from jax import lax
from jax.experimental import pallas as pl
from jax.experimental.pallas import tpu as pltpu
from jax.sharding import PartitionSpec as P

NX = 512
RADIUS = 16
IMPULSE = 2.0 / 16
TIME_STEP = 0.1
DIFFUSION = 0.05
NEAR = 8.0 * TIME_STEP / 12.0
FAR = TIME_STEP / 12.0
VMEM = 56 * 1024 * 1024
PACK_COST = DENSITY_COST = MODES_COST = (1e6, 1e5)
STATE_COST = MAIN_COST = (1e6, 4e8)


def pair(ref, *index):
    return jnp.concatenate([ref[(*index[:-1], 0, index[-1])], ref[(*index[:-1], 1, index[-1])]], axis=0)


def unpair(ref, value, *index):
    ref[(*index[:-1], 0, index[-1])] = value[:4]
    ref[(*index[:-1], 1, index[-1])] = value[4:]


def slots(shape):
    sub = lax.broadcasted_iota(jnp.int32, shape, len(shape) - 2)
    return jnp.where(sub >= 4, sub - 4, sub)


def turn(value, shift, axis):
    return pltpu.roll(value, shift % value.shape[axis], axis)


def gather_planes(values, plane):
    slot = slots(values[0].shape)
    out = turn(values[-1], len(values) - 1 - plane, 0)
    for c in reversed(range(len(values) - 1)):
        out = jnp.where(slot == c, turn(values[c], c - plane, 0), out)
    return out


def shared(rho, m, b):
    inv = 1.0 / rho
    return [x * inv for x in m], rho + 0.5 * (b[0] * b[0] + b[1] * b[1] + b[2] * b[2])


def fluxes(v, total, m, b, k):
    push = [m[i] * v[k] - b[i] * b[k] + (total if i == k else 0.0) for i in range(3)]
    turned = [None if i == k else v[k] * b[i] - b[k] * v[i] for i in range(3)]
    return push + turned


def pack_kernel(rho_ref, mz_ref, bx_ref, up_ref, down_ref):
    half = rho_ref.shape[1]

    def body(p, _):
        rho, mz, bx = pair(rho_ref, p), pair(mz_ref, 0, p), pair(bx_ref, 0, p)
        slot = slots(rho.shape)
        up = jnp.where(slot == 2, mz, gather_planes([rho, mz, mz, bx], 3))
        down = jnp.where(slot == 2, turn(mz, 1, 0), gather_planes([rho, mz, mz, bx], 0))
        up_ref[p] = up
        down_ref[p] = down
        return 0

    lax.fori_loop(0, half, body, 0)


def state_kernel(
    ev_ref, at_ref, rho_ref, mom_ref, mag_ref, pot_ref, before_ref, after_ref,
    u_ref, sb_out, sa_out, up_0, down_0, up_1, down_1, sb_ref, sa_ref, *, depth,
):
    half, ny = rho_ref.shape[1], rho_ref.shape[3]
    rows, events = 2 * half, ev_ref.shape[0] // 4
    row_start, plane_start = at_ref[0], at_ref[1]

    def raw(f, h, p):
        if f == 0:
            return rho_ref[h, p]
        if f == 7:
            return jnp.broadcast_to(pot_ref[pl.ds(h * half + p, 1), :], (4, ny))
        return mom_ref[f - 1, h, p] if f < 4 else mag_ref[f - 4, h, p]

    def fill(p, _):
        for f in range(8):
            u_ref[f, p + 2] = jnp.concatenate([raw(f, 0, p), raw(f, 1, p)], axis=0)
        return 0

    lax.fori_loop(0, half, fill, 0)
    for f in range(8):
        for j in range(2):
            u_ref[f, j] = jnp.concatenate([before_ref[f, j], raw(f, 0, half - 2 + j)], axis=0)
            u_ref[f, half + 2 + j] = jnp.concatenate([raw(f, 1, j), after_ref[f, j]], axis=0)
    sb_ref[...] = jnp.zeros_like(sb_ref)
    sa_ref[...] = jnp.zeros_like(sa_ref)

    shape = (4, 8, 128)
    slot = slots(shape)
    sub = lax.broadcasted_iota(jnp.int32, shape, 1)
    step = lax.broadcasted_iota(jnp.int32, shape, 0)
    lane = lax.broadcasted_iota(jnp.int32, shape, 2)

    def wrapped(distance, size):
        distance = jnp.where(distance >= size // 2, distance - size, distance)
        return jnp.where(distance < -(size // 2), distance + size, distance)

    def event(e, _):
        row, col, plane, count = (ev_ref[4 * e + i] for i in range(4))
        rel = wrapped(row - row_start - half, NX)
        rel = rel + half

        @pl.when((count > 0) & (rel > -2 - RADIUS) & (rel < rows + 2 + RADIUS))
        def _():
            base = plane_start - plane
            dz = wrapped(slot + base, depth).astype(jnp.float32)
            dzb = wrapped(jnp.where(slot == 2, -2, -1) + base, depth).astype(jnp.float32)
            dza = wrapped(jnp.where(slot == 2, 5, 4) + base, depth).astype(jnp.float32)
            share = lambda d: jnp.where(slot == 0, 1.0, jnp.where(slot == 3, 0.0, IMPULSE * d))
            first = jnp.bitwise_and(col - RADIUS, ny - 1) // 128
            second = jnp.bitwise_and(col + RADIUS - 1, ny - 1) // 128

            def tile(t, _):
                index = jnp.where(t == 0, first, second)
                lanes = pl.ds(pl.multiple_of(index * 128, 128), 128)
                dy = wrapped(lane + index * 128 - col, ny).astype(jnp.float32)
                dy2 = dy * dy
                for h in range(2):
                    weight = jnp.where((sub >= 4) == (h == 1), count, 0).astype(jnp.float32)
                    low = jnp.clip(rel - RADIUS + 1 - h * half + 2, 0, half + 4) // 4
                    high = (jnp.clip(rel + RADIUS - 1 - h * half + 2, -1, half + 3) + 4) // 4

                    def chunk(n, _):
                        q = pl.ds(n * 4, 4)
                        dx = (step + (n * 4 - 2 + h * half - rel)).astype(jnp.float32)
                        flat = dx * dx + dy2
                        size = lambda d: jnp.maximum(1.0 - (flat + d * d) * (1.0 / (RADIUS * RADIUS)), 0.0) * weight
                        w = size(dz)
                        u_ref[0, q, :, lanes] += w
                        w = w * IMPULSE
                        u_ref[1, q, :, lanes] += w * dx
                        u_ref[2, q, :, lanes] += w * dy
                        u_ref[3, q, :, lanes] += w * dz
                        sb_ref[q, :, lanes] += size(dzb) * share(dzb)
                        sa_ref[q, :, lanes] += size(dza) * share(dza)
                        return 0

                    lax.fori_loop(low, high, chunk, 0)
                return 0

            lax.fori_loop(0, jnp.where(first == second, 1, 2), tile, 0)

        return 0

    lax.fori_loop(0, events, event, 0)

    def group(up_ref, down_ref, first, count):
        def messages(g, _):
            sub = lax.broadcasted_iota(jnp.int32, (8, ny), 0)
            lasts = [jnp.zeros((8, ny), jnp.float32) for _ in range(2)]
            for j in range(4):
                r = 4 * g + j
                p = r + first
                sb_out[p] = sb_ref[p + 2]
                sa_out[p] = sa_ref[p + 2]
                u = [u_ref[f, p + 2] for f in range(7)]
                near = [u[1], u[2], u[5], u[6]]
                up_ref[r] = gather_planes(near, 3)
                down_ref[r] = gather_planes(near, 0)
                f = fluxes(*shared(u[0], u[1:4], u[4:7]), u[1:4], u[4:7], 2)
                up_ref[count + r] = gather_planes(f[:4], 2)
                down_ref[count + r] = gather_planes(f[:4], 1)
                for i, plane in enumerate((2, 1)):
                    for h in range(2):
                        moved = turn(f[4], 2 * j + h - 4 * h - plane, 0)
                        lasts[i] = jnp.where(sub == 2 * j + h, moved, lasts[i])
            up_ref[2 * count + g] = lasts[0]
            down_ref[2 * count + g] = lasts[1]
            return 0

        lax.fori_loop(0, count // 4, messages, 0)

    split = up_0.shape[0] * 4 // 9
    group(up_0, down_0, 0, split)
    group(up_1, down_1, split, half - split)


def ends(below, above, c):
    return jnp.where(slots(below.shape) == 3, turn(above, 3 - c, 0), turn(below, -c, 0))


def along_y(f, b):
    near, far = NEAR * f, FAR * f
    return turn(b + near, 1, 1) + turn(b - near, -1, 1) + turn(far, -2, 1) - turn(far, 2, 1)


def along_z(f, b, near_f, near_u, far_f):
    slot = slots(b.shape)
    first, last = slot == 0, slot == 3
    outer = DIFFUSION * near_u
    if f is None:
        return jnp.where(first, outer, turn(b, 1, 0)) + jnp.where(last, outer, turn(b, -1, 0))
    near = NEAR * f
    outer += jnp.where(first, NEAR, -NEAR) * near_f
    out = jnp.where(first, outer, turn(b + near, 1, 0)) + jnp.where(last, outer, turn(b - near, -1, 0))
    beyond = jnp.where(slot == 1, turn(near_f, 1, 0), jnp.where(slot == 2, turn(near_f, -1, 0), far_f))
    return out + FAR * (jnp.where(slot <= 1, turn(f, -2, 0), beyond) - jnp.where(slot >= 2, turn(f, 2, 0), beyond))


def density_kernel(u_ref, below_ref, above_ref, sb_ref, sa_ref, order_ref, high_ref, low_ref, out_ref, wave_ref, d_ref):
    half = below_ref.shape[0]
    rows = 2 * half

    def body(p, _):
        rho, my, mz = u_ref[0, p + 2], u_ref[2, p + 2], u_ref[3, p + 2]
        below, above = below_ref[p] + sb_ref[p], above_ref[p] + sa_ref[p]
        b = DIFFUSION * rho
        new = rho * (1.0 - 6.0 * DIFFUSION)
        new += DIFFUSION * (u_ref[0, p + 1] + u_ref[0, p + 3])
        new += NEAR * (u_ref[1, p + 1] - u_ref[1, p + 3]) + FAR * (u_ref[1, p + 4] - u_ref[1, p])
        new += along_y(my, b)
        new += along_z(mz, b, ends(below, above, 1), ends(below, above, 0), ends(below, above, 2))
        unpair(out_ref, new, p)
        d_ref[pl.ds(pl.multiple_of(p * 8, 8), 8), :] = new
        return 0

    lax.fori_loop(0, half, body, 0)
    d = d_ref[...]
    order = order_ref[...]
    dot = functools.partial(jnp.dot, preferred_element_type=jnp.float32)
    high = d.astype(jnp.bfloat16)
    low = (d - high.astype(jnp.float32)).astype(jnp.bfloat16)
    high = dot(order, high).astype(jnp.bfloat16)
    low = dot(order, low).astype(jnp.bfloat16)
    for part in range(2):
        c_high, c_low = high_ref[part], low_ref[part]
        wave = dot(high, c_high) + dot(high, c_low) + dot(low, c_high)
        peers, band = wave_ref.shape[0], wave_ref.shape[4]
        for j in range(peers):
            for z in range(4):
                wave_ref[j, part, z] = wave[z * rows : (z + 1) * rows, j * band : (j + 1) * band]


def last_plane(below, above, j):
    sub = lax.broadcasted_iota(jnp.int32, below.shape, 0)
    out = turn(below, -2 * j, 0)
    out = jnp.where(sub == 3, turn(above, 3 - 2 * j, 0), out)
    out = jnp.where(sub == 4, turn(below, 3 - 2 * j, 0), out)
    return jnp.where(sub == 7, turn(above, 6 - 2 * j, 0), out)


def main_kernel(
    u_hbm, ba_ref, aa_ref, sb_ref, sa_ref, bn_ref, an_ref, bf_ref, af_ref, bl_ref, al_ref, *rest, first,
):
    mom_ref, mag_ref, u_ref, f_ref, sem = rest[-5:]
    chunk, total = ba_ref.shape[0], u_ref.shape[1]
    start = pl.program_id(0) * chunk
    kept = (0, 1, 2, 4, 5)

    @pl.when(pl.program_id(0) == 0)
    def _():
        copy = pltpu.make_async_copy(u_hbm.at[:, pl.ds(first, total)], u_ref, sem)
        copy.start()
        copy.wait()

        def fx(q, _):
            u = [u_ref[f, q] for f in range(7)]
            f = fluxes(*shared(u[0], u[1:4], u[4:7]), u[1:4], u[4:7], 0)
            for i, c in enumerate(kept):
                f_ref[i, q] = f[c]
            return 0

        lax.fori_loop(0, total, fx, 0)

    def row(r, g, j):
        q = start + r + 2
        u = [u_ref[f, q] for f in range(7)]
        v, pressure = shared(u[0], u[1:4], u[4:7])
        fy = fluxes(v, pressure, u[1:4], u[4:7], 1)
        fz = fluxes(v, pressure, u[1:4], u[4:7], 2)
        ba, aa = ba_ref[r] + sb_ref[r], aa_ref[r] + sa_ref[r]
        bn, an, bf, af = bn_ref[r], an_ref[r], bf_ref[r], af_ref[r]
        hm = [ends(bn, an, 0), ends(bn, an, 1), ends(ba, aa, 1)]
        hb = [ends(ba, aa, 3), ends(bn, an, 2), ends(bn, an, 3)]
        fh = fluxes(*shared(ends(ba, aa, 0), hm, hb), hm, hb, 2)
        halo = hm + hb
        far = [ends(bf, af, c) for c in range(4)] + [last_plane(bl_ref[g], al_ref[g], j), None]
        for c in range(6):
            field = u[c + 1]
            new = field * (1.0 - 6.0 * DIFFUSION)
            new += DIFFUSION * (u_ref[c + 1, q - 1] + u_ref[c + 1, q + 1])
            if c in kept:
                i = kept.index(c)
                new += NEAR * (f_ref[i, q - 1] - f_ref[i, q + 1]) + FAR * (f_ref[i, q + 2] - f_ref[i, q - 2])
            b = DIFFUSION * field
            if fy[c] is None:
                new += turn(b, 1, 1) + turn(b, -1, 1)
            else:
                new += along_y(fy[c], b)
            new += along_z(fz[c], b, fh[c], halo[c], far[c])
            if c == 0:
                slope = NEAR * (u_ref[7, q - 1] - u_ref[7, q + 1]) + FAR * (u_ref[7, q + 2] - u_ref[7, q - 2])
                new += u[0] * slope
            if c == 1:
                potential = u_ref[7, q]
                slope = NEAR * (turn(potential, 1, 1) - turn(potential, -1, 1))
                new += u[0] * (slope + FAR * (turn(potential, -2, 1) - turn(potential, 2, 1)))
            if c < 3:
                unpair(mom_ref, new, c, r)
            else:
                unpair(mag_ref, new, c - 3, r)

    def body(g, _):
        for j in range(4):
            row(4 * g + j, g, j)
        return 0

    lax.fori_loop(0, chunk // 4, body, 0)


def modes_kernel(at_ref, w_ref, ch_ref, cl_ref, sh_ref, sl_ref, out_ref, *, turned):
    dot = functools.partial(jnp.dot, preferred_element_type=jnp.float32)
    planes, band, nx = out_ref.shape[1:]

    def split(part):
        if turned:
            x = jnp.concatenate([w_ref[part, z] for z in range(planes)], axis=0)
        else:
            column = lambda z: jnp.concatenate([w_ref[j, part, z] for j in range(w_ref.shape[0])], axis=0)
            x = jnp.concatenate([column(z).T for z in range(planes)], axis=0)
        high = x.astype(jnp.bfloat16)
        return high, (x - high.astype(jnp.float32)).astype(jnp.bfloat16)

    re, im = split(0), split(1)
    times = lambda x, h, l: dot(x[0], h[...]) + dot(x[0], l[...]) + dot(x[1], h[...])
    scale = 1.0 / math.sqrt(NX * nx)
    shape = (band, nx)
    ky = lax.broadcasted_iota(jnp.int32, shape, 0) + at_ref[2]
    kx = lax.broadcasted_iota(jnp.int32, shape, 1)
    keep = jnp.where((ky == 0) & (kx == 0), 0.0, scale)
    out_re = times(re, ch_ref, cl_ref) + times(im, sh_ref, sl_ref)
    out_im = times(im, ch_ref, cl_ref) - times(re, sh_ref, sl_ref)
    for z in range(planes):
        out_ref[0, z] = out_re[z * band : (z + 1) * band] * keep
        out_ref[1, z] = out_im[z * band : (z + 1) * band] * keep


def cost(flops, bytes_accessed):
    return pl.CostEstimate(flops=int(flops), bytes_accessed=int(bytes_accessed), transcendentals=0)


def tables(size):
    angle = (np.outer(np.arange(size), np.arange(size)) % size) * (2.0 * np.pi / size)
    result = []
    for table in (np.cos(angle), np.sin(angle)):
        high = table.astype(np.float32).astype(ml_dtypes.bfloat16)
        low = (table - high.astype(np.float64)).astype(np.float32).astype(ml_dtypes.bfloat16)
        result += [high, low]
    return result


def row_order(half):
    matrix = np.zeros((8 * half, 8 * half), np.float32)
    for z in range(4):
        for h in range(2):
            for p in range(half):
                matrix[(z * 2 + h) * half + p, p * 8 + h * 4 + z] = 1.0
    return matrix.astype(ml_dtypes.bfloat16)


def shift(block, axis, step):
    n = lax.axis_size(axis)
    return lax.ppermute(block, axis, [(i, (i + step) % n) for i in range(n)])


def on_device(density, momentum, magnetic, arm_potential, sn_cells, sn_counts):
    rows, planes, ny = density.shape
    half = rows // 2
    layers, across = lax.axis_size("gz"), lax.axis_size("xy")
    devices = layers * across
    tile_row, tile_plane = lax.axis_index("xy"), lax.axis_index("gz")
    field = rows * planes * ny
    f32 = jnp.float32
    shape = jax.ShapeDtypeStruct
    whole = pl.BlockSpec(memory_space=pltpu.VMEM)
    smem = pl.BlockSpec(memory_space=pltpu.SMEM)
    params = pltpu.CompilerParams(vmem_limit_bytes=VMEM)
    message = shape((2, half, planes, ny), f32)
    tile = shape((half, 8, ny), f32)
    n0 = max(4, half * 5 // 32 * 4)
    counts = (n0, half - n0)

    slots_here = sn_cells.shape[0]
    mine = jnp.concatenate([sn_cells, sn_counts[:, None]], axis=1).reshape(1, 1, 4 * slots_here)
    mine = jnp.pad(mine, ((0, 0), (0, 0), (0, -(4 * slots_here) % 128)))
    events = lax.all_to_all(
        jnp.broadcast_to(mine, (devices, 1, mine.shape[2])), ("gz", "xy"), split_axis=0, concat_axis=0, tiled=True
    )
    events = events[:, 0, : 4 * slots_here].reshape(-1)
    at = jnp.stack([tile_row * rows, tile_plane * planes, tile_row * (ny // across)]).astype(jnp.int32)

    rho = density.reshape(2, half, planes, ny)
    mom = momentum.reshape(3, 2, half, planes, ny)
    mag = magnetic.reshape(3, 2, half, planes, ny)

    def edge(s):
        potential = jnp.broadcast_to(arm_potential[s][None, :, None, :], (1, 2, planes, ny))
        return jnp.concatenate([density[None, s], momentum[:, s], magnetic[:, s], potential], axis=0)

    before = shift(edge(slice(rows - 2, rows)), "xy", 1)
    after = shift(edge(slice(0, 2)), "xy", -1)

    one = lambda f: pl.BlockSpec((1, 2, half, planes, ny), lambda i, f=f: (f, 0, 0, 0, 0))
    full = lambda s: pl.BlockSpec(s, lambda i: (0,) * len(s))
    up, down = pl.pallas_call(
        pack_kernel,
        grid=(1,),
        in_specs=[full(message.shape), one(2), one(0)],
        out_specs=[full(tile.shape)] * 2,
        out_shape=[tile] * 2,
        compiler_params=params,
        cost_estimate=cost(*PACK_COST),
        name="pack",
    )(rho, mom, mag)
    below_a, above_a = shift(up, "gz", 1), shift(down, "gz", -1)

    parcels = [shape((9 * n // 4, 8, ny), f32) for n in counts]
    side = pltpu.VMEM((half + 4, 8, ny), f32)
    state, sb, sa, up_0, down_0, up_1, down_1 = pl.pallas_call(
        functools.partial(state_kernel, depth=planes * layers),
        in_specs=[smem, smem] + [whole] * 6,
        out_specs=[whole] * 7,
        out_shape=[shape((8, half + 4, 8, ny), f32), tile, tile, parcels[0], parcels[0], parcels[1], parcels[1]],
        scratch_shapes=[side, side],
        compiler_params=params,
        cost_estimate=cost(*STATE_COST),
        name="state",
    )(events, at, rho, mom, mag, arm_potential, before, after)
    parcels_below = [shift(up_0, "gz", 1)]
    parcels_above = [shift(down_0, "gz", -1)]
    parcels_below.append(shift(up_1, "gz", 1))
    parcels_above.append(shift(down_1, "gz", -1))

    cos_high, cos_low, sin_high, sin_low = tables(ny)
    band = ny // across
    new_density, wave = pl.pallas_call(
        density_kernel,
        grid=(1,),
        in_specs=[
            full((4, half + 4, 8, ny)), full(tile.shape), full(tile.shape), full(tile.shape), full(tile.shape),
            full((8 * half, 8 * half)), full((2, ny, ny)), full((2, ny, ny)),
        ],
        out_specs=[full(message.shape), full((across, 2, planes, rows, band))],
        out_shape=[message, shape((across, 2, planes, rows, band), f32)],
        scratch_shapes=[pltpu.VMEM((8 * half, ny), f32)],
        compiler_params=params,
        cost_estimate=cost(*DENSITY_COST),
        name="density",
    )(
        state, below_a, above_a, sb, sa, row_order(half), np.stack([cos_high, -sin_high]), np.stack([cos_low, -sin_low]),
    )
    portion = lax.all_to_all(wave, "xy", split_axis=0, concat_axis=0, tiled=True)

    turned = band % 128 != 0
    if turned:
        portion = portion.transpose(1, 2, 4, 0, 3).reshape(2, planes, band, NX)
    modes = pl.pallas_call(
        functools.partial(modes_kernel, turned=turned),
        in_specs=[smem] + [whole] * 5,
        out_specs=whole,
        out_shape=shape((2, planes, band, NX), f32),
        compiler_params=params,
        cost_estimate=cost(*MODES_COST),
        name="modes",
    )(at, portion, *tables(NX))
    results = [shape((3, 2, half, planes, ny), f32)] * 2
    new = []
    for i, n in enumerate(counts):
        first = i * n0
        chunk = math.gcd(math.gcd(n0, half - n0), 8)
        here = pl.BlockSpec((chunk, 8, ny), lambda k, o=first // chunk: (o + k, 0, 0))
        near = pl.BlockSpec((chunk, 8, ny), lambda k: (k, 0, 0))
        far = pl.BlockSpec((chunk, 8, ny), lambda k, o=n // chunk: (o + k, 0, 0))
        last = pl.BlockSpec((chunk // 4, 8, ny), lambda k, o=8 * n // chunk: (o + k, 0, 0))
        three = pl.BlockSpec((3, 2, chunk, planes, ny), lambda k, o=first // chunk: (0, 0, o + k, 0, 0))
        below, above = parcels_below[i], parcels_above[i]
        extra = [*new, modes] if new else []
        new = pl.pallas_call(
            functools.partial(main_kernel, first=first),
            grid=(n // chunk,),
            in_specs=[pl.BlockSpec(memory_space=pl.ANY)] + [here] * 4 + [near] * 2 + [far] * 2 + [last] * 2
            + [pl.BlockSpec(memory_space=pl.ANY)] * len(extra),
            out_specs=[three, three],
            out_shape=results,
            scratch_shapes=[
                pltpu.VMEM((8, n + 4, 8, ny), f32), pltpu.VMEM((5, n + 4, 8, ny), f32), pltpu.SemaphoreType.DMA,
            ],
            input_output_aliases={11: 0, 12: 1} if new else {},
            compiler_params=pltpu.CompilerParams(vmem_limit_bytes=62 * 1024 * 1024),
            cost_estimate=cost(*MAIN_COST),
            name=f"main{i}",
        )(state, below_a, above_a, sb, sa, below, above, below, above, below, above, *extra)
    new_mom, new_mag = new

    return (
        new_density.reshape(rows, planes, ny),
        new_mom.reshape(3, rows, planes, ny),
        new_mag.reshape(3, rows, planes, ny),
        modes,
    )


def solution(mesh):
    in_specs = (
        P("xy", "gz", None),
        P(None, "xy", "gz", None),
        P(None, "xy", "gz", None),
        P("xy", None),
        P(("gz", "xy"), None),
        P(("gz", "xy")),
    )
    out_specs = (
        P("xy", "gz", None),
        P(None, "xy", "gz", None),
        P(None, "xy", "gz", None),
        P(None, "gz", "xy", None),
    )
    return jax.shard_map(
        on_device, mesh=mesh, in_specs=in_specs, out_specs=out_specs, check_vma=False
    )
```

```python
import functools
import math

import jax
import jax.numpy as jnp
import ml_dtypes
import numpy as np
from jax import lax
from jax.experimental import pallas as pl
from jax.experimental.pallas import tpu as pltpu
from jax.sharding import PartitionSpec as P

NX = 512
RADIUS = 16
IMPULSE = 2.0 / 16
TIME_STEP = 0.1
DIFFUSION = 0.05
NEAR = 8.0 * TIME_STEP / 12.0
FAR = TIME_STEP / 12.0
VMEM = 56 * 1024 * 1024
PACK_COST = DENSITY_COST = MODES_COST = (1e6, 1e5)
STATE_COST = MAIN_COST = (1e6, 4e8)


def pair(ref, *index):
    return jnp.concatenate([ref[(*index[:-1], 0, index[-1])], ref[(*index[:-1], 1, index[-1])]], axis=0)


def unpair(ref, value, *index):
    ref[(*index[:-1], 0, index[-1])] = value[:4]
    ref[(*index[:-1], 1, index[-1])] = value[4:]


def slots(shape):
    sub = lax.broadcasted_iota(jnp.int32, shape, len(shape) - 2)
    return jnp.where(sub >= 4, sub - 4, sub)


def turn(value, shift, axis):
    return pltpu.roll(value, shift % value.shape[axis], axis)


def gather_planes(values, plane):
    slot = slots(values[0].shape)
    out = turn(values[-1], len(values) - 1 - plane, 0)
    for c in reversed(range(len(values) - 1)):
        out = jnp.where(slot == c, turn(values[c], c - plane, 0), out)
    return out


def shared(rho, m, b):
    inv = 1.0 / rho
    return [x * inv for x in m], rho + 0.5 * (b[0] * b[0] + b[1] * b[1] + b[2] * b[2])


def fluxes(v, total, m, b, k):
    push = [m[i] * v[k] - b[i] * b[k] + (total if i == k else 0.0) for i in range(3)]
    turned = [None if i == k else v[k] * b[i] - b[k] * v[i] for i in range(3)]
    return push + turned


def pack_kernel(rho_ref, mz_ref, bx_ref, rho_a, mom_a, mag_a, pot_a, rho_z, mom_z, mag_z, pot_z, up_ref, down_ref, first_ref, last_ref):
    for ref, rho, mom, mag, pot, skip in (
        (first_ref, rho_a, mom_a, mag_a, pot_a, 0), (last_ref, rho_z, mom_z, mag_z, pot_z, pot_z.shape[0] - 2),
    ):
        for j in range(2):
            ref[0, j] = rho[0, j]
            for c in range(3):
                ref[1 + c, j] = mom[c, 0, j]
                ref[4 + c, j] = mag[c, 0, j]
            ref[7, j] = jnp.broadcast_to(pot[skip + j : skip + j + 1], ref.shape[2:])
    half = rho_ref.shape[1]

    def body(p, _):
        rho, mz, bx = pair(rho_ref, p), pair(mz_ref, 0, p), pair(bx_ref, 0, p)
        slot = slots(rho.shape)
        up = jnp.where(slot == 2, mz, gather_planes([rho, mz, mz, bx], 3))
        down = jnp.where(slot == 2, turn(mz, 1, 0), gather_planes([rho, mz, mz, bx], 0))
        up_ref[p] = up
        down_ref[p] = down
        return 0

    lax.fori_loop(0, half, body, 0)


def state_kernel(
    ev_ref, at_ref, rho_ref, mom_ref, mag_ref, pot_ref, before_ref, after_ref, rho_l, mom_l, mag_l, pot_l,
    rho_h, mom_h, mag_h, pot_h, u_out, edge_out, sb_out, sa_out, *rest, depth, counts,
):
    ups, downs, (s_ref, sb_ref, sa_ref) = rest[: len(rest) // 2 - 1], rest[len(rest) // 2 - 1 : -3], rest[-3:]
    half, ny = s_ref.shape[1] - 4, s_ref.shape[3]
    step_id = pl.program_id(0)

    @pl.when(step_id == 0)
    def _():
        deposit(ev_ref, at_ref, s_ref, sb_ref, sa_ref, depth)
        pieces = lambda rho, mom, mag, pot, j: (
            [rho[0, j]] + [mom[c, 0, j] for c in range(3)] + [mag[c, 0, j] for c in range(3)]
            + [jnp.broadcast_to(pot, (4, ny))]
        )
        for j in range(2):
            low = pieces(rho_l, mom_l, mag_l, pot_l[0, 6 + j : 7 + j], j)
            high = pieces(rho_h, mom_h, mag_h, pot_h[0, j : j + 1], j)
            for f in range(8):
                left = jnp.concatenate([before_ref[f, j], low[f]], axis=0)
                right = jnp.concatenate([high[f], after_ref[f, j]], axis=0)
                edge_out[f, j] = left + s_ref[f, j] if f < 4 else left
                edge_out[f, 2 + j] = right + s_ref[f, half + 2 + j] if f < 4 else right

    start = step_id * 8
    sub = lax.broadcasted_iota(jnp.int32, (8, ny), 0)
    begin = 0
    for up_ref, down_ref, count in zip(ups, downs, counts):

        @pl.when((step_id >= begin) & (step_id < begin + count))
        def _(up_ref=up_ref, down_ref=down_ref, begin=begin):
            k = step_id - begin

            def messages(g, _):
                lasts = [jnp.zeros((8, ny), jnp.float32) for _ in range(2)]
                for j in range(4):
                    r = 4 * g + j
                    q = start + r + 2
                    sb_out[r] = sb_ref[q]
                    sa_out[r] = sa_ref[q]
                    u = [pair(rho_ref, r) + s_ref[0, q]]
                    u += [pair(mom_ref, c, r) + s_ref[1 + c, q] for c in range(3)]
                    u += [pair(mag_ref, c, r) for c in range(3)]
                    for f in range(7):
                        u_out[f, r] = u[f]
                    rows = [jnp.broadcast_to(pot_ref[h, pl.ds(r, 1), :], (4, ny)) for h in range(2)]
                    u_out[7, r] = jnp.concatenate(rows, axis=0)
                    near = [u[1], u[2], u[5], u[6]]
                    up_ref[0, r] = gather_planes(near, 3)
                    down_ref[0, r] = gather_planes(near, 0)
                    f = fluxes(*shared(u[0], u[1:4], u[4:7]), u[1:4], u[4:7], 2)
                    up_ref[0, 8 + r] = gather_planes(f[:4], 2)
                    down_ref[0, 8 + r] = gather_planes(f[:4], 1)
                    for i, plane in enumerate((2, 1)):
                        for h in range(2):
                            moved = turn(f[4], 2 * j + h - 4 * h - plane, 0)
                            lasts[i] = jnp.where(sub == 2 * j + h, moved, lasts[i])
                up_ref[0, 16 + g] = lasts[0]
                down_ref[0, 16 + g] = lasts[1]
                return 0

            lax.fori_loop(0, 2, messages, 0)

        begin += count


def deposit(ev_ref, at_ref, s_ref, sb_ref, sa_ref, depth):
    half, ny = s_ref.shape[1] - 4, s_ref.shape[3]
    rows, events = 2 * half, ev_ref.shape[0] // 4
    row_start, plane_start = at_ref[0], at_ref[1]
    s_ref[...] = jnp.zeros_like(s_ref)
    sb_ref[...] = jnp.zeros_like(sb_ref)
    sa_ref[...] = jnp.zeros_like(sa_ref)

    shape = (4, 8, 128)
    slot = slots(shape)
    sub = lax.broadcasted_iota(jnp.int32, shape, 1)
    step = lax.broadcasted_iota(jnp.int32, shape, 0)
    lane = lax.broadcasted_iota(jnp.int32, shape, 2)

    def wrapped(distance, size):
        distance = jnp.where(distance >= size // 2, distance - size, distance)
        return jnp.where(distance < -(size // 2), distance + size, distance)

    def event(e, _):
        row, col, plane, count = (ev_ref[4 * e + i] for i in range(4))
        rel = wrapped(row - row_start - half, NX)
        rel = rel + half

        @pl.when((count > 0) & (rel > -2 - RADIUS) & (rel < rows + 2 + RADIUS))
        def _():
            base = plane_start - plane
            dz = wrapped(slot + base, depth).astype(jnp.float32)
            dzb = wrapped(jnp.where(slot == 2, -2, -1) + base, depth).astype(jnp.float32)
            dza = wrapped(jnp.where(slot == 2, 5, 4) + base, depth).astype(jnp.float32)
            share = lambda d: jnp.where(slot == 0, 1.0, jnp.where(slot == 3, 0.0, IMPULSE * d))
            first = jnp.bitwise_and(col - RADIUS, ny - 1) // 128
            second = jnp.bitwise_and(col + RADIUS - 1, ny - 1) // 128

            def tile(t, _):
                index = jnp.where(t == 0, first, second)
                lanes = pl.ds(pl.multiple_of(index * 128, 128), 128)
                dy = wrapped(lane + index * 128 - col, ny).astype(jnp.float32)
                dy2 = dy * dy
                for h in range(2):
                    weight = jnp.where((sub >= 4) == (h == 1), count, 0).astype(jnp.float32)
                    low = jnp.clip(rel - RADIUS + 1 - h * half + 2, 0, half + 4) // 4
                    high = (jnp.clip(rel + RADIUS - 1 - h * half + 2, -1, half + 3) + 4) // 4

                    def chunk(n, _):
                        q = pl.ds(n * 4, 4)
                        dx = (step + (n * 4 - 2 + h * half - rel)).astype(jnp.float32)
                        flat = dx * dx + dy2
                        size = lambda d: jnp.maximum(1.0 - (flat + d * d) * (1.0 / (RADIUS * RADIUS)), 0.0) * weight
                        w = size(dz)
                        s_ref[0, q, :, lanes] += w
                        w = w * IMPULSE
                        s_ref[1, q, :, lanes] += w * dx
                        s_ref[2, q, :, lanes] += w * dy
                        s_ref[3, q, :, lanes] += w * dz
                        sb_ref[q, :, lanes] += size(dzb) * share(dzb)
                        sa_ref[q, :, lanes] += size(dza) * share(dza)
                        return 0

                    lax.fori_loop(low, high, chunk, 0)
                return 0

            lax.fori_loop(0, jnp.where(first == second, 1, 2), tile, 0)

        return 0

    lax.fori_loop(0, events, event, 0)


def ends(below, above, c):
    return jnp.where(slots(below.shape) == 3, turn(above, 3 - c, 0), turn(below, -c, 0))


def along_y(f, b):
    near, far = NEAR * f, FAR * f
    return turn(b + near, 1, 1) + turn(b - near, -1, 1) + turn(far, -2, 1) - turn(far, 2, 1)


def along_z(f, b, near_f, near_u, far_f):
    slot = slots(b.shape)
    first, last = slot == 0, slot == 3
    outer = DIFFUSION * near_u
    if f is None:
        return jnp.where(first, outer, turn(b, 1, 0)) + jnp.where(last, outer, turn(b, -1, 0))
    near = NEAR * f
    outer += jnp.where(first, NEAR, -NEAR) * near_f
    out = jnp.where(first, outer, turn(b + near, 1, 0)) + jnp.where(last, outer, turn(b - near, -1, 0))
    beyond = jnp.where(slot == 1, turn(near_f, 1, 0), jnp.where(slot == 2, turn(near_f, -1, 0), far_f))
    return out + FAR * (jnp.where(slot <= 1, turn(f, -2, 0), beyond) - jnp.where(slot >= 2, turn(f, 2, 0), beyond))


def fetch(u_hbm, edge_hbm, u_ref, sem, first):
    fields, total = u_ref.shape[:2]
    half = u_hbm.shape[1]
    low, high = max(first - 2, 0), min(first + total - 2, half)
    copies = [pltpu.make_async_copy(u_hbm.at[:fields, low:high], u_ref.at[:, low - first + 2 : high - first + 2], sem.at[0])]
    if first == 0:
        copies.append(pltpu.make_async_copy(edge_hbm.at[:fields, 0:2], u_ref.at[:, 0:2], sem.at[1]))
    if first + total - 4 == half:
        copies.append(pltpu.make_async_copy(edge_hbm.at[:fields, 2:4], u_ref.at[:, total - 2 : total], sem.at[2]))
    for copy in copies:
        copy.start()
    for copy in copies:
        copy.wait()


def density_kernel(
    at_ref, u_hbm, edge_hbm, below_ref, above_ref, sb_ref, sa_ref, order_ref, high_ref, low_ref, out_ref, *rest,
):
    *waves, d_ref, w_ref, u_ref, sem = rest
    fetch(u_hbm, edge_hbm, u_ref, sem, 0)
    half = below_ref.shape[0]
    rows = 2 * half

    def body(p, _):
        rho, my, mz = u_ref[0, p + 2], u_ref[2, p + 2], u_ref[3, p + 2]
        below, above = below_ref[p] + sb_ref[p], above_ref[p] + sa_ref[p]
        b = DIFFUSION * rho
        new = rho * (1.0 - 6.0 * DIFFUSION)
        new += DIFFUSION * (u_ref[0, p + 1] + u_ref[0, p + 3])
        new += NEAR * (u_ref[1, p + 1] - u_ref[1, p + 3]) + FAR * (u_ref[1, p + 4] - u_ref[1, p])
        new += along_y(my, b)
        new += along_z(mz, b, ends(below, above, 1), ends(below, above, 0), ends(below, above, 2))
        unpair(out_ref, new, p)
        d_ref[pl.ds(pl.multiple_of(p * 8, 8), 8), :] = new
        return 0

    lax.fori_loop(0, half, body, 0)
    d = d_ref[...]
    order = order_ref[...]
    dot = functools.partial(jnp.dot, preferred_element_type=jnp.float32)
    high = d.astype(jnp.bfloat16)
    low = (d - high.astype(jnp.float32)).astype(jnp.bfloat16)
    high = dot(order, high).astype(jnp.bfloat16)
    low = dot(order, low).astype(jnp.bfloat16)
    for part in range(2):
        c_high, c_low = high_ref[part], low_ref[part]
        wave = dot(high, c_high) + dot(high, c_low) + dot(low, c_high)
        if len(waves) == 1:
            peers, band = waves[0].shape[0], waves[0].shape[4]
            for j in range(peers):
                for z in range(4):
                    waves[0][j, part, z] = wave[z * rows : (z + 1) * rows, j * band : (j + 1) * band]
            continue
        w_ref[...] = wave
        me = at_ref[0] // rows
        for s, ref in enumerate(waves):
            peer = jnp.where(me + s >= len(waves), me + s - len(waves), me + s)
            lanes = pl.ds(pl.multiple_of(peer * 128, 128) if ref.shape[3] == 128 else peer * ref.shape[3], ref.shape[3])
            for z in range(4):
                ref[part, z] = w_ref[z * rows : (z + 1) * rows, lanes]


def last_plane(below, above, j):
    sub = lax.broadcasted_iota(jnp.int32, below.shape, 0)
    out = turn(below, -2 * j, 0)
    out = jnp.where(sub == 3, turn(above, 3 - 2 * j, 0), out)
    out = jnp.where(sub == 4, turn(below, 3 - 2 * j, 0), out)
    return jnp.where(sub == 7, turn(above, 6 - 2 * j, 0), out)


def main_kernel(u_hbm, edge_hbm, ba_ref, aa_ref, sb_ref, sa_ref, from_below, from_above, *rest, first):
    mom_ref, mag_ref, u_ref, f_ref, sem = rest[-5:]
    chunk, total = ba_ref.shape[0], u_ref.shape[1]
    start = pl.program_id(0) * chunk
    kept = (0, 1, 2, 4, 5)

    @pl.when(pl.program_id(0) == 0)
    def _():
        fetch(u_hbm, edge_hbm, u_ref, sem, first)

        def fx(q, _):
            u = [u_ref[f, q] for f in range(7)]
            f = fluxes(*shared(u[0], u[1:4], u[4:7]), u[1:4], u[4:7], 0)
            for i, c in enumerate(kept):
                f_ref[i, q] = f[c]
            return 0

        lax.fori_loop(0, total, fx, 0)

    def row(r, g, j):
        q = start + r + 2
        u = [u_ref[f, q] for f in range(7)]
        v, pressure = shared(u[0], u[1:4], u[4:7])
        fy = fluxes(v, pressure, u[1:4], u[4:7], 1)
        fz = fluxes(v, pressure, u[1:4], u[4:7], 2)
        ba, aa = ba_ref[r] + sb_ref[r], aa_ref[r] + sa_ref[r]
        bn, an, bf, af = from_below[0, r], from_above[0, r], from_below[0, 8 + r], from_above[0, 8 + r]
        hm = [ends(bn, an, 0), ends(bn, an, 1), ends(ba, aa, 1)]
        hb = [ends(ba, aa, 3), ends(bn, an, 2), ends(bn, an, 3)]
        fh = fluxes(*shared(ends(ba, aa, 0), hm, hb), hm, hb, 2)
        halo = hm + hb
        far = [ends(bf, af, c) for c in range(4)] + [last_plane(from_below[0, 16 + g], from_above[0, 16 + g], j), None]
        for c in range(6):
            field = u[c + 1]
            new = field * (1.0 - 6.0 * DIFFUSION)
            new += DIFFUSION * (u_ref[c + 1, q - 1] + u_ref[c + 1, q + 1])
            if c in kept:
                i = kept.index(c)
                new += NEAR * (f_ref[i, q - 1] - f_ref[i, q + 1]) + FAR * (f_ref[i, q + 2] - f_ref[i, q - 2])
            b = DIFFUSION * field
            if fy[c] is None:
                new += turn(b, 1, 1) + turn(b, -1, 1)
            else:
                new += along_y(fy[c], b)
            new += along_z(fz[c], b, fh[c], halo[c], far[c])
            if c == 0:
                slope = NEAR * (u_ref[7, q - 1] - u_ref[7, q + 1]) + FAR * (u_ref[7, q + 2] - u_ref[7, q - 2])
                new += u[0] * slope
            if c == 1:
                potential = u_ref[7, q]
                slope = NEAR * (turn(potential, 1, 1) - turn(potential, -1, 1))
                new += u[0] * (slope + FAR * (turn(potential, -2, 1) - turn(potential, 2, 1)))
            if c < 3:
                unpair(mom_ref, new, c, r)
            else:
                unpair(mag_ref, new, c - 3, r)

    def body(g, _):
        for j in range(4):
            row(4 * g + j, g, j)
        return 0

    lax.fori_loop(0, chunk // 4, body, 0)


def modes_kernel(at_ref, *rest, turned):
    *pieces, ch_ref, cl_ref, sh_ref, sl_ref, out_ref, x_ref = rest
    dot = functools.partial(jnp.dot, preferred_element_type=jnp.float32)
    planes, band, nx = out_ref.shape[1:]

    def split(part):
        if turned:
            x = jnp.concatenate([pieces[0][part, z] for z in range(planes)], axis=0)
        else:
            width = nx // len(pieces)
            me = at_ref[0] // width
            for s, ref in enumerate(pieces):
                peer = jnp.where(me - s < 0, me - s + len(pieces), me - s)
                lanes = pl.ds(pl.multiple_of(peer * 128, 128) if width == 128 else peer * width, width)
                for z in range(planes):
                    x_ref[z * band : (z + 1) * band, lanes] = ref[part, z].T
            x = x_ref[...]
        high = x.astype(jnp.bfloat16)
        return high, (x - high.astype(jnp.float32)).astype(jnp.bfloat16)

    re, im = split(0), split(1)
    times = lambda x, h, l: dot(x[0], h[...]) + dot(x[0], l[...]) + dot(x[1], h[...])
    scale = 1.0 / math.sqrt(NX * nx)
    shape = (band, nx)
    ky = lax.broadcasted_iota(jnp.int32, shape, 0) + at_ref[2]
    kx = lax.broadcasted_iota(jnp.int32, shape, 1)
    keep = jnp.where((ky == 0) & (kx == 0), 0.0, scale)
    out_re = times(re, ch_ref, cl_ref) + times(im, sh_ref, sl_ref)
    out_im = times(im, ch_ref, cl_ref) - times(re, sh_ref, sl_ref)
    for z in range(planes):
        out_ref[0, z] = out_re[z * band : (z + 1) * band] * keep
        out_ref[1, z] = out_im[z * band : (z + 1) * band] * keep


def cost(flops, bytes_accessed):
    return pl.CostEstimate(flops=int(flops), bytes_accessed=int(bytes_accessed), transcendentals=0)


def tables(size):
    angle = (np.outer(np.arange(size), np.arange(size)) % size) * (2.0 * np.pi / size)
    result = []
    for table in (np.cos(angle), np.sin(angle)):
        high = table.astype(np.float32).astype(ml_dtypes.bfloat16)
        low = (table - high.astype(np.float64)).astype(np.float32).astype(ml_dtypes.bfloat16)
        result += [high, low]
    return result


def row_order(half):
    matrix = np.zeros((8 * half, 8 * half), np.float32)
    for z in range(4):
        for h in range(2):
            for p in range(half):
                matrix[(z * 2 + h) * half + p, p * 8 + h * 4 + z] = 1.0
    return matrix.astype(ml_dtypes.bfloat16)


def shift(block, axis, step):
    n = lax.axis_size(axis)
    return lax.ppermute(block, axis, [(i, (i + step) % n) for i in range(n)])


def on_device(density, momentum, magnetic, arm_potential, sn_cells, sn_counts):
    rows, planes, ny = density.shape
    half = rows // 2
    layers, across = lax.axis_size("gz"), lax.axis_size("xy")
    devices = layers * across
    tile_row, tile_plane = lax.axis_index("xy"), lax.axis_index("gz")
    field = rows * planes * ny
    f32 = jnp.float32
    shape = jax.ShapeDtypeStruct
    whole = pl.BlockSpec(memory_space=pltpu.VMEM)
    smem = pl.BlockSpec(memory_space=pltpu.SMEM)
    params = pltpu.CompilerParams(vmem_limit_bytes=VMEM)
    message = shape((2, half, planes, ny), f32)
    tile = shape((half, 8, ny), f32)
    steps = half // 8
    counts = (steps // 4, (steps - steps // 4) // 2, steps - steps // 4 - (steps - steps // 4) // 2) if steps >= 4 else (steps,)

    slots_here = sn_cells.shape[0]
    mine = jnp.concatenate([sn_cells, sn_counts[:, None]], axis=1).reshape(1, 1, 4 * slots_here)
    mine = jnp.pad(mine, ((0, 0), (0, 0), (0, -(4 * slots_here) % 128)))
    events = lax.all_to_all(
        jnp.broadcast_to(mine, (devices, 1, mine.shape[2])), ("gz", "xy"), split_axis=0, concat_axis=0, tiled=True
    )
    events = events[:, 0, : 4 * slots_here].reshape(-1)
    at = jnp.stack([tile_row * rows, tile_plane * planes, tile_row * (ny // across)]).astype(jnp.int32)

    rho = density.reshape(2, half, planes, ny)
    mom = momentum.reshape(3, 2, half, planes, ny)
    mag = magnetic.reshape(3, 2, half, planes, ny)

    pot = arm_potential.reshape(2, half, ny)
    one = lambda f: pl.BlockSpec((1, 2, half, planes, ny), lambda i, f=f: (f, 0, 0, 0, 0))
    full = lambda s: pl.BlockSpec(s, lambda i: (0,) * len(s))
    edges = shape((8, 2, planes, ny), f32)
    up, down, first_rows, last_rows = pl.pallas_call(
        pack_kernel,
        grid=(1,),
        in_specs=[full(message.shape), one(2), one(0)] + [
            spec
            for h, k in ((0, 0), (1, half // 2 - 1))
            for spec in (
                pl.BlockSpec((1, 2, planes, ny), lambda i, h=h, k=k: (h, k, 0, 0)),
                pl.BlockSpec((3, 1, 2, planes, ny), lambda i, h=h, k=k: (0, h, k, 0, 0)),
                pl.BlockSpec((3, 1, 2, planes, ny), lambda i, h=h, k=k: (0, h, k, 0, 0)),
                pl.BlockSpec((8, ny), lambda i, h=h: (h * (rows // 8 - 1), 0)),
            )
        ],
        out_specs=[full(tile.shape)] * 2 + [full(edges.shape)] * 2,
        out_shape=[tile] * 2 + [edges] * 2,
        compiler_params=params,
        cost_estimate=cost(*PACK_COST),
        name="pack",
    )(rho, mom, mag, *[rho, mom, mag, arm_potential] * 2)
    before, after = shift(last_rows, "xy", 1), shift(first_rows, "xy", -1)
    below_a, above_a = shift(up, "gz", 1), shift(down, "gz", -1)

    parcels = [shape((n, 18, 8, ny), f32) for n in counts]
    side = pltpu.VMEM((half + 4, 8, ny), f32)
    begins = [sum(counts[:i]) for i in range(len(counts))]
    parcel_specs = [
        pl.BlockSpec((1, 18, 8, ny), lambda i, b=b, n=n: (jnp.clip(i - b, 0, n - 1), 0, 0, 0)) for b, n in zip(begins, counts)
    ]
    eight = pl.BlockSpec((8, 8, ny), lambda i: (i, 0, 0))
    middle = [
        spec
        for h, k in ((0, steps - 1), (1, 0))
        for spec in (
            pl.BlockSpec((1, 2, planes, ny), lambda i, h=h, k=k: (h, k * 4 + 3 * (1 - h), 0, 0)),
            pl.BlockSpec((3, 1, 2, planes, ny), lambda i, h=h, k=k: (0, h, k * 4 + 3 * (1 - h), 0, 0)),
            pl.BlockSpec((3, 1, 2, planes, ny), lambda i, h=h, k=k: (0, h, k * 4 + 3 * (1 - h), 0, 0)),
            pl.BlockSpec((1, 8, ny), lambda i, h=h, k=k: (h, k, 0)),
        )
    ]
    rows_of = lambda n: pl.BlockSpec((n, 2, 8, planes, ny), lambda i: (0, 0, i, 0, 0))
    state, edge, sb, sa, *messages = pl.pallas_call(
        functools.partial(state_kernel, depth=planes * layers, counts=counts),
        grid=(steps,),
        in_specs=[
            smem, smem, pl.BlockSpec((2, 8, planes, ny), lambda i: (0, i, 0, 0)), rows_of(3), rows_of(3),
            pl.BlockSpec((2, 8, ny), lambda i: (0, i, 0)), full(edges.shape), full(edges.shape),
        ] + middle,
        out_specs=[pl.BlockSpec((8, 8, 8, ny), lambda i: (0, i, 0, 0)), full((8, 4, 8, ny)), eight, eight] + parcel_specs * 2,
        out_shape=[shape((8, half, 8, ny), f32), shape((8, 4, 8, ny), f32), tile, tile] + parcels * 2,
        scratch_shapes=[pltpu.VMEM((4, half + 4, 8, ny), f32), side, side],
        compiler_params=params,
        cost_estimate=cost(*STATE_COST),
        name="state",
    )(events, at, rho, mom, mag, pot, before, after, *[rho, mom, mag, pot] * 2)
    parcels_below, parcels_above = [], []
    for i in range(len(counts)):
        parcels_below.append(shift(messages[i], "gz", 1))
        parcels_above.append(shift(messages[len(counts) + i], "gz", -1))

    cos_high, cos_low, sin_high, sin_low = tables(ny)
    band = ny // across
    turned = band % 128 != 0 or rows % 128 != 0
    waves = [shape((across, 2, planes, rows, band), f32)] if turned else [shape((2, planes, rows, band), f32)] * across
    hbm = pl.BlockSpec(memory_space=pl.ANY)
    copies = pltpu.SemaphoreType.DMA((3,))
    new_density, *waves = pl.pallas_call(
        density_kernel,
        in_specs=[smem, hbm, hbm] + [whole] * 7,
        out_specs=[whole] * (1 + len(waves)),
        out_shape=[message, *waves],
        scratch_shapes=[
            pltpu.VMEM((8 * half, ny), f32), pltpu.VMEM((8 * half, ny), f32), pltpu.VMEM((4, half + 4, 8, ny), f32), copies,
        ],
        compiler_params=params,
        cost_estimate=cost(*DENSITY_COST),
        name="density",
    )(
        at, state, edge, below_a, above_a, sb, sa, row_order(half),
        np.stack([cos_high, -sin_high]), np.stack([cos_low, -sin_low]),
    )

    if turned:
        portion = lax.all_to_all(waves[0], "xy", split_axis=0, concat_axis=0, tiled=True)
        pieces = [portion.transpose(1, 2, 4, 0, 3).reshape(2, planes, band, NX)]
    else:
        pieces = waves[:1] + [shift(waves[s], "xy", s) for s in range(1, across)]
    modes = pl.pallas_call(
        functools.partial(modes_kernel, turned=turned),
        in_specs=[smem] + [whole] * (len(pieces) + 4),
        out_specs=whole,
        out_shape=shape((2, planes, band, NX), f32),
        scratch_shapes=[pltpu.VMEM((planes * band, NX), f32)],
        compiler_params=params,
        cost_estimate=cost(*MODES_COST),
        name="modes",
    )(at, *pieces, *tables(NX))
    results = [shape((3, 2, half, planes, ny), f32)] * 2
    new = []
    for i, n in enumerate(counts):
        chunk, first = 8, begins[i] * 8
        here = pl.BlockSpec((chunk, 8, ny), lambda k, o=begins[i]: (o + k, 0, 0))
        parcel = pl.BlockSpec((1, 18, 8, ny), lambda k: (k, 0, 0, 0))
        three = pl.BlockSpec((3, 2, chunk, planes, ny), lambda k, o=begins[i]: (0, 0, o + k, 0, 0))
        below, above = parcels_below[i], parcels_above[i]
        extra = [*new] + [modes] * (i > 0 and i == len(counts) - 1)
        new = pl.pallas_call(
            functools.partial(main_kernel, first=first),
            grid=(n,),
            in_specs=[hbm, hbm] + [here] * 4 + [parcel] * 2 + [hbm] * len(extra),
            out_specs=[three, three],
            out_shape=results,
            scratch_shapes=[
                pltpu.VMEM((8, n * 8 + 4, 8, ny), f32), pltpu.VMEM((5, n * 8 + 4, 8, ny), f32), copies,
            ],
            input_output_aliases={8: 0, 9: 1} if new else {},
            compiler_params=pltpu.CompilerParams(vmem_limit_bytes=62 * 1024 * 1024),
            cost_estimate=cost(*MAIN_COST),
            name=f"main{i}",
        )(state, edge, below_a, above_a, sb, sa, below, above, *extra)
    new_mom, new_mag = new

    return (
        new_density.reshape(rows, planes, ny),
        new_mom.reshape(3, rows, planes, ny),
        new_mag.reshape(3, rows, planes, ny),
        modes,
    )


def solution(mesh):
    in_specs = (
        P("xy", "gz", None),
        P(None, "xy", "gz", None),
        P(None, "xy", "gz", None),
        P("xy", None),
        P(("gz", "xy"), None),
        P(("gz", "xy")),
    )
    out_specs = (
        P("xy", "gz", None),
        P(None, "xy", "gz", None),
        P(None, "xy", "gz", None),
        P(None, "gz", "xy", None),
    )
    return jax.shard_map(
        on_device, mesh=mesh, in_specs=in_specs, out_specs=out_specs, check_vma=False
    )
```

```python
import functools
import math

import jax
import jax.numpy as jnp
import ml_dtypes
import numpy as np
from jax import lax
from jax.experimental import pallas as pl
from jax.experimental.pallas import tpu as pltpu
from jax.sharding import PartitionSpec as P

NX = 512
RADIUS = 16
IMPULSE = 2.0 / 16
TIME_STEP = 0.1
DIFFUSION = 0.05
NEAR = 8.0 * TIME_STEP / 12.0
FAR = TIME_STEP / 12.0
VMEM = 56 * 1024 * 1024
PACK_COST = DENSITY_COST = MODES_COST = (1e6, 1e5)
STATE_COST = (1e6, 4e8)
MAIN_COST = (1e12, 4e9)


def pair(ref, *index):
    return jnp.concatenate([ref[(*index[:-1], 0, index[-1])], ref[(*index[:-1], 1, index[-1])]], axis=0)


def unpair(ref, value, *index):
    ref[(*index[:-1], 0, index[-1])] = value[:4]
    ref[(*index[:-1], 1, index[-1])] = value[4:]


def slots(shape):
    sub = lax.broadcasted_iota(jnp.int32, shape, len(shape) - 2)
    return jnp.where(sub >= 4, sub - 4, sub)


def turn(value, shift, axis):
    return pltpu.roll(value, shift % value.shape[axis], axis)


def gather_planes(values, plane):
    slot = slots(values[0].shape)
    out = turn(values[-1], len(values) - 1 - plane, 0)
    for c in reversed(range(len(values) - 1)):
        out = jnp.where(slot == c, turn(values[c], c - plane, 0), out)
    return out


def shared(rho, m, b):
    inv = 1.0 / rho
    return [x * inv for x in m], rho + 0.5 * (b[0] * b[0] + b[1] * b[1] + b[2] * b[2])


def fluxes(v, total, m, b, k):
    push = [m[i] * v[k] - b[i] * b[k] + (total if i == k else 0.0) for i in range(3)]
    turned = [None if i == k else v[k] * b[i] - b[k] * v[i] for i in range(3)]
    return push + turned


def first_kernel(cell_ref, count_ref, rho_a, mom_a, mag_a, pot_a, rho_z, mom_z, mag_z, pot_z, ev_ref, first_ref, last_ref):
    shape = (1, ev_ref.shape[2])
    lane = lax.broadcasted_iota(jnp.int32, shape, 1)
    row = jnp.zeros(shape, jnp.int32)
    for e in range(count_ref.shape[0]):
        for i in range(4):
            row = jnp.where(lane == 4 * e + i, cell_ref[e, i] if i < 3 else count_ref[e], row)

    def copy(d, _):
        ev_ref[d] = row
        return 0

    lax.fori_loop(0, ev_ref.shape[0], copy, 0)
    for ref, rho, mom, mag, pot, skip in (
        (first_ref, rho_a, mom_a, mag_a, pot_a, 0), (last_ref, rho_z, mom_z, mag_z, pot_z, pot_z.shape[0] - 2),
    ):
        for j in range(2):
            ref[0, j] = rho[0, j]
            for c in range(3):
                ref[1 + c, j] = mom[c, 0, j]
                ref[4 + c, j] = mag[c, 0, j]
            ref[7, j] = jnp.broadcast_to(pot[skip + j : skip + j + 1], ref.shape[2:])


def pack_kernel(rho_ref, mz_ref, bx_ref, after_ref, up_ref, down_ref):
    half = rho_ref.shape[1]

    def body(p, _):
        rho, mz, bx = pair(rho_ref, p), pair(mz_ref, 0, p), pair(bx_ref, 0, p)
        slot = slots(rho.shape)
        up = jnp.where(slot == 2, mz, gather_planes([rho, mz, mz, bx], 3))
        down = jnp.where(slot == 2, turn(mz, 1, 0), gather_planes([rho, mz, mz, bx], 0))
        up_ref[p] = up
        down_ref[p] = down
        return 0

    lax.fori_loop(0, half, body, 0)


def state_kernel(
    ev_ref, rho_ref, mom_ref, mag_ref, pot_ref, before_ref, after_ref, rho_l, mom_l, mag_l, pot_l,
    rho_h, mom_h, mag_h, pot_h, u_out, edge_out, sb_out, sa_out, *rest, depth, counts, per_device,
):
    ups, downs, (s_ref, sb_ref, sa_ref) = rest[: len(rest) // 2 - 1], rest[len(rest) // 2 - 1 : -3], rest[-3:]
    half, ny = s_ref.shape[1] - 4, s_ref.shape[3]
    step_id = pl.program_id(0)

    @pl.when(step_id == 0)
    def _():
        deposit(ev_ref, s_ref, sb_ref, sa_ref, depth, per_device)
        pieces = lambda rho, mom, mag, pot, j: (
            [rho[0, j]] + [mom[c, 0, j] for c in range(3)] + [mag[c, 0, j] for c in range(3)]
            + [jnp.broadcast_to(pot, (4, ny))]
        )
        for j in range(2):
            low = pieces(rho_l, mom_l, mag_l, pot_l[0, 6 + j : 7 + j], j)
            high = pieces(rho_h, mom_h, mag_h, pot_h[0, j : j + 1], j)
            for f in range(8):
                left = jnp.concatenate([before_ref[f, j], low[f]], axis=0)
                right = jnp.concatenate([high[f], after_ref[f, j]], axis=0)
                edge_out[f, j] = left + s_ref[f, j] if f < 4 else left
                edge_out[f, 2 + j] = right + s_ref[f, half + 2 + j] if f < 4 else right

    start = step_id * 8
    sub = lax.broadcasted_iota(jnp.int32, (8, ny), 0)
    begin = 0
    for up_ref, down_ref, count in zip(ups, downs, counts):

        @pl.when((step_id >= begin) & (step_id < begin + count))
        def _(up_ref=up_ref, down_ref=down_ref, begin=begin):
            k = step_id - begin

            def messages(g, _):
                lasts = [jnp.zeros((8, ny), jnp.float32) for _ in range(2)]
                for j in range(4):
                    r = 4 * g + j
                    q = start + r + 2
                    sb_out[r] = sb_ref[q]
                    sa_out[r] = sa_ref[q]
                    u = [pair(rho_ref, r) + s_ref[0, q]]
                    u += [pair(mom_ref, c, r) + s_ref[1 + c, q] for c in range(3)]
                    u += [pair(mag_ref, c, r) for c in range(3)]
                    for f in range(7):
                        u_out[f, r] = u[f]
                    rows = [jnp.broadcast_to(pot_ref[h, pl.ds(r, 1), :], (4, ny)) for h in range(2)]
                    u_out[7, r] = jnp.concatenate(rows, axis=0)
                    near = [u[1], u[2], u[5], u[6]]
                    up_ref[0, r] = gather_planes(near, 3)
                    down_ref[0, r] = gather_planes(near, 0)
                    f = fluxes(*shared(u[0], u[1:4], u[4:7]), u[1:4], u[4:7], 2)
                    up_ref[0, 8 + r] = gather_planes(f[:4], 2)
                    down_ref[0, 8 + r] = gather_planes(f[:4], 1)
                    for i, plane in enumerate((2, 1)):
                        for h in range(2):
                            moved = turn(f[4], 2 * j + h - 4 * h - plane, 0)
                            lasts[i] = jnp.where(sub == 2 * j + h, moved, lasts[i])
                up_ref[0, 16 + g] = lasts[0]
                down_ref[0, 16 + g] = lasts[1]
                return 0

            lax.fori_loop(0, 2, messages, 0)

        begin += count


def deposit(ev_ref, s_ref, sb_ref, sa_ref, depth, per_device):
    half, ny = s_ref.shape[1] - 4, s_ref.shape[3]
    rows, events = 2 * half, ev_ref.shape[0] * per_device
    row_start, plane_start = lax.axis_index("xy") * rows, lax.axis_index("gz") * 4
    s_ref[...] = jnp.zeros_like(s_ref)
    sb_ref[...] = jnp.zeros_like(sb_ref)
    sa_ref[...] = jnp.zeros_like(sa_ref)

    shape = (4, 8, 128)
    slot = slots(shape)
    sub = lax.broadcasted_iota(jnp.int32, shape, 1)
    step = lax.broadcasted_iota(jnp.int32, shape, 0)
    lane = lax.broadcasted_iota(jnp.int32, shape, 2)

    def wrapped(distance, size):
        distance = jnp.where(distance >= size // 2, distance - size, distance)
        return jnp.where(distance < -(size // 2), distance + size, distance)

    def event(e, _):
        device, slot_id = (e, 0) if per_device == 1 else (lax.div(e, per_device), lax.rem(e, per_device))
        row, col, plane, count = (ev_ref[device, 0, 4 * slot_id + i] for i in range(4))
        rel = wrapped(row - row_start - half, NX)
        rel = rel + half

        @pl.when((count > 0) & (rel > -2 - RADIUS) & (rel < rows + 2 + RADIUS))
        def _():
            base = plane_start - plane
            dz = wrapped(slot + base, depth).astype(jnp.float32)
            dzb = wrapped(jnp.where(slot == 2, -2, -1) + base, depth).astype(jnp.float32)
            dza = wrapped(jnp.where(slot == 2, 5, 4) + base, depth).astype(jnp.float32)
            share = lambda d: jnp.where(slot == 0, 1.0, jnp.where(slot == 3, 0.0, IMPULSE * d))
            first = jnp.bitwise_and(col - RADIUS, ny - 1) // 128
            second = jnp.bitwise_and(col + RADIUS - 1, ny - 1) // 128

            def tile(t, _):
                index = jnp.where(t == 0, first, second)
                lanes = pl.ds(pl.multiple_of(index * 128, 128), 128)
                dy = wrapped(lane + index * 128 - col, ny).astype(jnp.float32)
                dy2 = dy * dy
                for h in range(2):
                    weight = jnp.where((sub >= 4) == (h == 1), count, 0).astype(jnp.float32)
                    low = jnp.clip(rel - RADIUS + 1 - h * half + 2, 0, half + 4) // 4
                    high = (jnp.clip(rel + RADIUS - 1 - h * half + 2, -1, half + 3) + 4) // 4

                    def chunk(n, _):
                        q = pl.ds(n * 4, 4)
                        dx = (step + (n * 4 - 2 + h * half - rel)).astype(jnp.float32)
                        flat = dx * dx + dy2
                        size = lambda d: jnp.maximum(1.0 - (flat + d * d) * (1.0 / (RADIUS * RADIUS)), 0.0) * weight
                        w = size(dz)
                        s_ref[0, q, :, lanes] += w
                        w = w * IMPULSE
                        s_ref[1, q, :, lanes] += w * dx
                        s_ref[2, q, :, lanes] += w * dy
                        s_ref[3, q, :, lanes] += w * dz
                        sb_ref[q, :, lanes] += size(dzb) * share(dzb)
                        sa_ref[q, :, lanes] += size(dza) * share(dza)
                        return 0

                    lax.fori_loop(low, high, chunk, 0)
                return 0

            lax.fori_loop(0, jnp.where(first == second, 1, 2), tile, 0)

        return 0

    lax.fori_loop(0, events, event, 0)


def ends(below, above, c):
    return jnp.where(slots(below.shape) == 3, turn(above, 3 - c, 0), turn(below, -c, 0))


def along_y(f, b):
    near, far = NEAR * f, FAR * f
    return turn(b + near, 1, 1) + turn(b - near, -1, 1) + turn(far, -2, 1) - turn(far, 2, 1)


def along_z(f, b, near_f, near_u, far_f):
    slot = slots(b.shape)
    first, last = slot == 0, slot == 3
    outer = DIFFUSION * near_u
    if f is None:
        return jnp.where(first, outer, turn(b, 1, 0)) + jnp.where(last, outer, turn(b, -1, 0))
    near = NEAR * f
    outer += jnp.where(first, NEAR, -NEAR) * near_f
    out = jnp.where(first, outer, turn(b + near, 1, 0)) + jnp.where(last, outer, turn(b - near, -1, 0))
    beyond = jnp.where(slot == 1, turn(near_f, 1, 0), jnp.where(slot == 2, turn(near_f, -1, 0), far_f))
    return out + FAR * (jnp.where(slot <= 1, turn(f, -2, 0), beyond) - jnp.where(slot >= 2, turn(f, 2, 0), beyond))


def fetch(u_hbm, edge_hbm, u_ref, sem, first):
    fields, total = u_ref.shape[:2]
    half = u_hbm.shape[1]
    low, high = max(first - 2, 0), min(first + total - 2, half)
    copies = [pltpu.make_async_copy(u_hbm.at[:fields, low:high], u_ref.at[:, low - first + 2 : high - first + 2], sem.at[0])]
    if first == 0:
        copies.append(pltpu.make_async_copy(edge_hbm.at[:fields, 0:2], u_ref.at[:, 0:2], sem.at[1]))
    if first + total - 4 == half:
        copies.append(pltpu.make_async_copy(edge_hbm.at[:fields, 2:4], u_ref.at[:, total - 2 : total], sem.at[2]))
    for copy in copies:
        copy.start()
    for copy in copies:
        copy.wait()


def density_kernel(
    u_hbm, edge_hbm, below_ref, above_ref, sb_ref, sa_ref, order_ref, high_ref, low_ref, out_ref, wave_ref, d_ref, u_ref, sem,
):
    fetch(u_hbm, edge_hbm, u_ref, sem, 0)
    half = below_ref.shape[0]
    rows = 2 * half

    def body(p, _):
        rho, my, mz = u_ref[0, p + 2], u_ref[2, p + 2], u_ref[3, p + 2]
        below, above = below_ref[p] + sb_ref[p], above_ref[p] + sa_ref[p]
        b = DIFFUSION * rho
        new = rho * (1.0 - 6.0 * DIFFUSION)
        new += DIFFUSION * (u_ref[0, p + 1] + u_ref[0, p + 3])
        new += NEAR * (u_ref[1, p + 1] - u_ref[1, p + 3]) + FAR * (u_ref[1, p + 4] - u_ref[1, p])
        new += along_y(my, b)
        new += along_z(mz, b, ends(below, above, 1), ends(below, above, 0), ends(below, above, 2))
        unpair(out_ref, new, p)
        d_ref[pl.ds(pl.multiple_of(p * 8, 8), 8), :] = new
        return 0

    lax.fori_loop(0, half, body, 0)
    d = d_ref[...]
    order = order_ref[...]
    dot = functools.partial(jnp.dot, preferred_element_type=jnp.float32)
    high = d.astype(jnp.bfloat16)
    low = (d - high.astype(jnp.float32)).astype(jnp.bfloat16)
    high = dot(order, high).astype(jnp.bfloat16)
    low = dot(order, low).astype(jnp.bfloat16)
    for part in range(2):
        c_high, c_low = high_ref[part], low_ref[part]
        wave = dot(high, c_high) + dot(high, c_low) + dot(low, c_high)
        peers, band = wave_ref.shape[0], wave_ref.shape[4]
        for j in range(peers):
            for z in range(4):
                wave_ref[j, part, z] = wave[z * rows : (z + 1) * rows, j * band : (j + 1) * band]


def last_plane(below, above, j):
    sub = lax.broadcasted_iota(jnp.int32, below.shape, 0)
    out = turn(below, -2 * j, 0)
    out = jnp.where(sub == 3, turn(above, 3 - 2 * j, 0), out)
    out = jnp.where(sub == 4, turn(below, 3 - 2 * j, 0), out)
    return jnp.where(sub == 7, turn(above, 6 - 2 * j, 0), out)


def main_kernel(u_hbm, edge_hbm, ba_ref, aa_ref, sb_ref, sa_ref, from_below, from_above, *rest, first):
    mom_ref, mag_ref, u_ref, f_ref, sem = rest[-5:]
    chunk, total = ba_ref.shape[0], u_ref.shape[1]
    start = pl.program_id(0) * chunk
    kept = (0, 1, 2, 4, 5)

    @pl.when(pl.program_id(0) == 0)
    def _():
        fetch(u_hbm, edge_hbm, u_ref, sem, first)

        def fx(q, _):
            u = [u_ref[f, q] for f in range(7)]
            f = fluxes(*shared(u[0], u[1:4], u[4:7]), u[1:4], u[4:7], 0)
            for i, c in enumerate(kept):
                f_ref[i, q] = f[c]
            return 0

        lax.fori_loop(0, total, fx, 0)

    def row(r, g, j):
        q = start + r + 2
        u = [u_ref[f, q] for f in range(7)]
        v, pressure = shared(u[0], u[1:4], u[4:7])
        fy = fluxes(v, pressure, u[1:4], u[4:7], 1)
        fz = fluxes(v, pressure, u[1:4], u[4:7], 2)
        ba, aa = ba_ref[r] + sb_ref[r], aa_ref[r] + sa_ref[r]
        bn, an, bf, af = from_below[0, r], from_above[0, r], from_below[0, 8 + r], from_above[0, 8 + r]
        hm = [ends(bn, an, 0), ends(bn, an, 1), ends(ba, aa, 1)]
        hb = [ends(ba, aa, 3), ends(bn, an, 2), ends(bn, an, 3)]
        fh = fluxes(*shared(ends(ba, aa, 0), hm, hb), hm, hb, 2)
        halo = hm + hb
        far = [ends(bf, af, c) for c in range(4)] + [last_plane(from_below[0, 16 + g], from_above[0, 16 + g], j), None]
        for c in range(6):
            field = u[c + 1]
            new = field * (1.0 - 6.0 * DIFFUSION)
            new += DIFFUSION * (u_ref[c + 1, q - 1] + u_ref[c + 1, q + 1])
            if c in kept:
                i = kept.index(c)
                new += NEAR * (f_ref[i, q - 1] - f_ref[i, q + 1]) + FAR * (f_ref[i, q + 2] - f_ref[i, q - 2])
            b = DIFFUSION * field
            if fy[c] is None:
                new += turn(b, 1, 1) + turn(b, -1, 1)
            else:
                new += along_y(fy[c], b)
            new += along_z(fz[c], b, fh[c], halo[c], far[c])
            if c == 0:
                slope = NEAR * (u_ref[7, q - 1] - u_ref[7, q + 1]) + FAR * (u_ref[7, q + 2] - u_ref[7, q - 2])
                new += u[0] * slope
            if c == 1:
                potential = u_ref[7, q]
                slope = NEAR * (turn(potential, 1, 1) - turn(potential, -1, 1))
                new += u[0] * (slope + FAR * (turn(potential, -2, 1) - turn(potential, 2, 1)))
            if c < 3:
                unpair(mom_ref, new, c, r)
            else:
                unpair(mag_ref, new, c - 3, r)

    def body(g, _):
        for j in range(4):
            row(4 * g + j, g, j)
        return 0

    lax.fori_loop(0, chunk // 4, body, 0)


def modes_kernel(w_ref, ch_ref, cl_ref, sh_ref, sl_ref, out_ref, x_ref, *, turned):
    dot = functools.partial(jnp.dot, preferred_element_type=jnp.float32)
    planes, band, nx = out_ref.shape[1:]

    def split(part):
        if turned:
            x = jnp.concatenate([w_ref[part, z] for z in range(planes)], axis=0)
        else:
            width = w_ref.shape[3]
            for s in range(w_ref.shape[0]):
                for z in range(planes):
                    x_ref[z * band : (z + 1) * band, s * width : (s + 1) * width] = w_ref[s, part, z].T
            x = x_ref[...]
        high = x.astype(jnp.bfloat16)
        return high, (x - high.astype(jnp.float32)).astype(jnp.bfloat16)

    re, im = split(0), split(1)
    times = lambda x, h, l: dot(x[0], h[...]) + dot(x[0], l[...]) + dot(x[1], h[...])
    scale = 1.0 / math.sqrt(NX * nx)
    shape = (band, nx)
    ky = lax.broadcasted_iota(jnp.int32, shape, 0) + lax.axis_index("xy") * band
    kx = lax.broadcasted_iota(jnp.int32, shape, 1)
    keep = jnp.where((ky == 0) & (kx == 0), 0.0, scale)
    out_re = times(re, ch_ref, cl_ref) + times(im, sh_ref, sl_ref)
    out_im = times(im, ch_ref, cl_ref) - times(re, sh_ref, sl_ref)
    for z in range(planes):
        out_ref[0, z] = out_re[z * band : (z + 1) * band] * keep
        out_ref[1, z] = out_im[z * band : (z + 1) * band] * keep


def cost(flops, bytes_accessed):
    return pl.CostEstimate(flops=int(flops), bytes_accessed=int(bytes_accessed), transcendentals=0)


def tables(size):
    angle = (np.outer(np.arange(size), np.arange(size)) % size) * (2.0 * np.pi / size)
    result = []
    for table in (np.cos(angle), np.sin(angle)):
        high = table.astype(np.float32).astype(ml_dtypes.bfloat16)
        low = (table - high.astype(np.float64)).astype(np.float32).astype(ml_dtypes.bfloat16)
        result += [high, low]
    return result


def row_order(half):
    matrix = np.zeros((8 * half, 8 * half), np.float32)
    for z in range(4):
        for h in range(2):
            for p in range(half):
                matrix[(z * 2 + h) * half + p, p * 8 + h * 4 + z] = 1.0
    return matrix.astype(ml_dtypes.bfloat16)


def shift(block, axis, step):
    n = lax.axis_size(axis)
    return lax.ppermute(block, axis, [(i, (i + step) % n) for i in range(n)])


def on_device(density, momentum, magnetic, arm_potential, sn_cells, sn_counts):
    rows, planes, ny = density.shape
    half = rows // 2
    layers, across = lax.axis_size("gz"), lax.axis_size("xy")
    devices = layers * across
    tile_row, tile_plane = lax.axis_index("xy"), lax.axis_index("gz")
    field = rows * planes * ny
    f32 = jnp.float32
    shape = jax.ShapeDtypeStruct
    whole = pl.BlockSpec(memory_space=pltpu.VMEM)
    smem = pl.BlockSpec(memory_space=pltpu.SMEM)
    params = pltpu.CompilerParams(vmem_limit_bytes=VMEM)
    message = shape((2, half, planes, ny), f32)
    tile = shape((half, 8, ny), f32)
    steps = half // 8
    counts = (steps * 5 // 8, steps - steps * 5 // 8) if steps >= 2 else (steps,)

    slots_here = sn_cells.shape[0]
    rho = density.reshape(2, half, planes, ny)
    mom = momentum.reshape(3, 2, half, planes, ny)
    mag = magnetic.reshape(3, 2, half, planes, ny)

    pot = arm_potential.reshape(2, half, ny)
    edges = shape((8, 2, planes, ny), f32)
    mine = shape((devices, 1, -(-4 * slots_here // 128) * 128), jnp.int32)
    full = lambda s: pl.BlockSpec(s, lambda i: (0,) * len(s))
    mine, first_rows, last_rows = pl.pallas_call(
        first_kernel,
        grid=(1,),
        in_specs=[smem, smem] + [
            spec
            for h, k in ((0, 0), (1, half // 2 - 1))
            for spec in (
                pl.BlockSpec((1, 2, planes, ny), lambda i, h=h, k=k: (h, k, 0, 0)),
                pl.BlockSpec((3, 1, 2, planes, ny), lambda i, h=h, k=k: (0, h, k, 0, 0)),
                pl.BlockSpec((3, 1, 2, planes, ny), lambda i, h=h, k=k: (0, h, k, 0, 0)),
                pl.BlockSpec((8, ny), lambda i, h=h: (h * (rows // 8 - 1), 0)),
            )
        ],
        out_specs=[full(mine.shape)] + [full(edges.shape)] * 2,
        out_shape=[mine] + [edges] * 2,
        compiler_params=params,
        cost_estimate=cost(*PACK_COST),
        name="first",
    )(sn_cells, sn_counts, *[rho, mom, mag, arm_potential] * 2)
    events = lax.all_to_all(mine, ("gz", "xy"), split_axis=0, concat_axis=0, tiled=True)
    before, after = shift(last_rows, "xy", 1), shift(first_rows, "xy", -1)

    some = math.gcd(half, 16)
    up, down = pl.pallas_call(
        pack_kernel,
        grid=(half // some,),
        in_specs=[pl.BlockSpec((2, some, planes, ny), lambda i: (0, i, 0, 0))] + [
            pl.BlockSpec((1, 2, some, planes, ny), lambda i, f=f: (f, 0, i, 0, 0)) for f in (2, 0)
        ] + [pl.BlockSpec(memory_space=pl.ANY)],
        out_specs=[pl.BlockSpec((some, 8, ny), lambda i: (i, 0, 0))] * 2,
        out_shape=[tile] * 2,
        compiler_params=params,
        cost_estimate=cost(*PACK_COST),
        name="pack",
    )(rho, mom, mag, mine)
    below_a, above_a = shift(up, "gz", 1), shift(down, "gz", -1)

    parcels = [shape((n, 18, 8, ny), f32) for n in counts]
    side = pltpu.VMEM((half + 4, 8, ny), f32)
    begins = [sum(counts[:i]) for i in range(len(counts))]
    parcel_specs = [
        pl.BlockSpec((1, 18, 8, ny), lambda i, b=b, n=n: (jnp.clip(i - b, 0, n - 1), 0, 0, 0)) for b, n in zip(begins, counts)
    ]
    eight = pl.BlockSpec((8, 8, ny), lambda i: (i, 0, 0))
    middle = [
        spec
        for h, k in ((0, steps - 1), (1, 0))
        for spec in (
            pl.BlockSpec((1, 2, planes, ny), lambda i, h=h, k=k: (h, k * 4 + 3 * (1 - h), 0, 0)),
            pl.BlockSpec((3, 1, 2, planes, ny), lambda i, h=h, k=k: (0, h, k * 4 + 3 * (1 - h), 0, 0)),
            pl.BlockSpec((3, 1, 2, planes, ny), lambda i, h=h, k=k: (0, h, k * 4 + 3 * (1 - h), 0, 0)),
            pl.BlockSpec((1, 8, ny), lambda i, h=h, k=k: (h, k, 0)),
        )
    ]
    rows_of = lambda n: pl.BlockSpec((n, 2, 8, planes, ny), lambda i: (0, 0, i, 0, 0))
    state, edge, sb, sa, *messages = pl.pallas_call(
        functools.partial(state_kernel, depth=planes * layers, counts=counts, per_device=slots_here),
        grid=(steps,),
        in_specs=[
            smem, pl.BlockSpec((2, 8, planes, ny), lambda i: (0, i, 0, 0)), rows_of(3), rows_of(3),
            pl.BlockSpec((2, 8, ny), lambda i: (0, i, 0)), full(edges.shape), full(edges.shape),
        ] + middle,
        out_specs=[pl.BlockSpec((8, 8, 8, ny), lambda i: (0, i, 0, 0)), full((8, 4, 8, ny)), eight, eight] + parcel_specs * 2,
        out_shape=[shape((8, half, 8, ny), f32), shape((8, 4, 8, ny), f32), tile, tile] + parcels * 2,
        scratch_shapes=[pltpu.VMEM((4, half + 4, 8, ny), f32), side, side],
        compiler_params=params,
        cost_estimate=cost(*STATE_COST),
        name="state",
    )(events, rho, mom, mag, pot, before, after, *[rho, mom, mag, pot] * 2)
    parcels_below, parcels_above = [], []
    for i in range(len(counts)):
        parcels_below.append(shift(messages[i], "gz", 1))
        parcels_above.append(shift(messages[len(counts) + i], "gz", -1))

    cos_high, cos_low, sin_high, sin_low = tables(ny)
    band = ny // across
    turned = band % 128 != 0 or rows % 128 != 0
    hbm = pl.BlockSpec(memory_space=pl.ANY)
    copies = pltpu.SemaphoreType.DMA((3,))
    new_density, wave = pl.pallas_call(
        density_kernel,
        in_specs=[hbm, hbm] + [whole] * 7,
        out_specs=[whole] * 2,
        out_shape=[message, shape((across, 2, planes, rows, band), f32)],
        scratch_shapes=[
            pltpu.VMEM((8 * half, ny), f32), pltpu.VMEM((4, half + 4, 8, ny), f32), copies,
        ],
        compiler_params=params,
        cost_estimate=cost(*DENSITY_COST),
        name="density",
    )(
        state, edge, below_a, above_a, sb, sa, row_order(half),
        np.stack([cos_high, -sin_high]), np.stack([cos_low, -sin_low]),
    )

    portion = lax.all_to_all(wave, "xy", split_axis=0, concat_axis=0, tiled=True)
    if turned:
        portion = portion.transpose(1, 2, 4, 0, 3).reshape(2, planes, band, NX)
    modes = pl.pallas_call(
        functools.partial(modes_kernel, turned=turned),
        in_specs=[whole] * 5,
        out_specs=whole,
        out_shape=shape((2, planes, band, NX), f32),
        scratch_shapes=[pltpu.VMEM((planes * band, NX), f32)],
        compiler_params=params,
        cost_estimate=cost(*MODES_COST),
        name="modes",
    )(portion, *tables(NX))
    results = [shape((3, 2, half, planes, ny), f32)] * 2
    new = []
    for i, n in enumerate(counts):
        chunk, first = 8, begins[i] * 8
        here = pl.BlockSpec((chunk, 8, ny), lambda k, o=begins[i]: (o + k, 0, 0))
        parcel = pl.BlockSpec((1, 18, 8, ny), lambda k: (k, 0, 0, 0))
        three = pl.BlockSpec((3, 2, chunk, planes, ny), lambda k, o=begins[i]: (0, 0, o + k, 0, 0))
        below, above = parcels_below[i], parcels_above[i]
        extra = [*new] + [modes] * (i > 0 and i == len(counts) - 1)
        new = pl.pallas_call(
            functools.partial(main_kernel, first=first),
            grid=(n,),
            in_specs=[hbm, hbm] + [here] * 4 + [parcel] * 2 + [hbm] * len(extra),
            out_specs=[three, three],
            out_shape=results,
            scratch_shapes=[
                pltpu.VMEM((8, n * 8 + 4, 8, ny), f32), pltpu.VMEM((5, n * 8 + 4, 8, ny), f32), copies,
            ],
            input_output_aliases={8: 0, 9: 1} if new else {},
            compiler_params=pltpu.CompilerParams(vmem_limit_bytes=62 * 1024 * 1024),
            cost_estimate=cost(*MAIN_COST),
            name=f"main{i}",
        )(state, edge, below_a, above_a, sb, sa, below, above, *extra)
    new_mom, new_mag = new

    return (
        new_density.reshape(rows, planes, ny),
        new_mom.reshape(3, rows, planes, ny),
        new_mag.reshape(3, rows, planes, ny),
        modes,
    )


def solution(mesh):
    in_specs = (
        P("xy", "gz", None),
        P(None, "xy", "gz", None),
        P(None, "xy", "gz", None),
        P("xy", None),
        P(("gz", "xy"), None),
        P(("gz", "xy")),
    )
    out_specs = (
        P("xy", "gz", None),
        P(None, "xy", "gz", None),
        P(None, "xy", "gz", None),
        P(None, "gz", "xy", None),
    )
    return jax.shard_map(
        on_device, mesh=mesh, in_specs=in_specs, out_specs=out_specs, check_vma=False
    )
```

```python
import functools
import math

import jax
import jax.numpy as jnp
import ml_dtypes
import numpy as np
from jax import lax
from jax.experimental import pallas as pl
from jax.experimental.pallas import tpu as pltpu
from jax.sharding import PartitionSpec as P

NX = 512
RADIUS = 16
IMPULSE = 2.0 / 16
TIME_STEP = 0.1
DIFFUSION = 0.05
NEAR = 8.0 * TIME_STEP / 12.0
FAR = TIME_STEP / 12.0
VMEM = 56 * 1024 * 1024
PACK_COST = DENSITY_COST = MODES_COST = (1e6, 1e5)
STATE_COST = (1e6, 4e8)
MAIN_COST = (1e12, 4e9)


def pair(ref, *index):
    return jnp.concatenate([ref[(*index[:-1], 0, index[-1])], ref[(*index[:-1], 1, index[-1])]], axis=0)


def unpair(ref, value, *index):
    ref[(*index[:-1], 0, index[-1])] = value[:4]
    ref[(*index[:-1], 1, index[-1])] = value[4:]


def slots(shape):
    sub = lax.broadcasted_iota(jnp.int32, shape, len(shape) - 2)
    return jnp.where(sub >= 4, sub - 4, sub)


def turn(value, shift, axis):
    return pltpu.roll(value, shift % value.shape[axis], axis)


def gather_planes(values, plane):
    slot = slots(values[0].shape)
    out = turn(values[-1], len(values) - 1 - plane, 0)
    for c in reversed(range(len(values) - 1)):
        out = jnp.where(slot == c, turn(values[c], c - plane, 0), out)
    return out


def shared(rho, m, b):
    inv = 1.0 / rho
    return [x * inv for x in m], rho + 0.5 * (b[0] * b[0] + b[1] * b[1] + b[2] * b[2])


def fluxes(v, total, m, b, k):
    push = [m[i] * v[k] - b[i] * b[k] + (total if i == k else 0.0) for i in range(3)]
    turned = [None if i == k else v[k] * b[i] - b[k] * v[i] for i in range(3)]
    return push + turned


def first_kernel(cell_ref, count_ref, rho_a, mom_a, mag_a, pot_a, rho_z, mom_z, mag_z, pot_z, ev_ref, first_ref, last_ref):
    shape = (1, ev_ref.shape[2])
    lane = lax.broadcasted_iota(jnp.int32, shape, 1)
    row = jnp.zeros(shape, jnp.int32)
    for e in range(count_ref.shape[0]):
        for i in range(4):
            row = jnp.where(lane == 4 * e + i, cell_ref[e, i] if i < 3 else count_ref[e], row)

    def copy(d, _):
        ev_ref[d] = row
        return 0

    lax.fori_loop(0, ev_ref.shape[0], copy, 0)
    for ref, rho, mom, mag, pot, skip in (
        (first_ref, rho_a, mom_a, mag_a, pot_a, 0), (last_ref, rho_z, mom_z, mag_z, pot_z, pot_z.shape[0] - 2),
    ):
        for j in range(2):
            ref[0, j] = rho[0, j]
            for c in range(3):
                ref[1 + c, j] = mom[c, 0, j]
                ref[4 + c, j] = mag[c, 0, j]
            ref[7, j] = jnp.broadcast_to(pot[skip + j : skip + j + 1], ref.shape[2:])


def pack_kernel(rho_ref, mz_ref, bx_ref, after_ref, up_ref, down_ref):
    half = rho_ref.shape[1]

    def body(p, _):
        rho, mz, bx = pair(rho_ref, p), pair(mz_ref, 0, p), pair(bx_ref, 0, p)
        slot = slots(rho.shape)
        up = jnp.where(slot == 2, mz, gather_planes([rho, mz, mz, bx], 3))
        down = jnp.where(slot == 2, turn(mz, 1, 0), gather_planes([rho, mz, mz, bx], 0))
        up_ref[p] = up
        down_ref[p] = down
        return 0

    lax.fori_loop(0, half, body, 0)


def write_messages(up_ref, down_ref, k, g, state):
    lasts = None
    for j in range(4):
        r = 4 * g + j
        u = state(j)
        sub = lax.broadcasted_iota(jnp.int32, u[0].shape, 0)
        near = [u[1], u[2], u[5], u[6]]
        up_ref[k, r] = gather_planes(near, 3)
        down_ref[k, r] = gather_planes(near, 0)
        f = fluxes(*shared(u[0], u[1:4], u[4:7]), u[1:4], u[4:7], 2)
        up_ref[k, 8 + r] = gather_planes(f[:4], 2)
        down_ref[k, 8 + r] = gather_planes(f[:4], 1)
        lasts = lasts or [f[4], f[4]]
        for i, plane in enumerate((2, 1)):
            for h in range(2):
                moved = turn(f[4], 2 * j + h - 4 * h - plane, 0)
                lasts[i] = jnp.where(sub == 2 * j + h, moved, lasts[i])
    up_ref[k, 16 + g] = lasts[0]
    down_ref[k, 16 + g] = lasts[1]


def state_kernel(
    ev_ref, rho_ref, mom_ref, mag_ref, pot_ref, before_ref, after_ref, rho_l, mom_l, mag_l, pot_l,
    rho_h, mom_h, mag_h, pot_h, u_out, edge_out, sb_out, sa_out, up_ref, down_ref, s_ref, sb_ref, sa_ref, *,
    depth, count, per_device,
):
    half, ny = s_ref.shape[1] - 4, s_ref.shape[3]
    step_id = pl.program_id(0)

    @pl.when(step_id == 0)
    def _():
        deposit(ev_ref, s_ref, sb_ref, sa_ref, depth, per_device)
        pieces = lambda rho, mom, mag, pot, j: (
            [rho[0, j]] + [mom[c, 0, j] for c in range(3)] + [mag[c, 0, j] for c in range(3)]
            + [jnp.broadcast_to(pot, (4, ny))]
        )
        for j in range(2):
            low = pieces(rho_l, mom_l, mag_l, pot_l[0, 6 + j : 7 + j], j)
            high = pieces(rho_h, mom_h, mag_h, pot_h[0, j : j + 1], j)
            for f in range(8):
                left = jnp.concatenate([before_ref[f, j], low[f]], axis=0)
                right = jnp.concatenate([high[f], after_ref[f, j]], axis=0)
                edge_out[f, j] = left + s_ref[f, j] if f < 4 else left
                edge_out[f, 2 + j] = right + s_ref[f, half + 2 + j] if f < 4 else right

    start = step_id * 8

    def body(g, send):
        def state(j):
            r = 4 * g + j
            q = start + r + 2
            sb_out[r] = sb_ref[q]
            sa_out[r] = sa_ref[q]
            u = [pair(rho_ref, r) + s_ref[0, q]]
            u += [pair(mom_ref, c, r) + s_ref[1 + c, q] for c in range(3)]
            u += [pair(mag_ref, c, r) for c in range(3)]
            for f in range(7):
                u_out[f, r] = u[f]
            rows = [jnp.broadcast_to(pot_ref[h, pl.ds(r, 1), :], (4, ny)) for h in range(2)]
            u_out[7, r] = jnp.concatenate(rows, axis=0)
            return u

        if send:
            write_messages(up_ref, down_ref, 0, g, state)
        else:
            for j in range(4):
                state(j)
        return 0

    @pl.when(step_id < count)
    def _():
        lax.fori_loop(0, 2, lambda g, _: body(g, True), 0)

    @pl.when(step_id >= count)
    def _():
        lax.fori_loop(0, 2, lambda g, _: body(g, False), 0)


def deposit(ev_ref, s_ref, sb_ref, sa_ref, depth, per_device):
    half, ny = s_ref.shape[1] - 4, s_ref.shape[3]
    rows, events = 2 * half, ev_ref.shape[0] * per_device
    row_start, plane_start = lax.axis_index("xy") * rows, lax.axis_index("gz") * 4
    s_ref[...] = jnp.zeros_like(s_ref)
    sb_ref[...] = jnp.zeros_like(sb_ref)
    sa_ref[...] = jnp.zeros_like(sa_ref)

    shape = (4, 8, 128)
    slot = slots(shape)
    sub = lax.broadcasted_iota(jnp.int32, shape, 1)
    step = lax.broadcasted_iota(jnp.int32, shape, 0)
    lane = lax.broadcasted_iota(jnp.int32, shape, 2)

    def wrapped(distance, size):
        distance = jnp.where(distance >= size // 2, distance - size, distance)
        return jnp.where(distance < -(size // 2), distance + size, distance)

    def event(e, _):
        device, slot_id = (e, 0) if per_device == 1 else (lax.div(e, per_device), lax.rem(e, per_device))
        row, col, plane, count = (ev_ref[device, 0, 4 * slot_id + i] for i in range(4))
        rel = wrapped(row - row_start - half, NX)
        rel = rel + half

        @pl.when((count > 0) & (rel > -2 - RADIUS) & (rel < rows + 2 + RADIUS))
        def _():
            base = plane_start - plane
            dz = wrapped(slot + base, depth).astype(jnp.float32)
            dzb = wrapped(jnp.where(slot == 2, -2, -1) + base, depth).astype(jnp.float32)
            dza = wrapped(jnp.where(slot == 2, 5, 4) + base, depth).astype(jnp.float32)
            share = lambda d: jnp.where(slot == 0, 1.0, jnp.where(slot == 3, 0.0, IMPULSE * d))
            first = jnp.bitwise_and(col - RADIUS, ny - 1) // 128
            second = jnp.bitwise_and(col + RADIUS - 1, ny - 1) // 128

            def tile(t, _):
                index = jnp.where(t == 0, first, second)
                lanes = pl.ds(pl.multiple_of(index * 128, 128), 128)
                dy = wrapped(lane + index * 128 - col, ny).astype(jnp.float32)
                dy2 = dy * dy
                for h in range(2):
                    weight = jnp.where((sub >= 4) == (h == 1), count, 0).astype(jnp.float32)
                    low = jnp.clip(rel - RADIUS + 1 - h * half + 2, 0, half + 4) // 4
                    high = (jnp.clip(rel + RADIUS - 1 - h * half + 2, -1, half + 3) + 4) // 4

                    def chunk(n, _):
                        q = pl.ds(n * 4, 4)
                        dx = (step + (n * 4 - 2 + h * half - rel)).astype(jnp.float32)
                        flat = dx * dx + dy2
                        size = lambda d: jnp.maximum(1.0 - (flat + d * d) * (1.0 / (RADIUS * RADIUS)), 0.0) * weight
                        w = size(dz)
                        s_ref[0, q, :, lanes] += w
                        w = w * IMPULSE
                        s_ref[1, q, :, lanes] += w * dx
                        s_ref[2, q, :, lanes] += w * dy
                        s_ref[3, q, :, lanes] += w * dz
                        sb_ref[q, :, lanes] += size(dzb) * share(dzb)
                        sa_ref[q, :, lanes] += size(dza) * share(dza)
                        return 0

                    lax.fori_loop(low, high, chunk, 0)
                return 0

            lax.fori_loop(0, jnp.where(first == second, 1, 2), tile, 0)

        return 0

    lax.fori_loop(0, events, event, 0)


def ends(below, above, c):
    return jnp.where(slots(below.shape) == 3, turn(above, 3 - c, 0), turn(below, -c, 0))


def along_y(f, b):
    near, far = NEAR * f, FAR * f
    return turn(b + near, 1, 1) + turn(b - near, -1, 1) + turn(far, -2, 1) - turn(far, 2, 1)


def along_z(f, b, near_f, near_u, far_f):
    slot = slots(b.shape)
    first, last = slot == 0, slot == 3
    outer = DIFFUSION * near_u
    if f is None:
        return jnp.where(first, outer, turn(b, 1, 0)) + jnp.where(last, outer, turn(b, -1, 0))
    near = NEAR * f
    outer += jnp.where(first, NEAR, -NEAR) * near_f
    out = jnp.where(first, outer, turn(b + near, 1, 0)) + jnp.where(last, outer, turn(b - near, -1, 0))
    beyond = jnp.where(slot == 1, turn(near_f, 1, 0), jnp.where(slot == 2, turn(near_f, -1, 0), far_f))
    return out + FAR * (jnp.where(slot <= 1, turn(f, -2, 0), beyond) - jnp.where(slot >= 2, turn(f, 2, 0), beyond))


def fetch(u_hbm, edge_hbm, u_ref, sem, first):
    fields, total = u_ref.shape[:2]
    half = u_hbm.shape[1]
    low, high = max(first - 2, 0), min(first + total - 2, half)
    copies = [pltpu.make_async_copy(u_hbm.at[:fields, low:high], u_ref.at[:, low - first + 2 : high - first + 2], sem.at[0])]
    if first == 0:
        copies.append(pltpu.make_async_copy(edge_hbm.at[:fields, 0:2], u_ref.at[:, 0:2], sem.at[1]))
    if first + total - 4 == half:
        copies.append(pltpu.make_async_copy(edge_hbm.at[:fields, 2:4], u_ref.at[:, total - 2 : total], sem.at[2]))
    for copy in copies:
        copy.start()
    for copy in copies:
        copy.wait()


def density_kernel(
    u_hbm, edge_hbm, below_ref, above_ref, sb_ref, sa_ref, order_ref, high_ref, low_ref, out_ref, wave_ref, *rest,
):
    *parcel, d_ref, u_ref, b_ref, sem = rest
    half = u_hbm.shape[1]
    field = None
    if parcel:
        field = pltpu.make_async_copy(u_hbm.at[4:7, half - b_ref.shape[1] :], b_ref, sem.at[3])
        field.start()
    fetch(u_hbm, edge_hbm, u_ref, sem, 0)
    half = below_ref.shape[0]
    rows = 2 * half

    def body(p, _):
        rho, my, mz = u_ref[0, p + 2], u_ref[2, p + 2], u_ref[3, p + 2]
        below, above = below_ref[p] + sb_ref[p], above_ref[p] + sa_ref[p]
        b = DIFFUSION * rho
        new = rho * (1.0 - 6.0 * DIFFUSION)
        new += DIFFUSION * (u_ref[0, p + 1] + u_ref[0, p + 3])
        new += NEAR * (u_ref[1, p + 1] - u_ref[1, p + 3]) + FAR * (u_ref[1, p + 4] - u_ref[1, p])
        new += along_y(my, b)
        new += along_z(mz, b, ends(below, above, 1), ends(below, above, 0), ends(below, above, 2))
        unpair(out_ref, new, p)
        d_ref[pl.ds(pl.multiple_of(p * 8, 8), 8), :] = new
        return 0

    lax.fori_loop(0, half, body, 0)
    d = d_ref[...]
    order = order_ref[...]
    dot = functools.partial(jnp.dot, preferred_element_type=jnp.float32)
    high = d.astype(jnp.bfloat16)
    low = (d - high.astype(jnp.float32)).astype(jnp.bfloat16)
    high = dot(order, high).astype(jnp.bfloat16)
    low = dot(order, low).astype(jnp.bfloat16)
    for part in range(2):
        c_high, c_low = high_ref[part], low_ref[part]
        wave = dot(high, c_high) + dot(high, c_low) + dot(low, c_high)
        peers, band = wave_ref.shape[0], wave_ref.shape[4]
        for j in range(peers):
            for z in range(4):
                wave_ref[j, part, z] = wave[z * rows : (z + 1) * rows, j * band : (j + 1) * band]
    if not parcel:
        return
    field.wait()
    first = half - b_ref.shape[1]

    def messages(n, _):
        r = n * 4
        state = lambda j: [u_ref[f, first + r + j + 2] for f in range(4)] + [b_ref[c, r + j] for c in range(3)]
        write_messages(*parcel, n // 2, n % 2, state)
        return 0

    lax.fori_loop(0, b_ref.shape[1] // 4, messages, 0)


def last_plane(below, above, j):
    sub = lax.broadcasted_iota(jnp.int32, below.shape, 0)
    out = turn(below, -2 * j, 0)
    out = jnp.where(sub == 3, turn(above, 3 - 2 * j, 0), out)
    out = jnp.where(sub == 4, turn(below, 3 - 2 * j, 0), out)
    return jnp.where(sub == 7, turn(above, 6 - 2 * j, 0), out)


def main_kernel(u_hbm, edge_hbm, ba_ref, aa_ref, sb_ref, sa_ref, from_below, from_above, *rest, first):
    mom_ref, mag_ref, u_ref, f_ref, sem = rest[-5:]
    chunk, total = ba_ref.shape[0], u_ref.shape[1]
    start = pl.program_id(0) * chunk
    kept = (0, 1, 2, 4, 5)

    @pl.when(pl.program_id(0) == 0)
    def _():
        fetch(u_hbm, edge_hbm, u_ref, sem, first)

        def fx(q, _):
            u = [u_ref[f, q] for f in range(7)]
            f = fluxes(*shared(u[0], u[1:4], u[4:7]), u[1:4], u[4:7], 0)
            for i, c in enumerate(kept):
                f_ref[i, q] = f[c]
            return 0

        lax.fori_loop(0, total, fx, 0)

    def row(r, g, j):
        q = start + r + 2
        u = [u_ref[f, q] for f in range(7)]
        v, pressure = shared(u[0], u[1:4], u[4:7])
        fy = fluxes(v, pressure, u[1:4], u[4:7], 1)
        fz = fluxes(v, pressure, u[1:4], u[4:7], 2)
        ba, aa = ba_ref[r] + sb_ref[r], aa_ref[r] + sa_ref[r]
        bn, an, bf, af = from_below[0, r], from_above[0, r], from_below[0, 8 + r], from_above[0, 8 + r]
        hm = [ends(bn, an, 0), ends(bn, an, 1), ends(ba, aa, 1)]
        hb = [ends(ba, aa, 3), ends(bn, an, 2), ends(bn, an, 3)]
        fh = fluxes(*shared(ends(ba, aa, 0), hm, hb), hm, hb, 2)
        halo = hm + hb
        far = [ends(bf, af, c) for c in range(4)] + [last_plane(from_below[0, 16 + g], from_above[0, 16 + g], j), None]
        for c in range(6):
            field = u[c + 1]
            new = field * (1.0 - 6.0 * DIFFUSION)
            new += DIFFUSION * (u_ref[c + 1, q - 1] + u_ref[c + 1, q + 1])
            if c in kept:
                i = kept.index(c)
                new += NEAR * (f_ref[i, q - 1] - f_ref[i, q + 1]) + FAR * (f_ref[i, q + 2] - f_ref[i, q - 2])
            b = DIFFUSION * field
            if fy[c] is None:
                new += turn(b, 1, 1) + turn(b, -1, 1)
            else:
                new += along_y(fy[c], b)
            new += along_z(fz[c], b, fh[c], halo[c], far[c])
            if c == 0:
                slope = NEAR * (u_ref[7, q - 1] - u_ref[7, q + 1]) + FAR * (u_ref[7, q + 2] - u_ref[7, q - 2])
                new += u[0] * slope
            if c == 1:
                potential = u_ref[7, q]
                slope = NEAR * (turn(potential, 1, 1) - turn(potential, -1, 1))
                new += u[0] * (slope + FAR * (turn(potential, -2, 1) - turn(potential, 2, 1)))
            if c < 3:
                unpair(mom_ref, new, c, r)
            else:
                unpair(mag_ref, new, c - 3, r)

    def body(g, _):
        for j in range(4):
            row(4 * g + j, g, j)
        return 0

    lax.fori_loop(0, chunk // 4, body, 0)


def modes_kernel(w_ref, ch_ref, cl_ref, sh_ref, sl_ref, out_ref, x_ref, *, turned):
    dot = functools.partial(jnp.dot, preferred_element_type=jnp.float32)
    planes, band, nx = out_ref.shape[1:]

    def split(part):
        if turned:
            x = jnp.concatenate([w_ref[part, z] for z in range(planes)], axis=0)
        else:
            width = w_ref.shape[3]
            for s in range(w_ref.shape[0]):
                for z in range(planes):
                    x_ref[z * band : (z + 1) * band, s * width : (s + 1) * width] = w_ref[s, part, z].T
            x = x_ref[...]
        high = x.astype(jnp.bfloat16)
        return high, (x - high.astype(jnp.float32)).astype(jnp.bfloat16)

    re, im = split(0), split(1)
    times = lambda x, h, l: dot(x[0], h[...]) + dot(x[0], l[...]) + dot(x[1], h[...])
    scale = 1.0 / math.sqrt(NX * nx)
    shape = (band, nx)
    ky = lax.broadcasted_iota(jnp.int32, shape, 0) + lax.axis_index("xy") * band
    kx = lax.broadcasted_iota(jnp.int32, shape, 1)
    keep = jnp.where((ky == 0) & (kx == 0), 0.0, scale)
    out_re = times(re, ch_ref, cl_ref) + times(im, sh_ref, sl_ref)
    out_im = times(im, ch_ref, cl_ref) - times(re, sh_ref, sl_ref)
    for z in range(planes):
        out_ref[0, z] = out_re[z * band : (z + 1) * band] * keep
        out_ref[1, z] = out_im[z * band : (z + 1) * band] * keep


def cost(flops, bytes_accessed):
    return pl.CostEstimate(flops=int(flops), bytes_accessed=int(bytes_accessed), transcendentals=0)


def tables(size):
    angle = (np.outer(np.arange(size), np.arange(size)) % size) * (2.0 * np.pi / size)
    result = []
    for table in (np.cos(angle), np.sin(angle)):
        high = table.astype(np.float32).astype(ml_dtypes.bfloat16)
        low = (table - high.astype(np.float64)).astype(np.float32).astype(ml_dtypes.bfloat16)
        result += [high, low]
    return result


def row_order(half):
    matrix = np.zeros((8 * half, 8 * half), np.float32)
    for z in range(4):
        for h in range(2):
            for p in range(half):
                matrix[(z * 2 + h) * half + p, p * 8 + h * 4 + z] = 1.0
    return matrix.astype(ml_dtypes.bfloat16)


def shift(block, axis, step):
    n = lax.axis_size(axis)
    return lax.ppermute(block, axis, [(i, (i + step) % n) for i in range(n)])


def on_device(density, momentum, magnetic, arm_potential, sn_cells, sn_counts):
    rows, planes, ny = density.shape
    half = rows // 2
    layers, across = lax.axis_size("gz"), lax.axis_size("xy")
    devices = layers * across
    tile_row, tile_plane = lax.axis_index("xy"), lax.axis_index("gz")
    field = rows * planes * ny
    f32 = jnp.float32
    shape = jax.ShapeDtypeStruct
    whole = pl.BlockSpec(memory_space=pltpu.VMEM)
    smem = pl.BlockSpec(memory_space=pltpu.SMEM)
    params = pltpu.CompilerParams(vmem_limit_bytes=VMEM)
    message = shape((2, half, planes, ny), f32)
    tile = shape((half, 8, ny), f32)
    steps = half // 8
    counts = (steps * 5 // 8, steps - steps * 5 // 8) if steps >= 2 else (steps,)

    slots_here = sn_cells.shape[0]
    rho = density.reshape(2, half, planes, ny)
    mom = momentum.reshape(3, 2, half, planes, ny)
    mag = magnetic.reshape(3, 2, half, planes, ny)

    pot = arm_potential.reshape(2, half, ny)
    edges = shape((8, 2, planes, ny), f32)
    mine = shape((devices, 1, -(-4 * slots_here // 128) * 128), jnp.int32)
    full = lambda s: pl.BlockSpec(s, lambda i: (0,) * len(s))
    mine, first_rows, last_rows = pl.pallas_call(
        first_kernel,
        grid=(1,),
        in_specs=[smem, smem] + [
            spec
            for h, k in ((0, 0), (1, half // 2 - 1))
            for spec in (
                pl.BlockSpec((1, 2, planes, ny), lambda i, h=h, k=k: (h, k, 0, 0)),
                pl.BlockSpec((3, 1, 2, planes, ny), lambda i, h=h, k=k: (0, h, k, 0, 0)),
                pl.BlockSpec((3, 1, 2, planes, ny), lambda i, h=h, k=k: (0, h, k, 0, 0)),
                pl.BlockSpec((8, ny), lambda i, h=h: (h * (rows // 8 - 1), 0)),
            )
        ],
        out_specs=[full(mine.shape)] + [full(edges.shape)] * 2,
        out_shape=[mine] + [edges] * 2,
        compiler_params=params,
        cost_estimate=cost(*PACK_COST),
        name="first",
    )(sn_cells, sn_counts, *[rho, mom, mag, arm_potential] * 2)
    events = lax.all_to_all(mine, ("gz", "xy"), split_axis=0, concat_axis=0, tiled=True)
    before, after = shift(last_rows, "xy", 1), shift(first_rows, "xy", -1)

    some = math.gcd(half, 16)
    up, down = pl.pallas_call(
        pack_kernel,
        grid=(half // some,),
        in_specs=[pl.BlockSpec((2, some, planes, ny), lambda i: (0, i, 0, 0))] + [
            pl.BlockSpec((1, 2, some, planes, ny), lambda i, f=f: (f, 0, i, 0, 0)) for f in (2, 0)
        ] + [pl.BlockSpec(memory_space=pl.ANY)],
        out_specs=[pl.BlockSpec((some, 8, ny), lambda i: (i, 0, 0))] * 2,
        out_shape=[tile] * 2,
        compiler_params=params,
        cost_estimate=cost(*PACK_COST),
        name="pack",
    )(rho, mom, mag, mine)
    below_a, above_a = shift(up, "gz", 1), shift(down, "gz", -1)

    parcels = [shape((n, 18, 8, ny), f32) for n in counts]
    side = pltpu.VMEM((half + 4, 8, ny), f32)
    begins = [sum(counts[:i]) for i in range(len(counts))]
    parcel = pl.BlockSpec((1, 18, 8, ny), lambda i: (jnp.minimum(i, counts[0] - 1), 0, 0, 0))
    eight = pl.BlockSpec((8, 8, ny), lambda i: (i, 0, 0))
    middle = [
        spec
        for h, k in ((0, steps - 1), (1, 0))
        for spec in (
            pl.BlockSpec((1, 2, planes, ny), lambda i, h=h, k=k: (h, k * 4 + 3 * (1 - h), 0, 0)),
            pl.BlockSpec((3, 1, 2, planes, ny), lambda i, h=h, k=k: (0, h, k * 4 + 3 * (1 - h), 0, 0)),
            pl.BlockSpec((3, 1, 2, planes, ny), lambda i, h=h, k=k: (0, h, k * 4 + 3 * (1 - h), 0, 0)),
            pl.BlockSpec((1, 8, ny), lambda i, h=h, k=k: (h, k, 0)),
        )
    ]
    rows_of = lambda n: pl.BlockSpec((n, 2, 8, planes, ny), lambda i: (0, 0, i, 0, 0))
    state, edge, sb, sa, up_0, down_0 = pl.pallas_call(
        functools.partial(state_kernel, depth=planes * layers, count=counts[0], per_device=slots_here),
        grid=(steps,),
        in_specs=[
            smem, pl.BlockSpec((2, 8, planes, ny), lambda i: (0, i, 0, 0)), rows_of(3), rows_of(3),
            pl.BlockSpec((2, 8, ny), lambda i: (0, i, 0)), full(edges.shape), full(edges.shape),
        ] + middle,
        out_specs=[pl.BlockSpec((8, 8, 8, ny), lambda i: (0, i, 0, 0)), full((8, 4, 8, ny)), eight, eight, parcel, parcel],
        out_shape=[shape((8, half, 8, ny), f32), shape((8, 4, 8, ny), f32), tile, tile, parcels[0], parcels[0]],
        scratch_shapes=[pltpu.VMEM((4, half + 4, 8, ny), f32), side, side],
        compiler_params=params,
        cost_estimate=cost(*STATE_COST),
        name="state",
    )(events, rho, mom, mag, pot, before, after, *[rho, mom, mag, pot] * 2)
    parcels_below, parcels_above = [shift(up_0, "gz", 1)], [shift(down_0, "gz", -1)]

    cos_high, cos_low, sin_high, sin_low = tables(ny)
    band = ny // across
    turned = band % 128 != 0 or rows % 128 != 0
    hbm = pl.BlockSpec(memory_space=pl.ANY)
    copies = pltpu.SemaphoreType.DMA((3,))
    more = parcels[1:] * 2
    new_density, wave, *messages = pl.pallas_call(
        density_kernel,
        in_specs=[hbm, hbm] + [whole] * 7,
        out_specs=[whole] * (2 + len(more)),
        out_shape=[message, shape((across, 2, planes, rows, band), f32), *more],
        scratch_shapes=[
            pltpu.VMEM((8 * half, ny), f32), pltpu.VMEM((4, half + 4, 8, ny), f32),
            pltpu.VMEM((3, counts[-1] * 8, 8, ny), f32), pltpu.SemaphoreType.DMA((4,)),
        ],
        compiler_params=params,
        cost_estimate=cost(*DENSITY_COST),
        name="density",
    )(
        state, edge, below_a, above_a, sb, sa, row_order(half),
        np.stack([cos_high, -sin_high]), np.stack([cos_low, -sin_low]),
    )

    if messages:
        parcels_below.append(shift(messages[0], "gz", 1))
        parcels_above.append(shift(messages[1], "gz", -1))
    portion = lax.all_to_all(wave, "xy", split_axis=0, concat_axis=0, tiled=True)
    if turned:
        portion = portion.transpose(1, 2, 4, 0, 3).reshape(2, planes, band, NX)
    modes = pl.pallas_call(
        functools.partial(modes_kernel, turned=turned),
        in_specs=[whole] * 5,
        out_specs=whole,
        out_shape=shape((2, planes, band, NX), f32),
        scratch_shapes=[pltpu.VMEM((planes * band, NX), f32)],
        compiler_params=params,
        cost_estimate=cost(*MODES_COST),
        name="modes",
    )(portion, *tables(NX))
    results = [shape((3, 2, half, planes, ny), f32)] * 2
    new = []
    for i, n in enumerate(counts):
        chunk, first = 8, begins[i] * 8
        here = pl.BlockSpec((chunk, 8, ny), lambda k, o=begins[i]: (o + k, 0, 0))
        parcel = pl.BlockSpec((1, 18, 8, ny), lambda k: (k, 0, 0, 0))
        three = pl.BlockSpec((3, 2, chunk, planes, ny), lambda k, o=begins[i]: (0, 0, o + k, 0, 0))
        below, above = parcels_below[i], parcels_above[i]
        extra = [*new] + [modes] * (i > 0 and i == len(counts) - 1)
        new = pl.pallas_call(
            functools.partial(main_kernel, first=first),
            grid=(n,),
            in_specs=[hbm, hbm] + [here] * 4 + [parcel] * 2 + [hbm] * len(extra),
            out_specs=[three, three],
            out_shape=results,
            scratch_shapes=[
                pltpu.VMEM((8, n * 8 + 4, 8, ny), f32), pltpu.VMEM((5, n * 8 + 4, 8, ny), f32), copies,
            ],
            input_output_aliases={8: 0, 9: 1} if new else {},
            compiler_params=pltpu.CompilerParams(vmem_limit_bytes=62 * 1024 * 1024),
            cost_estimate=cost(*MAIN_COST),
            name=f"main{i}",
        )(state, edge, below_a, above_a, sb, sa, below, above, *extra)
    new_mom, new_mag = new

    return (
        new_density.reshape(rows, planes, ny),
        new_mom.reshape(3, rows, planes, ny),
        new_mag.reshape(3, rows, planes, ny),
        modes,
    )


def solution(mesh):
    in_specs = (
        P("xy", "gz", None),
        P(None, "xy", "gz", None),
        P(None, "xy", "gz", None),
        P("xy", None),
        P(("gz", "xy"), None),
        P(("gz", "xy")),
    )
    out_specs = (
        P("xy", "gz", None),
        P(None, "xy", "gz", None),
        P(None, "xy", "gz", None),
        P(None, "gz", "xy", None),
    )
    return jax.shard_map(
        on_device, mesh=mesh, in_specs=in_specs, out_specs=out_specs, check_vma=False
    )
```

```python
import functools
import math

import jax
import jax.numpy as jnp
import ml_dtypes
import numpy as np
from jax import lax
from jax.experimental import pallas as pl
from jax.experimental.pallas import tpu as pltpu
from jax.sharding import PartitionSpec as P

NX = 512
RADIUS = 16
IMPULSE = 2.0 / 16
TIME_STEP = 0.1
DIFFUSION = 0.05
NEAR = 8.0 * TIME_STEP / 12.0
FAR = TIME_STEP / 12.0
VMEM = 56 * 1024 * 1024
PACK_COST = MODES_COST = (1e6, 1e5)
STATE_COST = DENSITY_COST = (1e6, 4e8)
MAIN_COST = (1e12, 4e9)


def pair(ref, *index):
    return jnp.concatenate([ref[(*index[:-1], 0, index[-1])], ref[(*index[:-1], 1, index[-1])]], axis=0)


def unpair(ref, value, *index):
    ref[(*index[:-1], 0, index[-1])] = value[:4]
    ref[(*index[:-1], 1, index[-1])] = value[4:]


def slots(shape):
    sub = lax.broadcasted_iota(jnp.int32, shape, len(shape) - 2)
    return jnp.where(sub >= 4, sub - 4, sub)


def turn(value, shift, axis):
    return pltpu.roll(value, shift % value.shape[axis], axis)


def gather_planes(values, plane):
    slot = slots(values[0].shape)
    out = turn(values[-1], len(values) - 1 - plane, 0)
    for c in reversed(range(len(values) - 1)):
        out = jnp.where(slot == c, turn(values[c], c - plane, 0), out)
    return out


def shared(rho, m, b):
    inv = 1.0 / rho
    return [x * inv for x in m], rho + 0.5 * (b[0] * b[0] + b[1] * b[1] + b[2] * b[2])


def fluxes(v, total, m, b, k):
    push = [m[i] * v[k] - b[i] * b[k] + (total if i == k else 0.0) for i in range(3)]
    turned = [None if i == k else v[k] * b[i] - b[k] * v[i] for i in range(3)]
    return push + turned


def first_kernel(cell_ref, count_ref, rho_a, mom_a, mag_a, pot_a, rho_z, mom_z, mag_z, pot_z, ev_ref, first_ref, last_ref):
    shape = (1, ev_ref.shape[2])
    lane = lax.broadcasted_iota(jnp.int32, shape, 1)
    row = jnp.zeros(shape, jnp.int32)
    for e in range(count_ref.shape[0]):
        for i in range(4):
            row = jnp.where(lane == 4 * e + i, cell_ref[e, i] if i < 3 else count_ref[e], row)

    def copy(d, _):
        ev_ref[d] = row
        return 0

    lax.fori_loop(0, ev_ref.shape[0], copy, 0)
    for ref, rho, mom, mag, pot, skip in (
        (first_ref, rho_a, mom_a, mag_a, pot_a, 0), (last_ref, rho_z, mom_z, mag_z, pot_z, pot_z.shape[0] - 2),
    ):
        for j in range(2):
            ref[0, j] = rho[0, j]
            for c in range(3):
                ref[1 + c, j] = mom[c, 0, j]
                ref[4 + c, j] = mag[c, 0, j]
            ref[7, j] = jnp.broadcast_to(pot[skip + j : skip + j + 1], ref.shape[2:])


def pack_kernel(rho_ref, mz_ref, bx_ref, after_ref, up_ref, down_ref):
    half = rho_ref.shape[1]

    def body(p, _):
        rho, mz, bx = pair(rho_ref, p), pair(mz_ref, 0, p), pair(bx_ref, 0, p)
        slot = slots(rho.shape)
        up = jnp.where(slot == 2, mz, gather_planes([rho, mz, mz, bx], 3))
        down = jnp.where(slot == 2, turn(mz, 1, 0), gather_planes([rho, mz, mz, bx], 0))
        up_ref[p] = up
        down_ref[p] = down
        return 0

    lax.fori_loop(0, half, body, 0)


def write_messages(up_ref, down_ref, k, g, state):
    lasts = None
    for j in range(4):
        r = 4 * g + j
        u = state(j)
        sub = lax.broadcasted_iota(jnp.int32, u[0].shape, 0)
        near = [u[1], u[2], u[5], u[6]]
        up_ref[k, r] = gather_planes(near, 3)
        down_ref[k, r] = gather_planes(near, 0)
        f = fluxes(*shared(u[0], u[1:4], u[4:7]), u[1:4], u[4:7], 2)
        up_ref[k, 8 + r] = gather_planes(f[:4], 2)
        down_ref[k, 8 + r] = gather_planes(f[:4], 1)
        lasts = lasts or [f[4], f[4]]
        for i, plane in enumerate((2, 1)):
            for h in range(2):
                moved = turn(f[4], 2 * j + h - 4 * h - plane, 0)
                lasts[i] = jnp.where(sub == 2 * j + h, moved, lasts[i])
    up_ref[k, 16 + g] = lasts[0]
    down_ref[k, 16 + g] = lasts[1]


def state_kernel(
    ev_ref, rho_ref, mom_ref, mag_ref, pot_ref, before_ref, after_ref, rho_l, mom_l, mag_l, pot_l,
    rho_h, mom_h, mag_h, pot_h, u_out, edge_out, sb_out, sa_out, up_ref, down_ref, s_ref, sb_ref, sa_ref, *,
    depth, count, per_device,
):
    half, ny = s_ref.shape[1] - 4, s_ref.shape[3]
    step_id = pl.program_id(0)

    @pl.when(step_id == 0)
    def _():
        deposit(ev_ref, s_ref, sb_ref, sa_ref, depth, per_device)
        pieces = lambda rho, mom, mag, pot, j: (
            [rho[0, j]] + [mom[c, 0, j] for c in range(3)] + [mag[c, 0, j] for c in range(3)]
            + [jnp.broadcast_to(pot, (4, ny))]
        )
        for j in range(2):
            low = pieces(rho_l, mom_l, mag_l, pot_l[0, 6 + j : 7 + j], j)
            high = pieces(rho_h, mom_h, mag_h, pot_h[0, j : j + 1], j)
            for f in range(8):
                left = jnp.concatenate([before_ref[f, j], low[f]], axis=0)
                right = jnp.concatenate([high[f], after_ref[f, j]], axis=0)
                edge_out[f, j] = left + s_ref[f, j] if f < 4 else left
                edge_out[f, 2 + j] = right + s_ref[f, half + 2 + j] if f < 4 else right

    start = step_id * 8

    def body(g, send):
        def state(j):
            r = 4 * g + j
            q = start + r + 2
            sb_out[r] = sb_ref[q]
            sa_out[r] = sa_ref[q]
            u = [pair(rho_ref, r) + s_ref[0, q]]
            u += [pair(mom_ref, c, r) + s_ref[1 + c, q] for c in range(3)]
            u += [pair(mag_ref, c, r) for c in range(3)]
            for f in range(7):
                u_out[f, r] = u[f]
            rows = [jnp.broadcast_to(pot_ref[h, pl.ds(r, 1), :], (4, ny)) for h in range(2)]
            u_out[7, r] = jnp.concatenate(rows, axis=0)
            return u

        if send:
            write_messages(up_ref, down_ref, 0, g, state)
        else:
            for j in range(4):
                state(j)
        return 0

    @pl.when(step_id < count)
    def _():
        lax.fori_loop(0, 2, lambda g, _: body(g, True), 0)

    @pl.when(step_id >= count)
    def _():
        lax.fori_loop(0, 2, lambda g, _: body(g, False), 0)


def deposit(ev_ref, s_ref, sb_ref, sa_ref, depth, per_device):
    half, ny = s_ref.shape[1] - 4, s_ref.shape[3]
    rows, events = 2 * half, ev_ref.shape[0] * per_device
    row_start, plane_start = lax.axis_index("xy") * rows, lax.axis_index("gz") * 4
    s_ref[...] = jnp.zeros_like(s_ref)
    sb_ref[...] = jnp.zeros_like(sb_ref)
    sa_ref[...] = jnp.zeros_like(sa_ref)

    shape = (4, 8, 128)
    slot = slots(shape)
    sub = lax.broadcasted_iota(jnp.int32, shape, 1)
    step = lax.broadcasted_iota(jnp.int32, shape, 0)
    lane = lax.broadcasted_iota(jnp.int32, shape, 2)

    def wrapped(distance, size):
        distance = jnp.where(distance >= size // 2, distance - size, distance)
        return jnp.where(distance < -(size // 2), distance + size, distance)

    def event(e, _):
        device, slot_id = (e, 0) if per_device == 1 else (lax.div(e, per_device), lax.rem(e, per_device))
        row, col, plane, count = (ev_ref[device, 0, 4 * slot_id + i] for i in range(4))
        rel = wrapped(row - row_start - half, NX)
        rel = rel + half

        @pl.when((count > 0) & (rel > -2 - RADIUS) & (rel < rows + 2 + RADIUS))
        def _():
            base = plane_start - plane
            dz = wrapped(slot + base, depth).astype(jnp.float32)
            dzb = wrapped(jnp.where(slot == 2, -2, -1) + base, depth).astype(jnp.float32)
            dza = wrapped(jnp.where(slot == 2, 5, 4) + base, depth).astype(jnp.float32)
            share = lambda d: jnp.where(slot == 0, 1.0, jnp.where(slot == 3, 0.0, IMPULSE * d))
            first = jnp.bitwise_and(col - RADIUS, ny - 1) // 128
            second = jnp.bitwise_and(col + RADIUS - 1, ny - 1) // 128

            def tile(t, _):
                index = jnp.where(t == 0, first, second)
                lanes = pl.ds(pl.multiple_of(index * 128, 128), 128)
                dy = wrapped(lane + index * 128 - col, ny).astype(jnp.float32)
                dy2 = dy * dy
                for h in range(2):
                    weight = jnp.where((sub >= 4) == (h == 1), count, 0).astype(jnp.float32)
                    low = jnp.clip(rel - RADIUS + 1 - h * half + 2, 0, half + 4) // 4
                    high = (jnp.clip(rel + RADIUS - 1 - h * half + 2, -1, half + 3) + 4) // 4

                    def chunk(n, _):
                        q = pl.ds(n * 4, 4)
                        dx = (step + (n * 4 - 2 + h * half - rel)).astype(jnp.float32)
                        flat = dx * dx + dy2
                        size = lambda d: jnp.maximum(1.0 - (flat + d * d) * (1.0 / (RADIUS * RADIUS)), 0.0) * weight
                        w = size(dz)
                        s_ref[0, q, :, lanes] += w
                        w = w * IMPULSE
                        s_ref[1, q, :, lanes] += w * dx
                        s_ref[2, q, :, lanes] += w * dy
                        s_ref[3, q, :, lanes] += w * dz
                        sb_ref[q, :, lanes] += size(dzb) * share(dzb)
                        sa_ref[q, :, lanes] += size(dza) * share(dza)
                        return 0

                    lax.fori_loop(low, high, chunk, 0)
                return 0

            lax.fori_loop(0, jnp.where(first == second, 1, 2), tile, 0)

        return 0

    lax.fori_loop(0, events, event, 0)


def ends(below, above, c):
    return jnp.where(slots(below.shape) == 3, turn(above, 3 - c, 0), turn(below, -c, 0))


def along_y(f, b):
    near, far = NEAR * f, FAR * f
    return turn(b + near, 1, 1) + turn(b - near, -1, 1) + turn(far, -2, 1) - turn(far, 2, 1)


def along_z(f, b, near_f, near_u, far_f):
    slot = slots(b.shape)
    first, last = slot == 0, slot == 3
    outer = DIFFUSION * near_u
    if f is None:
        return jnp.where(first, outer, turn(b, 1, 0)) + jnp.where(last, outer, turn(b, -1, 0))
    near = NEAR * f
    outer += jnp.where(first, NEAR, -NEAR) * near_f
    out = jnp.where(first, outer, turn(b + near, 1, 0)) + jnp.where(last, outer, turn(b - near, -1, 0))
    beyond = jnp.where(slot == 1, turn(near_f, 1, 0), jnp.where(slot == 2, turn(near_f, -1, 0), far_f))
    return out + FAR * (jnp.where(slot <= 1, turn(f, -2, 0), beyond) - jnp.where(slot >= 2, turn(f, 2, 0), beyond))


def fetch(u_hbm, edge_hbm, u_ref, sem, first):
    fields, total = u_ref.shape[:2]
    half = u_hbm.shape[1]
    low, high = max(first - 2, 0), min(first + total - 2, half)
    copies = [pltpu.make_async_copy(u_hbm.at[:fields, low:high], u_ref.at[:, low - first + 2 : high - first + 2], sem.at[0])]
    if first == 0:
        copies.append(pltpu.make_async_copy(edge_hbm.at[:fields, 0:2], u_ref.at[:, 0:2], sem.at[1]))
    if first + total - 4 == half:
        copies.append(pltpu.make_async_copy(edge_hbm.at[:fields, 2:4], u_ref.at[:, total - 2 : total], sem.at[2]))
    for copy in copies:
        copy.start()
    for copy in copies:
        copy.wait()


def density_kernel(
    u_hbm, edge_hbm, below_ref, above_ref, sb_ref, sa_ref, order_ref, high_ref, low_ref, out_ref, wave_ref, *rest,
):
    *parcel, d_ref, u_ref, b_ref, sem = rest
    half = u_hbm.shape[1]
    field = None
    if parcel:
        field = pltpu.make_async_copy(u_hbm.at[4:7, half - b_ref.shape[1] :], b_ref, sem.at[3])
        field.start()
    fetch(u_hbm, edge_hbm, u_ref, sem, 0)
    half = below_ref.shape[0]
    rows = 2 * half

    def body(p, _):
        rho, my, mz = u_ref[0, p + 2], u_ref[2, p + 2], u_ref[3, p + 2]
        below, above = below_ref[p] + sb_ref[p], above_ref[p] + sa_ref[p]
        b = DIFFUSION * rho
        new = rho * (1.0 - 6.0 * DIFFUSION)
        new += DIFFUSION * (u_ref[0, p + 1] + u_ref[0, p + 3])
        new += NEAR * (u_ref[1, p + 1] - u_ref[1, p + 3]) + FAR * (u_ref[1, p + 4] - u_ref[1, p])
        new += along_y(my, b)
        new += along_z(mz, b, ends(below, above, 1), ends(below, above, 0), ends(below, above, 2))
        unpair(out_ref, new, p)
        d_ref[pl.ds(pl.multiple_of(p * 8, 8), 8), :] = new
        return 0

    lax.fori_loop(0, half, body, 0)
    d = d_ref[...]
    order = order_ref[...]
    dot = functools.partial(jnp.dot, preferred_element_type=jnp.float32)
    high = d.astype(jnp.bfloat16)
    low = (d - high.astype(jnp.float32)).astype(jnp.bfloat16)
    high = dot(order, high).astype(jnp.bfloat16)
    low = dot(order, low).astype(jnp.bfloat16)
    for part in range(2):
        c_high, c_low = high_ref[part], low_ref[part]
        wave = dot(high, c_high) + dot(high, c_low) + dot(low, c_high)
        peers, band = wave_ref.shape[0], wave_ref.shape[4]
        for j in range(peers):
            for z in range(4):
                wave_ref[j, part, z] = wave[z * rows : (z + 1) * rows, j * band : (j + 1) * band]
    if not parcel:
        return
    field.wait()
    first = half - b_ref.shape[1]

    def messages(n, _):
        r = n * 4
        state = lambda j: [u_ref[f, first + r + j + 2] for f in range(4)] + [b_ref[c, r + j] for c in range(3)]
        write_messages(*parcel, n // 2, n % 2, state)
        return 0

    lax.fori_loop(0, b_ref.shape[1] // 4, messages, 0)


def last_plane(below, above, j):
    sub = lax.broadcasted_iota(jnp.int32, below.shape, 0)
    out = turn(below, -2 * j, 0)
    out = jnp.where(sub == 3, turn(above, 3 - 2 * j, 0), out)
    out = jnp.where(sub == 4, turn(below, 3 - 2 * j, 0), out)
    return jnp.where(sub == 7, turn(above, 6 - 2 * j, 0), out)


def main_kernel(u_hbm, edge_hbm, ba_ref, aa_ref, sb_ref, sa_ref, from_below, from_above, *rest, first):
    mom_ref, mag_ref, u_ref, f_ref, sem = rest[-5:]
    chunk, total = ba_ref.shape[0], u_ref.shape[1]
    start = pl.program_id(0) * chunk
    kept = (0, 1, 2, 4, 5)

    @pl.when(pl.program_id(0) == 0)
    def _():
        fetch(u_hbm, edge_hbm, u_ref, sem, first)

        def fx(q, _):
            u = [u_ref[f, q] for f in range(7)]
            f = fluxes(*shared(u[0], u[1:4], u[4:7]), u[1:4], u[4:7], 0)
            for i, c in enumerate(kept):
                f_ref[i, q] = f[c]
            return 0

        lax.fori_loop(0, total, fx, 0)

    def row(r, g, j):
        q = start + r + 2
        u = [u_ref[f, q] for f in range(7)]
        v, pressure = shared(u[0], u[1:4], u[4:7])
        fy = fluxes(v, pressure, u[1:4], u[4:7], 1)
        fz = fluxes(v, pressure, u[1:4], u[4:7], 2)
        ba, aa = ba_ref[r] + sb_ref[r], aa_ref[r] + sa_ref[r]
        bn, an, bf, af = from_below[0, r], from_above[0, r], from_below[0, 8 + r], from_above[0, 8 + r]
        hm = [ends(bn, an, 0), ends(bn, an, 1), ends(ba, aa, 1)]
        hb = [ends(ba, aa, 3), ends(bn, an, 2), ends(bn, an, 3)]
        fh = fluxes(*shared(ends(ba, aa, 0), hm, hb), hm, hb, 2)
        halo = hm + hb
        far = [ends(bf, af, c) for c in range(4)] + [last_plane(from_below[0, 16 + g], from_above[0, 16 + g], j), None]
        for c in range(6):
            field = u[c + 1]
            new = field * (1.0 - 6.0 * DIFFUSION)
            new += DIFFUSION * (u_ref[c + 1, q - 1] + u_ref[c + 1, q + 1])
            if c in kept:
                i = kept.index(c)
                new += NEAR * (f_ref[i, q - 1] - f_ref[i, q + 1]) + FAR * (f_ref[i, q + 2] - f_ref[i, q - 2])
            b = DIFFUSION * field
            if fy[c] is None:
                new += turn(b, 1, 1) + turn(b, -1, 1)
            else:
                new += along_y(fy[c], b)
            new += along_z(fz[c], b, fh[c], halo[c], far[c])
            if c == 0:
                slope = NEAR * (u_ref[7, q - 1] - u_ref[7, q + 1]) + FAR * (u_ref[7, q + 2] - u_ref[7, q - 2])
                new += u[0] * slope
            if c == 1:
                potential = u_ref[7, q]
                slope = NEAR * (turn(potential, 1, 1) - turn(potential, -1, 1))
                new += u[0] * (slope + FAR * (turn(potential, -2, 1) - turn(potential, 2, 1)))
            if c < 3:
                unpair(mom_ref, new, c, r)
            else:
                unpair(mag_ref, new, c - 3, r)

    def body(g, _):
        for j in range(4):
            row(4 * g + j, g, j)
        return 0

    lax.fori_loop(0, chunk // 4, body, 0)


def modes_kernel(w_ref, ch_ref, cl_ref, sh_ref, sl_ref, out_ref, x_ref, *, turned):
    dot = functools.partial(jnp.dot, preferred_element_type=jnp.float32)
    planes, band, nx = out_ref.shape[1:]

    def split(part):
        if turned:
            x = jnp.concatenate([w_ref[part, z] for z in range(planes)], axis=0)
        else:
            width = w_ref.shape[3]
            for s in range(w_ref.shape[0]):
                for z in range(planes):
                    x_ref[z * band : (z + 1) * band, s * width : (s + 1) * width] = w_ref[s, part, z].T
            x = x_ref[...]
        high = x.astype(jnp.bfloat16)
        return high, (x - high.astype(jnp.float32)).astype(jnp.bfloat16)

    re, im = split(0), split(1)
    times = lambda x, h, l: dot(x[0], h[...]) + dot(x[0], l[...]) + dot(x[1], h[...])
    scale = 1.0 / math.sqrt(NX * nx)
    shape = (band, nx)
    ky = lax.broadcasted_iota(jnp.int32, shape, 0) + lax.axis_index("xy") * band
    kx = lax.broadcasted_iota(jnp.int32, shape, 1)
    keep = jnp.where((ky == 0) & (kx == 0), 0.0, scale)
    out_re = times(re, ch_ref, cl_ref) + times(im, sh_ref, sl_ref)
    out_im = times(im, ch_ref, cl_ref) - times(re, sh_ref, sl_ref)
    for z in range(planes):
        out_ref[0, z] = out_re[z * band : (z + 1) * band] * keep
        out_ref[1, z] = out_im[z * band : (z + 1) * band] * keep


def cost(flops, bytes_accessed):
    return pl.CostEstimate(flops=int(flops), bytes_accessed=int(bytes_accessed), transcendentals=0)


def tables(size):
    angle = (np.outer(np.arange(size), np.arange(size)) % size) * (2.0 * np.pi / size)
    result = []
    for table in (np.cos(angle), np.sin(angle)):
        high = table.astype(np.float32).astype(ml_dtypes.bfloat16)
        low = (table - high.astype(np.float64)).astype(np.float32).astype(ml_dtypes.bfloat16)
        result += [high, low]
    return result


def row_order(half):
    matrix = np.zeros((8 * half, 8 * half), np.float32)
    for z in range(4):
        for h in range(2):
            for p in range(half):
                matrix[(z * 2 + h) * half + p, p * 8 + h * 4 + z] = 1.0
    return matrix.astype(ml_dtypes.bfloat16)


def shift(block, axis, step):
    n = lax.axis_size(axis)
    return lax.ppermute(block, axis, [(i, (i + step) % n) for i in range(n)])


def on_device(density, momentum, magnetic, arm_potential, sn_cells, sn_counts):
    rows, planes, ny = density.shape
    half = rows // 2
    layers, across = lax.axis_size("gz"), lax.axis_size("xy")
    devices = layers * across
    tile_row, tile_plane = lax.axis_index("xy"), lax.axis_index("gz")
    field = rows * planes * ny
    f32 = jnp.float32
    shape = jax.ShapeDtypeStruct
    whole = pl.BlockSpec(memory_space=pltpu.VMEM)
    smem = pl.BlockSpec(memory_space=pltpu.SMEM)
    params = pltpu.CompilerParams(vmem_limit_bytes=VMEM)
    message = shape((2, half, planes, ny), f32)
    tile = shape((half, 8, ny), f32)
    steps = half // 8
    counts = (steps * 5 // 8, steps - steps * 5 // 8) if steps >= 2 else (steps,)

    slots_here = sn_cells.shape[0]
    rho = density.reshape(2, half, planes, ny)
    mom = momentum.reshape(3, 2, half, planes, ny)
    mag = magnetic.reshape(3, 2, half, planes, ny)

    pot = arm_potential.reshape(2, half, ny)
    edges = shape((8, 2, planes, ny), f32)
    mine = shape((devices, 1, -(-4 * slots_here // 128) * 128), jnp.int32)
    full = lambda s: pl.BlockSpec(s, lambda i: (0,) * len(s))
    mine, first_rows, last_rows = pl.pallas_call(
        first_kernel,
        grid=(1,),
        in_specs=[smem, smem] + [
            spec
            for h, k in ((0, 0), (1, half // 2 - 1))
            for spec in (
                pl.BlockSpec((1, 2, planes, ny), lambda i, h=h, k=k: (h, k, 0, 0)),
                pl.BlockSpec((3, 1, 2, planes, ny), lambda i, h=h, k=k: (0, h, k, 0, 0)),
                pl.BlockSpec((3, 1, 2, planes, ny), lambda i, h=h, k=k: (0, h, k, 0, 0)),
                pl.BlockSpec((8, ny), lambda i, h=h: (h * (rows // 8 - 1), 0)),
            )
        ],
        out_specs=[full(mine.shape)] + [full(edges.shape)] * 2,
        out_shape=[mine] + [edges] * 2,
        compiler_params=params,
        cost_estimate=cost(*PACK_COST),
        name="first",
    )(sn_cells, sn_counts, *[rho, mom, mag, arm_potential] * 2)
    events = lax.all_to_all(mine, ("gz", "xy"), split_axis=0, concat_axis=0, tiled=True)
    before, after = shift(last_rows, "xy", 1), shift(first_rows, "xy", -1)

    some = math.gcd(half, 16)
    up, down = pl.pallas_call(
        pack_kernel,
        grid=(half // some,),
        in_specs=[pl.BlockSpec((2, some, planes, ny), lambda i: (0, i, 0, 0))] + [
            pl.BlockSpec((1, 2, some, planes, ny), lambda i, f=f: (f, 0, i, 0, 0)) for f in (2, 0)
        ] + [pl.BlockSpec(memory_space=pl.ANY)],
        out_specs=[pl.BlockSpec((some, 8, ny), lambda i: (i, 0, 0))] * 2,
        out_shape=[tile] * 2,
        compiler_params=params,
        cost_estimate=cost(*PACK_COST),
        name="pack",
    )(rho, mom, mag, mine)
    below_a, above_a = shift(up, "gz", 1), shift(down, "gz", -1)

    parcels = [shape((n, 18, 8, ny), f32) for n in counts]
    side = pltpu.VMEM((half + 4, 8, ny), f32)
    begins = [sum(counts[:i]) for i in range(len(counts))]
    parcel = pl.BlockSpec((1, 18, 8, ny), lambda i: (jnp.minimum(i, counts[0] - 1), 0, 0, 0))
    eight = pl.BlockSpec((8, 8, ny), lambda i: (i, 0, 0))
    middle = [
        spec
        for h, k in ((0, steps - 1), (1, 0))
        for spec in (
            pl.BlockSpec((1, 2, planes, ny), lambda i, h=h, k=k: (h, k * 4 + 3 * (1 - h), 0, 0)),
            pl.BlockSpec((3, 1, 2, planes, ny), lambda i, h=h, k=k: (0, h, k * 4 + 3 * (1 - h), 0, 0)),
            pl.BlockSpec((3, 1, 2, planes, ny), lambda i, h=h, k=k: (0, h, k * 4 + 3 * (1 - h), 0, 0)),
            pl.BlockSpec((1, 8, ny), lambda i, h=h, k=k: (h, k, 0)),
        )
    ]
    rows_of = lambda n: pl.BlockSpec((n, 2, 8, planes, ny), lambda i: (0, 0, i, 0, 0))
    state, edge, sb, sa, up_0, down_0 = pl.pallas_call(
        functools.partial(state_kernel, depth=planes * layers, count=counts[0], per_device=slots_here),
        grid=(steps,),
        in_specs=[
            smem, pl.BlockSpec((2, 8, planes, ny), lambda i: (0, i, 0, 0)), rows_of(3), rows_of(3),
            pl.BlockSpec((2, 8, ny), lambda i: (0, i, 0)), full(edges.shape), full(edges.shape),
        ] + middle,
        out_specs=[pl.BlockSpec((8, 8, 8, ny), lambda i: (0, i, 0, 0)), full((8, 4, 8, ny)), eight, eight, parcel, parcel],
        out_shape=[shape((8, half, 8, ny), f32), shape((8, 4, 8, ny), f32), tile, tile, parcels[0], parcels[0]],
        scratch_shapes=[pltpu.VMEM((4, half + 4, 8, ny), f32), side, side],
        compiler_params=params,
        cost_estimate=cost(*STATE_COST),
        name="state",
    )(events, rho, mom, mag, pot, before, after, *[rho, mom, mag, pot] * 2)
    parcels_below, parcels_above = [shift(up_0, "gz", 1)], [shift(down_0, "gz", -1)]

    cos_high, cos_low, sin_high, sin_low = tables(ny)
    band = ny // across
    turned = band % 128 != 0 or rows % 128 != 0
    hbm = pl.BlockSpec(memory_space=pl.ANY)
    copies = pltpu.SemaphoreType.DMA((3,))
    more = parcels[1:] * 2
    new_density, wave, *messages = pl.pallas_call(
        density_kernel,
        in_specs=[hbm, hbm] + [whole] * 7,
        out_specs=[whole] * (2 + len(more)),
        out_shape=[message, shape((across, 2, planes, rows, band), f32), *more],
        scratch_shapes=[
            pltpu.VMEM((8 * half, ny), f32), pltpu.VMEM((4, half + 4, 8, ny), f32),
            pltpu.VMEM((3, counts[-1] * 8, 8, ny), f32), pltpu.SemaphoreType.DMA((4,)),
        ],
        compiler_params=params,
        cost_estimate=cost(*DENSITY_COST),
        name="density",
    )(
        state, edge, below_a, above_a, sb, sa, row_order(half),
        np.stack([cos_high, -sin_high]), np.stack([cos_low, -sin_low]),
    )

    if messages:
        parcels_below.append(shift(messages[0], "gz", 1))
        parcels_above.append(shift(messages[1], "gz", -1))
    portion = lax.all_to_all(wave, "xy", split_axis=0, concat_axis=0, tiled=True)
    if turned:
        portion = portion.transpose(1, 2, 4, 0, 3).reshape(2, planes, band, NX)
    modes = pl.pallas_call(
        functools.partial(modes_kernel, turned=turned),
        in_specs=[whole] * 5,
        out_specs=whole,
        out_shape=shape((2, planes, band, NX), f32),
        scratch_shapes=[pltpu.VMEM((planes * band, NX), f32)],
        compiler_params=params,
        cost_estimate=cost(*MODES_COST),
        name="modes",
    )(portion, *tables(NX))
    results = [shape((3, 2, half, planes, ny), f32)] * 2
    new = []
    for i, n in enumerate(counts):
        chunk, first = 8, begins[i] * 8
        here = pl.BlockSpec((chunk, 8, ny), lambda k, o=begins[i]: (o + k, 0, 0))
        parcel = pl.BlockSpec((1, 18, 8, ny), lambda k: (k, 0, 0, 0))
        three = pl.BlockSpec((3, 2, chunk, planes, ny), lambda k, o=begins[i]: (0, 0, o + k, 0, 0))
        below, above = parcels_below[i], parcels_above[i]
        extra = [*new] + [modes] * (i > 0 and i == len(counts) - 1)
        new = pl.pallas_call(
            functools.partial(main_kernel, first=first),
            grid=(n,),
            in_specs=[hbm, hbm] + [here] * 4 + [parcel] * 2 + [hbm] * len(extra),
            out_specs=[three, three],
            out_shape=results,
            scratch_shapes=[
                pltpu.VMEM((8, n * 8 + 4, 8, ny), f32), pltpu.VMEM((5, n * 8 + 4, 8, ny), f32), copies,
            ],
            input_output_aliases={8: 0, 9: 1} if new else {},
            compiler_params=pltpu.CompilerParams(vmem_limit_bytes=62 * 1024 * 1024),
            cost_estimate=cost(*MAIN_COST),
            name=f"main{i}",
        )(state, edge, below_a, above_a, sb, sa, below, above, *extra)
    new_mom, new_mag = new

    return (
        new_density.reshape(rows, planes, ny),
        new_mom.reshape(3, rows, planes, ny),
        new_mag.reshape(3, rows, planes, ny),
        modes,
    )


def solution(mesh):
    in_specs = (
        P("xy", "gz", None),
        P(None, "xy", "gz", None),
        P(None, "xy", "gz", None),
        P("xy", None),
        P(("gz", "xy"), None),
        P(("gz", "xy")),
    )
    out_specs = (
        P("xy", "gz", None),
        P(None, "xy", "gz", None),
        P(None, "xy", "gz", None),
        P(None, "gz", "xy", None),
    )
    return jax.shard_map(
        on_device, mesh=mesh, in_specs=in_specs, out_specs=out_specs, check_vma=False
    )
```

```python
import functools
import math

import jax
import jax.numpy as jnp
import ml_dtypes
import numpy as np
from jax import lax
from jax.experimental import pallas as pl
from jax.experimental.pallas import tpu as pltpu
from jax.sharding import PartitionSpec as P

NX = 512
RADIUS = 16
IMPULSE = 2.0 / 16
TIME_STEP = 0.1
DIFFUSION = 0.05
NEAR = 8.0 * TIME_STEP / 12.0
FAR = TIME_STEP / 12.0
VMEM = 56 * 1024 * 1024
PACK_COST = MODES_COST = (1e6, 1e5)
STATE_COST = DENSITY_COST = (1e12, 4e9)
MAIN_COST = (1e12, 4e9)


def pair(ref, *index):
    return jnp.concatenate([ref[(*index[:-1], 0, index[-1])], ref[(*index[:-1], 1, index[-1])]], axis=0)


def unpair(ref, value, *index):
    ref[(*index[:-1], 0, index[-1])] = value[:4]
    ref[(*index[:-1], 1, index[-1])] = value[4:]


def slots(shape):
    sub = lax.broadcasted_iota(jnp.int32, shape, len(shape) - 2)
    return jnp.where(sub >= 4, sub - 4, sub)


def turn(value, shift, axis):
    return pltpu.roll(value, shift % value.shape[axis], axis)


def gather_planes(values, plane):
    slot = slots(values[0].shape)
    out = turn(values[-1], len(values) - 1 - plane, 0)
    for c in reversed(range(len(values) - 1)):
        out = jnp.where(slot == c, turn(values[c], c - plane, 0), out)
    return out


def shared(rho, m, b):
    inv = 1.0 / rho
    return [x * inv for x in m], rho + 0.5 * (b[0] * b[0] + b[1] * b[1] + b[2] * b[2])


def fluxes(v, total, m, b, k):
    push = [m[i] * v[k] - b[i] * b[k] + (total if i == k else 0.0) for i in range(3)]
    turned = [None if i == k else v[k] * b[i] - b[k] * v[i] for i in range(3)]
    return push + turned


def first_kernel(cell_ref, count_ref, rho_a, mom_a, mag_a, pot_a, rho_z, mom_z, mag_z, pot_z, ev_ref, first_ref, last_ref):
    shape = (1, ev_ref.shape[2])
    lane = lax.broadcasted_iota(jnp.int32, shape, 1)
    row = jnp.zeros(shape, jnp.int32)
    for e in range(count_ref.shape[0]):
        for i in range(4):
            row = jnp.where(lane == 4 * e + i, cell_ref[e, i] if i < 3 else count_ref[e], row)

    def copy(d, _):
        ev_ref[d] = row
        return 0

    lax.fori_loop(0, ev_ref.shape[0], copy, 0)
    for ref, rho, mom, mag, pot, skip in (
        (first_ref, rho_a, mom_a, mag_a, pot_a, 0), (last_ref, rho_z, mom_z, mag_z, pot_z, pot_z.shape[0] - 2),
    ):
        for j in range(2):
            ref[0, j] = rho[0, j]
            for c in range(3):
                ref[1 + c, j] = mom[c, 0, j]
                ref[4 + c, j] = mag[c, 0, j]
            ref[7, j] = jnp.broadcast_to(pot[skip + j : skip + j + 1], ref.shape[2:])


def pack_kernel(rho_ref, mz_ref, bx_ref, after_ref, up_ref, down_ref):
    half = rho_ref.shape[1]

    def body(p, _):
        rho, mz, bx = pair(rho_ref, p), pair(mz_ref, 0, p), pair(bx_ref, 0, p)
        slot = slots(rho.shape)
        up = jnp.where(slot == 2, mz, gather_planes([rho, mz, mz, bx], 3))
        down = jnp.where(slot == 2, turn(mz, 1, 0), gather_planes([rho, mz, mz, bx], 0))
        up_ref[p] = up
        down_ref[p] = down
        return 0

    lax.fori_loop(0, half, body, 0)


def write_messages(up_ref, down_ref, k, g, state):
    lasts = None
    for j in range(4):
        r = 4 * g + j
        u = state(j)
        sub = lax.broadcasted_iota(jnp.int32, u[0].shape, 0)
        near = [u[1], u[2], u[5], u[6]]
        up_ref[k, r] = gather_planes(near, 3)
        down_ref[k, r] = gather_planes(near, 0)
        f = fluxes(*shared(u[0], u[1:4], u[4:7]), u[1:4], u[4:7], 2)
        up_ref[k, 8 + r] = gather_planes(f[:4], 2)
        down_ref[k, 8 + r] = gather_planes(f[:4], 1)
        lasts = lasts or [f[4], f[4]]
        for i, plane in enumerate((2, 1)):
            for h in range(2):
                moved = turn(f[4], 2 * j + h - 4 * h - plane, 0)
                lasts[i] = jnp.where(sub == 2 * j + h, moved, lasts[i])
    up_ref[k, 16 + g] = lasts[0]
    down_ref[k, 16 + g] = lasts[1]


def state_kernel(
    ev_ref, rho_ref, mom_ref, mag_ref, pot_ref, before_ref, after_ref, rho_l, mom_l, mag_l, pot_l,
    rho_h, mom_h, mag_h, pot_h, u_out, edge_out, sb_out, sa_out, up_ref, down_ref, s_ref, sb_ref, sa_ref, *,
    depth, count, per_device,
):
    half, ny = s_ref.shape[1] - 4, s_ref.shape[3]
    step_id = pl.program_id(0)

    @pl.when(step_id == 0)
    def _():
        deposit(ev_ref, s_ref, sb_ref, sa_ref, depth, per_device)
        pieces = lambda rho, mom, mag, pot, j: (
            [rho[0, j]] + [mom[c, 0, j] for c in range(3)] + [mag[c, 0, j] for c in range(3)]
            + [jnp.broadcast_to(pot, (4, ny))]
        )
        for j in range(2):
            low = pieces(rho_l, mom_l, mag_l, pot_l[0, 6 + j : 7 + j], j)
            high = pieces(rho_h, mom_h, mag_h, pot_h[0, j : j + 1], j)
            for f in range(8):
                left = jnp.concatenate([before_ref[f, j], low[f]], axis=0)
                right = jnp.concatenate([high[f], after_ref[f, j]], axis=0)
                edge_out[f, j] = left + s_ref[f, j] if f < 4 else left
                edge_out[f, 2 + j] = right + s_ref[f, half + 2 + j] if f < 4 else right

    start = step_id * 8

    def body(g, send):
        def state(j):
            r = 4 * g + j
            q = start + r + 2
            sb_out[r] = sb_ref[q]
            sa_out[r] = sa_ref[q]
            u = [pair(rho_ref, r) + s_ref[0, q]]
            u += [pair(mom_ref, c, r) + s_ref[1 + c, q] for c in range(3)]
            u += [pair(mag_ref, c, r) for c in range(3)]
            for f in range(7):
                u_out[f, r] = u[f]
            rows = [jnp.broadcast_to(pot_ref[h, pl.ds(r, 1), :], (4, ny)) for h in range(2)]
            u_out[7, r] = jnp.concatenate(rows, axis=0)
            return u

        if send:
            write_messages(up_ref, down_ref, 0, g, state)
        else:
            for j in range(4):
                state(j)
        return 0

    @pl.when(step_id < count)
    def _():
        lax.fori_loop(0, 2, lambda g, _: body(g, True), 0)

    @pl.when(step_id >= count)
    def _():
        lax.fori_loop(0, 2, lambda g, _: body(g, False), 0)


def deposit(ev_ref, s_ref, sb_ref, sa_ref, depth, per_device):
    half, ny = s_ref.shape[1] - 4, s_ref.shape[3]
    rows, events = 2 * half, ev_ref.shape[0] * per_device
    row_start, plane_start = lax.axis_index("xy") * rows, lax.axis_index("gz") * 4
    s_ref[...] = jnp.zeros_like(s_ref)
    sb_ref[...] = jnp.zeros_like(sb_ref)
    sa_ref[...] = jnp.zeros_like(sa_ref)

    shape = (4, 8, 128)
    slot = slots(shape)
    sub = lax.broadcasted_iota(jnp.int32, shape, 1)
    step = lax.broadcasted_iota(jnp.int32, shape, 0)
    lane = lax.broadcasted_iota(jnp.int32, shape, 2)

    def wrapped(distance, size):
        distance = jnp.where(distance >= size // 2, distance - size, distance)
        return jnp.where(distance < -(size // 2), distance + size, distance)

    def event(e, _):
        device, slot_id = (e, 0) if per_device == 1 else (lax.div(e, per_device), lax.rem(e, per_device))
        row, col, plane, count = (ev_ref[device, 0, 4 * slot_id + i] for i in range(4))
        rel = wrapped(row - row_start - half, NX)
        rel = rel + half

        @pl.when((count > 0) & (rel > -2 - RADIUS) & (rel < rows + 2 + RADIUS))
        def _():
            base = plane_start - plane
            dz = wrapped(slot + base, depth).astype(jnp.float32)
            dzb = wrapped(jnp.where(slot == 2, -2, -1) + base, depth).astype(jnp.float32)
            dza = wrapped(jnp.where(slot == 2, 5, 4) + base, depth).astype(jnp.float32)
            share = lambda d: jnp.where(slot == 0, 1.0, jnp.where(slot == 3, 0.0, IMPULSE * d))
            first = jnp.bitwise_and(col - RADIUS, ny - 1) // 128
            second = jnp.bitwise_and(col + RADIUS - 1, ny - 1) // 128

            def tile(t, _):
                index = jnp.where(t == 0, first, second)
                lanes = pl.ds(pl.multiple_of(index * 128, 128), 128)
                dy = wrapped(lane + index * 128 - col, ny).astype(jnp.float32)
                dy2 = dy * dy
                for h in range(2):
                    weight = jnp.where((sub >= 4) == (h == 1), count, 0).astype(jnp.float32)
                    low = jnp.clip(rel - RADIUS + 1 - h * half + 2, 0, half + 4) // 4
                    high = (jnp.clip(rel + RADIUS - 1 - h * half + 2, -1, half + 3) + 4) // 4

                    def chunk(n, _):
                        q = pl.ds(n * 4, 4)
                        dx = (step + (n * 4 - 2 + h * half - rel)).astype(jnp.float32)
                        flat = dx * dx + dy2
                        size = lambda d: jnp.maximum(1.0 - (flat + d * d) * (1.0 / (RADIUS * RADIUS)), 0.0) * weight
                        w = size(dz)
                        s_ref[0, q, :, lanes] += w
                        w = w * IMPULSE
                        s_ref[1, q, :, lanes] += w * dx
                        s_ref[2, q, :, lanes] += w * dy
                        s_ref[3, q, :, lanes] += w * dz
                        sb_ref[q, :, lanes] += size(dzb) * share(dzb)
                        sa_ref[q, :, lanes] += size(dza) * share(dza)
                        return 0

                    lax.fori_loop(low, high, chunk, 0)
                return 0

            lax.fori_loop(0, jnp.where(first == second, 1, 2), tile, 0)

        return 0

    lax.fori_loop(0, events, event, 0)


def ends(below, above, c):
    return jnp.where(slots(below.shape) == 3, turn(above, 3 - c, 0), turn(below, -c, 0))


def along_y(f, b):
    near, far = NEAR * f, FAR * f
    return turn(b + near, 1, 1) + turn(b - near, -1, 1) + turn(far, -2, 1) - turn(far, 2, 1)


def along_z(f, b, near_f, near_u, far_f):
    slot = slots(b.shape)
    first, last = slot == 0, slot == 3
    outer = DIFFUSION * near_u
    if f is None:
        return jnp.where(first, outer, turn(b, 1, 0)) + jnp.where(last, outer, turn(b, -1, 0))
    near = NEAR * f
    outer += jnp.where(first, NEAR, -NEAR) * near_f
    out = jnp.where(first, outer, turn(b + near, 1, 0)) + jnp.where(last, outer, turn(b - near, -1, 0))
    beyond = jnp.where(slot == 1, turn(near_f, 1, 0), jnp.where(slot == 2, turn(near_f, -1, 0), far_f))
    return out + FAR * (jnp.where(slot <= 1, turn(f, -2, 0), beyond) - jnp.where(slot >= 2, turn(f, 2, 0), beyond))


def fetch(u_hbm, edge_hbm, u_ref, sem, first):
    fields, total = u_ref.shape[:2]
    half = u_hbm.shape[1]
    low, high = max(first - 2, 0), min(first + total - 2, half)
    copies = [pltpu.make_async_copy(u_hbm.at[:fields, low:high], u_ref.at[:, low - first + 2 : high - first + 2], sem.at[0])]
    if first == 0:
        copies.append(pltpu.make_async_copy(edge_hbm.at[:fields, 0:2], u_ref.at[:, 0:2], sem.at[1]))
    if first + total - 4 == half:
        copies.append(pltpu.make_async_copy(edge_hbm.at[:fields, 2:4], u_ref.at[:, total - 2 : total], sem.at[2]))
    for copy in copies:
        copy.start()
    for copy in copies:
        copy.wait()


def density_kernel(
    u_hbm, edge_hbm, below_ref, above_ref, sb_ref, sa_ref, order_ref, high_ref, low_ref, out_ref, wave_ref, *rest,
):
    *parcel, d_ref, u_ref, b_ref, sem = rest
    half = u_hbm.shape[1]
    field = None
    if parcel:
        field = pltpu.make_async_copy(u_hbm.at[4:7, half - b_ref.shape[1] :], b_ref, sem.at[3])
        field.start()
    fetch(u_hbm, edge_hbm, u_ref, sem, 0)
    half = below_ref.shape[0]
    rows = 2 * half

    def body(p, _):
        rho, my, mz = u_ref[0, p + 2], u_ref[2, p + 2], u_ref[3, p + 2]
        below, above = below_ref[p] + sb_ref[p], above_ref[p] + sa_ref[p]
        b = DIFFUSION * rho
        new = rho * (1.0 - 6.0 * DIFFUSION)
        new += DIFFUSION * (u_ref[0, p + 1] + u_ref[0, p + 3])
        new += NEAR * (u_ref[1, p + 1] - u_ref[1, p + 3]) + FAR * (u_ref[1, p + 4] - u_ref[1, p])
        new += along_y(my, b)
        new += along_z(mz, b, ends(below, above, 1), ends(below, above, 0), ends(below, above, 2))
        unpair(out_ref, new, p)
        d_ref[pl.ds(pl.multiple_of(p * 8, 8), 8), :] = new
        return 0

    lax.fori_loop(0, half, body, 0)
    d = d_ref[...]
    order = order_ref[...]
    dot = functools.partial(jnp.dot, preferred_element_type=jnp.float32)
    high = d.astype(jnp.bfloat16)
    low = (d - high.astype(jnp.float32)).astype(jnp.bfloat16)
    high = dot(order, high).astype(jnp.bfloat16)
    low = dot(order, low).astype(jnp.bfloat16)
    for part in range(2):
        c_high, c_low = high_ref[part], low_ref[part]
        wave = dot(high, c_high) + dot(high, c_low) + dot(low, c_high)
        peers, band = wave_ref.shape[0], wave_ref.shape[4]
        for j in range(peers):
            for z in range(4):
                wave_ref[j, part, z] = wave[z * rows : (z + 1) * rows, j * band : (j + 1) * band]
    if not parcel:
        return
    field.wait()
    first = half - b_ref.shape[1]

    def messages(n, _):
        r = n * 4
        state = lambda j: [u_ref[f, first + r + j + 2] for f in range(4)] + [b_ref[c, r + j] for c in range(3)]
        write_messages(*parcel, n // 2, n % 2, state)
        return 0

    lax.fori_loop(0, b_ref.shape[1] // 4, messages, 0)


def last_plane(below, above, j):
    sub = lax.broadcasted_iota(jnp.int32, below.shape, 0)
    out = turn(below, -2 * j, 0)
    out = jnp.where(sub == 3, turn(above, 3 - 2 * j, 0), out)
    out = jnp.where(sub == 4, turn(below, 3 - 2 * j, 0), out)
    return jnp.where(sub == 7, turn(above, 6 - 2 * j, 0), out)


def main_kernel(u_hbm, edge_hbm, ba_ref, aa_ref, sb_ref, sa_ref, from_below, from_above, *rest, first):
    mom_ref, mag_ref, u_ref, f_ref, sem = rest[-5:]
    chunk, total = ba_ref.shape[0], u_ref.shape[1]
    start = pl.program_id(0) * chunk
    kept = (0, 1, 2, 4, 5)

    @pl.when(pl.program_id(0) == 0)
    def _():
        fetch(u_hbm, edge_hbm, u_ref, sem, first)

        def fx(q, _):
            u = [u_ref[f, q] for f in range(7)]
            f = fluxes(*shared(u[0], u[1:4], u[4:7]), u[1:4], u[4:7], 0)
            for i, c in enumerate(kept):
                f_ref[i, q] = f[c]
            return 0

        lax.fori_loop(0, total, fx, 0)

    def row(r, g, j):
        q = start + r + 2
        u = [u_ref[f, q] for f in range(7)]
        v, pressure = shared(u[0], u[1:4], u[4:7])
        fy = fluxes(v, pressure, u[1:4], u[4:7], 1)
        fz = fluxes(v, pressure, u[1:4], u[4:7], 2)
        ba, aa = ba_ref[r] + sb_ref[r], aa_ref[r] + sa_ref[r]
        bn, an, bf, af = from_below[0, r], from_above[0, r], from_below[0, 8 + r], from_above[0, 8 + r]
        hm = [ends(bn, an, 0), ends(bn, an, 1), ends(ba, aa, 1)]
        hb = [ends(ba, aa, 3), ends(bn, an, 2), ends(bn, an, 3)]
        fh = fluxes(*shared(ends(ba, aa, 0), hm, hb), hm, hb, 2)
        halo = hm + hb
        far = [ends(bf, af, c) for c in range(4)] + [last_plane(from_below[0, 16 + g], from_above[0, 16 + g], j), None]
        for c in range(6):
            field = u[c + 1]
            new = field * (1.0 - 6.0 * DIFFUSION)
            new += DIFFUSION * (u_ref[c + 1, q - 1] + u_ref[c + 1, q + 1])
            if c in kept:
                i = kept.index(c)
                new += NEAR * (f_ref[i, q - 1] - f_ref[i, q + 1]) + FAR * (f_ref[i, q + 2] - f_ref[i, q - 2])
            b = DIFFUSION * field
            if fy[c] is None:
                new += turn(b, 1, 1) + turn(b, -1, 1)
            else:
                new += along_y(fy[c], b)
            new += along_z(fz[c], b, fh[c], halo[c], far[c])
            if c == 0:
                slope = NEAR * (u_ref[7, q - 1] - u_ref[7, q + 1]) + FAR * (u_ref[7, q + 2] - u_ref[7, q - 2])
                new += u[0] * slope
            if c == 1:
                potential = u_ref[7, q]
                slope = NEAR * (turn(potential, 1, 1) - turn(potential, -1, 1))
                new += u[0] * (slope + FAR * (turn(potential, -2, 1) - turn(potential, 2, 1)))
            if c < 3:
                unpair(mom_ref, new, c, r)
            else:
                unpair(mag_ref, new, c - 3, r)

    def body(g, _):
        for j in range(4):
            row(4 * g + j, g, j)
        return 0

    lax.fori_loop(0, chunk // 4, body, 0)


def modes_kernel(w_ref, ch_ref, cl_ref, sh_ref, sl_ref, out_ref, x_ref, *, turned):
    dot = functools.partial(jnp.dot, preferred_element_type=jnp.float32)
    planes, band, nx = out_ref.shape[1:]

    def split(part):
        if turned:
            x = jnp.concatenate([w_ref[part, z] for z in range(planes)], axis=0)
        else:
            width = w_ref.shape[3]
            for s in range(w_ref.shape[0]):
                for z in range(planes):
                    x_ref[z * band : (z + 1) * band, s * width : (s + 1) * width] = w_ref[s, part, z].T
            x = x_ref[...]
        high = x.astype(jnp.bfloat16)
        return high, (x - high.astype(jnp.float32)).astype(jnp.bfloat16)

    re, im = split(0), split(1)
    times = lambda x, h, l: dot(x[0], h[...]) + dot(x[0], l[...]) + dot(x[1], h[...])
    scale = 1.0 / math.sqrt(NX * nx)
    shape = (band, nx)
    ky = lax.broadcasted_iota(jnp.int32, shape, 0) + lax.axis_index("xy") * band
    kx = lax.broadcasted_iota(jnp.int32, shape, 1)
    keep = jnp.where((ky == 0) & (kx == 0), 0.0, scale)
    out_re = times(re, ch_ref, cl_ref) + times(im, sh_ref, sl_ref)
    out_im = times(im, ch_ref, cl_ref) - times(re, sh_ref, sl_ref)
    for z in range(planes):
        out_ref[0, z] = out_re[z * band : (z + 1) * band] * keep
        out_ref[1, z] = out_im[z * band : (z + 1) * band] * keep


def cost(flops, bytes_accessed):
    return pl.CostEstimate(flops=int(flops), bytes_accessed=int(bytes_accessed), transcendentals=0)


def tables(size):
    angle = (np.outer(np.arange(size), np.arange(size)) % size) * (2.0 * np.pi / size)
    result = []
    for table in (np.cos(angle), np.sin(angle)):
        high = table.astype(np.float32).astype(ml_dtypes.bfloat16)
        low = (table - high.astype(np.float64)).astype(np.float32).astype(ml_dtypes.bfloat16)
        result += [high, low]
    return result


def row_order(half):
    matrix = np.zeros((8 * half, 8 * half), np.float32)
    for z in range(4):
        for h in range(2):
            for p in range(half):
                matrix[(z * 2 + h) * half + p, p * 8 + h * 4 + z] = 1.0
    return matrix.astype(ml_dtypes.bfloat16)


def shift(block, axis, step):
    n = lax.axis_size(axis)
    return lax.ppermute(block, axis, [(i, (i + step) % n) for i in range(n)])


def on_device(density, momentum, magnetic, arm_potential, sn_cells, sn_counts):
    rows, planes, ny = density.shape
    half = rows // 2
    layers, across = lax.axis_size("gz"), lax.axis_size("xy")
    devices = layers * across
    tile_row, tile_plane = lax.axis_index("xy"), lax.axis_index("gz")
    field = rows * planes * ny
    f32 = jnp.float32
    shape = jax.ShapeDtypeStruct
    whole = pl.BlockSpec(memory_space=pltpu.VMEM)
    smem = pl.BlockSpec(memory_space=pltpu.SMEM)
    params = pltpu.CompilerParams(vmem_limit_bytes=VMEM)
    message = shape((2, half, planes, ny), f32)
    tile = shape((half, 8, ny), f32)
    steps = half // 8
    counts = (steps * 5 // 8, steps - steps * 5 // 8) if steps >= 2 else (steps,)

    slots_here = sn_cells.shape[0]
    rho = density.reshape(2, half, planes, ny)
    mom = momentum.reshape(3, 2, half, planes, ny)
    mag = magnetic.reshape(3, 2, half, planes, ny)

    pot = arm_potential.reshape(2, half, ny)
    edges = shape((8, 2, planes, ny), f32)
    mine = shape((devices, 1, -(-4 * slots_here // 128) * 128), jnp.int32)
    full = lambda s: pl.BlockSpec(s, lambda i: (0,) * len(s))
    mine, first_rows, last_rows = pl.pallas_call(
        first_kernel,
        grid=(1,),
        in_specs=[smem, smem] + [
            spec
            for h, k in ((0, 0), (1, half // 2 - 1))
            for spec in (
                pl.BlockSpec((1, 2, planes, ny), lambda i, h=h, k=k: (h, k, 0, 0)),
                pl.BlockSpec((3, 1, 2, planes, ny), lambda i, h=h, k=k: (0, h, k, 0, 0)),
                pl.BlockSpec((3, 1, 2, planes, ny), lambda i, h=h, k=k: (0, h, k, 0, 0)),
                pl.BlockSpec((8, ny), lambda i, h=h: (h * (rows // 8 - 1), 0)),
            )
        ],
        out_specs=[full(mine.shape)] + [full(edges.shape)] * 2,
        out_shape=[mine] + [edges] * 2,
        compiler_params=params,
        cost_estimate=cost(*PACK_COST),
        name="first",
    )(sn_cells, sn_counts, *[rho, mom, mag, arm_potential] * 2)
    events = lax.all_to_all(mine, ("gz", "xy"), split_axis=0, concat_axis=0, tiled=True)
    before, after = shift(last_rows, "xy", 1), shift(first_rows, "xy", -1)

    some = math.gcd(half, 16)
    up, down = pl.pallas_call(
        pack_kernel,
        grid=(half // some,),
        in_specs=[pl.BlockSpec((2, some, planes, ny), lambda i: (0, i, 0, 0))] + [
            pl.BlockSpec((1, 2, some, planes, ny), lambda i, f=f: (f, 0, i, 0, 0)) for f in (2, 0)
        ] + [pl.BlockSpec(memory_space=pl.ANY)],
        out_specs=[pl.BlockSpec((some, 8, ny), lambda i: (i, 0, 0))] * 2,
        out_shape=[tile] * 2,
        compiler_params=params,
        cost_estimate=cost(*PACK_COST),
        name="pack",
    )(rho, mom, mag, mine)
    below_a, above_a = shift(up, "gz", 1), shift(down, "gz", -1)

    parcels = [shape((n, 18, 8, ny), f32) for n in counts]
    side = pltpu.VMEM((half + 4, 8, ny), f32)
    begins = [sum(counts[:i]) for i in range(len(counts))]
    parcel = pl.BlockSpec((1, 18, 8, ny), lambda i: (jnp.minimum(i, counts[0] - 1), 0, 0, 0))
    eight = pl.BlockSpec((8, 8, ny), lambda i: (i, 0, 0))
    middle = [
        spec
        for h, k in ((0, steps - 1), (1, 0))
        for spec in (
            pl.BlockSpec((1, 2, planes, ny), lambda i, h=h, k=k: (h, k * 4 + 3 * (1 - h), 0, 0)),
            pl.BlockSpec((3, 1, 2, planes, ny), lambda i, h=h, k=k: (0, h, k * 4 + 3 * (1 - h), 0, 0)),
            pl.BlockSpec((3, 1, 2, planes, ny), lambda i, h=h, k=k: (0, h, k * 4 + 3 * (1 - h), 0, 0)),
            pl.BlockSpec((1, 8, ny), lambda i, h=h, k=k: (h, k, 0)),
        )
    ]
    rows_of = lambda n: pl.BlockSpec((n, 2, 8, planes, ny), lambda i: (0, 0, i, 0, 0))
    state, edge, sb, sa, up_0, down_0 = pl.pallas_call(
        functools.partial(state_kernel, depth=planes * layers, count=counts[0], per_device=slots_here),
        grid=(steps,),
        in_specs=[
            smem, pl.BlockSpec((2, 8, planes, ny), lambda i: (0, i, 0, 0)), rows_of(3), rows_of(3),
            pl.BlockSpec((2, 8, ny), lambda i: (0, i, 0)), full(edges.shape), full(edges.shape),
        ] + middle,
        out_specs=[pl.BlockSpec((8, 8, 8, ny), lambda i: (0, i, 0, 0)), full((8, 4, 8, ny)), eight, eight, parcel, parcel],
        out_shape=[shape((8, half, 8, ny), f32), shape((8, 4, 8, ny), f32), tile, tile, parcels[0], parcels[0]],
        scratch_shapes=[pltpu.VMEM((4, half + 4, 8, ny), f32), side, side],
        compiler_params=params,
        cost_estimate=cost(*STATE_COST),
        name="state",
    )(events, rho, mom, mag, pot, before, after, *[rho, mom, mag, pot] * 2)
    parcels_below, parcels_above = [shift(up_0, "gz", 1)], [shift(down_0, "gz", -1)]

    cos_high, cos_low, sin_high, sin_low = tables(ny)
    band = ny // across
    turned = band % 128 != 0 or rows % 128 != 0
    hbm = pl.BlockSpec(memory_space=pl.ANY)
    copies = pltpu.SemaphoreType.DMA((3,))
    more = parcels[1:] * 2
    new_density, wave, *messages = pl.pallas_call(
        density_kernel,
        in_specs=[hbm, hbm] + [whole] * 7,
        out_specs=[whole] * (2 + len(more)),
        out_shape=[message, shape((across, 2, planes, rows, band), f32), *more],
        scratch_shapes=[
            pltpu.VMEM((8 * half, ny), f32), pltpu.VMEM((4, half + 4, 8, ny), f32),
            pltpu.VMEM((3, counts[-1] * 8, 8, ny), f32), pltpu.SemaphoreType.DMA((4,)),
        ],
        compiler_params=params,
        cost_estimate=cost(*DENSITY_COST),
        name="density",
    )(
        state, edge, below_a, above_a, sb, sa, row_order(half),
        np.stack([cos_high, -sin_high]), np.stack([cos_low, -sin_low]),
    )

    if messages:
        parcels_below.append(shift(messages[0], "gz", 1))
        parcels_above.append(shift(messages[1], "gz", -1))
    portion = lax.all_to_all(wave, "xy", split_axis=0, concat_axis=0, tiled=True)
    if turned:
        portion = portion.transpose(1, 2, 4, 0, 3).reshape(2, planes, band, NX)
    modes = pl.pallas_call(
        functools.partial(modes_kernel, turned=turned),
        in_specs=[whole] * 5,
        out_specs=whole,
        out_shape=shape((2, planes, band, NX), f32),
        scratch_shapes=[pltpu.VMEM((planes * band, NX), f32)],
        compiler_params=params,
        cost_estimate=cost(*MODES_COST),
        name="modes",
    )(portion, *tables(NX))
    results = [shape((3, 2, half, planes, ny), f32)] * 2
    new = []
    for i, n in enumerate(counts):
        chunk, first = 8, begins[i] * 8
        here = pl.BlockSpec((chunk, 8, ny), lambda k, o=begins[i]: (o + k, 0, 0))
        parcel = pl.BlockSpec((1, 18, 8, ny), lambda k: (k, 0, 0, 0))
        three = pl.BlockSpec((3, 2, chunk, planes, ny), lambda k, o=begins[i]: (0, 0, o + k, 0, 0))
        below, above = parcels_below[i], parcels_above[i]
        extra = [*new] + [modes] * (i > 0 and i == len(counts) - 1)
        new = pl.pallas_call(
            functools.partial(main_kernel, first=first),
            grid=(n,),
            in_specs=[hbm, hbm] + [here] * 4 + [parcel] * 2 + [hbm] * len(extra),
            out_specs=[three, three],
            out_shape=results,
            scratch_shapes=[
                pltpu.VMEM((8, n * 8 + 4, 8, ny), f32), pltpu.VMEM((5, n * 8 + 4, 8, ny), f32), copies,
            ],
            input_output_aliases={8: 0, 9: 1} if new else {},
            compiler_params=pltpu.CompilerParams(vmem_limit_bytes=62 * 1024 * 1024),
            cost_estimate=cost(*MAIN_COST),
            name=f"main{i}",
        )(state, edge, below_a, above_a, sb, sa, below, above, *extra)
    new_mom, new_mag = new

    return (
        new_density.reshape(rows, planes, ny),
        new_mom.reshape(3, rows, planes, ny),
        new_mag.reshape(3, rows, planes, ny),
        modes,
    )


def solution(mesh):
    in_specs = (
        P("xy", "gz", None),
        P(None, "xy", "gz", None),
        P(None, "xy", "gz", None),
        P("xy", None),
        P(("gz", "xy"), None),
        P(("gz", "xy")),
    )
    out_specs = (
        P("xy", "gz", None),
        P(None, "xy", "gz", None),
        P(None, "xy", "gz", None),
        P(None, "gz", "xy", None),
    )
    return jax.shard_map(
        on_device, mesh=mesh, in_specs=in_specs, out_specs=out_specs, check_vma=False
    )
```

```python
import functools
import math

import jax
import jax.numpy as jnp
import ml_dtypes
import numpy as np
from jax import lax
from jax.experimental import pallas as pl
from jax.experimental.pallas import tpu as pltpu
from jax.sharding import PartitionSpec as P

NX = 512
RADIUS = 16
IMPULSE = 2.0 / 16
TIME_STEP = 0.1
DIFFUSION = 0.05
NEAR = 8.0 * TIME_STEP / 12.0
FAR = TIME_STEP / 12.0
VMEM = 56 * 1024 * 1024
PACK_COST = MODES_COST = (1e6, 1e5)
STATE_COST = DENSITY_COST = (1e12, 4e9)
MAIN_COST = (1e12, 4e9)


def pair(ref, *index):
    return jnp.concatenate([ref[(*index[:-1], 0, index[-1])], ref[(*index[:-1], 1, index[-1])]], axis=0)


def unpair(ref, value, *index):
    ref[(*index[:-1], 0, index[-1])] = value[:4]
    ref[(*index[:-1], 1, index[-1])] = value[4:]


def slots(shape):
    sub = lax.broadcasted_iota(jnp.int32, shape, len(shape) - 2)
    return jnp.where(sub >= 4, sub - 4, sub)


def turn(value, shift, axis):
    return pltpu.roll(value, shift % value.shape[axis], axis)


def gather_planes(values, plane):
    slot = slots(values[0].shape)
    out = turn(values[-1], len(values) - 1 - plane, 0)
    for c in reversed(range(len(values) - 1)):
        out = jnp.where(slot == c, turn(values[c], c - plane, 0), out)
    return out


def collect(values, plane):
    sub = lax.broadcasted_iota(jnp.int32, values[0].shape, 0)
    out = turn(values[0], -plane, 0)
    for n in range(1, 8):
        j, h = n // 2, n % 2
        out = jnp.where(sub == n, turn(values[j], n - 4 * h - plane, 0), out)
    return out


def shared(rho, m, b):
    inv = 1.0 / rho
    return [x * inv for x in m], rho + 0.5 * (b[0] * b[0] + b[1] * b[1] + b[2] * b[2])


def fluxes(v, total, m, b, k):
    push = [m[i] * v[k] - b[i] * b[k] + (total if i == k else 0.0) for i in range(3)]
    turned = [None if i == k else v[k] * b[i] - b[k] * v[i] for i in range(3)]
    return push + turned


def first_kernel(cell_ref, count_ref, rho_a, mom_a, mag_a, pot_a, rho_z, mom_z, mag_z, pot_z, ev_ref, first_ref, last_ref):
    shape = (1, ev_ref.shape[2])
    lane = lax.broadcasted_iota(jnp.int32, shape, 1)
    row = jnp.zeros(shape, jnp.int32)
    for e in range(count_ref.shape[0]):
        for i in range(4):
            row = jnp.where(lane == 4 * e + i, cell_ref[e, i] if i < 3 else count_ref[e], row)

    def copy(d, _):
        ev_ref[d] = row
        return 0

    lax.fori_loop(0, ev_ref.shape[0], copy, 0)
    for ref, rho, mom, mag, pot, skip in (
        (first_ref, rho_a, mom_a, mag_a, pot_a, 0), (last_ref, rho_z, mom_z, mag_z, pot_z, pot_z.shape[0] - 2),
    ):
        for j in range(2):
            ref[0, j] = rho[0, j]
            for c in range(3):
                ref[1 + c, j] = mom[c, 0, j]
                ref[4 + c, j] = mag[c, 0, j]
            ref[7, j] = jnp.broadcast_to(pot[skip + j : skip + j + 1], ref.shape[2:])


def pack_kernel(rho_ref, mz_ref, after_ref, up_ref, down_ref):
    def body(g, _):
        rho = [pair(rho_ref, 4 * g + j) for j in range(4)]
        mz = [pair(mz_ref, 0, 4 * g + j) for j in range(4)]
        for i, (values, up, down) in enumerate(((rho, 3, 0), (mz, 3, 0), (mz, 2, 1))):
            up_ref[g, i] = collect(values, up)
            down_ref[g, i] = collect(values, down)
        return 0

    lax.fori_loop(0, rho_ref.shape[1] // 4, body, 0)


def write_messages(up_ref, down_ref, k, g, state):
    fluxes_by, bx = [], []
    for j in range(4):
        r = 4 * g + j
        u = state(j)
        near = [u[1], u[2], u[5], u[6]]
        up_ref[k, r] = gather_planes(near, 3)
        down_ref[k, r] = gather_planes(near, 0)
        f = fluxes(*shared(u[0], u[1:4], u[4:7]), u[1:4], u[4:7], 2)
        up_ref[k, 8 + r] = gather_planes(f[:4], 2)
        down_ref[k, 8 + r] = gather_planes(f[:4], 1)
        fluxes_by.append(f[4])
        bx.append(u[4])
    up_ref[k, 16 + g] = collect(fluxes_by, 2)
    down_ref[k, 16 + g] = collect(fluxes_by, 1)
    up_ref[k, 18 + g] = collect(bx, 3)
    down_ref[k, 18 + g] = collect(bx, 0)


def state_kernel(
    ev_ref, rho_ref, mom_ref, mag_ref, pot_ref, before_ref, after_ref, rho_l, mom_l, mag_l, pot_l,
    rho_h, mom_h, mag_h, pot_h, u_out, edge_out, sb_out, sa_out, up_ref, down_ref, s_ref, sb_ref, sa_ref, *,
    depth, count, per_device,
):
    half, ny = s_ref.shape[1] - 4, s_ref.shape[3]
    step_id = pl.program_id(0)

    @pl.when(step_id == 0)
    def _():
        deposit(ev_ref, s_ref, sb_ref, sa_ref, depth, per_device)
        pieces = lambda rho, mom, mag, pot, j: (
            [rho[0, j]] + [mom[c, 0, j] for c in range(3)] + [mag[c, 0, j] for c in range(3)]
            + [jnp.broadcast_to(pot, (4, ny))]
        )
        for j in range(2):
            low = pieces(rho_l, mom_l, mag_l, pot_l[0, 6 + j : 7 + j], j)
            high = pieces(rho_h, mom_h, mag_h, pot_h[0, j : j + 1], j)
            for f in range(8):
                left = jnp.concatenate([before_ref[f, j], low[f]], axis=0)
                right = jnp.concatenate([high[f], after_ref[f, j]], axis=0)
                edge_out[f, j] = left + s_ref[f, j] if f < 4 else left
                edge_out[f, 2 + j] = right + s_ref[f, half + 2 + j] if f < 4 else right

    start = step_id * 8

    def body(g, send):
        def state(j):
            r = 4 * g + j
            q = start + r + 2
            sb_out[r] = sb_ref[q]
            sa_out[r] = sa_ref[q]
            u = [pair(rho_ref, r) + s_ref[0, q]]
            u += [pair(mom_ref, c, r) + s_ref[1 + c, q] for c in range(3)]
            u += [pair(mag_ref, c, r) for c in range(3)]
            for f in range(7):
                u_out[f, r] = u[f]
            rows = [jnp.broadcast_to(pot_ref[h, pl.ds(r, 1), :], (4, ny)) for h in range(2)]
            u_out[7, r] = jnp.concatenate(rows, axis=0)
            return u

        if send:
            write_messages(up_ref, down_ref, 0, g, state)
        else:
            for j in range(4):
                state(j)
        return 0

    @pl.when(step_id < count)
    def _():
        lax.fori_loop(0, 2, lambda g, _: body(g, True), 0)

    @pl.when(step_id >= count)
    def _():
        lax.fori_loop(0, 2, lambda g, _: body(g, False), 0)


def deposit(ev_ref, s_ref, sb_ref, sa_ref, depth, per_device):
    half, ny = s_ref.shape[1] - 4, s_ref.shape[3]
    rows, events = 2 * half, ev_ref.shape[0] * per_device
    row_start, plane_start = lax.axis_index("xy") * rows, lax.axis_index("gz") * 4
    s_ref[...] = jnp.zeros_like(s_ref)
    sb_ref[...] = jnp.zeros_like(sb_ref)
    sa_ref[...] = jnp.zeros_like(sa_ref)

    shape = (4, 8, 128)
    slot = slots(shape)
    sub = lax.broadcasted_iota(jnp.int32, shape, 1)
    step = lax.broadcasted_iota(jnp.int32, shape, 0)
    lane = lax.broadcasted_iota(jnp.int32, shape, 2)

    def wrapped(distance, size):
        distance = jnp.where(distance >= size // 2, distance - size, distance)
        return jnp.where(distance < -(size // 2), distance + size, distance)

    def event(e, _):
        device, slot_id = (e, 0) if per_device == 1 else (lax.div(e, per_device), lax.rem(e, per_device))
        row, col, plane, count = (ev_ref[device, 0, 4 * slot_id + i] for i in range(4))
        rel = wrapped(row - row_start - half, NX)
        rel = rel + half

        @pl.when((count > 0) & (rel > -2 - RADIUS) & (rel < rows + 2 + RADIUS))
        def _():
            base = plane_start - plane
            dz = wrapped(slot + base, depth).astype(jnp.float32)
            dzb = wrapped(jnp.where(slot == 2, -2, -1) + base, depth).astype(jnp.float32)
            dza = wrapped(jnp.where(slot == 2, 5, 4) + base, depth).astype(jnp.float32)
            share = lambda d: jnp.where(slot == 0, 1.0, jnp.where(slot == 3, 0.0, IMPULSE * d))
            first = jnp.bitwise_and(col - RADIUS, ny - 1) // 128
            second = jnp.bitwise_and(col + RADIUS - 1, ny - 1) // 128

            def tile(t, _):
                index = jnp.where(t == 0, first, second)
                lanes = pl.ds(pl.multiple_of(index * 128, 128), 128)
                dy = wrapped(lane + index * 128 - col, ny).astype(jnp.float32)
                dy2 = dy * dy
                for h in range(2):
                    weight = jnp.where((sub >= 4) == (h == 1), count, 0).astype(jnp.float32)
                    low = jnp.clip(rel - RADIUS + 1 - h * half + 2, 0, half + 4) // 4
                    high = (jnp.clip(rel + RADIUS - 1 - h * half + 2, -1, half + 3) + 4) // 4

                    def chunk(n, _):
                        q = pl.ds(n * 4, 4)
                        dx = (step + (n * 4 - 2 + h * half - rel)).astype(jnp.float32)
                        flat = dx * dx + dy2
                        size = lambda d: jnp.maximum(1.0 - (flat + d * d) * (1.0 / (RADIUS * RADIUS)), 0.0) * weight
                        w = size(dz)
                        s_ref[0, q, :, lanes] += w
                        w = w * IMPULSE
                        s_ref[1, q, :, lanes] += w * dx
                        s_ref[2, q, :, lanes] += w * dy
                        s_ref[3, q, :, lanes] += w * dz
                        sb_ref[q, :, lanes] += size(dzb) * share(dzb)
                        sa_ref[q, :, lanes] += size(dza) * share(dza)
                        return 0

                    lax.fori_loop(low, high, chunk, 0)
                return 0

            lax.fori_loop(0, jnp.where(first == second, 1, 2), tile, 0)

        return 0

    lax.fori_loop(0, events, event, 0)


def ends(below, above, c):
    return jnp.where(slots(below.shape) == 3, turn(above, 3 - c, 0), turn(below, -c, 0))


def along_y(f, b):
    near, far = NEAR * f, FAR * f
    return turn(b + near, 1, 1) + turn(b - near, -1, 1) + turn(far, -2, 1) - turn(far, 2, 1)


def along_z(f, b, near_f, near_u, far_f):
    slot = slots(b.shape)
    first, last = slot == 0, slot == 3
    outer = DIFFUSION * near_u
    if f is None:
        return jnp.where(first, outer, turn(b, 1, 0)) + jnp.where(last, outer, turn(b, -1, 0))
    near = NEAR * f
    outer += jnp.where(first, NEAR, -NEAR) * near_f
    out = jnp.where(first, outer, turn(b + near, 1, 0)) + jnp.where(last, outer, turn(b - near, -1, 0))
    beyond = jnp.where(slot == 1, turn(near_f, 1, 0), jnp.where(slot == 2, turn(near_f, -1, 0), far_f))
    return out + FAR * (jnp.where(slot <= 1, turn(f, -2, 0), beyond) - jnp.where(slot >= 2, turn(f, 2, 0), beyond))


def fetch(u_hbm, edge_hbm, u_ref, sem, first):
    fields, total = u_ref.shape[:2]
    half = u_hbm.shape[1]
    low, high = max(first - 2, 0), min(first + total - 2, half)
    copies = [pltpu.make_async_copy(u_hbm.at[:fields, low:high], u_ref.at[:, low - first + 2 : high - first + 2], sem.at[0])]
    if first == 0:
        copies.append(pltpu.make_async_copy(edge_hbm.at[:fields, 0:2], u_ref.at[:, 0:2], sem.at[1]))
    if first + total - 4 == half:
        copies.append(pltpu.make_async_copy(edge_hbm.at[:fields, 2:4], u_ref.at[:, total - 2 : total], sem.at[2]))
    for copy in copies:
        copy.start()
    for copy in copies:
        copy.wait()


def density_kernel(
    u_hbm, edge_hbm, below_ref, above_ref, sb_ref, sa_ref, order_ref, high_ref, low_ref, out_ref, wave_ref,
    rho_out, mz_out, *rest,
):
    *parcel, d_ref, u_ref, b_ref, sem = rest
    half = u_hbm.shape[1]
    field = None
    if parcel:
        field = pltpu.make_async_copy(u_hbm.at[4:7, half - b_ref.shape[1] :], b_ref, sem.at[3])
        field.start()
    fetch(u_hbm, edge_hbm, u_ref, sem, 0)
    rows = 2 * half

    def row(p, g, j):
        rho, my, mz = u_ref[0, p + 2], u_ref[2, p + 2], u_ref[3, p + 2]
        sb, sa = sb_ref[p], sa_ref[p]
        halo = [last_plane(below_ref[g, i], above_ref[g, i], j) + ends(sb, sa, i) for i in range(3)]
        rho_out[p], mz_out[p] = halo[:2]
        b = DIFFUSION * rho
        new = rho * (1.0 - 6.0 * DIFFUSION)
        new += DIFFUSION * (u_ref[0, p + 1] + u_ref[0, p + 3])
        new += NEAR * (u_ref[1, p + 1] - u_ref[1, p + 3]) + FAR * (u_ref[1, p + 4] - u_ref[1, p])
        new += along_y(my, b)
        new += along_z(mz, b, halo[1], halo[0], halo[2])
        unpair(out_ref, new, p)
        d_ref[pl.ds(pl.multiple_of(p * 8, 8), 8), :] = new

    def body(g, _):
        for j in range(4):
            row(4 * g + j, g, j)
        return 0

    lax.fori_loop(0, half // 4, body, 0)
    d = d_ref[...]
    order = order_ref[...]
    dot = functools.partial(jnp.dot, preferred_element_type=jnp.float32)
    high = d.astype(jnp.bfloat16)
    low = (d - high.astype(jnp.float32)).astype(jnp.bfloat16)
    high = dot(order, high).astype(jnp.bfloat16)
    low = dot(order, low).astype(jnp.bfloat16)
    for part in range(2):
        c_high, c_low = high_ref[part], low_ref[part]
        wave = dot(high, c_high) + dot(high, c_low) + dot(low, c_high)
        peers, band = wave_ref.shape[0], wave_ref.shape[4]
        for j in range(peers):
            for z in range(4):
                wave_ref[j, part, z] = wave[z * rows : (z + 1) * rows, j * band : (j + 1) * band]
    if not parcel:
        return
    field.wait()
    first = half - b_ref.shape[1]

    def messages(n, _):
        r = n * 4
        state = lambda j: [u_ref[f, first + r + j + 2] for f in range(4)] + [b_ref[c, r + j] for c in range(3)]
        write_messages(*parcel, n // 2, n % 2, state)
        return 0

    lax.fori_loop(0, b_ref.shape[1] // 4, messages, 0)


def last_plane(below, above, j):
    sub = lax.broadcasted_iota(jnp.int32, below.shape, 0)
    out = turn(below, -2 * j, 0)
    out = jnp.where(sub == 3, turn(above, 3 - 2 * j, 0), out)
    out = jnp.where(sub == 4, turn(below, 3 - 2 * j, 0), out)
    return jnp.where(sub == 7, turn(above, 6 - 2 * j, 0), out)


def main_kernel(u_hbm, edge_hbm, rho_ref, mz_ref, from_below, from_above, *rest, first):
    mom_ref, mag_ref, u_ref, f_ref, sem = rest[-5:]
    chunk, total, half = rho_ref.shape[0], u_ref.shape[1], u_hbm.shape[1]
    step_id = pl.program_id(0)
    start = step_id * chunk
    kept = (0, 1, 2, 4, 5)

    def copies(i):
        low = 0 if i == 0 else chunk * i + 4
        high = chunk * (i + 1) + 4
        a, b = max(first - 2 + low, 0), min(first - 2 + high, half)
        at = a - first + 2
        result = [(u_hbm.at[:, a:b], u_ref.at[:, at : at + b - a], sem.at[i])]
        if first - 2 + low < 0:
            result.append((edge_hbm.at[:, 0:2], u_ref.at[:, 0:2], sem.at[total // chunk]))
        if first - 2 + high > half:
            result.append((edge_hbm.at[:, 2:4], u_ref.at[:, total - 2 : total], sem.at[total // chunk + 1]))
        return [pltpu.make_async_copy(*c) for c in result]

    @pl.when(step_id == 0)
    def _():
        for i in range(total // chunk):
            for copy in copies(i):
                copy.start()

    for i in range(total // chunk):

        @pl.when(step_id == i)
        def _(i=i):
            for copy in copies(i):
                copy.wait()

    def fx(q, _):
        u = [u_ref[f, q] for f in range(7)]
        f = fluxes(*shared(u[0], u[1:4], u[4:7]), u[1:4], u[4:7], 0)
        for i, c in enumerate(kept):
            f_ref[i, q] = f[c]
        return 0

    lax.fori_loop(jnp.where(step_id == 0, 0, start + 4), start + chunk + 4, fx, 0)

    def row(r, g, j):
        q = start + r + 2
        u = [u_ref[f, q] for f in range(7)]
        v, pressure = shared(u[0], u[1:4], u[4:7])
        fy = fluxes(v, pressure, u[1:4], u[4:7], 1)
        fz = fluxes(v, pressure, u[1:4], u[4:7], 2)
        bn, an, bf, af = from_below[0, r], from_above[0, r], from_below[0, 8 + r], from_above[0, 8 + r]
        hm = [ends(bn, an, 0), ends(bn, an, 1), mz_ref[r]]
        hb = [last_plane(from_below[0, 18 + g], from_above[0, 18 + g], j), ends(bn, an, 2), ends(bn, an, 3)]
        fh = fluxes(*shared(rho_ref[r], hm, hb), hm, hb, 2)
        halo = hm + hb
        far = [ends(bf, af, c) for c in range(4)] + [last_plane(from_below[0, 16 + g], from_above[0, 16 + g], j), None]
        for c in range(6):
            field = u[c + 1]
            new = field * (1.0 - 6.0 * DIFFUSION)
            new += DIFFUSION * (u_ref[c + 1, q - 1] + u_ref[c + 1, q + 1])
            if c in kept:
                i = kept.index(c)
                new += NEAR * (f_ref[i, q - 1] - f_ref[i, q + 1]) + FAR * (f_ref[i, q + 2] - f_ref[i, q - 2])
            b = DIFFUSION * field
            if fy[c] is None:
                new += turn(b, 1, 1) + turn(b, -1, 1)
            else:
                new += along_y(fy[c], b)
            new += along_z(fz[c], b, fh[c], halo[c], far[c])
            if c == 0:
                slope = NEAR * (u_ref[7, q - 1] - u_ref[7, q + 1]) + FAR * (u_ref[7, q + 2] - u_ref[7, q - 2])
                new += u[0] * slope
            if c == 1:
                potential = u_ref[7, q]
                slope = NEAR * (turn(potential, 1, 1) - turn(potential, -1, 1))
                new += u[0] * (slope + FAR * (turn(potential, -2, 1) - turn(potential, 2, 1)))
            if c < 3:
                unpair(mom_ref, new, c, r)
            else:
                unpair(mag_ref, new, c - 3, r)

    def body(g, _):
        for j in range(4):
            row(4 * g + j, g, j)
        return 0

    lax.fori_loop(0, chunk // 4, body, 0)


def modes_kernel(w_ref, ch_ref, cl_ref, sh_ref, sl_ref, out_ref, x_ref, *, turned):
    dot = functools.partial(jnp.dot, preferred_element_type=jnp.float32)
    planes, band, nx = out_ref.shape[1:]

    def split(part):
        if turned:
            x = jnp.concatenate([w_ref[part, z] for z in range(planes)], axis=0)
        else:
            width = w_ref.shape[3]
            for s in range(w_ref.shape[0]):
                for z in range(planes):
                    x_ref[z * band : (z + 1) * band, s * width : (s + 1) * width] = w_ref[s, part, z].T
            x = x_ref[...]
        high = x.astype(jnp.bfloat16)
        return high, (x - high.astype(jnp.float32)).astype(jnp.bfloat16)

    re, im = split(0), split(1)
    times = lambda x, h, l: dot(x[0], h[...]) + dot(x[0], l[...]) + dot(x[1], h[...])
    scale = 1.0 / math.sqrt(NX * nx)
    shape = (band, nx)
    ky = lax.broadcasted_iota(jnp.int32, shape, 0) + lax.axis_index("xy") * band
    kx = lax.broadcasted_iota(jnp.int32, shape, 1)
    keep = jnp.where((ky == 0) & (kx == 0), 0.0, scale)
    out_re = times(re, ch_ref, cl_ref) + times(im, sh_ref, sl_ref)
    out_im = times(im, ch_ref, cl_ref) - times(re, sh_ref, sl_ref)
    for z in range(planes):
        out_ref[0, z] = out_re[z * band : (z + 1) * band] * keep
        out_ref[1, z] = out_im[z * band : (z + 1) * band] * keep


def cost(flops, bytes_accessed):
    return pl.CostEstimate(flops=int(flops), bytes_accessed=int(bytes_accessed), transcendentals=0)


def tables(size):
    angle = (np.outer(np.arange(size), np.arange(size)) % size) * (2.0 * np.pi / size)
    result = []
    for table in (np.cos(angle), np.sin(angle)):
        high = table.astype(np.float32).astype(ml_dtypes.bfloat16)
        low = (table - high.astype(np.float64)).astype(np.float32).astype(ml_dtypes.bfloat16)
        result += [high, low]
    return result


def row_order(half):
    matrix = np.zeros((8 * half, 8 * half), np.float32)
    for z in range(4):
        for h in range(2):
            for p in range(half):
                matrix[(z * 2 + h) * half + p, p * 8 + h * 4 + z] = 1.0
    return matrix.astype(ml_dtypes.bfloat16)


def shift(block, axis, step):
    n = lax.axis_size(axis)
    return lax.ppermute(block, axis, [(i, (i + step) % n) for i in range(n)])


def on_device(density, momentum, magnetic, arm_potential, sn_cells, sn_counts):
    rows, planes, ny = density.shape
    half = rows // 2
    layers, across = lax.axis_size("gz"), lax.axis_size("xy")
    devices = layers * across
    tile_row, tile_plane = lax.axis_index("xy"), lax.axis_index("gz")
    field = rows * planes * ny
    f32 = jnp.float32
    shape = jax.ShapeDtypeStruct
    whole = pl.BlockSpec(memory_space=pltpu.VMEM)
    smem = pl.BlockSpec(memory_space=pltpu.SMEM)
    params = pltpu.CompilerParams(vmem_limit_bytes=VMEM)
    message = shape((2, half, planes, ny), f32)
    tile = shape((half, 8, ny), f32)
    steps = half // 8
    counts = (steps * 5 // 8, steps - steps * 5 // 8) if steps >= 2 else (steps,)

    slots_here = sn_cells.shape[0]
    rho = density.reshape(2, half, planes, ny)
    mom = momentum.reshape(3, 2, half, planes, ny)
    mag = magnetic.reshape(3, 2, half, planes, ny)

    pot = arm_potential.reshape(2, half, ny)
    edges = shape((8, 2, planes, ny), f32)
    mine = shape((devices, 1, -(-4 * slots_here // 128) * 128), jnp.int32)
    full = lambda s: pl.BlockSpec(s, lambda i: (0,) * len(s))
    mine, first_rows, last_rows = pl.pallas_call(
        first_kernel,
        grid=(1,),
        in_specs=[smem, smem] + [
            spec
            for h, k in ((0, 0), (1, half // 2 - 1))
            for spec in (
                pl.BlockSpec((1, 2, planes, ny), lambda i, h=h, k=k: (h, k, 0, 0)),
                pl.BlockSpec((3, 1, 2, planes, ny), lambda i, h=h, k=k: (0, h, k, 0, 0)),
                pl.BlockSpec((3, 1, 2, planes, ny), lambda i, h=h, k=k: (0, h, k, 0, 0)),
                pl.BlockSpec((8, ny), lambda i, h=h: (h * (rows // 8 - 1), 0)),
            )
        ],
        out_specs=[full(mine.shape)] + [full(edges.shape)] * 2,
        out_shape=[mine] + [edges] * 2,
        compiler_params=params,
        cost_estimate=cost(*PACK_COST),
        name="first",
    )(sn_cells, sn_counts, *[rho, mom, mag, arm_potential] * 2)
    events = lax.all_to_all(mine, ("gz", "xy"), split_axis=0, concat_axis=0, tiled=True)
    before, after = shift(last_rows, "xy", 1), shift(first_rows, "xy", -1)

    some = math.gcd(half, 16)
    up, down = pl.pallas_call(
        pack_kernel,
        grid=(half // some,),
        in_specs=[pl.BlockSpec((2, some, planes, ny), lambda i: (0, i, 0, 0))] + [
            pl.BlockSpec((1, 2, some, planes, ny), lambda i, f=f: (f, 0, i, 0, 0)) for f in (2,)
        ] + [pl.BlockSpec(memory_space=pl.ANY)],
        out_specs=[pl.BlockSpec((some // 4, 3, 8, ny), lambda i: (i, 0, 0, 0))] * 2,
        out_shape=[shape((half // 4, 3, 8, ny), f32)] * 2,
        compiler_params=params,
        cost_estimate=cost(*PACK_COST),
        name="pack",
    )(rho, mom, mine)
    below_a, above_a = shift(up, "gz", 1), shift(down, "gz", -1)

    parcels = [shape((n, 20, 8, ny), f32) for n in counts]
    side = pltpu.VMEM((half + 4, 8, ny), f32)
    begins = [sum(counts[:i]) for i in range(len(counts))]
    parcel = pl.BlockSpec((1, 20, 8, ny), lambda i: (jnp.minimum(i, counts[0] - 1), 0, 0, 0))
    eight = pl.BlockSpec((8, 8, ny), lambda i: (i, 0, 0))
    middle = [
        spec
        for h, k in ((0, steps - 1), (1, 0))
        for spec in (
            pl.BlockSpec((1, 2, planes, ny), lambda i, h=h, k=k: (h, k * 4 + 3 * (1 - h), 0, 0)),
            pl.BlockSpec((3, 1, 2, planes, ny), lambda i, h=h, k=k: (0, h, k * 4 + 3 * (1 - h), 0, 0)),
            pl.BlockSpec((3, 1, 2, planes, ny), lambda i, h=h, k=k: (0, h, k * 4 + 3 * (1 - h), 0, 0)),
            pl.BlockSpec((1, 8, ny), lambda i, h=h, k=k: (h, k, 0)),
        )
    ]
    rows_of = lambda n: pl.BlockSpec((n, 2, 8, planes, ny), lambda i: (0, 0, i, 0, 0))
    state, edge, sb, sa, up_0, down_0 = pl.pallas_call(
        functools.partial(state_kernel, depth=planes * layers, count=counts[0], per_device=slots_here),
        grid=(steps,),
        in_specs=[
            smem, pl.BlockSpec((2, 8, planes, ny), lambda i: (0, i, 0, 0)), rows_of(3), rows_of(3),
            pl.BlockSpec((2, 8, ny), lambda i: (0, i, 0)), full(edges.shape), full(edges.shape),
        ] + middle,
        out_specs=[pl.BlockSpec((8, 8, 8, ny), lambda i: (0, i, 0, 0)), full((8, 4, 8, ny)), eight, eight, parcel, parcel],
        out_shape=[shape((8, half, 8, ny), f32), shape((8, 4, 8, ny), f32), tile, tile, parcels[0], parcels[0]],
        scratch_shapes=[pltpu.VMEM((4, half + 4, 8, ny), f32), side, side],
        compiler_params=params,
        cost_estimate=cost(*STATE_COST),
        name="state",
    )(events, rho, mom, mag, pot, before, after, *[rho, mom, mag, pot] * 2)
    parcels_below, parcels_above = [shift(up_0, "gz", 1)], [shift(down_0, "gz", -1)]

    cos_high, cos_low, sin_high, sin_low = tables(ny)
    band = ny // across
    turned = band % 128 != 0 or rows % 128 != 0
    hbm = pl.BlockSpec(memory_space=pl.ANY)
    more = parcels[1:] * 2
    new_density, wave, rho_halo, mz_halo, *messages = pl.pallas_call(
        density_kernel,
        in_specs=[hbm, hbm] + [whole] * 7,
        out_specs=[whole] * (4 + len(more)),
        out_shape=[message, shape((across, 2, planes, rows, band), f32), tile, tile, *more],
        scratch_shapes=[
            pltpu.VMEM((8 * half, ny), f32), pltpu.VMEM((4, half + 4, 8, ny), f32),
            pltpu.VMEM((3, counts[-1] * 8, 8, ny), f32), pltpu.SemaphoreType.DMA((4,)),
        ],
        compiler_params=params,
        cost_estimate=cost(*DENSITY_COST),
        name="density",
    )(
        state, edge, below_a, above_a, sb, sa, row_order(half),
        np.stack([cos_high, -sin_high]), np.stack([cos_low, -sin_low]),
    )

    if messages:
        parcels_below.append(shift(messages[0], "gz", 1))
        parcels_above.append(shift(messages[1], "gz", -1))
    portion = lax.all_to_all(wave, "xy", split_axis=0, concat_axis=0, tiled=True)
    if turned:
        portion = portion.transpose(1, 2, 4, 0, 3).reshape(2, planes, band, NX)
    modes = pl.pallas_call(
        functools.partial(modes_kernel, turned=turned),
        in_specs=[whole] * 5,
        out_specs=whole,
        out_shape=shape((2, planes, band, NX), f32),
        scratch_shapes=[pltpu.VMEM((planes * band, NX), f32)],
        compiler_params=params,
        cost_estimate=cost(*MODES_COST),
        name="modes",
    )(portion, *tables(NX))
    results = [shape((3, 2, half, planes, ny), f32)] * 2
    new = []
    for i, n in enumerate(counts):
        chunk, first = 8, begins[i] * 8
        here = pl.BlockSpec((chunk, 8, ny), lambda k, o=begins[i]: (o + k, 0, 0))
        parcel = pl.BlockSpec((1, 20, 8, ny), lambda k: (k, 0, 0, 0))
        three = pl.BlockSpec((3, 2, chunk, planes, ny), lambda k, o=begins[i]: (0, 0, o + k, 0, 0))
        below, above = parcels_below[i], parcels_above[i]
        extra = [*new] + [modes] * (i > 0 and i == len(counts) - 1)
        new = pl.pallas_call(
            functools.partial(main_kernel, first=first),
            grid=(n,),
            in_specs=[hbm, hbm] + [here] * 2 + [parcel] * 2 + [hbm] * len(extra),
            out_specs=[three, three],
            out_shape=results,
            scratch_shapes=[
                pltpu.VMEM((8, n * 8 + 4, 8, ny), f32), pltpu.VMEM((5, n * 8 + 4, 8, ny), f32), pltpu.SemaphoreType.DMA((n + 2,)),
            ],
            input_output_aliases={6: 0, 7: 1} if new else {},
            compiler_params=pltpu.CompilerParams(vmem_limit_bytes=62 * 1024 * 1024),
            cost_estimate=cost(*MAIN_COST),
            name=f"main{i}",
        )(state, edge, rho_halo, mz_halo, below, above, *extra)
    new_mom, new_mag = new

    return (
        new_density.reshape(rows, planes, ny),
        new_mom.reshape(3, rows, planes, ny),
        new_mag.reshape(3, rows, planes, ny),
        modes,
    )


def solution(mesh):
    in_specs = (
        P("xy", "gz", None),
        P(None, "xy", "gz", None),
        P(None, "xy", "gz", None),
        P("xy", None),
        P(("gz", "xy"), None),
        P(("gz", "xy")),
    )
    out_specs = (
        P("xy", "gz", None),
        P(None, "xy", "gz", None),
        P(None, "xy", "gz", None),
        P(None, "gz", "xy", None),
    )
    return jax.shard_map(
        on_device, mesh=mesh, in_specs=in_specs, out_specs=out_specs, check_vma=False
    )
```

```python
import functools
import math

import jax
import jax.numpy as jnp
import ml_dtypes
import numpy as np
from jax import lax
from jax.experimental import pallas as pl
from jax.experimental.pallas import tpu as pltpu
from jax.sharding import PartitionSpec as P

NX = 512
RADIUS = 16
IMPULSE = 2.0 / 16
TIME_STEP = 0.1
DIFFUSION = 0.05
NEAR = 8.0 * TIME_STEP / 12.0
FAR = TIME_STEP / 12.0
VMEM = 56 * 1024 * 1024
PACK_COST = MODES_COST = (1e6, 1e5)
STATE_COST = DENSITY_COST = (1e12, 4e9)
MAIN_COST = (1e12, 4e9)


def pair(ref, *index):
    return jnp.concatenate([ref[(*index[:-1], 0, index[-1])], ref[(*index[:-1], 1, index[-1])]], axis=0)


def unpair(ref, value, *index):
    ref[(*index[:-1], 0, index[-1])] = value[:4]
    ref[(*index[:-1], 1, index[-1])] = value[4:]


def slots(shape):
    sub = lax.broadcasted_iota(jnp.int32, shape, len(shape) - 2)
    return jnp.where(sub >= 4, sub - 4, sub)


def turn(value, shift, axis):
    return pltpu.roll(value, shift % value.shape[axis], axis)


def gather_planes(values, plane):
    slot = slots(values[0].shape)
    out = turn(values[-1], len(values) - 1 - plane, 0)
    for c in reversed(range(len(values) - 1)):
        out = jnp.where(slot == c, turn(values[c], c - plane, 0), out)
    return out


def collect(values, plane):
    sub = lax.broadcasted_iota(jnp.int32, values[0].shape, 0)
    out = turn(values[0], -plane, 0)
    for n in range(1, 8):
        j, h = n // 2, n % 2
        out = jnp.where(sub == n, turn(values[j], n - 4 * h - plane, 0), out)
    return out


def shared(rho, m, b):
    inv = 1.0 / rho
    return [x * inv for x in m], rho + 0.5 * (b[0] * b[0] + b[1] * b[1] + b[2] * b[2])


def fluxes(v, total, m, b, k):
    push = [m[i] * v[k] - b[i] * b[k] + (total if i == k else 0.0) for i in range(3)]
    turned = [None if i == k else v[k] * b[i] - b[k] * v[i] for i in range(3)]
    return push + turned


def first_kernel(cell_ref, count_ref, rho_a, mom_a, mag_a, pot_a, rho_z, mom_z, mag_z, pot_z, ev_ref, first_ref, last_ref):
    shape = (1, ev_ref.shape[2])
    lane = lax.broadcasted_iota(jnp.int32, shape, 1)
    row = jnp.zeros(shape, jnp.int32)
    for e in range(count_ref.shape[0]):
        for i in range(4):
            row = jnp.where(lane == 4 * e + i, cell_ref[e, i] if i < 3 else count_ref[e], row)

    def copy(d, _):
        ev_ref[d] = row
        return 0

    lax.fori_loop(0, ev_ref.shape[0], copy, 0)
    for ref, rho, mom, mag, pot, skip in (
        (first_ref, rho_a, mom_a, mag_a, pot_a, 0), (last_ref, rho_z, mom_z, mag_z, pot_z, pot_z.shape[0] - 2),
    ):
        for j in range(2):
            ref[0, j] = rho[0, j]
            for c in range(3):
                ref[1 + c, j] = mom[c, 0, j]
                ref[4 + c, j] = mag[c, 0, j]
            ref[7, j] = jnp.broadcast_to(pot[skip + j : skip + j + 1], ref.shape[2:])


def pack_kernel(rho_ref, mz_ref, after_ref, up_ref, down_ref):
    def body(g, _):
        rho = [pair(rho_ref, 4 * g + j) for j in range(4)]
        mz = [pair(mz_ref, 0, 4 * g + j) for j in range(4)]
        for i, (values, up, down) in enumerate(((rho, 3, 0), (mz, 3, 0), (mz, 2, 1))):
            up_ref[g, i] = collect(values, up)
            down_ref[g, i] = collect(values, down)
        return 0

    lax.fori_loop(0, rho_ref.shape[1] // 4, body, 0)


def write_messages(up_ref, down_ref, k, g, state):
    fluxes_by, bx = [], []
    for j in range(4):
        r = 4 * g + j
        u = state(j)
        near = [u[1], u[2], u[5], u[6]]
        up_ref[k, r] = gather_planes(near, 3)
        down_ref[k, r] = gather_planes(near, 0)
        f = fluxes(*shared(u[0], u[1:4], u[4:7]), u[1:4], u[4:7], 2)
        up_ref[k, 8 + r] = gather_planes(f[:4], 2)
        down_ref[k, 8 + r] = gather_planes(f[:4], 1)
        fluxes_by.append(f[4])
        bx.append(u[4])
    up_ref[k, 16 + g] = collect(fluxes_by, 2)
    down_ref[k, 16 + g] = collect(fluxes_by, 1)
    up_ref[k, 18 + g] = collect(bx, 3)
    down_ref[k, 18 + g] = collect(bx, 0)


def state_kernel(
    ev_ref, rho_ref, mom_ref, mag_ref, pot_ref, before_ref, after_ref, rho_l, mom_l, mag_l, pot_l,
    rho_h, mom_h, mag_h, pot_h, u_out, edge_out, sb_out, sa_out, up_ref, down_ref, s_ref, sb_ref, sa_ref, *,
    depth, count, per_device,
):
    half, ny = s_ref.shape[1] - 4, s_ref.shape[3]
    step_id = pl.program_id(0)

    @pl.when(step_id == 0)
    def _():
        deposit(ev_ref, s_ref, sb_ref, sa_ref, depth, per_device)
        pieces = lambda rho, mom, mag, pot, j: (
            [rho[0, j]] + [mom[c, 0, j] for c in range(3)] + [mag[c, 0, j] for c in range(3)]
            + [jnp.broadcast_to(pot, (4, ny))]
        )
        for j in range(2):
            low = pieces(rho_l, mom_l, mag_l, pot_l[0, 6 + j : 7 + j], j)
            high = pieces(rho_h, mom_h, mag_h, pot_h[0, j : j + 1], j)
            for f in range(8):
                left = jnp.concatenate([before_ref[f, j], low[f]], axis=0)
                right = jnp.concatenate([high[f], after_ref[f, j]], axis=0)
                edge_out[f, j] = left + s_ref[f, j] if f < 4 else left
                edge_out[f, 2 + j] = right + s_ref[f, half + 2 + j] if f < 4 else right

    start = step_id * 8

    def body(g, send):
        def state(j):
            r = 4 * g + j
            q = start + r + 2
            sb_out[r] = sb_ref[q]
            sa_out[r] = sa_ref[q]
            u = [pair(rho_ref, r) + s_ref[0, q]]
            u += [pair(mom_ref, c, r) + s_ref[1 + c, q] for c in range(3)]
            u += [pair(mag_ref, c, r) for c in range(3)]
            for f in range(7):
                u_out[f, r] = u[f]
            rows = [jnp.broadcast_to(pot_ref[h, pl.ds(r, 1), :], (4, ny)) for h in range(2)]
            u_out[7, r] = jnp.concatenate(rows, axis=0)
            return u

        if send:
            write_messages(up_ref, down_ref, 0, g, state)
        else:
            for j in range(4):
                state(j)
        return 0

    @pl.when(step_id < count)
    def _():
        lax.fori_loop(0, 2, lambda g, _: body(g, True), 0)

    @pl.when(step_id >= count)
    def _():
        lax.fori_loop(0, 2, lambda g, _: body(g, False), 0)


def deposit(ev_ref, s_ref, sb_ref, sa_ref, depth, per_device):
    half, ny = s_ref.shape[1] - 4, s_ref.shape[3]
    rows, events = 2 * half, ev_ref.shape[0] * per_device
    row_start, plane_start = lax.axis_index("xy") * rows, lax.axis_index("gz") * 4
    s_ref[...] = jnp.zeros_like(s_ref)
    sb_ref[...] = jnp.zeros_like(sb_ref)
    sa_ref[...] = jnp.zeros_like(sa_ref)

    shape = (4, 8, 128)
    slot = slots(shape)
    sub = lax.broadcasted_iota(jnp.int32, shape, 1)
    step = lax.broadcasted_iota(jnp.int32, shape, 0)
    lane = lax.broadcasted_iota(jnp.int32, shape, 2)

    def wrapped(distance, size):
        distance = jnp.where(distance >= size // 2, distance - size, distance)
        return jnp.where(distance < -(size // 2), distance + size, distance)

    def event(e, _):
        device, slot_id = (e, 0) if per_device == 1 else (lax.div(e, per_device), lax.rem(e, per_device))
        row, col, plane, count = (ev_ref[device, 0, 4 * slot_id + i] for i in range(4))
        rel = wrapped(row - row_start - half, NX)
        rel = rel + half

        @pl.when((count > 0) & (rel > -2 - RADIUS) & (rel < rows + 2 + RADIUS))
        def _():
            base = plane_start - plane
            dz = wrapped(slot + base, depth).astype(jnp.float32)
            dzb = wrapped(jnp.where(slot == 2, -2, -1) + base, depth).astype(jnp.float32)
            dza = wrapped(jnp.where(slot == 2, 5, 4) + base, depth).astype(jnp.float32)
            share = lambda d: jnp.where(slot == 0, 1.0, jnp.where(slot == 3, 0.0, IMPULSE * d))
            first = jnp.bitwise_and(col - RADIUS, ny - 1) // 128
            second = jnp.bitwise_and(col + RADIUS - 1, ny - 1) // 128

            def tile(t, _):
                index = jnp.where(t == 0, first, second)
                lanes = pl.ds(pl.multiple_of(index * 128, 128), 128)
                dy = wrapped(lane + index * 128 - col, ny).astype(jnp.float32)
                dy2 = dy * dy
                for h in range(2):
                    weight = jnp.where((sub >= 4) == (h == 1), count, 0).astype(jnp.float32)
                    low = jnp.clip(rel - RADIUS + 1 - h * half + 2, 0, half + 4) // 4
                    high = (jnp.clip(rel + RADIUS - 1 - h * half + 2, -1, half + 3) + 4) // 4

                    def chunk(n, _):
                        q = pl.ds(n * 4, 4)
                        dx = (step + (n * 4 - 2 + h * half - rel)).astype(jnp.float32)
                        flat = dx * dx + dy2
                        size = lambda d: jnp.maximum(1.0 - (flat + d * d) * (1.0 / (RADIUS * RADIUS)), 0.0) * weight
                        w = size(dz)
                        s_ref[0, q, :, lanes] += w
                        w = w * IMPULSE
                        s_ref[1, q, :, lanes] += w * dx
                        s_ref[2, q, :, lanes] += w * dy
                        s_ref[3, q, :, lanes] += w * dz
                        sb_ref[q, :, lanes] += size(dzb) * share(dzb)
                        sa_ref[q, :, lanes] += size(dza) * share(dza)
                        return 0

                    lax.fori_loop(low, high, chunk, 0)
                return 0

            lax.fori_loop(0, jnp.where(first == second, 1, 2), tile, 0)

        return 0

    lax.fori_loop(0, events, event, 0)


def ends(below, above, c):
    return jnp.where(slots(below.shape) == 3, turn(above, 3 - c, 0), turn(below, -c, 0))


def along_y(f, b):
    near, far = NEAR * f, FAR * f
    return turn(b + near, 1, 1) + turn(b - near, -1, 1) + turn(far, -2, 1) - turn(far, 2, 1)


def along_z(f, b, near_f, near_u, far_f):
    slot = slots(b.shape)
    first, last = slot == 0, slot == 3
    outer = DIFFUSION * near_u
    if f is None:
        return jnp.where(first, outer, turn(b, 1, 0)) + jnp.where(last, outer, turn(b, -1, 0))
    near = NEAR * f
    outer += jnp.where(first, NEAR, -NEAR) * near_f
    out = jnp.where(first, outer, turn(b + near, 1, 0)) + jnp.where(last, outer, turn(b - near, -1, 0))
    beyond = jnp.where(slot == 1, turn(near_f, 1, 0), jnp.where(slot == 2, turn(near_f, -1, 0), far_f))
    return out + FAR * (jnp.where(slot <= 1, turn(f, -2, 0), beyond) - jnp.where(slot >= 2, turn(f, 2, 0), beyond))


def fetch(u_hbm, edge_hbm, u_ref, sem, first):
    fields, total = u_ref.shape[:2]
    half = u_hbm.shape[1]
    low, high = max(first - 2, 0), min(first + total - 2, half)
    copies = [pltpu.make_async_copy(u_hbm.at[:fields, low:high], u_ref.at[:, low - first + 2 : high - first + 2], sem.at[0])]
    if first == 0:
        copies.append(pltpu.make_async_copy(edge_hbm.at[:fields, 0:2], u_ref.at[:, 0:2], sem.at[1]))
    if first + total - 4 == half:
        copies.append(pltpu.make_async_copy(edge_hbm.at[:fields, 2:4], u_ref.at[:, total - 2 : total], sem.at[2]))
    for copy in copies:
        copy.start()
    for copy in copies:
        copy.wait()


def density_kernel(
    u_hbm, edge_hbm, below_ref, above_ref, sb_ref, sa_ref, order_ref, high_ref, low_ref, out_ref, wave_ref,
    rho_out, mz_out, *rest, begin,
):
    *parcel, d_ref, u_ref, b_ref, sem = rest
    half = u_hbm.shape[1]
    field = None
    if parcel:
        field = pltpu.make_async_copy(u_hbm.at[4:7, begin : begin + b_ref.shape[1]], b_ref, sem.at[3])
        field.start()
    fetch(u_hbm, edge_hbm, u_ref, sem, 0)
    rows = 2 * half

    def row(p, g, j):
        rho, my, mz = u_ref[0, p + 2], u_ref[2, p + 2], u_ref[3, p + 2]
        sb, sa = sb_ref[p], sa_ref[p]
        halo = [last_plane(below_ref[g, i], above_ref[g, i], j) + ends(sb, sa, i) for i in range(3)]
        rho_out[p], mz_out[p] = halo[:2]
        b = DIFFUSION * rho
        new = rho * (1.0 - 6.0 * DIFFUSION)
        new += DIFFUSION * (u_ref[0, p + 1] + u_ref[0, p + 3])
        new += NEAR * (u_ref[1, p + 1] - u_ref[1, p + 3]) + FAR * (u_ref[1, p + 4] - u_ref[1, p])
        new += along_y(my, b)
        new += along_z(mz, b, halo[1], halo[0], halo[2])
        unpair(out_ref, new, p)
        d_ref[pl.ds(pl.multiple_of(p * 8, 8), 8), :] = new

    def body(g, _):
        for j in range(4):
            row(4 * g + j, g, j)
        return 0

    lax.fori_loop(0, half // 4, body, 0)
    d = d_ref[...]
    order = order_ref[...]
    dot = functools.partial(jnp.dot, preferred_element_type=jnp.float32)
    high = d.astype(jnp.bfloat16)
    low = (d - high.astype(jnp.float32)).astype(jnp.bfloat16)
    high = dot(order, high).astype(jnp.bfloat16)
    low = dot(order, low).astype(jnp.bfloat16)
    for part in range(2):
        c_high, c_low = high_ref[part], low_ref[part]
        wave = dot(high, c_high) + dot(high, c_low) + dot(low, c_high)
        peers, band = wave_ref.shape[0], wave_ref.shape[4]
        for j in range(peers):
            for z in range(4):
                wave_ref[j, part, z] = wave[z * rows : (z + 1) * rows, j * band : (j + 1) * band]
    if not parcel:
        return
    field.wait()
    first = begin

    row = 0
    for up_ref, down_ref in zip(parcel[: len(parcel) // 2], parcel[len(parcel) // 2 :]):

        def messages(n, _, up_ref=up_ref, down_ref=down_ref, row=row):
            r = n * 4 + row
            state = lambda j: [u_ref[f, first + r + j + 2] for f in range(4)] + [b_ref[c, r + j] for c in range(3)]
            write_messages(up_ref, down_ref, n // 2, n % 2, state)
            return 0

        lax.fori_loop(0, up_ref.shape[0] * 2, messages, 0)
        row += up_ref.shape[0] * 8


def last_plane(below, above, j):
    sub = lax.broadcasted_iota(jnp.int32, below.shape, 0)
    out = turn(below, -2 * j, 0)
    out = jnp.where(sub == 3, turn(above, 3 - 2 * j, 0), out)
    out = jnp.where(sub == 4, turn(below, 3 - 2 * j, 0), out)
    return jnp.where(sub == 7, turn(above, 6 - 2 * j, 0), out)


def main_kernel(u_hbm, edge_hbm, rho_ref, mz_ref, from_below, from_above, *rest, first, emit):
    if emit:
        *rest, later_ref, later_sem = rest
        *rest, up_ref, down_ref, u_ref, f_ref, sem = rest
        rest = [*rest, u_ref, f_ref, sem]
        later = pltpu.make_async_copy(u_hbm.at[:7, u_hbm.shape[1] - later_ref.shape[1] :], later_ref, later_sem)
    mom_ref, mag_ref, u_ref, f_ref, sem = rest[-5:]
    chunk, total, half = rho_ref.shape[0], u_ref.shape[1], u_hbm.shape[1]
    step_id = pl.program_id(0)
    start = step_id * chunk
    kept = (0, 1, 2, 4, 5)

    def copies(i):
        low = 0 if i == 0 else chunk * i + 4
        high = chunk * (i + 1) + 4
        a, b = max(first - 2 + low, 0), min(first - 2 + high, half)
        at = a - first + 2
        result = [(u_hbm.at[:, a:b], u_ref.at[:, at : at + b - a], sem.at[i])]
        if first - 2 + low < 0:
            result.append((edge_hbm.at[:, 0:2], u_ref.at[:, 0:2], sem.at[total // chunk]))
        if first - 2 + high > half:
            result.append((edge_hbm.at[:, 2:4], u_ref.at[:, total - 2 : total], sem.at[total // chunk + 1]))
        return [pltpu.make_async_copy(*c) for c in result]

    @pl.when(step_id == 0)
    def _():
        for i in range(total // chunk):
            for copy in copies(i):
                copy.start()
        if emit:
            later.start()

    for i in range(total // chunk):

        @pl.when(step_id == i)
        def _(i=i):
            for copy in copies(i):
                copy.wait()

    def fx(q, _):
        u = [u_ref[f, q] for f in range(7)]
        f = fluxes(*shared(u[0], u[1:4], u[4:7]), u[1:4], u[4:7], 0)
        for i, c in enumerate(kept):
            f_ref[i, q] = f[c]
        return 0

    lax.fori_loop(jnp.where(step_id == 0, 0, start + 4), start + chunk + 4, fx, 0)

    def row(r, g, j):
        q = start + r + 2
        u = [u_ref[f, q] for f in range(7)]
        v, pressure = shared(u[0], u[1:4], u[4:7])
        fy = fluxes(v, pressure, u[1:4], u[4:7], 1)
        fz = fluxes(v, pressure, u[1:4], u[4:7], 2)
        bn, an, bf, af = from_below[0, r], from_above[0, r], from_below[0, 8 + r], from_above[0, 8 + r]
        hm = [ends(bn, an, 0), ends(bn, an, 1), mz_ref[r]]
        hb = [last_plane(from_below[0, 18 + g], from_above[0, 18 + g], j), ends(bn, an, 2), ends(bn, an, 3)]
        fh = fluxes(*shared(rho_ref[r], hm, hb), hm, hb, 2)
        halo = hm + hb
        far = [ends(bf, af, c) for c in range(4)] + [last_plane(from_below[0, 16 + g], from_above[0, 16 + g], j), None]
        for c in range(6):
            field = u[c + 1]
            new = field * (1.0 - 6.0 * DIFFUSION)
            new += DIFFUSION * (u_ref[c + 1, q - 1] + u_ref[c + 1, q + 1])
            if c in kept:
                i = kept.index(c)
                new += NEAR * (f_ref[i, q - 1] - f_ref[i, q + 1]) + FAR * (f_ref[i, q + 2] - f_ref[i, q - 2])
            b = DIFFUSION * field
            if fy[c] is None:
                new += turn(b, 1, 1) + turn(b, -1, 1)
            else:
                new += along_y(fy[c], b)
            new += along_z(fz[c], b, fh[c], halo[c], far[c])
            if c == 0:
                slope = NEAR * (u_ref[7, q - 1] - u_ref[7, q + 1]) + FAR * (u_ref[7, q + 2] - u_ref[7, q - 2])
                new += u[0] * slope
            if c == 1:
                potential = u_ref[7, q]
                slope = NEAR * (turn(potential, 1, 1) - turn(potential, -1, 1))
                new += u[0] * (slope + FAR * (turn(potential, -2, 1) - turn(potential, 2, 1)))
            if c < 3:
                unpair(mom_ref, new, c, r)
            else:
                unpair(mag_ref, new, c - 3, r)

    def body(g, _):
        for j in range(4):
            row(4 * g + j, g, j)
        return 0

    lax.fori_loop(0, chunk // 4, body, 0)

    if emit:

        @pl.when(step_id == pl.num_programs(0) - 1)
        def _():
            later.wait()

            def messages(n, _):
                state = lambda j: [later_ref[f, n * 4 + j] for f in range(7)]
                write_messages(up_ref, down_ref, n // 2, n % 2, state)
                return 0

            lax.fori_loop(0, later_ref.shape[1] // 4, messages, 0)


def modes_kernel(w_ref, ch_ref, cl_ref, sh_ref, sl_ref, out_ref, x_ref, *, turned):
    dot = functools.partial(jnp.dot, preferred_element_type=jnp.float32)
    planes, band, nx = out_ref.shape[1:]

    def split(part):
        if turned:
            x = jnp.concatenate([w_ref[part, z] for z in range(planes)], axis=0)
        else:
            width = w_ref.shape[3]
            for s in range(w_ref.shape[0]):
                for z in range(planes):
                    x_ref[z * band : (z + 1) * band, s * width : (s + 1) * width] = w_ref[s, part, z].T
            x = x_ref[...]
        high = x.astype(jnp.bfloat16)
        return high, (x - high.astype(jnp.float32)).astype(jnp.bfloat16)

    re, im = split(0), split(1)
    times = lambda x, h, l: dot(x[0], h[...]) + dot(x[0], l[...]) + dot(x[1], h[...])
    scale = 1.0 / math.sqrt(NX * nx)
    shape = (band, nx)
    ky = lax.broadcasted_iota(jnp.int32, shape, 0) + lax.axis_index("xy") * band
    kx = lax.broadcasted_iota(jnp.int32, shape, 1)
    keep = jnp.where((ky == 0) & (kx == 0), 0.0, scale)
    out_re = times(re, ch_ref, cl_ref) + times(im, sh_ref, sl_ref)
    out_im = times(im, ch_ref, cl_ref) - times(re, sh_ref, sl_ref)
    for z in range(planes):
        out_ref[0, z] = out_re[z * band : (z + 1) * band] * keep
        out_ref[1, z] = out_im[z * band : (z + 1) * band] * keep


def cost(flops, bytes_accessed):
    return pl.CostEstimate(flops=int(flops), bytes_accessed=int(bytes_accessed), transcendentals=0)


def tables(size):
    angle = (np.outer(np.arange(size), np.arange(size)) % size) * (2.0 * np.pi / size)
    result = []
    for table in (np.cos(angle), np.sin(angle)):
        high = table.astype(np.float32).astype(ml_dtypes.bfloat16)
        low = (table - high.astype(np.float64)).astype(np.float32).astype(ml_dtypes.bfloat16)
        result += [high, low]
    return result


def row_order(half):
    matrix = np.zeros((8 * half, 8 * half), np.float32)
    for z in range(4):
        for h in range(2):
            for p in range(half):
                matrix[(z * 2 + h) * half + p, p * 8 + h * 4 + z] = 1.0
    return matrix.astype(ml_dtypes.bfloat16)


def shift(block, axis, step):
    n = lax.axis_size(axis)
    return lax.ppermute(block, axis, [(i, (i + step) % n) for i in range(n)])


def on_device(density, momentum, magnetic, arm_potential, sn_cells, sn_counts):
    rows, planes, ny = density.shape
    half = rows // 2
    layers, across = lax.axis_size("gz"), lax.axis_size("xy")
    devices = layers * across
    tile_row, tile_plane = lax.axis_index("xy"), lax.axis_index("gz")
    field = rows * planes * ny
    f32 = jnp.float32
    shape = jax.ShapeDtypeStruct
    whole = pl.BlockSpec(memory_space=pltpu.VMEM)
    smem = pl.BlockSpec(memory_space=pltpu.SMEM)
    params = pltpu.CompilerParams(vmem_limit_bytes=VMEM)
    message = shape((2, half, planes, ny), f32)
    tile = shape((half, 8, ny), f32)
    steps = half // 8
    counts = (steps - steps // 4 * 2, steps // 4, steps // 4) if steps >= 4 else (steps,)

    slots_here = sn_cells.shape[0]
    rho = density.reshape(2, half, planes, ny)
    mom = momentum.reshape(3, 2, half, planes, ny)
    mag = magnetic.reshape(3, 2, half, planes, ny)

    pot = arm_potential.reshape(2, half, ny)
    edges = shape((8, 2, planes, ny), f32)
    mine = shape((devices, 1, -(-4 * slots_here // 128) * 128), jnp.int32)
    full = lambda s: pl.BlockSpec(s, lambda i: (0,) * len(s))
    mine, first_rows, last_rows = pl.pallas_call(
        first_kernel,
        grid=(1,),
        in_specs=[smem, smem] + [
            spec
            for h, k in ((0, 0), (1, half // 2 - 1))
            for spec in (
                pl.BlockSpec((1, 2, planes, ny), lambda i, h=h, k=k: (h, k, 0, 0)),
                pl.BlockSpec((3, 1, 2, planes, ny), lambda i, h=h, k=k: (0, h, k, 0, 0)),
                pl.BlockSpec((3, 1, 2, planes, ny), lambda i, h=h, k=k: (0, h, k, 0, 0)),
                pl.BlockSpec((8, ny), lambda i, h=h: (h * (rows // 8 - 1), 0)),
            )
        ],
        out_specs=[full(mine.shape)] + [full(edges.shape)] * 2,
        out_shape=[mine] + [edges] * 2,
        compiler_params=params,
        cost_estimate=cost(*PACK_COST),
        name="first",
    )(sn_cells, sn_counts, *[rho, mom, mag, arm_potential] * 2)
    events = lax.all_to_all(mine, ("gz", "xy"), split_axis=0, concat_axis=0, tiled=True)
    before, after = shift(last_rows, "xy", 1), shift(first_rows, "xy", -1)

    some = math.gcd(half, 16)
    up, down = pl.pallas_call(
        pack_kernel,
        grid=(half // some,),
        in_specs=[pl.BlockSpec((2, some, planes, ny), lambda i: (0, i, 0, 0))] + [
            pl.BlockSpec((1, 2, some, planes, ny), lambda i, f=f: (f, 0, i, 0, 0)) for f in (2,)
        ] + [pl.BlockSpec(memory_space=pl.ANY)],
        out_specs=[pl.BlockSpec((some // 4, 3, 8, ny), lambda i: (i, 0, 0, 0))] * 2,
        out_shape=[shape((half // 4, 3, 8, ny), f32)] * 2,
        compiler_params=params,
        cost_estimate=cost(*PACK_COST),
        name="pack",
    )(rho, mom, mine)
    below_a, above_a = shift(up, "gz", 1), shift(down, "gz", -1)

    parcels = [shape((n, 20, 8, ny), f32) for n in counts]
    side = pltpu.VMEM((half + 4, 8, ny), f32)
    begins = [sum(counts[:i]) for i in range(len(counts))]
    parcel = pl.BlockSpec((1, 20, 8, ny), lambda i: (jnp.minimum(i, counts[0] - 1), 0, 0, 0))
    eight = pl.BlockSpec((8, 8, ny), lambda i: (i, 0, 0))
    middle = [
        spec
        for h, k in ((0, steps - 1), (1, 0))
        for spec in (
            pl.BlockSpec((1, 2, planes, ny), lambda i, h=h, k=k: (h, k * 4 + 3 * (1 - h), 0, 0)),
            pl.BlockSpec((3, 1, 2, planes, ny), lambda i, h=h, k=k: (0, h, k * 4 + 3 * (1 - h), 0, 0)),
            pl.BlockSpec((3, 1, 2, planes, ny), lambda i, h=h, k=k: (0, h, k * 4 + 3 * (1 - h), 0, 0)),
            pl.BlockSpec((1, 8, ny), lambda i, h=h, k=k: (h, k, 0)),
        )
    ]
    rows_of = lambda n: pl.BlockSpec((n, 2, 8, planes, ny), lambda i: (0, 0, i, 0, 0))
    state, edge, sb, sa, up_0, down_0 = pl.pallas_call(
        functools.partial(state_kernel, depth=planes * layers, count=counts[0], per_device=slots_here),
        grid=(steps,),
        in_specs=[
            smem, pl.BlockSpec((2, 8, planes, ny), lambda i: (0, i, 0, 0)), rows_of(3), rows_of(3),
            pl.BlockSpec((2, 8, ny), lambda i: (0, i, 0)), full(edges.shape), full(edges.shape),
        ] + middle,
        out_specs=[pl.BlockSpec((8, 8, 8, ny), lambda i: (0, i, 0, 0)), full((8, 4, 8, ny)), eight, eight, parcel, parcel],
        out_shape=[shape((8, half, 8, ny), f32), shape((8, 4, 8, ny), f32), tile, tile, parcels[0], parcels[0]],
        scratch_shapes=[pltpu.VMEM((4, half + 4, 8, ny), f32), side, side],
        compiler_params=params,
        cost_estimate=cost(*STATE_COST),
        name="state",
    )(events, rho, mom, mag, pot, before, after, *[rho, mom, mag, pot] * 2)
    parcels_below, parcels_above = [shift(up_0, "gz", 1)], [shift(down_0, "gz", -1)]

    cos_high, cos_low, sin_high, sin_low = tables(ny)
    band = ny // across
    turned = band % 128 != 0 or rows % 128 != 0
    hbm = pl.BlockSpec(memory_space=pl.ANY)
    more = parcels[1:2] * 2
    new_density, wave, rho_halo, mz_halo, *messages = pl.pallas_call(
        functools.partial(density_kernel, begin=counts[0] * 8),
        in_specs=[hbm, hbm] + [whole] * 7,
        out_specs=[whole] * (4 + len(more)),
        out_shape=[message, shape((across, 2, planes, rows, band), f32), tile, tile, *more],
        scratch_shapes=[
            pltpu.VMEM((8 * half, ny), f32), pltpu.VMEM((4, half + 4, 8, ny), f32),
            pltpu.VMEM((3, counts[min(1, len(counts) - 1)] * 8, 8, ny), f32), pltpu.SemaphoreType.DMA((4,)),
        ],
        compiler_params=params,
        cost_estimate=cost(*DENSITY_COST),
        name="density",
    )(
        state, edge, below_a, above_a, sb, sa, row_order(half),
        np.stack([cos_high, -sin_high]), np.stack([cos_low, -sin_low]),
    )

    for up, down in zip(messages[: len(messages) // 2], messages[len(messages) // 2 :]):
        parcels_below.append(shift(up, "gz", 1))
        parcels_above.append(shift(down, "gz", -1))
    portion = lax.all_to_all(wave, "xy", split_axis=0, concat_axis=0, tiled=True)
    if turned:
        portion = portion.transpose(1, 2, 4, 0, 3).reshape(2, planes, band, NX)
    modes = pl.pallas_call(
        functools.partial(modes_kernel, turned=turned),
        in_specs=[whole] * 5,
        out_specs=whole,
        out_shape=shape((2, planes, band, NX), f32),
        scratch_shapes=[pltpu.VMEM((planes * band, NX), f32)],
        compiler_params=params,
        cost_estimate=cost(*MODES_COST),
        name="modes",
    )(portion, *tables(NX))
    results = [shape((3, 2, half, planes, ny), f32)] * 2
    new = []
    for i, n in enumerate(counts):
        emit = i == 0 and len(counts) == 3
        sent = parcels[2:] * 2 if emit else []
        if i == 2:
            parcels_below.append(shift(messages[0], "gz", 1))
            parcels_above.append(shift(messages[1], "gz", -1))
        chunk, first = 8, begins[i] * 8
        here = pl.BlockSpec((chunk, 8, ny), lambda k, o=begins[i]: (o + k, 0, 0))
        parcel = pl.BlockSpec((1, 20, 8, ny), lambda k: (k, 0, 0, 0))
        three = pl.BlockSpec((3, 2, chunk, planes, ny), lambda k, o=begins[i]: (0, 0, o + k, 0, 0))
        below, above = parcels_below[i], parcels_above[i]
        extra = [*new] + [modes] * (i > 0 and i == len(counts) - 1)
        *new, = pl.pallas_call(
            functools.partial(main_kernel, first=first, emit=emit),
            grid=(n,),
            in_specs=[hbm, hbm] + [here] * 2 + [parcel] * 2 + [hbm] * len(extra),
            out_specs=[three, three] + [full(p.shape) for p in sent],
            out_shape=results + sent,
            scratch_shapes=[
                pltpu.VMEM((8, n * 8 + 4, 8, ny), f32), pltpu.VMEM((5, n * 8 + 4, 8, ny), f32), pltpu.SemaphoreType.DMA((n + 2,)),
            ] + ([pltpu.VMEM((7, counts[2] * 8, 8, ny), f32), pltpu.SemaphoreType.DMA] if emit else []),
            input_output_aliases={6: 0, 7: 1} if new else {},
            compiler_params=pltpu.CompilerParams(vmem_limit_bytes=62 * 1024 * 1024),
            cost_estimate=cost(*MAIN_COST),
            name=f"main{i}",
        )(state, edge, rho_halo, mz_halo, below, above, *extra)
        if emit:
            new, messages = new[:2], new[2:]
    new_mom, new_mag = new

    return (
        new_density.reshape(rows, planes, ny),
        new_mom.reshape(3, rows, planes, ny),
        new_mag.reshape(3, rows, planes, ny),
        modes,
    )


def solution(mesh):
    in_specs = (
        P("xy", "gz", None),
        P(None, "xy", "gz", None),
        P(None, "xy", "gz", None),
        P("xy", None),
        P(("gz", "xy"), None),
        P(("gz", "xy")),
    )
    out_specs = (
        P("xy", "gz", None),
        P(None, "xy", "gz", None),
        P(None, "xy", "gz", None),
        P(None, "gz", "xy", None),
    )
    return jax.shard_map(
        on_device, mesh=mesh, in_specs=in_specs, out_specs=out_specs, check_vma=False
    )
```

```python
import functools
import math

import jax
import jax.numpy as jnp
import ml_dtypes
import numpy as np
from jax import lax
from jax.experimental import pallas as pl
from jax.experimental.pallas import tpu as pltpu
from jax.sharding import PartitionSpec as P

NX = 512
RADIUS = 16
IMPULSE = 2.0 / 16
TIME_STEP = 0.1
DIFFUSION = 0.05
NEAR = 8.0 * TIME_STEP / 12.0
FAR = TIME_STEP / 12.0
VMEM = 56 * 1024 * 1024
PACK_COST = MODES_COST = (1e6, 1e5)
STATE_COST = DENSITY_COST = (1e12, 4e9)
MAIN_COST = (1e12, 4e9)


def pair(ref, *index):
    return jnp.concatenate([ref[(*index[:-1], 0, index[-1])], ref[(*index[:-1], 1, index[-1])]], axis=0)


def unpair(ref, value, *index):
    ref[(*index[:-1], 0, index[-1])] = value[:4]
    ref[(*index[:-1], 1, index[-1])] = value[4:]


def slots(shape):
    sub = lax.broadcasted_iota(jnp.int32, shape, len(shape) - 2)
    return jnp.where(sub >= 4, sub - 4, sub)


def turn(value, shift, axis):
    return pltpu.roll(value, shift % value.shape[axis], axis)


def gather_planes(values, plane):
    slot = slots(values[0].shape)
    out = turn(values[-1], len(values) - 1 - plane, 0)
    for c in reversed(range(len(values) - 1)):
        out = jnp.where(slot == c, turn(values[c], c - plane, 0), out)
    return out


def collect(values, plane):
    sub = lax.broadcasted_iota(jnp.int32, values[0].shape, 0)
    out = turn(values[0], -plane, 0)
    for n in range(1, 8):
        j, h = n // 2, n % 2
        out = jnp.where(sub == n, turn(values[j], n - 4 * h - plane, 0), out)
    return out


def shared(rho, m, b):
    inv = 1.0 / rho
    return [x * inv for x in m], rho + 0.5 * (b[0] * b[0] + b[1] * b[1] + b[2] * b[2])


def fluxes(v, total, m, b, k):
    push = [m[i] * v[k] - b[i] * b[k] + (total if i == k else 0.0) for i in range(3)]
    turned = [None if i == k else v[k] * b[i] - b[k] * v[i] for i in range(3)]
    return push + turned


def first_kernel(cell_ref, count_ref, rho_a, mom_a, mag_a, pot_a, rho_z, mom_z, mag_z, pot_z, ev_ref, first_ref, last_ref):
    shape = (1, ev_ref.shape[2])
    lane = lax.broadcasted_iota(jnp.int32, shape, 1)
    row = jnp.zeros(shape, jnp.int32)
    for e in range(count_ref.shape[0]):
        for i in range(4):
            row = jnp.where(lane == 4 * e + i, cell_ref[e, i] if i < 3 else count_ref[e], row)

    def copy(d, _):
        ev_ref[d] = row
        return 0

    lax.fori_loop(0, ev_ref.shape[0], copy, 0)
    for ref, rho, mom, mag, pot, skip in (
        (first_ref, rho_a, mom_a, mag_a, pot_a, 0), (last_ref, rho_z, mom_z, mag_z, pot_z, pot_z.shape[0] - 2),
    ):
        for j in range(2):
            ref[0, j] = rho[0, j]
            for c in range(3):
                ref[1 + c, j] = mom[c, 0, j]
                ref[4 + c, j] = mag[c, 0, j]
            ref[7, j] = jnp.broadcast_to(pot[skip + j : skip + j + 1], ref.shape[2:])


def pack_kernel(rho_ref, mz_ref, after_ref, up_ref, down_ref):
    def body(g, _):
        rho = [pair(rho_ref, 4 * g + j) for j in range(4)]
        mz = [pair(mz_ref, 0, 4 * g + j) for j in range(4)]
        for i, (values, up, down) in enumerate(((rho, 3, 0), (mz, 3, 0), (mz, 2, 1))):
            up_ref[g, i] = collect(values, up)
            down_ref[g, i] = collect(values, down)
        return 0

    lax.fori_loop(0, rho_ref.shape[1] // 4, body, 0)


def write_messages(up_ref, down_ref, k, g, state):
    fluxes_by, bx = [], []
    for j in range(4):
        r = 4 * g + j
        u = state(j)
        near = [u[1], u[2], u[5], u[6]]
        up_ref[k, r] = gather_planes(near, 3)
        down_ref[k, r] = gather_planes(near, 0)
        f = fluxes(*shared(u[0], u[1:4], u[4:7]), u[1:4], u[4:7], 2)
        up_ref[k, 8 + r] = gather_planes(f[:4], 2)
        down_ref[k, 8 + r] = gather_planes(f[:4], 1)
        fluxes_by.append(f[4])
        bx.append(u[4])
    up_ref[k, 16 + g] = collect(fluxes_by, 2)
    down_ref[k, 16 + g] = collect(fluxes_by, 1)
    up_ref[k, 18 + g] = collect(bx, 3)
    down_ref[k, 18 + g] = collect(bx, 0)


def state_kernel(
    ev_ref, rho_ref, mom_ref, mag_ref, pot_ref, before_ref, after_ref, rho_l, mom_l, mag_l, pot_l,
    rho_h, mom_h, mag_h, pot_h, u_out, edge_out, sb_out, sa_out, up_ref, down_ref, s_ref, sb_ref, sa_ref, *,
    depth, count, per_device, steps,
):
    half, ny = 8 * steps, s_ref.shape[3]
    step_id = pl.program_id(0)

    @pl.when(step_id == 0)
    def _():
        deposit(ev_ref, s_ref, sb_ref, sa_ref, depth, per_device, half)
        pieces = lambda rho, mom, mag, pot, j: (
            [rho[0, j]] + [mom[c, 0, j] for c in range(3)] + [mag[c, 0, j] for c in range(3)]
            + [jnp.broadcast_to(pot, (4, ny))]
        )
        for j in range(2):
            low = pieces(rho_l, mom_l, mag_l, pot_l[0, 6 + j : 7 + j], j)
            high = pieces(rho_h, mom_h, mag_h, pot_h[0, j : j + 1], j)
            for f in range(8):
                left = jnp.concatenate([before_ref[f, j], low[f]], axis=0)
                right = jnp.concatenate([high[f], after_ref[f, j]], axis=0)
                edge_out[f, j] = left + s_ref[f, j] if f < 4 else left
                edge_out[f, 2 + j] = right + s_ref[f, half + 2 + j] if f < 4 else right

    start = step_id * 8

    def body(g, send):
        def state(j):
            r = 4 * g + j
            q = start + r + 2
            sb_out[r] = sb_ref[q]
            sa_out[r] = sa_ref[q]
            u = [pair(rho_ref, r) + s_ref[0, q]]
            u += [pair(mom_ref, c, r) + s_ref[1 + c, q] for c in range(3)]
            u += [pair(mag_ref, c, r) for c in range(3)]
            for f in range(7):
                u_out[f, r] = u[f]
            rows = [jnp.broadcast_to(pot_ref[h, pl.ds(r, 1), :], (4, ny)) for h in range(2)]
            u_out[7, r] = jnp.concatenate(rows, axis=0)
            return u

        if send:
            write_messages(up_ref, down_ref, 0, g, state)
        else:
            for j in range(4):
                state(j)
        return 0

    @pl.when(step_id < count)
    def _():
        lax.fori_loop(0, 2, lambda g, _: body(g, True), 0)

    @pl.when(step_id >= count)
    def _():
        lax.fori_loop(0, 2, lambda g, _: body(g, False), 0)


def deposit(ev_ref, s_ref, sb_ref, sa_ref, depth, per_device, half):
    ny = s_ref.shape[3]
    rows, events = 2 * half, ev_ref.shape[0] * per_device
    row_start, plane_start = lax.axis_index("xy") * rows, lax.axis_index("gz") * 4
    s_ref[...] = jnp.zeros_like(s_ref)
    sb_ref[...] = jnp.zeros_like(sb_ref)
    sa_ref[...] = jnp.zeros_like(sa_ref)

    shape = (8, 8, 128)
    slot = slots(shape)
    sub = lax.broadcasted_iota(jnp.int32, shape, 1)
    step = lax.broadcasted_iota(jnp.int32, shape, 0)
    lane = lax.broadcasted_iota(jnp.int32, shape, 2)

    def wrapped(distance, size):
        distance = jnp.where(distance >= size // 2, distance - size, distance)
        return jnp.where(distance < -(size // 2), distance + size, distance)

    def event(e, _):
        device, slot_id = (e, 0) if per_device == 1 else (lax.div(e, per_device), lax.rem(e, per_device))
        row, col, plane, count = (ev_ref[device, 0, 4 * slot_id + i] for i in range(4))
        rel = wrapped(row - row_start - half, NX)
        rel = rel + half

        @pl.when((count > 0) & (rel > -2 - RADIUS) & (rel < rows + 2 + RADIUS))
        def _():
            base = plane_start - plane
            dz = wrapped(slot + base, depth).astype(jnp.float32)
            dzb = wrapped(jnp.where(slot == 2, -2, -1) + base, depth).astype(jnp.float32)
            dza = wrapped(jnp.where(slot == 2, 5, 4) + base, depth).astype(jnp.float32)
            share = lambda d: jnp.where(slot == 0, 1.0, jnp.where(slot == 3, 0.0, IMPULSE * d))
            first = jnp.bitwise_and(col - RADIUS, ny - 1) // 128
            second = jnp.bitwise_and(col + RADIUS - 1, ny - 1) // 128

            def tile(t, _):
                index = jnp.where(t == 0, first, second)
                lanes = pl.ds(pl.multiple_of(index * 128, 128), 128)
                dy = wrapped(lane + index * 128 - col, ny).astype(jnp.float32)
                dy2 = dy * dy
                for h in range(2):
                    weight = jnp.where((sub >= 4) == (h == 1), count, 0).astype(jnp.float32)
                    low = jnp.clip(rel - RADIUS + 1 - h * half + 2, 0, s_ref.shape[1]) // 8
                    high = (jnp.clip(rel + RADIUS - 1 - h * half + 2, -1, half + 3) + 8) // 8

                    def chunk(n, _):
                        q = pl.ds(n * 8, 8)
                        dx = (step + (n * 8 - 2 + h * half - rel)).astype(jnp.float32)
                        flat = dx * dx + dy2
                        size = lambda d: jnp.maximum(1.0 - (flat + d * d) * (1.0 / (RADIUS * RADIUS)), 0.0) * weight
                        w = size(dz)
                        s_ref[0, q, :, lanes] += w
                        w = w * IMPULSE
                        s_ref[1, q, :, lanes] += w * dx
                        s_ref[2, q, :, lanes] += w * dy
                        s_ref[3, q, :, lanes] += w * dz
                        sb_ref[q, :, lanes] += size(dzb) * share(dzb)
                        sa_ref[q, :, lanes] += size(dza) * share(dza)
                        return 0

                    lax.fori_loop(low, high, chunk, 0)
                return 0

            lax.fori_loop(0, jnp.where(first == second, 1, 2), tile, 0)

        return 0

    lax.fori_loop(0, events, event, 0)


def ends(below, above, c):
    return jnp.where(slots(below.shape) == 3, turn(above, 3 - c, 0), turn(below, -c, 0))


def along_y(f, b):
    near, far = NEAR * f, FAR * f
    return turn(b + near, 1, 1) + turn(b - near, -1, 1) + turn(far, -2, 1) - turn(far, 2, 1)


def along_z(f, b, near_f, near_u, far_f):
    slot = slots(b.shape)
    first, last = slot == 0, slot == 3
    outer = DIFFUSION * near_u
    if f is None:
        return jnp.where(first, outer, turn(b, 1, 0)) + jnp.where(last, outer, turn(b, -1, 0))
    near = NEAR * f
    outer += jnp.where(first, NEAR, -NEAR) * near_f
    out = jnp.where(first, outer, turn(b + near, 1, 0)) + jnp.where(last, outer, turn(b - near, -1, 0))
    beyond = jnp.where(slot == 1, turn(near_f, 1, 0), jnp.where(slot == 2, turn(near_f, -1, 0), far_f))
    return out + FAR * (jnp.where(slot <= 1, turn(f, -2, 0), beyond) - jnp.where(slot >= 2, turn(f, 2, 0), beyond))


def fetch(u_hbm, edge_hbm, u_ref, sem, first):
    fields, total = u_ref.shape[:2]
    half = u_hbm.shape[1]
    low, high = max(first - 2, 0), min(first + total - 2, half)
    copies = [pltpu.make_async_copy(u_hbm.at[:fields, low:high], u_ref.at[:, low - first + 2 : high - first + 2], sem.at[0])]
    if first == 0:
        copies.append(pltpu.make_async_copy(edge_hbm.at[:fields, 0:2], u_ref.at[:, 0:2], sem.at[1]))
    if first + total - 4 == half:
        copies.append(pltpu.make_async_copy(edge_hbm.at[:fields, 2:4], u_ref.at[:, total - 2 : total], sem.at[2]))
    for copy in copies:
        copy.start()
    for copy in copies:
        copy.wait()


def density_kernel(
    u_hbm, edge_hbm, below_ref, above_ref, sb_ref, sa_ref, order_ref, high_ref, low_ref, out_ref, wave_ref,
    rho_out, mz_out, *rest,
):
    *parcel, d_ref, u_ref, b_ref, sem = rest
    half = u_hbm.shape[1]
    field = None
    if parcel:
        field = pltpu.make_async_copy(u_hbm.at[4:7, half - b_ref.shape[1] :], b_ref, sem.at[3])
        field.start()
    fetch(u_hbm, edge_hbm, u_ref, sem, 0)
    rows = 2 * half

    def row(p, g, j):
        rho, my, mz = u_ref[0, p + 2], u_ref[2, p + 2], u_ref[3, p + 2]
        sb, sa = sb_ref[p], sa_ref[p]
        halo = [last_plane(below_ref[g, i], above_ref[g, i], j) + ends(sb, sa, i) for i in range(3)]
        rho_out[p], mz_out[p] = halo[:2]
        b = DIFFUSION * rho
        new = rho * (1.0 - 6.0 * DIFFUSION)
        new += DIFFUSION * (u_ref[0, p + 1] + u_ref[0, p + 3])
        new += NEAR * (u_ref[1, p + 1] - u_ref[1, p + 3]) + FAR * (u_ref[1, p + 4] - u_ref[1, p])
        new += along_y(my, b)
        new += along_z(mz, b, halo[1], halo[0], halo[2])
        unpair(out_ref, new, p)
        d_ref[pl.ds(pl.multiple_of(p * 8, 8), 8), :] = new

    def body(g, _):
        for j in range(4):
            row(4 * g + j, g, j)
        return 0

    lax.fori_loop(0, half // 4, body, 0)
    d = d_ref[...]
    order = order_ref[...]
    dot = functools.partial(jnp.dot, preferred_element_type=jnp.float32)
    high = d.astype(jnp.bfloat16)
    low = (d - high.astype(jnp.float32)).astype(jnp.bfloat16)
    high = dot(order, high).astype(jnp.bfloat16)
    low = dot(order, low).astype(jnp.bfloat16)
    for part in range(2):
        c_high, c_low = high_ref[part], low_ref[part]
        wave = dot(high, c_high) + dot(high, c_low) + dot(low, c_high)
        peers, band = wave_ref.shape[0], wave_ref.shape[4]
        for j in range(peers):
            for z in range(4):
                wave_ref[j, part, z] = wave[z * rows : (z + 1) * rows, j * band : (j + 1) * band]
    if not parcel:
        return
    field.wait()
    first = half - b_ref.shape[1]

    def messages(n, _):
        r = n * 4
        state = lambda j: [u_ref[f, first + r + j + 2] for f in range(4)] + [b_ref[c, r + j] for c in range(3)]
        write_messages(*parcel, n // 2, n % 2, state)
        return 0

    lax.fori_loop(0, b_ref.shape[1] // 4, messages, 0)


def last_plane(below, above, j):
    sub = lax.broadcasted_iota(jnp.int32, below.shape, 0)
    out = turn(below, -2 * j, 0)
    out = jnp.where(sub == 3, turn(above, 3 - 2 * j, 0), out)
    out = jnp.where(sub == 4, turn(below, 3 - 2 * j, 0), out)
    return jnp.where(sub == 7, turn(above, 6 - 2 * j, 0), out)


def main_kernel(u_hbm, edge_hbm, rho_ref, mz_ref, from_below, from_above, *rest, first):
    mom_ref, mag_ref, u_ref, f_ref, sem = rest[-5:]
    chunk, total, half = rho_ref.shape[0], u_ref.shape[1], u_hbm.shape[1]
    step_id = pl.program_id(0)
    start = step_id * chunk
    kept = (0, 1, 2, 4, 5)

    def copies(i):
        low = 0 if i == 0 else chunk * i + 4
        high = chunk * (i + 1) + 4
        a, b = max(first - 2 + low, 0), min(first - 2 + high, half)
        at = a - first + 2
        result = [(u_hbm.at[:, a:b], u_ref.at[:, at : at + b - a], sem.at[i])]
        if first - 2 + low < 0:
            result.append((edge_hbm.at[:, 0:2], u_ref.at[:, 0:2], sem.at[total // chunk]))
        if first - 2 + high > half:
            result.append((edge_hbm.at[:, 2:4], u_ref.at[:, total - 2 : total], sem.at[total // chunk + 1]))
        return [pltpu.make_async_copy(*c) for c in result]

    @pl.when(step_id == 0)
    def _():
        for i in range(total // chunk):
            for copy in copies(i):
                copy.start()

    for i in range(total // chunk):

        @pl.when(step_id == i)
        def _(i=i):
            for copy in copies(i):
                copy.wait()

    def fx(q, _):
        u = [u_ref[f, q] for f in range(7)]
        f = fluxes(*shared(u[0], u[1:4], u[4:7]), u[1:4], u[4:7], 0)
        for i, c in enumerate(kept):
            f_ref[i, q] = f[c]
        return 0

    lax.fori_loop(jnp.where(step_id == 0, 0, start + 4), start + chunk + 4, fx, 0)

    def row(r, g, j):
        q = start + r + 2
        u = [u_ref[f, q] for f in range(7)]
        v, pressure = shared(u[0], u[1:4], u[4:7])
        fy = fluxes(v, pressure, u[1:4], u[4:7], 1)
        fz = fluxes(v, pressure, u[1:4], u[4:7], 2)
        bn, an, bf, af = from_below[0, r], from_above[0, r], from_below[0, 8 + r], from_above[0, 8 + r]
        hm = [ends(bn, an, 0), ends(bn, an, 1), mz_ref[r]]
        hb = [last_plane(from_below[0, 18 + g], from_above[0, 18 + g], j), ends(bn, an, 2), ends(bn, an, 3)]
        fh = fluxes(*shared(rho_ref[r], hm, hb), hm, hb, 2)
        halo = hm + hb
        far = [ends(bf, af, c) for c in range(4)] + [last_plane(from_below[0, 16 + g], from_above[0, 16 + g], j), None]
        for c in range(6):
            field = u[c + 1]
            new = field * (1.0 - 6.0 * DIFFUSION)
            new += DIFFUSION * (u_ref[c + 1, q - 1] + u_ref[c + 1, q + 1])
            if c in kept:
                i = kept.index(c)
                new += NEAR * (f_ref[i, q - 1] - f_ref[i, q + 1]) + FAR * (f_ref[i, q + 2] - f_ref[i, q - 2])
            b = DIFFUSION * field
            if fy[c] is None:
                new += turn(b, 1, 1) + turn(b, -1, 1)
            else:
                new += along_y(fy[c], b)
            new += along_z(fz[c], b, fh[c], halo[c], far[c])
            if c == 0:
                slope = NEAR * (u_ref[7, q - 1] - u_ref[7, q + 1]) + FAR * (u_ref[7, q + 2] - u_ref[7, q - 2])
                new += u[0] * slope
            if c == 1:
                potential = u_ref[7, q]
                slope = NEAR * (turn(potential, 1, 1) - turn(potential, -1, 1))
                new += u[0] * (slope + FAR * (turn(potential, -2, 1) - turn(potential, 2, 1)))
            if c < 3:
                unpair(mom_ref, new, c, r)
            else:
                unpair(mag_ref, new, c - 3, r)

    def body(g, _):
        for j in range(4):
            row(4 * g + j, g, j)
        return 0

    lax.fori_loop(0, chunk // 4, body, 0)


def modes_kernel(w_ref, ch_ref, cl_ref, mh_ref, ml_ref, ph_ref, pl_ref, out_ref, x_ref, *, turned):
    dot = functools.partial(jnp.dot, preferred_element_type=jnp.float32)
    planes, band, nx = out_ref.shape[1:]

    def gathered(part):
        if turned:
            x = jnp.concatenate([w_ref[part, z] for z in range(planes)], axis=0)
        else:
            width = w_ref.shape[3]
            for s in range(w_ref.shape[0]):
                for z in range(planes):
                    x_ref[z * band : (z + 1) * band, s * width : (s + 1) * width] = w_ref[s, part, z].T
            x = x_ref[...]
        return x

    def split(x):
        high = x.astype(jnp.bfloat16)
        return high, (x - high.astype(jnp.float32)).astype(jnp.bfloat16)

    re, im = gathered(0), gathered(1)
    times = lambda x, h, l: dot(x[0], h[...]) + dot(x[0], l[...]) + dot(x[1], h[...])
    scale = 1.0 / math.sqrt(NX * nx)
    shape = (band, nx)
    ky = lax.broadcasted_iota(jnp.int32, shape, 0) + lax.axis_index("xy") * band
    kx = lax.broadcasted_iota(jnp.int32, shape, 1)
    keep = jnp.where((ky == 0) & (kx == 0), 0.0, scale)
    both = times(split(re + im), ch_ref, cl_ref)
    out_re = both - times(split(im), mh_ref, ml_ref)
    out_im = both - times(split(re), ph_ref, pl_ref)
    for z in range(planes):
        out_ref[0, z] = out_re[z * band : (z + 1) * band] * keep
        out_ref[1, z] = out_im[z * band : (z + 1) * band] * keep


def cost(flops, bytes_accessed):
    return pl.CostEstimate(flops=int(flops), bytes_accessed=int(bytes_accessed), transcendentals=0)


def tables(size):
    angle = (np.outer(np.arange(size), np.arange(size)) % size) * (2.0 * np.pi / size)
    cosine, sine = np.cos(angle), np.sin(angle)
    result = []
    for table in (cosine, sine, cosine - sine, cosine + sine):
        high = table.astype(np.float32).astype(ml_dtypes.bfloat16)
        low = (table - high.astype(np.float64)).astype(np.float32).astype(ml_dtypes.bfloat16)
        result += [high, low]
    return result


def row_order(half):
    matrix = np.zeros((8 * half, 8 * half), np.float32)
    for z in range(4):
        for h in range(2):
            for p in range(half):
                matrix[(z * 2 + h) * half + p, p * 8 + h * 4 + z] = 1.0
    return matrix.astype(ml_dtypes.bfloat16)


def shift(block, axis, step):
    n = lax.axis_size(axis)
    return lax.ppermute(block, axis, [(i, (i + step) % n) for i in range(n)])


def on_device(density, momentum, magnetic, arm_potential, sn_cells, sn_counts):
    rows, planes, ny = density.shape
    half = rows // 2
    layers, across = lax.axis_size("gz"), lax.axis_size("xy")
    devices = layers * across
    tile_row, tile_plane = lax.axis_index("xy"), lax.axis_index("gz")
    field = rows * planes * ny
    f32 = jnp.float32
    shape = jax.ShapeDtypeStruct
    whole = pl.BlockSpec(memory_space=pltpu.VMEM)
    smem = pl.BlockSpec(memory_space=pltpu.SMEM)
    params = pltpu.CompilerParams(vmem_limit_bytes=VMEM)
    message = shape((2, half, planes, ny), f32)
    tile = shape((half, 8, ny), f32)
    steps = half // 8
    counts = (steps * 5 // 8, steps - steps * 5 // 8) if steps >= 2 else (steps,)

    slots_here = sn_cells.shape[0]
    rho = density.reshape(2, half, planes, ny)
    mom = momentum.reshape(3, 2, half, planes, ny)
    mag = magnetic.reshape(3, 2, half, planes, ny)

    pot = arm_potential.reshape(2, half, ny)
    edges = shape((8, 2, planes, ny), f32)
    mine = shape((devices, 1, -(-4 * slots_here // 128) * 128), jnp.int32)
    full = lambda s: pl.BlockSpec(s, lambda i: (0,) * len(s))
    mine, first_rows, last_rows = pl.pallas_call(
        first_kernel,
        grid=(1,),
        in_specs=[smem, smem] + [
            spec
            for h, k in ((0, 0), (1, half // 2 - 1))
            for spec in (
                pl.BlockSpec((1, 2, planes, ny), lambda i, h=h, k=k: (h, k, 0, 0)),
                pl.BlockSpec((3, 1, 2, planes, ny), lambda i, h=h, k=k: (0, h, k, 0, 0)),
                pl.BlockSpec((3, 1, 2, planes, ny), lambda i, h=h, k=k: (0, h, k, 0, 0)),
                pl.BlockSpec((8, ny), lambda i, h=h: (h * (rows // 8 - 1), 0)),
            )
        ],
        out_specs=[full(mine.shape)] + [full(edges.shape)] * 2,
        out_shape=[mine] + [edges] * 2,
        compiler_params=params,
        cost_estimate=cost(*PACK_COST),
        name="first",
    )(sn_cells, sn_counts, *[rho, mom, mag, arm_potential] * 2)
    events = lax.all_to_all(mine, ("gz", "xy"), split_axis=0, concat_axis=0, tiled=True)
    before, after = shift(last_rows, "xy", 1), shift(first_rows, "xy", -1)

    some = math.gcd(half, 16)
    up, down = pl.pallas_call(
        pack_kernel,
        grid=(half // some,),
        in_specs=[pl.BlockSpec((2, some, planes, ny), lambda i: (0, i, 0, 0))] + [
            pl.BlockSpec((1, 2, some, planes, ny), lambda i, f=f: (f, 0, i, 0, 0)) for f in (2,)
        ] + [pl.BlockSpec(memory_space=pl.ANY)],
        out_specs=[pl.BlockSpec((some // 4, 3, 8, ny), lambda i: (i, 0, 0, 0))] * 2,
        out_shape=[shape((half // 4, 3, 8, ny), f32)] * 2,
        compiler_params=params,
        cost_estimate=cost(*PACK_COST),
        name="pack",
    )(rho, mom, mine)
    below_a, above_a = shift(up, "gz", 1), shift(down, "gz", -1)

    parcels = [shape((n, 20, 8, ny), f32) for n in counts]
    side = pltpu.VMEM((half + 8, 8, ny), f32)
    begins = [sum(counts[:i]) for i in range(len(counts))]
    parcel = pl.BlockSpec((1, 20, 8, ny), lambda i: (jnp.minimum(i, counts[0] - 1), 0, 0, 0))
    eight = pl.BlockSpec((8, 8, ny), lambda i: (i, 0, 0))
    middle = [
        spec
        for h, k in ((0, steps - 1), (1, 0))
        for spec in (
            pl.BlockSpec((1, 2, planes, ny), lambda i, h=h, k=k: (h, k * 4 + 3 * (1 - h), 0, 0)),
            pl.BlockSpec((3, 1, 2, planes, ny), lambda i, h=h, k=k: (0, h, k * 4 + 3 * (1 - h), 0, 0)),
            pl.BlockSpec((3, 1, 2, planes, ny), lambda i, h=h, k=k: (0, h, k * 4 + 3 * (1 - h), 0, 0)),
            pl.BlockSpec((1, 8, ny), lambda i, h=h, k=k: (h, k, 0)),
        )
    ]
    rows_of = lambda n: pl.BlockSpec((n, 2, 8, planes, ny), lambda i: (0, 0, i, 0, 0))
    state, edge, sb, sa, up_0, down_0 = pl.pallas_call(
        functools.partial(state_kernel, depth=planes * layers, count=counts[0], per_device=slots_here, steps=steps),
        grid=(steps,),
        in_specs=[
            smem, pl.BlockSpec((2, 8, planes, ny), lambda i: (0, i, 0, 0)), rows_of(3), rows_of(3),
            pl.BlockSpec((2, 8, ny), lambda i: (0, i, 0)), full(edges.shape), full(edges.shape),
        ] + middle,
        out_specs=[pl.BlockSpec((8, 8, 8, ny), lambda i: (0, i, 0, 0)), full((8, 4, 8, ny)), eight, eight, parcel, parcel],
        out_shape=[shape((8, half, 8, ny), f32), shape((8, 4, 8, ny), f32), tile, tile, parcels[0], parcels[0]],
        scratch_shapes=[pltpu.VMEM((4, half + 8, 8, ny), f32), side, side],
        compiler_params=params,
        cost_estimate=cost(*STATE_COST),
        name="state",
    )(events, rho, mom, mag, pot, before, after, *[rho, mom, mag, pot] * 2)
    parcels_below, parcels_above = [shift(up_0, "gz", 1)], [shift(down_0, "gz", -1)]

    cos_high, cos_low, sin_high, sin_low = tables(ny)[:4]
    turns = tables(NX)
    band = ny // across
    turned = band % 128 != 0 or rows % 128 != 0
    hbm = pl.BlockSpec(memory_space=pl.ANY)
    more = parcels[1:] * 2
    new_density, wave, rho_halo, mz_halo, *messages = pl.pallas_call(
        density_kernel,
        in_specs=[hbm, hbm] + [whole] * 7,
        out_specs=[whole] * (4 + len(more)),
        out_shape=[message, shape((across, 2, planes, rows, band), f32), tile, tile, *more],
        scratch_shapes=[
            pltpu.VMEM((8 * half, ny), f32), pltpu.VMEM((4, half + 4, 8, ny), f32),
            pltpu.VMEM((3, counts[-1] * 8, 8, ny), f32), pltpu.SemaphoreType.DMA((4,)),
        ],
        compiler_params=params,
        cost_estimate=cost(*DENSITY_COST),
        name="density",
    )(
        state, edge, below_a, above_a, sb, sa, row_order(half),
        np.stack([cos_high, -sin_high]), np.stack([cos_low, -sin_low]),
    )

    if messages:
        parcels_below.append(shift(messages[0], "gz", 1))
        parcels_above.append(shift(messages[1], "gz", -1))
    portion = lax.all_to_all(wave, "xy", split_axis=0, concat_axis=0, tiled=True)
    if turned:
        portion = portion.transpose(1, 2, 4, 0, 3).reshape(2, planes, band, NX)
    modes = pl.pallas_call(
        functools.partial(modes_kernel, turned=turned),
        in_specs=[whole] * 7,
        out_specs=whole,
        out_shape=shape((2, planes, band, NX), f32),
        scratch_shapes=[pltpu.VMEM((planes * band, NX), f32)],
        compiler_params=params,
        cost_estimate=cost(*MODES_COST),
        name="modes",
    )(portion, *turns[:2], *turns[4:])
    results = [shape((3, 2, half, planes, ny), f32)] * 2
    new = []
    for i, n in enumerate(counts):
        chunk, first = 8, begins[i] * 8
        here = pl.BlockSpec((chunk, 8, ny), lambda k, o=begins[i]: (o + k, 0, 0))
        parcel = pl.BlockSpec((1, 20, 8, ny), lambda k: (k, 0, 0, 0))
        three = pl.BlockSpec((3, 2, chunk, planes, ny), lambda k, o=begins[i]: (0, 0, o + k, 0, 0))
        below, above = parcels_below[i], parcels_above[i]
        extra = [*new] + [modes] * (i > 0 and i == len(counts) - 1)
        new = pl.pallas_call(
            functools.partial(main_kernel, first=first),
            grid=(n,),
            in_specs=[hbm, hbm] + [here] * 2 + [parcel] * 2 + [hbm] * len(extra),
            out_specs=[three, three],
            out_shape=results,
            scratch_shapes=[
                pltpu.VMEM((8, n * 8 + 4, 8, ny), f32), pltpu.VMEM((5, n * 8 + 4, 8, ny), f32), pltpu.SemaphoreType.DMA((n + 2,)),
            ],
            input_output_aliases={6: 0, 7: 1} if new else {},
            compiler_params=pltpu.CompilerParams(vmem_limit_bytes=62 * 1024 * 1024),
            cost_estimate=cost(*MAIN_COST),
            name=f"main{i}",
        )(state, edge, rho_halo, mz_halo, below, above, *extra)
    new_mom, new_mag = new

    return (
        new_density.reshape(rows, planes, ny),
        new_mom.reshape(3, rows, planes, ny),
        new_mag.reshape(3, rows, planes, ny),
        modes,
    )


def solution(mesh):
    in_specs = (
        P("xy", "gz", None),
        P(None, "xy", "gz", None),
        P(None, "xy", "gz", None),
        P("xy", None),
        P(("gz", "xy"), None),
        P(("gz", "xy")),
    )
    out_specs = (
        P("xy", "gz", None),
        P(None, "xy", "gz", None),
        P(None, "xy", "gz", None),
        P(None, "gz", "xy", None),
    )
    return jax.shard_map(
        on_device, mesh=mesh, in_specs=in_specs, out_specs=out_specs, check_vma=False
    )
```

```python
import functools
import math

import jax
import jax.numpy as jnp
import ml_dtypes
import numpy as np
from jax import lax
from jax.experimental import pallas as pl
from jax.experimental.pallas import tpu as pltpu
from jax.sharding import PartitionSpec as P

NX = 512
RADIUS = 16
IMPULSE = 2.0 / 16
TIME_STEP = 0.1
DIFFUSION = 0.05
NEAR = 8.0 * TIME_STEP / 12.0
FAR = TIME_STEP / 12.0
VMEM = 56 * 1024 * 1024
PACK_COST = MODES_COST = (1e6, 1e5)
STATE_COST = DENSITY_COST = (1e12, 4e9)
MAIN_COST = (1e12, 4e9)


def pair(ref, *index):
    return jnp.concatenate([ref[(*index[:-1], 0, index[-1])], ref[(*index[:-1], 1, index[-1])]], axis=0)


def unpair(ref, value, *index):
    ref[(*index[:-1], 0, index[-1])] = value[:4]
    ref[(*index[:-1], 1, index[-1])] = value[4:]


def slots(shape):
    sub = lax.broadcasted_iota(jnp.int32, shape, len(shape) - 2)
    return jnp.where(sub >= 4, sub - 4, sub)


def turn(value, shift, axis):
    return pltpu.roll(value, shift % value.shape[axis], axis)


def gather_planes(values, plane):
    slot = slots(values[0].shape)
    out = turn(values[-1], len(values) - 1 - plane, 0)
    for c in reversed(range(len(values) - 1)):
        out = jnp.where(slot == c, turn(values[c], c - plane, 0), out)
    return out


def collect(values, plane):
    sub = lax.broadcasted_iota(jnp.int32, values[0].shape, 0)
    out = turn(values[0], -plane, 0)
    for n in range(1, 8):
        j, h = n // 2, n % 2
        out = jnp.where(sub == n, turn(values[j], n - 4 * h - plane, 0), out)
    return out


def shared(rho, m, b):
    inv = 1.0 / rho
    return [x * inv for x in m], rho + 0.5 * (b[0] * b[0] + b[1] * b[1] + b[2] * b[2])


def fluxes(v, total, m, b, k):
    push = [m[i] * v[k] - b[i] * b[k] + (total if i == k else 0.0) for i in range(3)]
    turned = [None if i == k else v[k] * b[i] - b[k] * v[i] for i in range(3)]
    return push + turned


def first_kernel(cell_ref, count_ref, rho_a, mom_a, mag_a, pot_a, rho_z, mom_z, mag_z, pot_z, ev_ref, first_ref, last_ref):
    shape = (1, ev_ref.shape[2])
    lane = lax.broadcasted_iota(jnp.int32, shape, 1)
    row = jnp.zeros(shape, jnp.int32)
    for e in range(count_ref.shape[0]):
        for i in range(4):
            row = jnp.where(lane == 4 * e + i, cell_ref[e, i] if i < 3 else count_ref[e], row)

    def copy(d, _):
        ev_ref[d] = row
        return 0

    lax.fori_loop(0, ev_ref.shape[0], copy, 0)
    for ref, rho, mom, mag, pot, skip in (
        (first_ref, rho_a, mom_a, mag_a, pot_a, 0), (last_ref, rho_z, mom_z, mag_z, pot_z, pot_z.shape[0] - 2),
    ):
        for j in range(2):
            ref[0, j] = rho[0, j]
            for c in range(3):
                ref[1 + c, j] = mom[c, 0, j]
                ref[4 + c, j] = mag[c, 0, j]
            ref[7, j] = jnp.broadcast_to(pot[skip + j : skip + j + 1], ref.shape[2:])


def pack_kernel(rho_ref, mz_ref, after_ref, up_ref, down_ref):
    def body(g, _):
        rho = [pair(rho_ref, 4 * g + j) for j in range(4)]
        mz = [pair(mz_ref, 0, 4 * g + j) for j in range(4)]
        for i, (values, up, down) in enumerate(((rho, 3, 0), (mz, 3, 0), (mz, 2, 1))):
            up_ref[g, i] = collect(values, up)
            down_ref[g, i] = collect(values, down)
        return 0

    lax.fori_loop(0, rho_ref.shape[1] // 4, body, 0)


def write_messages(up_ref, down_ref, k, g, state):
    fluxes_by, bx = [], []
    for j in range(4):
        r = 4 * g + j
        u = state(j)
        near = [u[1], u[2], u[5], u[6]]
        up_ref[k, r] = gather_planes(near, 3)
        down_ref[k, r] = gather_planes(near, 0)
        f = fluxes(*shared(u[0], u[1:4], u[4:7]), u[1:4], u[4:7], 2)
        up_ref[k, 8 + r] = gather_planes(f[:4], 2)
        down_ref[k, 8 + r] = gather_planes(f[:4], 1)
        fluxes_by.append(f[4])
        bx.append(u[4])
    up_ref[k, 16 + g] = collect(fluxes_by, 2)
    down_ref[k, 16 + g] = collect(fluxes_by, 1)
    up_ref[k, 18 + g] = collect(bx, 3)
    down_ref[k, 18 + g] = collect(bx, 0)


def state_kernel(
    ev_ref, rho_ref, mom_ref, mag_ref, pot_ref, before_ref, after_ref, rho_l, mom_l, mag_l, pot_l,
    rho_h, mom_h, mag_h, pot_h, u_out, edge_out, sb_out, sa_out, up_ref, down_ref, s_ref, sb_ref, sa_ref, *,
    depth, count, per_device, steps,
):
    half, ny = 8 * steps, s_ref.shape[3]
    step_id = pl.program_id(0)

    @pl.when(step_id == 0)
    def _():
        deposit(ev_ref, s_ref, sb_ref, sa_ref, depth, per_device, half)
        pieces = lambda rho, mom, mag, pot, j: (
            [rho[0, j]] + [mom[c, 0, j] for c in range(3)] + [mag[c, 0, j] for c in range(3)]
            + [jnp.broadcast_to(pot, (4, ny))]
        )
        for j in range(2):
            low = pieces(rho_l, mom_l, mag_l, pot_l[0, 6 + j : 7 + j], j)
            high = pieces(rho_h, mom_h, mag_h, pot_h[0, j : j + 1], j)
            for f in range(8):
                left = jnp.concatenate([before_ref[f, j], low[f]], axis=0)
                right = jnp.concatenate([high[f], after_ref[f, j]], axis=0)
                edge_out[f, j] = left + s_ref[f, j] if f < 4 else left
                edge_out[f, 2 + j] = right + s_ref[f, half + 2 + j] if f < 4 else right

    start = step_id * 8

    def body(g, send):
        def state(j):
            r = 4 * g + j
            q = start + r + 2
            sb_out[r] = sb_ref[q]
            sa_out[r] = sa_ref[q]
            u = [pair(rho_ref, r) + s_ref[0, q]]
            u += [pair(mom_ref, c, r) + s_ref[1 + c, q] for c in range(3)]
            u += [pair(mag_ref, c, r) for c in range(3)]
            for f in range(7):
                u_out[f, r] = u[f]
            rows = [jnp.broadcast_to(pot_ref[h, pl.ds(r, 1), :], (4, ny)) for h in range(2)]
            u_out[7, r] = jnp.concatenate(rows, axis=0)
            return u

        if send:
            write_messages(up_ref, down_ref, 0, g, state)
        else:
            for j in range(4):
                state(j)
        return 0

    @pl.when(step_id < count)
    def _():
        lax.fori_loop(0, 2, lambda g, _: body(g, True), 0)

    @pl.when(step_id >= count)
    def _():
        lax.fori_loop(0, 2, lambda g, _: body(g, False), 0)


def deposit(ev_ref, s_ref, sb_ref, sa_ref, depth, per_device, half):
    ny = s_ref.shape[3]
    rows, events = 2 * half, ev_ref.shape[0] * per_device
    row_start, plane_start = lax.axis_index("xy") * rows, lax.axis_index("gz") * 4
    s_ref[...] = jnp.zeros_like(s_ref)
    sb_ref[...] = jnp.zeros_like(sb_ref)
    sa_ref[...] = jnp.zeros_like(sa_ref)

    shape = (8, 8, 128)
    slot = slots(shape)
    sub = lax.broadcasted_iota(jnp.int32, shape, 1)
    step = lax.broadcasted_iota(jnp.int32, shape, 0)
    lane = lax.broadcasted_iota(jnp.int32, shape, 2)

    def wrapped(distance, size):
        distance = jnp.where(distance >= size // 2, distance - size, distance)
        return jnp.where(distance < -(size // 2), distance + size, distance)

    def event(e, _):
        device, slot_id = (e, 0) if per_device == 1 else (lax.div(e, per_device), lax.rem(e, per_device))
        row, col, plane, count = (ev_ref[device, 0, 4 * slot_id + i] for i in range(4))
        rel = wrapped(row - row_start - half, NX)
        rel = rel + half

        @pl.when((count > 0) & (rel > -2 - RADIUS) & (rel < rows + 2 + RADIUS))
        def _():
            base = plane_start - plane
            dz = wrapped(slot + base, depth).astype(jnp.float32)
            dzb = wrapped(jnp.where(slot == 2, -2, -1) + base, depth).astype(jnp.float32)
            dza = wrapped(jnp.where(slot == 2, 5, 4) + base, depth).astype(jnp.float32)
            share = lambda d: jnp.where(slot == 0, 1.0, jnp.where(slot == 3, 0.0, IMPULSE * d))
            first = jnp.bitwise_and(col - RADIUS, ny - 1) // 128
            second = jnp.bitwise_and(col + RADIUS - 1, ny - 1) // 128

            def tile(t, _):
                index = jnp.where(t == 0, first, second)
                lanes = pl.ds(pl.multiple_of(index * 128, 128), 128)
                dy = wrapped(lane + index * 128 - col, ny).astype(jnp.float32)
                dy2 = dy * dy
                for h in range(2):
                    weight = jnp.where((sub >= 4) == (h == 1), count, 0).astype(jnp.float32)
                    low = jnp.clip(rel - RADIUS + 1 - h * half + 2, 0, s_ref.shape[1]) // 8
                    high = (jnp.clip(rel + RADIUS - 1 - h * half + 2, -1, half + 3) + 8) // 8

                    def chunk(n, _):
                        q = pl.ds(n * 8, 8)
                        dx = (step + (n * 8 - 2 + h * half - rel)).astype(jnp.float32)
                        flat = dx * dx + dy2
                        size = lambda d: jnp.maximum(1.0 - (flat + d * d) * (1.0 / (RADIUS * RADIUS)), 0.0) * weight
                        w = size(dz)
                        s_ref[0, q, :, lanes] += w
                        w = w * IMPULSE
                        s_ref[1, q, :, lanes] += w * dx
                        s_ref[2, q, :, lanes] += w * dy
                        s_ref[3, q, :, lanes] += w * dz
                        sb_ref[q, :, lanes] += size(dzb) * share(dzb)
                        sa_ref[q, :, lanes] += size(dza) * share(dza)
                        return 0

                    lax.fori_loop(low, high, chunk, 0)
                return 0

            lax.fori_loop(0, jnp.where(first == second, 1, 2), tile, 0)

        return 0

    lax.fori_loop(0, events, event, 0)


def ends(below, above, c):
    return jnp.where(slots(below.shape) == 3, turn(above, 3 - c, 0), turn(below, -c, 0))


def along_y(f, b):
    near, far = NEAR * f, FAR * f
    return turn(b + near, 1, 1) + turn(b - near, -1, 1) + turn(far, -2, 1) - turn(far, 2, 1)


def along_z(f, b, near_f, near_u, far_f):
    slot = slots(b.shape)
    first, last = slot == 0, slot == 3
    outer = DIFFUSION * near_u
    if f is None:
        return jnp.where(first, outer, turn(b, 1, 0)) + jnp.where(last, outer, turn(b, -1, 0))
    near = NEAR * f
    outer += jnp.where(first, NEAR, -NEAR) * near_f
    out = jnp.where(first, outer, turn(b + near, 1, 0)) + jnp.where(last, outer, turn(b - near, -1, 0))
    beyond = jnp.where(slot == 1, turn(near_f, 1, 0), jnp.where(slot == 2, turn(near_f, -1, 0), far_f))
    return out + FAR * (jnp.where(slot <= 1, turn(f, -2, 0), beyond) - jnp.where(slot >= 2, turn(f, 2, 0), beyond))


def fetch(u_hbm, edge_hbm, u_ref, sem, first):
    fields, total = u_ref.shape[:2]
    half = u_hbm.shape[1]
    low, high = max(first - 2, 0), min(first + total - 2, half)
    copies = [pltpu.make_async_copy(u_hbm.at[:fields, low:high], u_ref.at[:, low - first + 2 : high - first + 2], sem.at[0])]
    if first == 0:
        copies.append(pltpu.make_async_copy(edge_hbm.at[:fields, 0:2], u_ref.at[:, 0:2], sem.at[1]))
    if first + total - 4 == half:
        copies.append(pltpu.make_async_copy(edge_hbm.at[:fields, 2:4], u_ref.at[:, total - 2 : total], sem.at[2]))
    for copy in copies:
        copy.start()
    for copy in copies:
        copy.wait()


def density_kernel(
    u_hbm, edge_hbm, below_ref, above_ref, sb_ref, sa_ref, order_ref, high_ref, low_ref, out_ref, wave_ref,
    rho_out, mz_out, *rest,
):
    *parcel, d_ref, u_ref, b_ref, sem = rest
    half = u_hbm.shape[1]
    field = None
    if parcel:
        field = pltpu.make_async_copy(u_hbm.at[4:7, half - b_ref.shape[1] :], b_ref, sem.at[3])
        field.start()
    fetch(u_hbm, edge_hbm, u_ref, sem, 0)
    rows = 2 * half

    def row(p, g, j):
        rho, my, mz = u_ref[0, p + 2], u_ref[2, p + 2], u_ref[3, p + 2]
        sb, sa = sb_ref[p], sa_ref[p]
        halo = [last_plane(below_ref[g, i], above_ref[g, i], j) + ends(sb, sa, i) for i in range(3)]
        rho_out[p], mz_out[p] = halo[:2]
        b = DIFFUSION * rho
        new = rho * (1.0 - 6.0 * DIFFUSION)
        new += DIFFUSION * (u_ref[0, p + 1] + u_ref[0, p + 3])
        new += NEAR * (u_ref[1, p + 1] - u_ref[1, p + 3]) + FAR * (u_ref[1, p + 4] - u_ref[1, p])
        new += along_y(my, b)
        new += along_z(mz, b, halo[1], halo[0], halo[2])
        unpair(out_ref, new, p)
        d_ref[pl.ds(pl.multiple_of(p * 8, 8), 8), :] = new

    def body(g, _):
        for j in range(4):
            row(4 * g + j, g, j)
        return 0

    lax.fori_loop(0, half // 4, body, 0)
    d = d_ref[...]
    order = order_ref[...]
    dot = functools.partial(jnp.dot, preferred_element_type=jnp.float32)
    high = d.astype(jnp.bfloat16)
    low = (d - high.astype(jnp.float32)).astype(jnp.bfloat16)
    high = dot(order, high).astype(jnp.bfloat16)
    low = dot(order, low).astype(jnp.bfloat16)
    for part in range(2):
        c_high, c_low = high_ref[part], low_ref[part]
        wave = dot(high, c_high) + dot(high, c_low) + dot(low, c_high)
        peers, band = wave_ref.shape[0], wave_ref.shape[4]
        for j in range(peers):
            for z in range(4):
                wave_ref[j, part, z] = wave[z * rows : (z + 1) * rows, j * band : (j + 1) * band]
    if not parcel:
        return
    field.wait()
    first = half - b_ref.shape[1]

    def messages(n, _):
        r = n * 4
        state = lambda j: [u_ref[f, first + r + j + 2] for f in range(4)] + [b_ref[c, r + j] for c in range(3)]
        write_messages(*parcel, n // 2, n % 2, state)
        return 0

    lax.fori_loop(0, b_ref.shape[1] // 4, messages, 0)


def last_plane(below, above, j):
    sub = lax.broadcasted_iota(jnp.int32, below.shape, 0)
    out = turn(below, -2 * j, 0)
    out = jnp.where(sub == 3, turn(above, 3 - 2 * j, 0), out)
    out = jnp.where(sub == 4, turn(below, 3 - 2 * j, 0), out)
    return jnp.where(sub == 7, turn(above, 6 - 2 * j, 0), out)


def halo_planes(rho_ref, mz_ref, from_below, from_above, r, g, j):
    bn, an, bf, af = from_below[0, r], from_above[0, r], from_below[0, 8 + r], from_above[0, 8 + r]
    hm = [ends(bn, an, 0), ends(bn, an, 1), mz_ref[r]]
    hb = [last_plane(from_below[0, 18 + g], from_above[0, 18 + g], j), ends(bn, an, 2), ends(bn, an, 3)]
    fh = fluxes(*shared(rho_ref[r], hm, hb), hm, hb, 2)
    halo = hm + hb
    far = [ends(bf, af, c) for c in range(4)] + [last_plane(from_below[0, 16 + g], from_above[0, 16 + g], j), None]
    return fh, halo, far


def halo_kernel(rho_ref, mz_ref, from_below, from_above, mom_in, mag_in, *rest):
    mom_ref, mag_ref = rest[-2:]

    def row(r, g, j):
        fh, halo, far = halo_planes(rho_ref, mz_ref, from_below, from_above, r, g, j)
        slot = slots(halo[0].shape)
        first, last = slot == 0, slot == 3
        for c in range(6):
            add = DIFFUSION * halo[c]
            if fh[c] is not None:
                add += jnp.where(first, NEAR, -NEAR) * fh[c]
            add = jnp.where(first | last, add, 0.0)
            if fh[c] is not None:
                beyond = jnp.where(slot == 1, turn(fh[c], 1, 0), jnp.where(slot == 2, turn(fh[c], -1, 0), far[c]))
                add += jnp.where(slot >= 2, FAR, -FAR) * beyond
            if c < 3:
                unpair(mom_ref, pair(mom_in, c, r) + add, c, r)
            else:
                unpair(mag_ref, pair(mag_in, c - 3, r) + add, c - 3, r)

    def body(g, _):
        for j in range(4):
            row(4 * g + j, g, j)
        return 0

    lax.fori_loop(0, 2, body, 0)


def main_kernel(u_hbm, edge_hbm, rho_ref, mz_ref, from_below, from_above, *rest, first, inner):
    mom_ref, mag_ref, u_ref, f_ref, sem = rest[-5:]
    chunk, total, half = 8, u_ref.shape[1], u_hbm.shape[1]
    step_id = pl.program_id(0)
    start = step_id * chunk
    kept = (0, 1, 2, 4, 5)

    def copies(i):
        low = 0 if i == 0 else chunk * i + 4
        high = chunk * (i + 1) + 4
        a, b = max(first - 2 + low, 0), min(first - 2 + high, half)
        at = a - first + 2
        result = [(u_hbm.at[:, a:b], u_ref.at[:, at : at + b - a], sem.at[i])]
        if first - 2 + low < 0:
            result.append((edge_hbm.at[:, 0:2], u_ref.at[:, 0:2], sem.at[total // chunk]))
        if first - 2 + high > half:
            result.append((edge_hbm.at[:, 2:4], u_ref.at[:, total - 2 : total], sem.at[total // chunk + 1]))
        return [pltpu.make_async_copy(*c) for c in result]

    @pl.when(step_id == 0)
    def _():
        for i in range(total // chunk):
            for copy in copies(i):
                copy.start()

    for i in range(total // chunk):

        @pl.when(step_id == i)
        def _(i=i):
            for copy in copies(i):
                copy.wait()

    def fx(q, _):
        u = [u_ref[f, q] for f in range(7)]
        f = fluxes(*shared(u[0], u[1:4], u[4:7]), u[1:4], u[4:7], 0)
        for i, c in enumerate(kept):
            f_ref[i, q] = f[c]
        return 0

    lax.fori_loop(jnp.where(step_id == 0, 0, start + 4), start + chunk + 4, fx, 0)

    def row(r, g, j):
        q = start + r + 2
        u = [u_ref[f, q] for f in range(7)]
        v, pressure = shared(u[0], u[1:4], u[4:7])
        fy = fluxes(v, pressure, u[1:4], u[4:7], 1)
        fz = fluxes(v, pressure, u[1:4], u[4:7], 2)
        if inner:
            zero = jnp.zeros_like(u[0])
            fh = halo = far = [zero] * 5 + [None]
            halo = [zero] * 6
        else:
            fh, halo, far = halo_planes(rho_ref, mz_ref, from_below, from_above, r, g, j)
        for c in range(6):
            field = u[c + 1]
            new = field * (1.0 - 6.0 * DIFFUSION)
            new += DIFFUSION * (u_ref[c + 1, q - 1] + u_ref[c + 1, q + 1])
            if c in kept:
                i = kept.index(c)
                new += NEAR * (f_ref[i, q - 1] - f_ref[i, q + 1]) + FAR * (f_ref[i, q + 2] - f_ref[i, q - 2])
            b = DIFFUSION * field
            if fy[c] is None:
                new += turn(b, 1, 1) + turn(b, -1, 1)
            else:
                new += along_y(fy[c], b)
            new += along_z(fz[c], b, fh[c], halo[c], far[c])
            if c == 0:
                slope = NEAR * (u_ref[7, q - 1] - u_ref[7, q + 1]) + FAR * (u_ref[7, q + 2] - u_ref[7, q - 2])
                new += u[0] * slope
            if c == 1:
                potential = u_ref[7, q]
                slope = NEAR * (turn(potential, 1, 1) - turn(potential, -1, 1))
                new += u[0] * (slope + FAR * (turn(potential, -2, 1) - turn(potential, 2, 1)))
            if c < 3:
                unpair(mom_ref, new, c, r)
            else:
                unpair(mag_ref, new, c - 3, r)

    def body(g, _):
        for j in range(4):
            row(4 * g + j, g, j)
        return 0

    lax.fori_loop(0, chunk // 4, body, 0)


def modes_kernel(w_ref, ch_ref, cl_ref, mh_ref, ml_ref, ph_ref, pl_ref, out_ref, x_ref, *, turned):
    dot = functools.partial(jnp.dot, preferred_element_type=jnp.float32)
    planes, band, nx = out_ref.shape[1:]

    def gathered(part):
        if turned:
            x = jnp.concatenate([w_ref[part, z] for z in range(planes)], axis=0)
        else:
            width = w_ref.shape[3]
            for s in range(w_ref.shape[0]):
                for z in range(planes):
                    x_ref[z * band : (z + 1) * band, s * width : (s + 1) * width] = w_ref[s, part, z].T
            x = x_ref[...]
        return x

    def split(x):
        high = x.astype(jnp.bfloat16)
        return high, (x - high.astype(jnp.float32)).astype(jnp.bfloat16)

    re, im = gathered(0), gathered(1)
    times = lambda x, h, l: dot(x[0], h[...]) + dot(x[0], l[...]) + dot(x[1], h[...])
    scale = 1.0 / math.sqrt(NX * nx)
    shape = (band, nx)
    ky = lax.broadcasted_iota(jnp.int32, shape, 0) + lax.axis_index("xy") * band
    kx = lax.broadcasted_iota(jnp.int32, shape, 1)
    keep = jnp.where((ky == 0) & (kx == 0), 0.0, scale)
    both = times(split(re + im), ch_ref, cl_ref)
    out_re = both - times(split(im), mh_ref, ml_ref)
    out_im = both - times(split(re), ph_ref, pl_ref)
    for z in range(planes):
        out_ref[0, z] = out_re[z * band : (z + 1) * band] * keep
        out_ref[1, z] = out_im[z * band : (z + 1) * band] * keep


def cost(flops, bytes_accessed):
    return pl.CostEstimate(flops=int(flops), bytes_accessed=int(bytes_accessed), transcendentals=0)


def tables(size):
    angle = (np.outer(np.arange(size), np.arange(size)) % size) * (2.0 * np.pi / size)
    cosine, sine = np.cos(angle), np.sin(angle)
    result = []
    for table in (cosine, sine, cosine - sine, cosine + sine):
        high = table.astype(np.float32).astype(ml_dtypes.bfloat16)
        low = (table - high.astype(np.float64)).astype(np.float32).astype(ml_dtypes.bfloat16)
        result += [high, low]
    return result


def row_order(half):
    matrix = np.zeros((8 * half, 8 * half), np.float32)
    for z in range(4):
        for h in range(2):
            for p in range(half):
                matrix[(z * 2 + h) * half + p, p * 8 + h * 4 + z] = 1.0
    return matrix.astype(ml_dtypes.bfloat16)


def shift(block, axis, step):
    n = lax.axis_size(axis)
    return lax.ppermute(block, axis, [(i, (i + step) % n) for i in range(n)])


def on_device(density, momentum, magnetic, arm_potential, sn_cells, sn_counts):
    rows, planes, ny = density.shape
    half = rows // 2
    layers, across = lax.axis_size("gz"), lax.axis_size("xy")
    devices = layers * across
    tile_row, tile_plane = lax.axis_index("xy"), lax.axis_index("gz")
    field = rows * planes * ny
    f32 = jnp.float32
    shape = jax.ShapeDtypeStruct
    whole = pl.BlockSpec(memory_space=pltpu.VMEM)
    smem = pl.BlockSpec(memory_space=pltpu.SMEM)
    params = pltpu.CompilerParams(vmem_limit_bytes=VMEM)
    message = shape((2, half, planes, ny), f32)
    tile = shape((half, 8, ny), f32)
    steps = half // 8
    counts = (steps * 5 // 8, steps - steps * 5 // 8) if steps >= 2 else (steps,)

    slots_here = sn_cells.shape[0]
    rho = density.reshape(2, half, planes, ny)
    mom = momentum.reshape(3, 2, half, planes, ny)
    mag = magnetic.reshape(3, 2, half, planes, ny)

    pot = arm_potential.reshape(2, half, ny)
    edges = shape((8, 2, planes, ny), f32)
    mine = shape((devices, 1, -(-4 * slots_here // 128) * 128), jnp.int32)
    full = lambda s: pl.BlockSpec(s, lambda i: (0,) * len(s))
    mine, first_rows, last_rows = pl.pallas_call(
        first_kernel,
        grid=(1,),
        in_specs=[smem, smem] + [
            spec
            for h, k in ((0, 0), (1, half // 2 - 1))
            for spec in (
                pl.BlockSpec((1, 2, planes, ny), lambda i, h=h, k=k: (h, k, 0, 0)),
                pl.BlockSpec((3, 1, 2, planes, ny), lambda i, h=h, k=k: (0, h, k, 0, 0)),
                pl.BlockSpec((3, 1, 2, planes, ny), lambda i, h=h, k=k: (0, h, k, 0, 0)),
                pl.BlockSpec((8, ny), lambda i, h=h: (h * (rows // 8 - 1), 0)),
            )
        ],
        out_specs=[full(mine.shape)] + [full(edges.shape)] * 2,
        out_shape=[mine] + [edges] * 2,
        compiler_params=params,
        cost_estimate=cost(*PACK_COST),
        name="first",
    )(sn_cells, sn_counts, *[rho, mom, mag, arm_potential] * 2)
    events = lax.all_to_all(mine, ("gz", "xy"), split_axis=0, concat_axis=0, tiled=True)
    before, after = shift(last_rows, "xy", 1), shift(first_rows, "xy", -1)

    some = math.gcd(half, 16)
    up, down = pl.pallas_call(
        pack_kernel,
        grid=(half // some,),
        in_specs=[pl.BlockSpec((2, some, planes, ny), lambda i: (0, i, 0, 0))] + [
            pl.BlockSpec((1, 2, some, planes, ny), lambda i, f=f: (f, 0, i, 0, 0)) for f in (2,)
        ] + [pl.BlockSpec(memory_space=pl.ANY)],
        out_specs=[pl.BlockSpec((some // 4, 3, 8, ny), lambda i: (i, 0, 0, 0))] * 2,
        out_shape=[shape((half // 4, 3, 8, ny), f32)] * 2,
        compiler_params=params,
        cost_estimate=cost(*PACK_COST),
        name="pack",
    )(rho, mom, mine)
    below_a, above_a = shift(up, "gz", 1), shift(down, "gz", -1)

    parcels = [shape((n, 20, 8, ny), f32) for n in counts]
    side = pltpu.VMEM((half + 8, 8, ny), f32)
    begins = [sum(counts[:i]) for i in range(len(counts))]
    parcel = pl.BlockSpec((1, 20, 8, ny), lambda i: (jnp.minimum(i, counts[0] - 1), 0, 0, 0))
    eight = pl.BlockSpec((8, 8, ny), lambda i: (i, 0, 0))
    middle = [
        spec
        for h, k in ((0, steps - 1), (1, 0))
        for spec in (
            pl.BlockSpec((1, 2, planes, ny), lambda i, h=h, k=k: (h, k * 4 + 3 * (1 - h), 0, 0)),
            pl.BlockSpec((3, 1, 2, planes, ny), lambda i, h=h, k=k: (0, h, k * 4 + 3 * (1 - h), 0, 0)),
            pl.BlockSpec((3, 1, 2, planes, ny), lambda i, h=h, k=k: (0, h, k * 4 + 3 * (1 - h), 0, 0)),
            pl.BlockSpec((1, 8, ny), lambda i, h=h, k=k: (h, k, 0)),
        )
    ]
    rows_of = lambda n: pl.BlockSpec((n, 2, 8, planes, ny), lambda i: (0, 0, i, 0, 0))
    state, edge, sb, sa, up_0, down_0 = pl.pallas_call(
        functools.partial(state_kernel, depth=planes * layers, count=counts[0], per_device=slots_here, steps=steps),
        grid=(steps,),
        in_specs=[
            smem, pl.BlockSpec((2, 8, planes, ny), lambda i: (0, i, 0, 0)), rows_of(3), rows_of(3),
            pl.BlockSpec((2, 8, ny), lambda i: (0, i, 0)), full(edges.shape), full(edges.shape),
        ] + middle,
        out_specs=[pl.BlockSpec((8, 8, 8, ny), lambda i: (0, i, 0, 0)), full((8, 4, 8, ny)), eight, eight, parcel, parcel],
        out_shape=[shape((8, half, 8, ny), f32), shape((8, 4, 8, ny), f32), tile, tile, parcels[0], parcels[0]],
        scratch_shapes=[pltpu.VMEM((4, half + 8, 8, ny), f32), side, side],
        compiler_params=params,
        cost_estimate=cost(*STATE_COST),
        name="state",
    )(events, rho, mom, mag, pot, before, after, *[rho, mom, mag, pot] * 2)
    parcels_below, parcels_above = [shift(up_0, "gz", 1)], [shift(down_0, "gz", -1)]

    cos_high, cos_low, sin_high, sin_low = tables(ny)[:4]
    turns = tables(NX)
    band = ny // across
    turned = band % 128 != 0 or rows % 128 != 0
    hbm = pl.BlockSpec(memory_space=pl.ANY)
    more = parcels[1:] * 2
    new_density, wave, rho_halo, mz_halo, *messages = pl.pallas_call(
        density_kernel,
        in_specs=[hbm, hbm] + [whole] * 7,
        out_specs=[whole] * (4 + len(more)),
        out_shape=[message, shape((across, 2, planes, rows, band), f32), tile, tile, *more],
        scratch_shapes=[
            pltpu.VMEM((8 * half, ny), f32), pltpu.VMEM((4, half + 4, 8, ny), f32),
            pltpu.VMEM((3, counts[-1] * 8, 8, ny), f32), pltpu.SemaphoreType.DMA((4,)),
        ],
        compiler_params=params,
        cost_estimate=cost(*DENSITY_COST),
        name="density",
    )(
        state, edge, below_a, above_a, sb, sa, row_order(half),
        np.stack([cos_high, -sin_high]), np.stack([cos_low, -sin_low]),
    )

    if messages:
        parcels_below.append(shift(messages[0], "gz", 1))
        parcels_above.append(shift(messages[1], "gz", -1))
    portion = lax.all_to_all(wave, "xy", split_axis=0, concat_axis=0, tiled=True)
    if turned:
        portion = portion.transpose(1, 2, 4, 0, 3).reshape(2, planes, band, NX)
    modes = pl.pallas_call(
        functools.partial(modes_kernel, turned=turned),
        in_specs=[whole] * 7,
        out_specs=whole,
        out_shape=shape((2, planes, band, NX), f32),
        scratch_shapes=[pltpu.VMEM((planes * band, NX), f32)],
        compiler_params=params,
        cost_estimate=cost(*MODES_COST),
        name="modes",
    )(portion, *turns[:2], *turns[4:])
    results = [shape((3, 2, half, planes, ny), f32)] * 2
    three = lambda b: pl.BlockSpec((3, 2, 8, planes, ny), lambda k: (0, 0, b + k, 0, 0))
    here = lambda b: pl.BlockSpec((8, 8, ny), lambda k: (b + k, 0, 0))
    parcel = pl.BlockSpec((1, 20, 8, ny), lambda k: (k, 0, 0, 0))
    wide = pltpu.CompilerParams(vmem_limit_bytes=62 * 1024 * 1024)

    def main(i, inner, name, *new):
        n, b = counts[i], begins[i]
        halos = [hbm] * 4 if inner else [here(b)] * 2 + [parcel] * 2
        parts = (rho_halo, mz_halo) if inner else (parcels_below[i], parcels_above[i])
        return pl.pallas_call(
            functools.partial(main_kernel, first=b * 8, inner=inner),
            grid=(n,),
            in_specs=[hbm, hbm] + halos + [hbm] * len(new),
            out_specs=[three(b), three(b)],
            out_shape=results,
            scratch_shapes=[
                pltpu.VMEM((8, n * 8 + 4, 8, ny), f32), pltpu.VMEM((5, n * 8 + 4, 8, ny), f32),
                pltpu.SemaphoreType.DMA((n + 2,)),
            ],
            input_output_aliases={6: 0, 7: 1} if new else {},
            compiler_params=wide,
            cost_estimate=cost(*MAIN_COST),
            name=name,
        )(state, edge, rho_halo, mz_halo, *parts, *new)

    if len(counts) == 1:
        new = main(0, False, "main0")
    else:
        new = main(0, False, "main0", *main(1, True, "inner1"))
        n, b = counts[1], begins[1]
        new = pl.pallas_call(
            halo_kernel,
            grid=(n,),
            in_specs=[here(b)] * 2 + [parcel] * 2 + [three(b)] * 2 + [hbm],
            out_specs=[three(b)] * 2,
            out_shape=results,
            input_output_aliases={4: 0, 5: 1},
            compiler_params=wide,
            cost_estimate=cost(*MAIN_COST),
            name="halo1",
        )(rho_halo, mz_halo, parcels_below[1], parcels_above[1], *new, modes)
    new_mom, new_mag = new

    return (
        new_density.reshape(rows, planes, ny),
        new_mom.reshape(3, rows, planes, ny),
        new_mag.reshape(3, rows, planes, ny),
        modes,
    )


def solution(mesh):
    in_specs = (
        P("xy", "gz", None),
        P(None, "xy", "gz", None),
        P(None, "xy", "gz", None),
        P("xy", None),
        P(("gz", "xy"), None),
        P(("gz", "xy")),
    )
    out_specs = (
        P("xy", "gz", None),
        P(None, "xy", "gz", None),
        P(None, "xy", "gz", None),
        P(None, "gz", "xy", None),
    )
    return jax.shard_map(
        on_device, mesh=mesh, in_specs=in_specs, out_specs=out_specs, check_vma=False
    )
```

```python
import functools
import math

import jax
import jax.numpy as jnp
import ml_dtypes
import numpy as np
from jax import lax
from jax.experimental import pallas as pl
from jax.experimental.pallas import tpu as pltpu
from jax.sharding import PartitionSpec as P

NX = 512
RADIUS = 16
IMPULSE = 2.0 / 16
TIME_STEP = 0.1
DIFFUSION = 0.05
NEAR = 8.0 * TIME_STEP / 12.0
FAR = TIME_STEP / 12.0
VMEM = 56 * 1024 * 1024
PACK_COST = MODES_COST = (1e6, 1e5)
STATE_COST = DENSITY_COST = (1e12, 4e9)
MAIN_COST = (1e12, 4e9)


def pair(ref, *index):
    return jnp.concatenate([ref[(*index[:-1], 0, index[-1])], ref[(*index[:-1], 1, index[-1])]], axis=0)


def unpair(ref, value, *index):
    ref[(*index[:-1], 0, index[-1])] = value[:4]
    ref[(*index[:-1], 1, index[-1])] = value[4:]


def slots(shape):
    sub = lax.broadcasted_iota(jnp.int32, shape, len(shape) - 2)
    return jnp.where(sub >= 4, sub - 4, sub)


def turn(value, shift, axis):
    return pltpu.roll(value, shift % value.shape[axis], axis)


def gather_planes(values, plane):
    slot = slots(values[0].shape)
    out = turn(values[-1], len(values) - 1 - plane, 0)
    for c in reversed(range(len(values) - 1)):
        out = jnp.where(slot == c, turn(values[c], c - plane, 0), out)
    return out


def collect(values, plane):
    sub = lax.broadcasted_iota(jnp.int32, values[0].shape, 0)
    out = turn(values[0], -plane, 0)
    for n in range(1, 8):
        j, h = n // 2, n % 2
        out = jnp.where(sub == n, turn(values[j], n - 4 * h - plane, 0), out)
    return out


def shared(rho, m, b):
    inv = 1.0 / rho
    return [x * inv for x in m], rho + 0.5 * (b[0] * b[0] + b[1] * b[1] + b[2] * b[2])


def fluxes(v, total, m, b, k):
    push = [m[i] * v[k] - b[i] * b[k] + (total if i == k else 0.0) for i in range(3)]
    turned = [None if i == k else v[k] * b[i] - b[k] * v[i] for i in range(3)]
    return push + turned


def first_kernel(cell_ref, count_ref, rho_a, mom_a, mag_a, pot_a, rho_z, mom_z, mag_z, pot_z, ev_ref, first_ref, last_ref):
    shape = (1, ev_ref.shape[2])
    lane = lax.broadcasted_iota(jnp.int32, shape, 1)
    row = jnp.zeros(shape, jnp.int32)
    for e in range(count_ref.shape[0]):
        for i in range(4):
            row = jnp.where(lane == 4 * e + i, cell_ref[e, i] if i < 3 else count_ref[e], row)

    def copy(d, _):
        ev_ref[d] = row
        return 0

    lax.fori_loop(0, ev_ref.shape[0], copy, 0)
    for ref, rho, mom, mag, pot, skip in (
        (first_ref, rho_a, mom_a, mag_a, pot_a, 0), (last_ref, rho_z, mom_z, mag_z, pot_z, pot_z.shape[0] - 2),
    ):
        for j in range(2):
            ref[0, j] = rho[0, j]
            for c in range(3):
                ref[1 + c, j] = mom[c, 0, j]
                ref[4 + c, j] = mag[c, 0, j]
            ref[7, j] = jnp.broadcast_to(pot[skip + j : skip + j + 1], ref.shape[2:])


def pack_kernel(rho_ref, mz_ref, after_ref, up_ref, down_ref):
    def body(g, _):
        rho = [pair(rho_ref, 4 * g + j) for j in range(4)]
        mz = [pair(mz_ref, 0, 4 * g + j) for j in range(4)]
        for i, (values, up, down) in enumerate(((rho, 3, 0), (mz, 3, 0), (mz, 2, 1))):
            up_ref[g, i] = collect(values, up)
            down_ref[g, i] = collect(values, down)
        return 0

    lax.fori_loop(0, rho_ref.shape[1] // 4, body, 0)


def write_messages(up_ref, down_ref, k, g, state):
    fluxes_by, bx = [], []
    for j in range(4):
        r = 4 * g + j
        u = state(j)
        near = [u[1], u[2], u[5], u[6]]
        up_ref[k, r] = gather_planes(near, 3)
        down_ref[k, r] = gather_planes(near, 0)
        f = fluxes(*shared(u[0], u[1:4], u[4:7]), u[1:4], u[4:7], 2)
        up_ref[k, 8 + r] = gather_planes(f[:4], 2)
        down_ref[k, 8 + r] = gather_planes(f[:4], 1)
        fluxes_by.append(f[4])
        bx.append(u[4])
    up_ref[k, 16 + g] = collect(fluxes_by, 2)
    down_ref[k, 16 + g] = collect(fluxes_by, 1)
    up_ref[k, 18 + g] = collect(bx, 3)
    down_ref[k, 18 + g] = collect(bx, 0)


def state_kernel(
    ev_ref, rho_ref, mom_ref, mag_ref, pot_ref, before_ref, after_ref, rho_l, mom_l, mag_l, pot_l,
    rho_h, mom_h, mag_h, pot_h, u_out, edge_out, sb_out, sa_out, up_ref, down_ref, s_ref, sb_ref, sa_ref, *,
    depth, count, per_device, steps,
):
    half, ny = 8 * steps, s_ref.shape[3]
    step_id = pl.program_id(0)

    @pl.when(step_id == 0)
    def _():
        deposit(ev_ref, s_ref, sb_ref, sa_ref, depth, per_device, half)
        pieces = lambda rho, mom, mag, pot, j: (
            [rho[0, j]] + [mom[c, 0, j] for c in range(3)] + [mag[c, 0, j] for c in range(3)]
            + [jnp.broadcast_to(pot, (4, ny))]
        )
        for j in range(2):
            low = pieces(rho_l, mom_l, mag_l, pot_l[0, 6 + j : 7 + j], j)
            high = pieces(rho_h, mom_h, mag_h, pot_h[0, j : j + 1], j)
            for f in range(8):
                left = jnp.concatenate([before_ref[f, j], low[f]], axis=0)
                right = jnp.concatenate([high[f], after_ref[f, j]], axis=0)
                edge_out[f, j] = left + s_ref[f, j] if f < 4 else left
                edge_out[f, 2 + j] = right + s_ref[f, half + 2 + j] if f < 4 else right

    start = step_id * 8

    def body(g, send):
        def state(j):
            r = 4 * g + j
            q = start + r + 2
            sb_out[r] = sb_ref[q]
            sa_out[r] = sa_ref[q]
            u = [pair(rho_ref, r) + s_ref[0, q]]
            u += [pair(mom_ref, c, r) + s_ref[1 + c, q] for c in range(3)]
            u += [pair(mag_ref, c, r) for c in range(3)]
            for f in range(7):
                u_out[f, r] = u[f]
            rows = [jnp.broadcast_to(pot_ref[h, pl.ds(r, 1), :], (4, ny)) for h in range(2)]
            u_out[7, r] = jnp.concatenate(rows, axis=0)
            return u

        if send:
            write_messages(up_ref, down_ref, 0, g, state)
        else:
            for j in range(4):
                state(j)
        return 0

    @pl.when(step_id < count)
    def _():
        lax.fori_loop(0, 2, lambda g, _: body(g, True), 0)

    @pl.when(step_id >= count)
    def _():
        lax.fori_loop(0, 2, lambda g, _: body(g, False), 0)


def deposit(ev_ref, s_ref, sb_ref, sa_ref, depth, per_device, half):
    ny = s_ref.shape[3]
    rows, events = 2 * half, ev_ref.shape[0] * per_device
    row_start, plane_start = lax.axis_index("xy") * rows, lax.axis_index("gz") * 4
    s_ref[...] = jnp.zeros_like(s_ref)
    sb_ref[...] = jnp.zeros_like(sb_ref)
    sa_ref[...] = jnp.zeros_like(sa_ref)

    shape = (8, 8, 128)
    slot = slots(shape)
    sub = lax.broadcasted_iota(jnp.int32, shape, 1)
    step = lax.broadcasted_iota(jnp.int32, shape, 0)
    lane = lax.broadcasted_iota(jnp.int32, shape, 2)

    def wrapped(distance, size):
        distance = jnp.where(distance >= size // 2, distance - size, distance)
        return jnp.where(distance < -(size // 2), distance + size, distance)

    def event(e, _):
        device, slot_id = (e, 0) if per_device == 1 else (lax.div(e, per_device), lax.rem(e, per_device))
        row, col, plane, count = (ev_ref[device, 0, 4 * slot_id + i] for i in range(4))
        rel = wrapped(row - row_start - half, NX)
        rel = rel + half

        @pl.when((count > 0) & (rel > -2 - RADIUS) & (rel < rows + 2 + RADIUS))
        def _():
            base = plane_start - plane
            dz = wrapped(slot + base, depth).astype(jnp.float32)
            dzb = wrapped(jnp.where(slot == 2, -2, -1) + base, depth).astype(jnp.float32)
            dza = wrapped(jnp.where(slot == 2, 5, 4) + base, depth).astype(jnp.float32)
            share = lambda d: jnp.where(slot == 0, 1.0, jnp.where(slot == 3, 0.0, IMPULSE * d))
            first = jnp.bitwise_and(col - RADIUS, ny - 1) // 128
            second = jnp.bitwise_and(col + RADIUS - 1, ny - 1) // 128

            def tile(t, _):
                index = jnp.where(t == 0, first, second)
                lanes = pl.ds(pl.multiple_of(index * 128, 128), 128)
                dy = wrapped(lane + index * 128 - col, ny).astype(jnp.float32)
                dy2 = dy * dy
                for h in range(2):
                    weight = jnp.where((sub >= 4) == (h == 1), count, 0).astype(jnp.float32)
                    low = jnp.clip(rel - RADIUS + 1 - h * half + 2, 0, s_ref.shape[1]) // 8
                    high = (jnp.clip(rel + RADIUS - 1 - h * half + 2, -1, half + 3) + 8) // 8

                    def chunk(n, _):
                        q = pl.ds(n * 8, 8)
                        dx = (step + (n * 8 - 2 + h * half - rel)).astype(jnp.float32)
                        flat = dx * dx + dy2
                        size = lambda d: jnp.maximum(1.0 - (flat + d * d) * (1.0 / (RADIUS * RADIUS)), 0.0) * weight
                        w = size(dz)
                        s_ref[0, q, :, lanes] += w
                        w = w * IMPULSE
                        s_ref[1, q, :, lanes] += w * dx
                        s_ref[2, q, :, lanes] += w * dy
                        s_ref[3, q, :, lanes] += w * dz
                        sb_ref[q, :, lanes] += size(dzb) * share(dzb)
                        sa_ref[q, :, lanes] += size(dza) * share(dza)
                        return 0

                    lax.fori_loop(low, high, chunk, 0)
                return 0

            lax.fori_loop(0, jnp.where(first == second, 1, 2), tile, 0)

        return 0

    lax.fori_loop(0, events, event, 0)


def ends(below, above, c):
    return jnp.where(slots(below.shape) == 3, turn(above, 3 - c, 0), turn(below, -c, 0))


def along_y(f, b):
    near, far = NEAR * f, FAR * f
    return turn(b + near, 1, 1) + turn(b - near, -1, 1) + turn(far, -2, 1) - turn(far, 2, 1)


def along_z(f, b, near_f, near_u, far_f):
    slot = slots(b.shape)
    first, last = slot == 0, slot == 3
    outer = DIFFUSION * near_u
    if f is None:
        return jnp.where(first, outer, turn(b, 1, 0)) + jnp.where(last, outer, turn(b, -1, 0))
    near = NEAR * f
    outer += jnp.where(first, NEAR, -NEAR) * near_f
    out = jnp.where(first, outer, turn(b + near, 1, 0)) + jnp.where(last, outer, turn(b - near, -1, 0))
    beyond = jnp.where(slot == 1, turn(near_f, 1, 0), jnp.where(slot == 2, turn(near_f, -1, 0), far_f))
    return out + FAR * (jnp.where(slot <= 1, turn(f, -2, 0), beyond) - jnp.where(slot >= 2, turn(f, 2, 0), beyond))


def fetch(u_hbm, edge_hbm, u_ref, sem, first):
    fields, total = u_ref.shape[:2]
    half = u_hbm.shape[1]
    low, high = max(first - 2, 0), min(first + total - 2, half)
    copies = [pltpu.make_async_copy(u_hbm.at[:fields, low:high], u_ref.at[:, low - first + 2 : high - first + 2], sem.at[0])]
    if first == 0:
        copies.append(pltpu.make_async_copy(edge_hbm.at[:fields, 0:2], u_ref.at[:, 0:2], sem.at[1]))
    if first + total - 4 == half:
        copies.append(pltpu.make_async_copy(edge_hbm.at[:fields, 2:4], u_ref.at[:, total - 2 : total], sem.at[2]))
    for copy in copies:
        copy.start()
    for copy in copies:
        copy.wait()


def density_kernel(
    u_hbm, edge_hbm, below_ref, above_ref, sb_ref, sa_ref, order_ref, high_ref, low_ref, out_ref, wave_ref,
    rho_out, mz_out, *rest,
):
    *parcel, d_ref, u_ref, b_ref, sem = rest
    half = u_hbm.shape[1]
    field = None
    if parcel:
        field = pltpu.make_async_copy(u_hbm.at[4:7, half - b_ref.shape[1] :], b_ref, sem.at[3])
        field.start()
    fetch(u_hbm, edge_hbm, u_ref, sem, 0)
    rows = 2 * half

    def row(p, g, j):
        rho, my, mz = u_ref[0, p + 2], u_ref[2, p + 2], u_ref[3, p + 2]
        sb, sa = sb_ref[p], sa_ref[p]
        halo = [last_plane(below_ref[g, i], above_ref[g, i], j) + ends(sb, sa, i) for i in range(3)]
        rho_out[p], mz_out[p] = halo[:2]
        b = DIFFUSION * rho
        new = rho * (1.0 - 6.0 * DIFFUSION)
        new += DIFFUSION * (u_ref[0, p + 1] + u_ref[0, p + 3])
        new += NEAR * (u_ref[1, p + 1] - u_ref[1, p + 3]) + FAR * (u_ref[1, p + 4] - u_ref[1, p])
        new += along_y(my, b)
        new += along_z(mz, b, halo[1], halo[0], halo[2])
        unpair(out_ref, new, p)
        d_ref[pl.ds(pl.multiple_of(p * 8, 8), 8), :] = new

    def body(g, _):
        for j in range(4):
            row(4 * g + j, g, j)
        return 0

    lax.fori_loop(0, half // 4, body, 0)
    d = d_ref[...]
    order = order_ref[...]
    dot = functools.partial(jnp.dot, preferred_element_type=jnp.float32)
    high = d.astype(jnp.bfloat16)
    low = (d - high.astype(jnp.float32)).astype(jnp.bfloat16)
    high = dot(order, high).astype(jnp.bfloat16)
    low = dot(order, low).astype(jnp.bfloat16)
    for part in range(2):
        c_high, c_low = high_ref[part], low_ref[part]
        wave = dot(high, c_high) + dot(high, c_low) + dot(low, c_high)
        peers, band = wave_ref.shape[0], wave_ref.shape[4]
        for j in range(peers):
            for z in range(4):
                wave_ref[j, part, z] = wave[z * rows : (z + 1) * rows, j * band : (j + 1) * band]
    if not parcel:
        return
    field.wait()
    first = half - b_ref.shape[1]

    def messages(n, _):
        r = n * 4
        state = lambda j: [u_ref[f, first + r + j + 2] for f in range(4)] + [b_ref[c, r + j] for c in range(3)]
        write_messages(*parcel, n // 2, n % 2, state)
        return 0

    lax.fori_loop(0, b_ref.shape[1] // 4, messages, 0)


def last_plane(below, above, j):
    sub = lax.broadcasted_iota(jnp.int32, below.shape, 0)
    out = turn(below, -2 * j, 0)
    out = jnp.where(sub == 3, turn(above, 3 - 2 * j, 0), out)
    out = jnp.where(sub == 4, turn(below, 3 - 2 * j, 0), out)
    return jnp.where(sub == 7, turn(above, 6 - 2 * j, 0), out)


def halo_planes(rho_ref, mz_ref, from_below, from_above, r, g, j):
    bn, an, bf, af = from_below[0, r], from_above[0, r], from_below[0, 8 + r], from_above[0, 8 + r]
    hm = [ends(bn, an, 0), ends(bn, an, 1), mz_ref[r]]
    hb = [last_plane(from_below[0, 18 + g], from_above[0, 18 + g], j), ends(bn, an, 2), ends(bn, an, 3)]
    fh = fluxes(*shared(rho_ref[r], hm, hb), hm, hb, 2)
    halo = hm + hb
    far = [ends(bf, af, c) for c in range(4)] + [last_plane(from_below[0, 16 + g], from_above[0, 16 + g], j), None]
    return fh, halo, far


def halo_kernel(rho_ref, mz_ref, from_below, from_above, mom_in, mag_in, *rest):
    mom_ref, mag_ref = rest[-2:]

    def row(r, g, j):
        fh, halo, far = halo_planes(rho_ref, mz_ref, from_below, from_above, r, g, j)
        slot = slots(halo[0].shape)
        first, last = slot == 0, slot == 3
        for c in range(6):
            add = DIFFUSION * halo[c]
            if fh[c] is not None:
                add += jnp.where(first, NEAR, -NEAR) * fh[c]
            add = jnp.where(first | last, add, 0.0)
            if fh[c] is not None:
                beyond = jnp.where(slot == 1, turn(fh[c], 1, 0), jnp.where(slot == 2, turn(fh[c], -1, 0), far[c]))
                add += jnp.where(slot >= 2, FAR, -FAR) * beyond
            if c < 3:
                unpair(mom_ref, pair(mom_in, c, r) + add, c, r)
            else:
                unpair(mag_ref, pair(mag_in, c - 3, r) + add, c - 3, r)

    def body(g, _):
        for j in range(4):
            row(4 * g + j, g, j)
        return 0

    lax.fori_loop(0, 2, body, 0)


def main_kernel(u_hbm, edge_hbm, rho_ref, mz_ref, from_below, from_above, *rest, first, inner):
    mom_ref, mag_ref, u_ref, f_ref, sem = rest[-5:]
    chunk, total, half = 8, u_ref.shape[1], u_hbm.shape[1]
    step_id = pl.program_id(0)
    start = step_id * chunk
    kept = (0, 1, 2, 4, 5)

    def copies(i):
        low = 0 if i == 0 else chunk * i + 4
        high = chunk * (i + 1) + 4
        a, b = max(first - 2 + low, 0), min(first - 2 + high, half)
        at = a - first + 2
        result = [(u_hbm.at[:, a:b], u_ref.at[:, at : at + b - a], sem.at[i])]
        if first - 2 + low < 0:
            result.append((edge_hbm.at[:, 0:2], u_ref.at[:, 0:2], sem.at[total // chunk]))
        if first - 2 + high > half:
            result.append((edge_hbm.at[:, 2:4], u_ref.at[:, total - 2 : total], sem.at[total // chunk + 1]))
        return [pltpu.make_async_copy(*c) for c in result]

    @pl.when(step_id == 0)
    def _():
        for i in range(total // chunk):
            for copy in copies(i):
                copy.start()

    for i in range(total // chunk):

        @pl.when(step_id == i)
        def _(i=i):
            for copy in copies(i):
                copy.wait()

    def fx(q, _):
        u = [u_ref[f, q] for f in range(7)]
        f = fluxes(*shared(u[0], u[1:4], u[4:7]), u[1:4], u[4:7], 0)
        for i, c in enumerate(kept):
            f_ref[i, q] = f[c]
        return 0

    lax.fori_loop(jnp.where(step_id == 0, 0, start + 4), start + chunk + 4, fx, 0)

    def row(r, g, j):
        q = start + r + 2
        u = [u_ref[f, q] for f in range(7)]
        v, pressure = shared(u[0], u[1:4], u[4:7])
        fy = fluxes(v, pressure, u[1:4], u[4:7], 1)
        fz = fluxes(v, pressure, u[1:4], u[4:7], 2)
        if inner:
            zero = jnp.zeros_like(u[0])
            fh = halo = far = [zero] * 5 + [None]
            halo = [zero] * 6
        else:
            fh, halo, far = halo_planes(rho_ref, mz_ref, from_below, from_above, r, g, j)
        for c in range(6):
            field = u[c + 1]
            new = field * (1.0 - 6.0 * DIFFUSION)
            new += DIFFUSION * (u_ref[c + 1, q - 1] + u_ref[c + 1, q + 1])
            if c in kept:
                i = kept.index(c)
                new += NEAR * (f_ref[i, q - 1] - f_ref[i, q + 1]) + FAR * (f_ref[i, q + 2] - f_ref[i, q - 2])
            b = DIFFUSION * field
            if fy[c] is None:
                new += turn(b, 1, 1) + turn(b, -1, 1)
            else:
                new += along_y(fy[c], b)
            new += along_z(fz[c], b, fh[c], halo[c], far[c])
            if c == 0:
                slope = NEAR * (u_ref[7, q - 1] - u_ref[7, q + 1]) + FAR * (u_ref[7, q + 2] - u_ref[7, q - 2])
                new += u[0] * slope
            if c == 1:
                potential = u_ref[7, q]
                slope = NEAR * (turn(potential, 1, 1) - turn(potential, -1, 1))
                new += u[0] * (slope + FAR * (turn(potential, -2, 1) - turn(potential, 2, 1)))
            if c < 3:
                unpair(mom_ref, new, c, r)
            else:
                unpair(mag_ref, new, c - 3, r)

    def body(g, _):
        for j in range(4):
            row(4 * g + j, g, j)
        return 0

    lax.fori_loop(0, chunk // 4, body, 0)


def modes_kernel(w_ref, ch_ref, cl_ref, mh_ref, ml_ref, ph_ref, pl_ref, out_ref, x_ref, *, turned):
    dot = functools.partial(jnp.dot, preferred_element_type=jnp.float32)
    planes, band, nx = out_ref.shape[1:]

    def gathered(part):
        if turned:
            x = jnp.concatenate([w_ref[part, z] for z in range(planes)], axis=0)
        else:
            width = w_ref.shape[3]
            for s in range(w_ref.shape[0]):
                for z in range(planes):
                    x_ref[z * band : (z + 1) * band, s * width : (s + 1) * width] = w_ref[s, part, z].T
            x = x_ref[...]
        return x

    def split(x):
        high = x.astype(jnp.bfloat16)
        return high, (x - high.astype(jnp.float32)).astype(jnp.bfloat16)

    re, im = gathered(0), gathered(1)
    times = lambda x, h, l: dot(x[0], h[...]) + dot(x[0], l[...]) + dot(x[1], h[...])
    scale = 1.0 / math.sqrt(NX * nx)
    shape = (band, nx)
    ky = lax.broadcasted_iota(jnp.int32, shape, 0) + lax.axis_index("xy") * band
    kx = lax.broadcasted_iota(jnp.int32, shape, 1)
    keep = jnp.where((ky == 0) & (kx == 0), 0.0, scale)
    both = times(split(re + im), ch_ref, cl_ref)
    out_re = both - times(split(im), mh_ref, ml_ref)
    out_im = both - times(split(re), ph_ref, pl_ref)
    for z in range(planes):
        out_ref[0, z] = out_re[z * band : (z + 1) * band] * keep
        out_ref[1, z] = out_im[z * band : (z + 1) * band] * keep


def cost(flops, bytes_accessed):
    return pl.CostEstimate(flops=int(flops), bytes_accessed=int(bytes_accessed), transcendentals=0)


def tables(size):
    angle = (np.outer(np.arange(size), np.arange(size)) % size) * (2.0 * np.pi / size)
    cosine, sine = np.cos(angle), np.sin(angle)
    result = []
    for table in (cosine, sine, cosine - sine, cosine + sine):
        high = table.astype(np.float32).astype(ml_dtypes.bfloat16)
        low = (table - high.astype(np.float64)).astype(np.float32).astype(ml_dtypes.bfloat16)
        result += [high, low]
    return result


def row_order(half):
    matrix = np.zeros((8 * half, 8 * half), np.float32)
    for z in range(4):
        for h in range(2):
            for p in range(half):
                matrix[(z * 2 + h) * half + p, p * 8 + h * 4 + z] = 1.0
    return matrix.astype(ml_dtypes.bfloat16)


def shift(block, axis, step):
    n = lax.axis_size(axis)
    return lax.ppermute(block, axis, [(i, (i + step) % n) for i in range(n)])


def on_device(density, momentum, magnetic, arm_potential, sn_cells, sn_counts):
    rows, planes, ny = density.shape
    half = rows // 2
    layers, across = lax.axis_size("gz"), lax.axis_size("xy")
    devices = layers * across
    tile_row, tile_plane = lax.axis_index("xy"), lax.axis_index("gz")
    field = rows * planes * ny
    f32 = jnp.float32
    shape = jax.ShapeDtypeStruct
    whole = pl.BlockSpec(memory_space=pltpu.VMEM)
    smem = pl.BlockSpec(memory_space=pltpu.SMEM)
    params = pltpu.CompilerParams(vmem_limit_bytes=VMEM)
    message = shape((2, half, planes, ny), f32)
    tile = shape((half, 8, ny), f32)
    steps = half // 8
    counts = (steps - steps // 2, steps // 2) if steps >= 2 else (steps,)

    slots_here = sn_cells.shape[0]
    rho = density.reshape(2, half, planes, ny)
    mom = momentum.reshape(3, 2, half, planes, ny)
    mag = magnetic.reshape(3, 2, half, planes, ny)

    pot = arm_potential.reshape(2, half, ny)
    edges = shape((8, 2, planes, ny), f32)
    mine = shape((devices, 1, -(-4 * slots_here // 128) * 128), jnp.int32)
    full = lambda s: pl.BlockSpec(s, lambda i: (0,) * len(s))
    mine, first_rows, last_rows = pl.pallas_call(
        first_kernel,
        grid=(1,),
        in_specs=[smem, smem] + [
            spec
            for h, k in ((0, 0), (1, half // 2 - 1))
            for spec in (
                pl.BlockSpec((1, 2, planes, ny), lambda i, h=h, k=k: (h, k, 0, 0)),
                pl.BlockSpec((3, 1, 2, planes, ny), lambda i, h=h, k=k: (0, h, k, 0, 0)),
                pl.BlockSpec((3, 1, 2, planes, ny), lambda i, h=h, k=k: (0, h, k, 0, 0)),
                pl.BlockSpec((8, ny), lambda i, h=h: (h * (rows // 8 - 1), 0)),
            )
        ],
        out_specs=[full(mine.shape)] + [full(edges.shape)] * 2,
        out_shape=[mine] + [edges] * 2,
        compiler_params=params,
        cost_estimate=cost(*PACK_COST),
        name="first",
    )(sn_cells, sn_counts, *[rho, mom, mag, arm_potential] * 2)
    events = lax.all_to_all(mine, ("gz", "xy"), split_axis=0, concat_axis=0, tiled=True)
    before, after = shift(last_rows, "xy", 1), shift(first_rows, "xy", -1)

    some = math.gcd(half, 16)
    up, down = pl.pallas_call(
        pack_kernel,
        grid=(half // some,),
        in_specs=[pl.BlockSpec((2, some, planes, ny), lambda i: (0, i, 0, 0))] + [
            pl.BlockSpec((1, 2, some, planes, ny), lambda i, f=f: (f, 0, i, 0, 0)) for f in (2,)
        ] + [pl.BlockSpec(memory_space=pl.ANY)],
        out_specs=[pl.BlockSpec((some // 4, 3, 8, ny), lambda i: (i, 0, 0, 0))] * 2,
        out_shape=[shape((half // 4, 3, 8, ny), f32)] * 2,
        compiler_params=params,
        cost_estimate=cost(*PACK_COST),
        name="pack",
    )(rho, mom, mine)
    below_a, above_a = shift(up, "gz", 1), shift(down, "gz", -1)

    parcels = [shape((n, 20, 8, ny), f32) for n in counts]
    side = pltpu.VMEM((half + 8, 8, ny), f32)
    begins = [sum(counts[:i]) for i in range(len(counts))]
    parcel = pl.BlockSpec((1, 20, 8, ny), lambda i: (jnp.minimum(i, counts[0] - 1), 0, 0, 0))
    eight = pl.BlockSpec((8, 8, ny), lambda i: (i, 0, 0))
    middle = [
        spec
        for h, k in ((0, steps - 1), (1, 0))
        for spec in (
            pl.BlockSpec((1, 2, planes, ny), lambda i, h=h, k=k: (h, k * 4 + 3 * (1 - h), 0, 0)),
            pl.BlockSpec((3, 1, 2, planes, ny), lambda i, h=h, k=k: (0, h, k * 4 + 3 * (1 - h), 0, 0)),
            pl.BlockSpec((3, 1, 2, planes, ny), lambda i, h=h, k=k: (0, h, k * 4 + 3 * (1 - h), 0, 0)),
            pl.BlockSpec((1, 8, ny), lambda i, h=h, k=k: (h, k, 0)),
        )
    ]
    rows_of = lambda n: pl.BlockSpec((n, 2, 8, planes, ny), lambda i: (0, 0, i, 0, 0))
    state, edge, sb, sa, up_0, down_0 = pl.pallas_call(
        functools.partial(state_kernel, depth=planes * layers, count=counts[0], per_device=slots_here, steps=steps),
        grid=(steps,),
        in_specs=[
            smem, pl.BlockSpec((2, 8, planes, ny), lambda i: (0, i, 0, 0)), rows_of(3), rows_of(3),
            pl.BlockSpec((2, 8, ny), lambda i: (0, i, 0)), full(edges.shape), full(edges.shape),
        ] + middle,
        out_specs=[pl.BlockSpec((8, 8, 8, ny), lambda i: (0, i, 0, 0)), full((8, 4, 8, ny)), eight, eight, parcel, parcel],
        out_shape=[shape((8, half, 8, ny), f32), shape((8, 4, 8, ny), f32), tile, tile, parcels[0], parcels[0]],
        scratch_shapes=[pltpu.VMEM((4, half + 8, 8, ny), f32), side, side],
        compiler_params=params,
        cost_estimate=cost(*STATE_COST),
        name="state",
    )(events, rho, mom, mag, pot, before, after, *[rho, mom, mag, pot] * 2)
    parcels_below, parcels_above = [shift(up_0, "gz", 1)], [shift(down_0, "gz", -1)]

    cos_high, cos_low, sin_high, sin_low = tables(ny)[:4]
    turns = tables(NX)
    band = ny // across
    turned = band % 128 != 0 or rows % 128 != 0
    hbm = pl.BlockSpec(memory_space=pl.ANY)
    more = parcels[1:] * 2
    new_density, wave, rho_halo, mz_halo, *messages = pl.pallas_call(
        density_kernel,
        in_specs=[hbm, hbm] + [whole] * 7,
        out_specs=[whole] * (4 + len(more)),
        out_shape=[message, shape((across, 2, planes, rows, band), f32), tile, tile, *more],
        scratch_shapes=[
            pltpu.VMEM((8 * half, ny), f32), pltpu.VMEM((4, half + 4, 8, ny), f32),
            pltpu.VMEM((3, counts[-1] * 8, 8, ny), f32), pltpu.SemaphoreType.DMA((4,)),
        ],
        compiler_params=params,
        cost_estimate=cost(*DENSITY_COST),
        name="density",
    )(
        state, edge, below_a, above_a, sb, sa, row_order(half),
        np.stack([cos_high, -sin_high]), np.stack([cos_low, -sin_low]),
    )

    if messages:
        parcels_below.append(shift(messages[0], "gz", 1))
        parcels_above.append(shift(messages[1], "gz", -1))
    portion = lax.all_to_all(wave, "xy", split_axis=0, concat_axis=0, tiled=True)
    if turned:
        portion = portion.transpose(1, 2, 4, 0, 3).reshape(2, planes, band, NX)
    modes = pl.pallas_call(
        functools.partial(modes_kernel, turned=turned),
        in_specs=[whole] * 7,
        out_specs=whole,
        out_shape=shape((2, planes, band, NX), f32),
        scratch_shapes=[pltpu.VMEM((planes * band, NX), f32)],
        compiler_params=params,
        cost_estimate=cost(*MODES_COST),
        name="modes",
    )(portion, *turns[:2], *turns[4:])
    results = [shape((3, 2, half, planes, ny), f32)] * 2
    three = lambda b: pl.BlockSpec((3, 2, 8, planes, ny), lambda k: (0, 0, b + k, 0, 0))
    here = lambda b: pl.BlockSpec((8, 8, ny), lambda k: (b + k, 0, 0))
    parcel = pl.BlockSpec((1, 20, 8, ny), lambda k: (k, 0, 0, 0))
    wide = pltpu.CompilerParams(vmem_limit_bytes=62 * 1024 * 1024)

    def main(i, inner, name, *new):
        n, b = counts[i], begins[i]
        halos = [hbm] * 4 if inner else [here(b)] * 2 + [parcel] * 2
        parts = (rho_halo, mz_halo) if inner else (parcels_below[i], parcels_above[i])
        return pl.pallas_call(
            functools.partial(main_kernel, first=b * 8, inner=inner),
            grid=(n,),
            in_specs=[hbm, hbm] + halos + [hbm] * len(new),
            out_specs=[three(b), three(b)],
            out_shape=results,
            scratch_shapes=[
                pltpu.VMEM((8, n * 8 + 4, 8, ny), f32), pltpu.VMEM((5, n * 8 + 4, 8, ny), f32),
                pltpu.SemaphoreType.DMA((n + 2,)),
            ],
            input_output_aliases={6: 0, 7: 1} if new else {},
            compiler_params=wide,
            cost_estimate=cost(*MAIN_COST),
            name=name,
        )(state, edge, rho_halo, mz_halo, *parts, *new)

    if len(counts) == 1:
        new = main(0, False, "main0")
    else:
        new = main(0, False, "main0", *main(1, True, "inner1"))
        n, b = counts[1], begins[1]
        new = pl.pallas_call(
            halo_kernel,
            grid=(n,),
            in_specs=[here(b)] * 2 + [parcel] * 2 + [three(b)] * 2 + [hbm],
            out_specs=[three(b)] * 2,
            out_shape=results,
            input_output_aliases={4: 0, 5: 1},
            compiler_params=wide,
            cost_estimate=cost(*MAIN_COST),
            name="halo1",
        )(rho_halo, mz_halo, parcels_below[1], parcels_above[1], *new, modes)
    new_mom, new_mag = new

    return (
        new_density.reshape(rows, planes, ny),
        new_mom.reshape(3, rows, planes, ny),
        new_mag.reshape(3, rows, planes, ny),
        modes,
    )


def solution(mesh):
    in_specs = (
        P("xy", "gz", None),
        P(None, "xy", "gz", None),
        P(None, "xy", "gz", None),
        P("xy", None),
        P(("gz", "xy"), None),
        P(("gz", "xy")),
    )
    out_specs = (
        P("xy", "gz", None),
        P(None, "xy", "gz", None),
        P(None, "xy", "gz", None),
        P(None, "gz", "xy", None),
    )
    return jax.shard_map(
        on_device, mesh=mesh, in_specs=in_specs, out_specs=out_specs, check_vma=False
    )
```

```python
import functools
import math

import jax
import jax.numpy as jnp
import ml_dtypes
import numpy as np
from jax import lax
from jax.experimental import pallas as pl
from jax.experimental.pallas import tpu as pltpu
from jax.sharding import PartitionSpec as P

NX = 512
RADIUS = 16
IMPULSE = 2.0 / 16
TIME_STEP = 0.1
DIFFUSION = 0.05
NEAR = 8.0 * TIME_STEP / 12.0
FAR = TIME_STEP / 12.0
VMEM = 62 * 1024 * 1024
PACK_COST = MODES_COST = (1e6, 1e5)
STATE_COST = DENSITY_COST = (1e12, 4e9)
MAIN_COST = (1e12, 4e9)


def pair(ref, *index):
    return jnp.concatenate([ref[(*index[:-1], 0, index[-1])], ref[(*index[:-1], 1, index[-1])]], axis=0)


def unpair(ref, value, *index):
    ref[(*index[:-1], 0, index[-1])] = value[:4]
    ref[(*index[:-1], 1, index[-1])] = value[4:]


def slots(shape):
    sub = lax.broadcasted_iota(jnp.int32, shape, len(shape) - 2)
    return jnp.where(sub >= 4, sub - 4, sub)


def turn(value, shift, axis):
    return pltpu.roll(value, shift % value.shape[axis], axis)


def gather_planes(values, plane):
    slot = slots(values[0].shape)
    out = turn(values[-1], len(values) - 1 - plane, 0)
    for c in reversed(range(len(values) - 1)):
        out = jnp.where(slot == c, turn(values[c], c - plane, 0), out)
    return out


def collect(values, plane):
    sub = lax.broadcasted_iota(jnp.int32, values[0].shape, 0)
    out = turn(values[0], -plane, 0)
    for n in range(1, 8):
        j, h = n // 2, n % 2
        out = jnp.where(sub == n, turn(values[j], n - 4 * h - plane, 0), out)
    return out


def shared(rho, m, b):
    inv = 1.0 / rho
    return [x * inv for x in m], rho + 0.5 * (b[0] * b[0] + b[1] * b[1] + b[2] * b[2])


def fluxes(v, total, m, b, k):
    push = [m[i] * v[k] - b[i] * b[k] + (total if i == k else 0.0) for i in range(3)]
    turned = [None if i == k else v[k] * b[i] - b[k] * v[i] for i in range(3)]
    return push + turned


def first_kernel(cell_ref, count_ref, rho_a, mom_a, mag_a, pot_a, rho_z, mom_z, mag_z, pot_z, ev_ref, first_ref, last_ref):
    shape = (1, ev_ref.shape[2])
    lane = lax.broadcasted_iota(jnp.int32, shape, 1)
    row = jnp.zeros(shape, jnp.int32)
    for e in range(count_ref.shape[0]):
        for i in range(4):
            row = jnp.where(lane == 4 * e + i, cell_ref[e, i] if i < 3 else count_ref[e], row)

    def copy(d, _):
        ev_ref[d] = row
        return 0

    lax.fori_loop(0, ev_ref.shape[0], copy, 0)
    for ref, rho, mom, mag, pot, skip in (
        (first_ref, rho_a, mom_a, mag_a, pot_a, 0), (last_ref, rho_z, mom_z, mag_z, pot_z, pot_z.shape[0] - 2),
    ):
        for j in range(2):
            ref[0, j] = rho[0, j]
            for c in range(3):
                ref[1 + c, j] = mom[c, 0, j]
                ref[4 + c, j] = mag[c, 0, j]
            ref[7, j] = jnp.broadcast_to(pot[skip + j : skip + j + 1], ref.shape[2:])


def pack_kernel(rho_ref, mz_ref, after_ref, up_ref, down_ref):
    def body(g, _):
        rho = [pair(rho_ref, 4 * g + j) for j in range(4)]
        mz = [pair(mz_ref, 0, 4 * g + j) for j in range(4)]
        for i, (values, up, down) in enumerate(((rho, 3, 0), (mz, 3, 0), (mz, 2, 1))):
            up_ref[g, i] = collect(values, up)
            down_ref[g, i] = collect(values, down)
        return 0

    lax.fori_loop(0, rho_ref.shape[1] // 4, body, 0)


def write_messages(up_ref, down_ref, k, g, state):
    fluxes_by, bx = [], []
    for j in range(4):
        r = 4 * g + j
        u = state(j)
        near = [u[1], u[2], u[5], u[6]]
        up_ref[k, r] = gather_planes(near, 3)
        down_ref[k, r] = gather_planes(near, 0)
        f = fluxes(*shared(u[0], u[1:4], u[4:7]), u[1:4], u[4:7], 2)
        up_ref[k, 8 + r] = gather_planes(f[:4], 2)
        down_ref[k, 8 + r] = gather_planes(f[:4], 1)
        fluxes_by.append(f[4])
        bx.append(u[4])
    up_ref[k, 16 + g] = collect(fluxes_by, 2)
    down_ref[k, 16 + g] = collect(fluxes_by, 1)
    up_ref[k, 18 + g] = collect(bx, 3)
    down_ref[k, 18 + g] = collect(bx, 0)


def state_kernel(
    ev_ref, rho_ref, mom_ref, mag_ref, pot_ref, before_ref, after_ref, rho_l, mom_l, mag_l, pot_l,
    rho_h, mom_h, mag_h, pot_h, u_out, edge_out, sb_out, sa_out, up_ref, down_ref, s_ref, sb_ref, sa_ref, *,
    depth, count, per_device, steps,
):
    half, ny = 8 * steps, s_ref.shape[3]
    step_id = pl.program_id(0)

    @pl.when(step_id == 0)
    def _():
        deposit(ev_ref, s_ref, sb_ref, sa_ref, depth, per_device, half)
        pieces = lambda rho, mom, mag, pot, j: (
            [rho[0, j]] + [mom[c, 0, j] for c in range(3)] + [mag[c, 0, j] for c in range(3)]
            + [jnp.broadcast_to(pot, (4, ny))]
        )
        for j in range(2):
            low = pieces(rho_l, mom_l, mag_l, pot_l[0, 6 + j : 7 + j], j)
            high = pieces(rho_h, mom_h, mag_h, pot_h[0, j : j + 1], j)
            for f in range(8):
                left = jnp.concatenate([before_ref[f, j], low[f]], axis=0)
                right = jnp.concatenate([high[f], after_ref[f, j]], axis=0)
                edge_out[f, j] = left + s_ref[f, j] if f < 4 else left
                edge_out[f, 2 + j] = right + s_ref[f, half + 2 + j] if f < 4 else right

    start = step_id * 8

    def body(g, send):
        def state(j):
            r = 4 * g + j
            q = start + r + 2
            sb_out[r] = sb_ref[q]
            sa_out[r] = sa_ref[q]
            u = [pair(rho_ref, r) + s_ref[0, q]]
            u += [pair(mom_ref, c, r) + s_ref[1 + c, q] for c in range(3)]
            u += [pair(mag_ref, c, r) for c in range(3)]
            for f in range(7):
                u_out[f, r] = u[f]
            rows = [jnp.broadcast_to(pot_ref[h, pl.ds(r, 1), :], (4, ny)) for h in range(2)]
            u_out[7, r] = jnp.concatenate(rows, axis=0)
            return u

        if send:
            write_messages(up_ref, down_ref, 0, g, state)
        else:
            for j in range(4):
                state(j)
        return 0

    @pl.when(step_id < count)
    def _():
        lax.fori_loop(0, 2, lambda g, _: body(g, True), 0)

    @pl.when(step_id >= count)
    def _():
        lax.fori_loop(0, 2, lambda g, _: body(g, False), 0)


def deposit(ev_ref, s_ref, sb_ref, sa_ref, depth, per_device, half):
    ny = s_ref.shape[3]
    rows, events = 2 * half, ev_ref.shape[0] * per_device
    row_start, plane_start = lax.axis_index("xy") * rows, lax.axis_index("gz") * 4
    s_ref[...] = jnp.zeros_like(s_ref)
    sb_ref[...] = jnp.zeros_like(sb_ref)
    sa_ref[...] = jnp.zeros_like(sa_ref)

    shape = (8, 8, 128)
    slot = slots(shape)
    sub = lax.broadcasted_iota(jnp.int32, shape, 1)
    step = lax.broadcasted_iota(jnp.int32, shape, 0)
    lane = lax.broadcasted_iota(jnp.int32, shape, 2)

    def wrapped(distance, size):
        distance = jnp.where(distance >= size // 2, distance - size, distance)
        return jnp.where(distance < -(size // 2), distance + size, distance)

    def event(e, _):
        device, slot_id = (e, 0) if per_device == 1 else (lax.div(e, per_device), lax.rem(e, per_device))
        row, col, plane, count = (ev_ref[device, 0, 4 * slot_id + i] for i in range(4))
        rel = wrapped(row - row_start - half, NX)
        rel = rel + half

        @pl.when((count > 0) & (rel > -2 - RADIUS) & (rel < rows + 2 + RADIUS))
        def _():
            base = plane_start - plane
            dz = wrapped(slot + base, depth).astype(jnp.float32)
            dzb = wrapped(jnp.where(slot == 2, -2, -1) + base, depth).astype(jnp.float32)
            dza = wrapped(jnp.where(slot == 2, 5, 4) + base, depth).astype(jnp.float32)
            share = lambda d: jnp.where(slot == 0, 1.0, jnp.where(slot == 3, 0.0, IMPULSE * d))
            first = jnp.bitwise_and(col - RADIUS, ny - 1) // 128
            second = jnp.bitwise_and(col + RADIUS - 1, ny - 1) // 128

            def tile(t, _):
                index = jnp.where(t == 0, first, second)
                lanes = pl.ds(pl.multiple_of(index * 128, 128), 128)
                dy = wrapped(lane + index * 128 - col, ny).astype(jnp.float32)
                dy2 = dy * dy
                for h in range(2):
                    weight = jnp.where((sub >= 4) == (h == 1), count, 0).astype(jnp.float32)
                    low = jnp.clip(rel - RADIUS + 1 - h * half + 2, 0, s_ref.shape[1]) // 8
                    high = (jnp.clip(rel + RADIUS - 1 - h * half + 2, -1, half + 3) + 8) // 8

                    def chunk(n, _):
                        q = pl.ds(n * 8, 8)
                        dx = (step + (n * 8 - 2 + h * half - rel)).astype(jnp.float32)
                        flat = dx * dx + dy2
                        size = lambda d: jnp.maximum(1.0 - (flat + d * d) * (1.0 / (RADIUS * RADIUS)), 0.0) * weight
                        w = size(dz)
                        s_ref[0, q, :, lanes] += w
                        w = w * IMPULSE
                        s_ref[1, q, :, lanes] += w * dx
                        s_ref[2, q, :, lanes] += w * dy
                        s_ref[3, q, :, lanes] += w * dz
                        sb_ref[q, :, lanes] += size(dzb) * share(dzb)
                        sa_ref[q, :, lanes] += size(dza) * share(dza)
                        return 0

                    lax.fori_loop(low, high, chunk, 0)
                return 0

            lax.fori_loop(0, jnp.where(first == second, 1, 2), tile, 0)

        return 0

    lax.fori_loop(0, events, event, 0)


def ends(below, above, c):
    return jnp.where(slots(below.shape) == 3, turn(above, 3 - c, 0), turn(below, -c, 0))


def along_y(f, b):
    near, far = NEAR * f, FAR * f
    return turn(b + near, 1, 1) + turn(b - near, -1, 1) + turn(far, -2, 1) - turn(far, 2, 1)


def along_z(f, b, near_f, near_u, far_f):
    slot = slots(b.shape)
    first, last = slot == 0, slot == 3
    outer = DIFFUSION * near_u
    if f is None:
        return jnp.where(first, outer, turn(b, 1, 0)) + jnp.where(last, outer, turn(b, -1, 0))
    near = NEAR * f
    outer += jnp.where(first, NEAR, -NEAR) * near_f
    out = jnp.where(first, outer, turn(b + near, 1, 0)) + jnp.where(last, outer, turn(b - near, -1, 0))
    beyond = jnp.where(slot == 1, turn(near_f, 1, 0), jnp.where(slot == 2, turn(near_f, -1, 0), far_f))
    return out + FAR * (jnp.where(slot <= 1, turn(f, -2, 0), beyond) - jnp.where(slot >= 2, turn(f, 2, 0), beyond))


def fetch(u_hbm, edge_hbm, u_ref, sem, first):
    fields, total = u_ref.shape[:2]
    half = u_hbm.shape[1]
    low, high = max(first - 2, 0), min(first + total - 2, half)
    copies = [pltpu.make_async_copy(u_hbm.at[:fields, low:high], u_ref.at[:, low - first + 2 : high - first + 2], sem.at[0])]
    if first == 0:
        copies.append(pltpu.make_async_copy(edge_hbm.at[:fields, 0:2], u_ref.at[:, 0:2], sem.at[1]))
    if first + total - 4 == half:
        copies.append(pltpu.make_async_copy(edge_hbm.at[:fields, 2:4], u_ref.at[:, total - 2 : total], sem.at[2]))
    for copy in copies:
        copy.start()
    for copy in copies:
        copy.wait()


def density_kernel(
    u_hbm, edge_hbm, below_ref, above_ref, sb_ref, sa_ref, order_ref, high_ref, low_ref, out_ref, wave_ref,
    rho_out, mz_out, *rest,
):
    *parcel, d_ref, u_ref, b_ref, sem = rest
    half = u_hbm.shape[1]
    field = None
    if parcel:
        field = pltpu.make_async_copy(u_hbm.at[4:7, half - b_ref.shape[1] :], b_ref, sem.at[3])
        field.start()
    fetch(u_hbm, edge_hbm, u_ref, sem, 0)
    rows = 2 * half

    def row(p, g, j):
        rho, my, mz = u_ref[0, p + 2], u_ref[2, p + 2], u_ref[3, p + 2]
        sb, sa = sb_ref[p], sa_ref[p]
        halo = [last_plane(below_ref[g, i], above_ref[g, i], j) + ends(sb, sa, i) for i in range(3)]
        rho_out[p], mz_out[p] = halo[:2]
        b = DIFFUSION * rho
        new = rho * (1.0 - 6.0 * DIFFUSION)
        new += DIFFUSION * (u_ref[0, p + 1] + u_ref[0, p + 3])
        new += NEAR * (u_ref[1, p + 1] - u_ref[1, p + 3]) + FAR * (u_ref[1, p + 4] - u_ref[1, p])
        new += along_y(my, b)
        new += along_z(mz, b, halo[1], halo[0], halo[2])
        unpair(out_ref, new, p)
        d_ref[pl.ds(pl.multiple_of(p * 8, 8), 8), :] = new

    def body(g, _):
        for j in range(4):
            row(4 * g + j, g, j)
        return 0

    lax.fori_loop(0, half // 4, body, 0)
    d = d_ref[...]
    order = order_ref[...]
    dot = functools.partial(jnp.dot, preferred_element_type=jnp.float32)
    high = d.astype(jnp.bfloat16)
    low = (d - high.astype(jnp.float32)).astype(jnp.bfloat16)
    high = dot(order, high).astype(jnp.bfloat16)
    low = dot(order, low).astype(jnp.bfloat16)
    for part in range(2):
        c_high, c_low = high_ref[part], low_ref[part]
        wave = dot(high, c_high) + dot(high, c_low) + dot(low, c_high)
        peers, band = wave_ref.shape[0], wave_ref.shape[4]
        for j in range(peers):
            for z in range(4):
                wave_ref[j, part, z] = wave[z * rows : (z + 1) * rows, j * band : (j + 1) * band]
    if not parcel:
        return
    field.wait()
    first = half - b_ref.shape[1]

    def messages(n, _):
        r = n * 4
        state = lambda j: [u_ref[f, first + r + j + 2] for f in range(4)] + [b_ref[c, r + j] for c in range(3)]
        write_messages(*parcel, n // 2, n % 2, state)
        return 0

    lax.fori_loop(0, b_ref.shape[1] // 4, messages, 0)


def last_plane(below, above, j):
    sub = lax.broadcasted_iota(jnp.int32, below.shape, 0)
    out = turn(below, -2 * j, 0)
    out = jnp.where(sub == 3, turn(above, 3 - 2 * j, 0), out)
    out = jnp.where(sub == 4, turn(below, 3 - 2 * j, 0), out)
    return jnp.where(sub == 7, turn(above, 6 - 2 * j, 0), out)


def halo_planes(rho_ref, mz_ref, from_below, from_above, r, g, j):
    bn, an, bf, af = from_below[0, r], from_above[0, r], from_below[0, 8 + r], from_above[0, 8 + r]
    hm = [ends(bn, an, 0), ends(bn, an, 1), mz_ref[r]]
    hb = [last_plane(from_below[0, 18 + g], from_above[0, 18 + g], j), ends(bn, an, 2), ends(bn, an, 3)]
    fh = fluxes(*shared(rho_ref[r], hm, hb), hm, hb, 2)
    halo = hm + hb
    far = [ends(bf, af, c) for c in range(4)] + [last_plane(from_below[0, 16 + g], from_above[0, 16 + g], j), None]
    return fh, halo, far


def halo_kernel(rho_ref, mz_ref, from_below, from_above, mom_in, mag_in, *rest):
    mom_ref, mag_ref = rest[-2:]

    def row(r, g, j):
        fh, halo, far = halo_planes(rho_ref, mz_ref, from_below, from_above, r, g, j)
        slot = slots(halo[0].shape)
        first, last = slot == 0, slot == 3
        for c in range(6):
            add = DIFFUSION * halo[c]
            if fh[c] is not None:
                add += jnp.where(first, NEAR, -NEAR) * fh[c]
            add = jnp.where(first | last, add, 0.0)
            if fh[c] is not None:
                beyond = jnp.where(slot == 1, turn(fh[c], 1, 0), jnp.where(slot == 2, turn(fh[c], -1, 0), far[c]))
                add += jnp.where(slot >= 2, FAR, -FAR) * beyond
            if c < 3:
                unpair(mom_ref, pair(mom_in, c, r) + add, c, r)
            else:
                unpair(mag_ref, pair(mag_in, c - 3, r) + add, c - 3, r)

    def body(g, _):
        for j in range(4):
            row(4 * g + j, g, j)
        return 0

    lax.fori_loop(0, 2, body, 0)


def main_kernel(u_hbm, edge_hbm, rho_ref, mz_ref, from_below, from_above, *rest, first, inner):
    mom_ref, mag_ref, u_ref, f_ref, sem = rest[-5:]
    chunk, total, half = 8, u_ref.shape[1], u_hbm.shape[1]
    step_id = pl.program_id(0)
    start = step_id * chunk
    kept = (0, 1, 2, 4, 5)

    def copies(i):
        low = 0 if i == 0 else chunk * i + 4
        high = chunk * (i + 1) + 4
        a, b = max(first - 2 + low, 0), min(first - 2 + high, half)
        at = a - first + 2
        result = [(u_hbm.at[:, a:b], u_ref.at[:, at : at + b - a], sem.at[i])]
        if first - 2 + low < 0:
            result.append((edge_hbm.at[:, 0:2], u_ref.at[:, 0:2], sem.at[total // chunk]))
        if first - 2 + high > half:
            result.append((edge_hbm.at[:, 2:4], u_ref.at[:, total - 2 : total], sem.at[total // chunk + 1]))
        return [pltpu.make_async_copy(*c) for c in result]

    @pl.when(step_id == 0)
    def _():
        for i in range(total // chunk):
            for copy in copies(i):
                copy.start()

    for i in range(total // chunk):

        @pl.when(step_id == i)
        def _(i=i):
            for copy in copies(i):
                copy.wait()

    def fx(q, _):
        u = [u_ref[f, q] for f in range(7)]
        f = fluxes(*shared(u[0], u[1:4], u[4:7]), u[1:4], u[4:7], 0)
        for i, c in enumerate(kept):
            f_ref[i, q] = f[c]
        return 0

    lax.fori_loop(jnp.where(step_id == 0, 0, start + 4), start + chunk + 4, fx, 0)

    def row(r, g, j):
        q = start + r + 2
        u = [u_ref[f, q] for f in range(7)]
        v, pressure = shared(u[0], u[1:4], u[4:7])
        fy = fluxes(v, pressure, u[1:4], u[4:7], 1)
        fz = fluxes(v, pressure, u[1:4], u[4:7], 2)
        if inner:
            zero = jnp.zeros_like(u[0])
            fh = halo = far = [zero] * 5 + [None]
            halo = [zero] * 6
        else:
            fh, halo, far = halo_planes(rho_ref, mz_ref, from_below, from_above, r, g, j)
        for c in range(6):
            field = u[c + 1]
            new = field * (1.0 - 6.0 * DIFFUSION)
            new += DIFFUSION * (u_ref[c + 1, q - 1] + u_ref[c + 1, q + 1])
            if c in kept:
                i = kept.index(c)
                new += NEAR * (f_ref[i, q - 1] - f_ref[i, q + 1]) + FAR * (f_ref[i, q + 2] - f_ref[i, q - 2])
            b = DIFFUSION * field
            if fy[c] is None:
                new += turn(b, 1, 1) + turn(b, -1, 1)
            else:
                new += along_y(fy[c], b)
            new += along_z(fz[c], b, fh[c], halo[c], far[c])
            if c == 0:
                slope = NEAR * (u_ref[7, q - 1] - u_ref[7, q + 1]) + FAR * (u_ref[7, q + 2] - u_ref[7, q - 2])
                new += u[0] * slope
            if c == 1:
                potential = u_ref[7, q]
                slope = NEAR * (turn(potential, 1, 1) - turn(potential, -1, 1))
                new += u[0] * (slope + FAR * (turn(potential, -2, 1) - turn(potential, 2, 1)))
            if c < 3:
                unpair(mom_ref, new, c, r)
            else:
                unpair(mag_ref, new, c - 3, r)

    def body(g, _):
        for j in range(4):
            row(4 * g + j, g, j)
        return 0

    lax.fori_loop(0, chunk // 4, body, 0)


def modes_kernel(w_ref, ch_ref, cl_ref, mh_ref, ml_ref, ph_ref, pl_ref, out_ref, x_ref, *, turned):
    dot = functools.partial(jnp.dot, preferred_element_type=jnp.float32)
    planes, band, nx = out_ref.shape[1:]

    def gathered(part):
        if turned:
            x = jnp.concatenate([w_ref[part, z] for z in range(planes)], axis=0)
        else:
            width = w_ref.shape[3]
            for s in range(w_ref.shape[0]):
                for z in range(planes):
                    x_ref[z * band : (z + 1) * band, s * width : (s + 1) * width] = w_ref[s, part, z].T
            x = x_ref[...]
        return x

    def split(x):
        high = x.astype(jnp.bfloat16)
        return high, (x - high.astype(jnp.float32)).astype(jnp.bfloat16)

    re, im = gathered(0), gathered(1)
    times = lambda x, h, l: dot(x[0], h[...]) + dot(x[0], l[...]) + dot(x[1], h[...])
    scale = 1.0 / math.sqrt(NX * nx)
    shape = (band, nx)
    ky = lax.broadcasted_iota(jnp.int32, shape, 0) + lax.axis_index("xy") * band
    kx = lax.broadcasted_iota(jnp.int32, shape, 1)
    keep = jnp.where((ky == 0) & (kx == 0), 0.0, scale)
    both = times(split(re + im), ch_ref, cl_ref)
    out_re = both - times(split(im), mh_ref, ml_ref)
    out_im = both - times(split(re), ph_ref, pl_ref)
    for z in range(planes):
        out_ref[0, z] = out_re[z * band : (z + 1) * band] * keep
        out_ref[1, z] = out_im[z * band : (z + 1) * band] * keep


def cost(flops, bytes_accessed):
    return pl.CostEstimate(flops=int(flops), bytes_accessed=int(bytes_accessed), transcendentals=0)


def tables(size):
    angle = (np.outer(np.arange(size), np.arange(size)) % size) * (2.0 * np.pi / size)
    cosine, sine = np.cos(angle), np.sin(angle)
    result = []
    for table in (cosine, sine, cosine - sine, cosine + sine):
        high = table.astype(np.float32).astype(ml_dtypes.bfloat16)
        low = (table - high.astype(np.float64)).astype(np.float32).astype(ml_dtypes.bfloat16)
        result += [high, low]
    return result


def row_order(half):
    matrix = np.zeros((8 * half, 8 * half), np.float32)
    for z in range(4):
        for h in range(2):
            for p in range(half):
                matrix[(z * 2 + h) * half + p, p * 8 + h * 4 + z] = 1.0
    return matrix.astype(ml_dtypes.bfloat16)


def shift(block, axis, step):
    n = lax.axis_size(axis)
    return lax.ppermute(block, axis, [(i, (i + step) % n) for i in range(n)])


def on_device(density, momentum, magnetic, arm_potential, sn_cells, sn_counts):
    rows, planes, ny = density.shape
    half = rows // 2
    layers, across = lax.axis_size("gz"), lax.axis_size("xy")
    devices = layers * across
    tile_row, tile_plane = lax.axis_index("xy"), lax.axis_index("gz")
    field = rows * planes * ny
    f32 = jnp.float32
    shape = jax.ShapeDtypeStruct
    whole = pl.BlockSpec(memory_space=pltpu.VMEM)
    smem = pl.BlockSpec(memory_space=pltpu.SMEM)
    params = pltpu.CompilerParams(vmem_limit_bytes=VMEM)
    message = shape((2, half, planes, ny), f32)
    tile = shape((half, 8, ny), f32)
    steps = half // 8
    counts = (steps * 5 // 8, steps - steps * 5 // 8) if steps >= 2 else (steps,)

    slots_here = sn_cells.shape[0]
    rho = density.reshape(2, half, planes, ny)
    mom = momentum.reshape(3, 2, half, planes, ny)
    mag = magnetic.reshape(3, 2, half, planes, ny)

    pot = arm_potential.reshape(2, half, ny)
    edges = shape((8, 2, planes, ny), f32)
    mine = shape((devices, 1, -(-4 * slots_here // 128) * 128), jnp.int32)
    full = lambda s: pl.BlockSpec(s, lambda i: (0,) * len(s))
    mine, first_rows, last_rows = pl.pallas_call(
        first_kernel,
        grid=(1,),
        in_specs=[smem, smem] + [
            spec
            for h, k in ((0, 0), (1, half // 2 - 1))
            for spec in (
                pl.BlockSpec((1, 2, planes, ny), lambda i, h=h, k=k: (h, k, 0, 0)),
                pl.BlockSpec((3, 1, 2, planes, ny), lambda i, h=h, k=k: (0, h, k, 0, 0)),
                pl.BlockSpec((3, 1, 2, planes, ny), lambda i, h=h, k=k: (0, h, k, 0, 0)),
                pl.BlockSpec((8, ny), lambda i, h=h: (h * (rows // 8 - 1), 0)),
            )
        ],
        out_specs=[full(mine.shape)] + [full(edges.shape)] * 2,
        out_shape=[mine] + [edges] * 2,
        compiler_params=params,
        cost_estimate=cost(*PACK_COST),
        name="first",
    )(sn_cells, sn_counts, *[rho, mom, mag, arm_potential] * 2)
    events = lax.all_to_all(mine, ("gz", "xy"), split_axis=0, concat_axis=0, tiled=True)
    before, after = shift(last_rows, "xy", 1), shift(first_rows, "xy", -1)

    some = math.gcd(half, 32)
    up, down = pl.pallas_call(
        pack_kernel,
        grid=(half // some,),
        in_specs=[pl.BlockSpec((2, some, planes, ny), lambda i: (0, i, 0, 0))] + [
            pl.BlockSpec((1, 2, some, planes, ny), lambda i, f=f: (f, 0, i, 0, 0)) for f in (2,)
        ] + [pl.BlockSpec(memory_space=pl.ANY)],
        out_specs=[pl.BlockSpec((some // 4, 3, 8, ny), lambda i: (i, 0, 0, 0))] * 2,
        out_shape=[shape((half // 4, 3, 8, ny), f32)] * 2,
        compiler_params=params,
        cost_estimate=cost(*PACK_COST),
        name="pack",
    )(rho, mom, mine)
    below_a, above_a = shift(up, "gz", 1), shift(down, "gz", -1)

    parcels = [shape((n, 20, 8, ny), f32) for n in counts]
    side = pltpu.VMEM((half + 8, 8, ny), f32)
    begins = [sum(counts[:i]) for i in range(len(counts))]
    parcel = pl.BlockSpec((1, 20, 8, ny), lambda i: (jnp.minimum(i, counts[0] - 1), 0, 0, 0))
    eight = pl.BlockSpec((8, 8, ny), lambda i: (i, 0, 0))
    middle = [
        spec
        for h, k in ((0, steps - 1), (1, 0))
        for spec in (
            pl.BlockSpec((1, 2, planes, ny), lambda i, h=h, k=k: (h, k * 4 + 3 * (1 - h), 0, 0)),
            pl.BlockSpec((3, 1, 2, planes, ny), lambda i, h=h, k=k: (0, h, k * 4 + 3 * (1 - h), 0, 0)),
            pl.BlockSpec((3, 1, 2, planes, ny), lambda i, h=h, k=k: (0, h, k * 4 + 3 * (1 - h), 0, 0)),
            pl.BlockSpec((1, 8, ny), lambda i, h=h, k=k: (h, k, 0)),
        )
    ]
    rows_of = lambda n: pl.BlockSpec((n, 2, 8, planes, ny), lambda i: (0, 0, i, 0, 0))
    state, edge, sb, sa, up_0, down_0 = pl.pallas_call(
        functools.partial(state_kernel, depth=planes * layers, count=counts[0], per_device=slots_here, steps=steps),
        grid=(steps,),
        in_specs=[
            smem, pl.BlockSpec((2, 8, planes, ny), lambda i: (0, i, 0, 0)), rows_of(3), rows_of(3),
            pl.BlockSpec((2, 8, ny), lambda i: (0, i, 0)), full(edges.shape), full(edges.shape),
        ] + middle,
        out_specs=[pl.BlockSpec((8, 8, 8, ny), lambda i: (0, i, 0, 0)), full((8, 4, 8, ny)), eight, eight, parcel, parcel],
        out_shape=[shape((8, half, 8, ny), f32), shape((8, 4, 8, ny), f32), tile, tile, parcels[0], parcels[0]],
        scratch_shapes=[pltpu.VMEM((4, half + 8, 8, ny), f32), side, side],
        compiler_params=params,
        cost_estimate=cost(*STATE_COST),
        name="state",
    )(events, rho, mom, mag, pot, before, after, *[rho, mom, mag, pot] * 2)
    parcels_below, parcels_above = [shift(up_0, "gz", 1)], [shift(down_0, "gz", -1)]

    cos_high, cos_low, sin_high, sin_low = tables(ny)[:4]
    turns = tables(NX)
    band = ny // across
    turned = band % 128 != 0 or rows % 128 != 0
    hbm = pl.BlockSpec(memory_space=pl.ANY)
    more = parcels[1:] * 2
    new_density, wave, rho_halo, mz_halo, *messages = pl.pallas_call(
        density_kernel,
        in_specs=[hbm, hbm] + [whole] * 7,
        out_specs=[whole] * (4 + len(more)),
        out_shape=[message, shape((across, 2, planes, rows, band), f32), tile, tile, *more],
        scratch_shapes=[
            pltpu.VMEM((8 * half, ny), f32), pltpu.VMEM((4, half + 4, 8, ny), f32),
            pltpu.VMEM((3, counts[-1] * 8, 8, ny), f32), pltpu.SemaphoreType.DMA((4,)),
        ],
        compiler_params=params,
        cost_estimate=cost(*DENSITY_COST),
        name="density",
    )(
        state, edge, below_a, above_a, sb, sa, row_order(half),
        np.stack([cos_high, -sin_high]), np.stack([cos_low, -sin_low]),
    )

    if messages:
        parcels_below.append(shift(messages[0], "gz", 1))
        parcels_above.append(shift(messages[1], "gz", -1))
    portion = lax.all_to_all(wave, "xy", split_axis=0, concat_axis=0, tiled=True)
    if turned:
        portion = portion.transpose(1, 2, 4, 0, 3).reshape(2, planes, band, NX)
    modes = pl.pallas_call(
        functools.partial(modes_kernel, turned=turned),
        in_specs=[whole] * 7,
        out_specs=whole,
        out_shape=shape((2, planes, band, NX), f32),
        scratch_shapes=[pltpu.VMEM((planes * band, NX), f32)],
        compiler_params=params,
        cost_estimate=cost(*MODES_COST),
        name="modes",
    )(portion, *turns[:2], *turns[4:])
    results = [shape((3, 2, half, planes, ny), f32)] * 2
    three = lambda b: pl.BlockSpec((3, 2, 8, planes, ny), lambda k: (0, 0, b + k, 0, 0))
    here = lambda b: pl.BlockSpec((8, 8, ny), lambda k: (b + k, 0, 0))
    parcel = pl.BlockSpec((1, 20, 8, ny), lambda k: (k, 0, 0, 0))
    wide = pltpu.CompilerParams(vmem_limit_bytes=62 * 1024 * 1024)

    def main(i, inner, name, *new):
        n, b = counts[i], begins[i]
        halos = [hbm] * 4 if inner else [here(b)] * 2 + [parcel] * 2
        parts = (rho_halo, mz_halo) if inner else (parcels_below[i], parcels_above[i])
        return pl.pallas_call(
            functools.partial(main_kernel, first=b * 8, inner=inner),
            grid=(n,),
            in_specs=[hbm, hbm] + halos + [hbm] * len(new),
            out_specs=[three(b), three(b)],
            out_shape=results,
            scratch_shapes=[
                pltpu.VMEM((8, n * 8 + 4, 8, ny), f32), pltpu.VMEM((5, n * 8 + 4, 8, ny), f32),
                pltpu.SemaphoreType.DMA((n + 2,)),
            ],
            input_output_aliases={6: 0, 7: 1} if new else {},
            compiler_params=wide,
            cost_estimate=cost(*MAIN_COST),
            name=name,
        )(state, edge, rho_halo, mz_halo, *parts, *new)

    if len(counts) == 1:
        new = main(0, False, "main0")
    else:
        new = main(0, False, "main0", *main(1, True, "inner1"))
        n, b = counts[1], begins[1]
        new = pl.pallas_call(
            halo_kernel,
            grid=(n,),
            in_specs=[here(b)] * 2 + [parcel] * 2 + [three(b)] * 2 + [hbm],
            out_specs=[three(b)] * 2,
            out_shape=results,
            input_output_aliases={4: 0, 5: 1},
            compiler_params=wide,
            cost_estimate=cost(*MAIN_COST),
            name="halo1",
        )(rho_halo, mz_halo, parcels_below[1], parcels_above[1], *new, modes)
    new_mom, new_mag = new

    return (
        new_density.reshape(rows, planes, ny),
        new_mom.reshape(3, rows, planes, ny),
        new_mag.reshape(3, rows, planes, ny),
        modes,
    )


def solution(mesh):
    in_specs = (
        P("xy", "gz", None),
        P(None, "xy", "gz", None),
        P(None, "xy", "gz", None),
        P("xy", None),
        P(("gz", "xy"), None),
        P(("gz", "xy")),
    )
    out_specs = (
        P("xy", "gz", None),
        P(None, "xy", "gz", None),
        P(None, "xy", "gz", None),
        P(None, "gz", "xy", None),
    )
    return jax.shard_map(
        on_device, mesh=mesh, in_specs=in_specs, out_specs=out_specs, check_vma=False
    )
```
